32 devices in a mesh: dp: 8 (over z, x), seq: 4 (over y, core).
Axes of the slice: x: 2, y: 2, z: 4, core: 2. Of those that a mesh axis runs over, the one named last changes fastest.
Arguments:
- hidden_in: bfloat16 [16384, 576], P(('dp', 'seq')), may hold values from -6 to 6
- span_order: int32 [128], P(('dp', 'seq')), may hold values from 0 to 3, as said below
- attention_norm_gain: bfloat16 [576], replicated, may hold values from 0.5 to 1.5
- query_weight: bfloat16 [331776], P(('dp', 'seq')), may hold values from -0.5 to 0.5
- key_weight: bfloat16 [110592], P(('dp', 'seq')), may hold values from -0.25 to 0.25
- value_weight: bfloat16 [110592], P(('dp', 'seq')), may hold values from -0.25 to 0.25
- output_weight: bfloat16 [331776], P(('dp', 'seq')), may hold values from -2 to 2
- feedforward_gain: bfloat16 [576], replicated, may hold values from 0.5 to 1.5
- gate_weight: bfloat16 [884736], P(('dp', 'seq')), may hold values from -0.25 to 0.25
- up_weight: bfloat16 [884736], P(('dp', 'seq')), may hold values from -0.25 to 0.25
- down_weight: bfloat16 [884736], P(('dp', 'seq')), may hold values from -0.15625 to 0.15625
- out_grad: bfloat16 [16384, 576], P(('dp', 'seq')), may hold values from -6 to 6
Outputs:
- hidden_out: bfloat16 [16384, 576], P(('dp', 'seq'))
- hidden_grad: bfloat16 [16384, 576], P(('dp', 'seq'))
- attn_gain_grad: float32 [576], replicated
- w_query_grad: float32 [331776], P(('dp', 'seq'))
- w_key_grad: float32 [110592], P(('dp', 'seq'))
- w_value_grad: float32 [110592], P(('dp', 'seq'))
- w_out_grad: float32 [331776], P(('dp', 'seq'))
- ffn_gain_grad: float32 [576], replicated
- w_gate_grad: float32 [884736], P(('dp', 'seq'))
- w_up_grad: float32 [884736], P(('dp', 'seq'))
- w_down_grad: float32 [884736], P(('dp', 'seq'))
The draws below stay inside these ranges and needn't reach their ends.
Inputs may be any that keep to these rules, and one draw needn't show every extreme that they name: `span_order`: for each micro-batch and each group of 4 devices along seq that share a dp index, that micro-batch's entries on those devices are a permutation of 0 to 3.
All inputs are finite; a program needn't handle non-finite values.
Results may differ from the reference program's by a relative error of at most 0.015.
The reference program's roundings to bfloat16 on the way count: a program that leaves them out, or rounds other values in their place, can miss the bound.
Values may be sent and summed in bfloat16 or wider, within the bound.
No kernel may reach another device: no remote copies, remote signals or barrier semaphores. Data moves between devices by JAX's collectives and lax.ppermute only.
A program may use at most 128 MiB of HBM per device.

```python
import math
import jax
import jax.numpy as jnp
from jax import lax

MODEL_WIDTH = 576
QUERY_HEADS = 9
KEY_VALUE_HEADS = 3
HEAD_WIDTH = 64
HIDDEN_UNITS = 1536
SPAN = 128
MB = 4
SLOTS = 1
ROWS = 128
SEQ_LEN = 512
TOKENS = 16384
N_DP = 8
N_SEQ = 4


def draw_span_order(key, part):
    key = jax.random.fold_in(key, 7)
    sequence_keys = jax.random.split(key, N_DP * MB)
    orders = jax.vmap(lambda single: jax.random.permutation(single, N_SEQ * SLOTS))(sequence_keys)
    orders = orders.reshape(N_DP, MB, N_SEQ, SLOTS).transpose(0, 2, 1, 3)
    return orders.reshape(N_DP * N_SEQ * MB * SLOTS).astype(jnp.int32)


def level_of(key, extent, cuts, smallest, top_value):
    def one(axis_at, parts):
        heights = jax.random.uniform(jax.random.fold_in(jax.random.fold_in(key, 6), axis_at), (parts,), jnp.float32, smallest / len(cuts), top_value / len(cuts))
        return jnp.repeat(jnp.exp(heights), extent[axis_at] // parts).reshape((-1,) + (1,) * (len(extent) - axis_at - 1))

    loudness = one(*cuts[0])
    for cut in cuts[1:]:
        loudness = loudness * one(*cut)
    return loudness


def noise(key, dims, scale, most, pieces=(), kind=jnp.bfloat16):
    drawn = scale * jax.random.normal(key, dims, jnp.float32)
    if pieces:
        drawn = drawn * level_of(key, dims, pieces, -0.22, 0.18)
    return jnp.clip(drawn, -most, most).astype(kind)


def setup_inputs(seed: int = 0) -> dict:
    streams_of = jax.random.split(jax.random.key(seed), 13)
    hidden_in = noise(streams_of[0], (TOKENS, MODEL_WIDTH), 1.0, 6.0, ((0, 32),))
    span_order = draw_span_order(jax.random.fold_in(streams_of[12], 71), 0)
    attention_norm_gain = jnp.clip(1.0 + 0.1 * jax.random.normal(streams_of[2], (MODEL_WIDTH,), jnp.float32), 0.5, 1.5).astype(jnp.bfloat16)
    query_weight = noise(streams_of[3], (MODEL_WIDTH * QUERY_HEADS * HEAD_WIDTH,), (MODEL_WIDTH // 4) ** -0.5, 0.5, ((0, 32),))
    key_weight = noise(streams_of[4], (MODEL_WIDTH * KEY_VALUE_HEADS * HEAD_WIDTH,), MODEL_WIDTH ** -0.5, 0.25, ((0, 32),))
    value_weight = noise(streams_of[5], (MODEL_WIDTH * KEY_VALUE_HEADS * HEAD_WIDTH,), MODEL_WIDTH ** -0.5, 0.25, ((0, 32),))
    output_weight = noise(streams_of[6], (QUERY_HEADS * HEAD_WIDTH * MODEL_WIDTH,), (max(QUERY_HEADS * HEAD_WIDTH // 64, 2)) ** -0.5, 2.0, ((0, 32),))
    feedforward_gain = jnp.clip(1.0 + 0.1 * jax.random.normal(streams_of[7], (MODEL_WIDTH,), jnp.float32), 0.5, 1.5).astype(jnp.bfloat16)
    gate_weight = noise(streams_of[8], (MODEL_WIDTH * HIDDEN_UNITS,), MODEL_WIDTH ** -0.5, 0.25, ((0, 32),))
    up_weight = noise(streams_of[9], (MODEL_WIDTH * HIDDEN_UNITS,), MODEL_WIDTH ** -0.5, 0.25, ((0, 32),))
    down_weight = noise(streams_of[10], (HIDDEN_UNITS * MODEL_WIDTH,), HIDDEN_UNITS ** -0.5, 0.15625, ((0, 32),))
    out_grad = noise(streams_of[11], (TOKENS, MODEL_WIDTH), 1.0, 6.0, ((0, 32),))
    return {"hidden_in": hidden_in, "span_order": span_order, "attention_norm_gain": attention_norm_gain, "query_weight": query_weight, "key_weight": key_weight, "value_weight": value_weight, "output_weight": output_weight, "feedforward_gain": feedforward_gain, "gate_weight": gate_weight, "up_weight": up_weight, "down_weight": down_weight, "out_grad": out_grad}


EPSILON = 1e-05

@jax.custom_vjp
def lowered_state(v):
    return lax.optimization_barrier(v.astype(jnp.bfloat16)).astype(jnp.float32)

@jax.custom_vjp
def low_back(v):
    return v

def low_keep(v):
    return (lowered_state(v), None)

def low_pass(kept, grad):
    return (grad,)

def back_keep(v):
    return (v, None)

def back_low(kept, grad):
    return (lowered_state(grad),)
lowered_state.defvjp(low_keep, low_pass)
low_back.defvjp(back_keep, back_low)

def norm_rows(value_rows, gain_vec):
    factor = lax.rsqrt(lax.optimization_barrier(jnp.mean(value_rows * value_rows, axis=-1, keepdims=True)) + EPSILON)
    return value_rows * factor * gain_vec

def angle_tables(positions, head_size):
    frequency = jnp.exp(jnp.arange(head_size // 2, dtype=jnp.float32) * (-2.0 * math.log(10000.0) / head_size))
    angles = positions.astype(jnp.float32)[:, None] * frequency[None, :]
    angles = jnp.concatenate([angles, angles], axis=-1)[:, None, :]
    return (jnp.cos(angles), jnp.sin(angles))

def apply_rotation(value_rows, cosine_table, sine_values):
    half_size = value_rows.shape[-1] // 2
    turned = jnp.concatenate([-value_rows[..., half_size:], value_rows[..., :half_size]], axis=-1)
    return value_rows * cosine_table + turned * sine_values

def attend(query_rows, keys_after_rotation, value_rows, positions):
    sequence_length = query_rows.shape[0]
    block_length = math.gcd(sequence_length, 512)
    factor = 1.0 / math.sqrt(HEAD_WIDTH)
    highest = lax.Precision.HIGHEST

    def query_block(initial):
        row_block = lax.dynamic_slice_in_dim(query_rows, initial, block_length)
        row_place = lax.dynamic_slice_in_dim(positions, initial, block_length)
        raw_scores = jnp.einsum('qkgd,skd->kgqs', row_block, keys_after_rotation, precision=highest)
        scores = low_back(raw_scores * factor)
        scores = jnp.where(row_place[:, None] >= positions[None, :], scores, -1e+30)
        layer_weights = jax.nn.softmax(scores, axis=-1)
        return jnp.einsum('kgqs,skd->qkgd', lowered_state(layer_weights), value_rows, precision=highest)
    starts = jnp.arange(sequence_length // block_length, dtype=jnp.int32) * block_length
    mixed = lax.map(jax.checkpoint(query_block), starts)
    return mixed.reshape(sequence_length, QUERY_HEADS * HEAD_WIDTH)

def decoder_layer(layer_input, positions, attention_norm_gain, query_weight, key_weight, value_weight, output_weight, feedforward_gain, gate_weight, up_weight, down_weight):
    sequence_length = layer_input.shape[0]
    highest = lax.Precision.HIGHEST
    query_group_width = QUERY_HEADS // KEY_VALUE_HEADS
    normed = lowered_state(norm_rows(layer_input, attention_norm_gain))
    query_rows = low_back(jnp.dot(normed, query_weight, precision=highest))
    unrotated_keys = low_back(jnp.dot(normed, key_weight, precision=highest))
    value_rows = lowered_state(low_back(jnp.dot(normed, value_weight, precision=highest)))
    cosine_table, sine_values = angle_tables(positions, HEAD_WIDTH)
    query_rows = lowered_state(apply_rotation(query_rows.reshape(sequence_length, QUERY_HEADS, HEAD_WIDTH), cosine_table, sine_values)).reshape(sequence_length, KEY_VALUE_HEADS, query_group_width, HEAD_WIDTH)
    keys_after_rotation = lowered_state(apply_rotation(unrotated_keys.reshape(sequence_length, KEY_VALUE_HEADS, HEAD_WIDTH), cosine_table, sine_values))
    value_rows = value_rows.reshape(sequence_length, KEY_VALUE_HEADS, HEAD_WIDTH)
    merged = lowered_state(low_back(attend(query_rows, keys_after_rotation, value_rows, positions)))
    middle = layer_input + low_back(jnp.dot(merged, output_weight, precision=highest))
    normed_two = lowered_state(norm_rows(middle, feedforward_gain))
    gate_act = low_back(jnp.dot(normed_two, gate_weight, precision=highest))
    upward = low_back(jnp.dot(normed_two, up_weight, precision=highest))
    hidden = lowered_state(jax.nn.silu(gate_act) * upward)
    return middle + low_back(jnp.dot(hidden, down_weight, precision=highest))

def reference(hidden_in, span_order, attention_norm_gain, query_weight, key_weight, value_weight, output_weight, feedforward_gain, gate_weight, up_weight, down_weight, out_grad):
    layer_weights = (attention_norm_gain.astype(jnp.float32), query_weight.astype(jnp.float32).reshape(MODEL_WIDTH, QUERY_HEADS * HEAD_WIDTH), key_weight.astype(jnp.float32).reshape(MODEL_WIDTH, KEY_VALUE_HEADS * HEAD_WIDTH), value_weight.astype(jnp.float32).reshape(MODEL_WIDTH, KEY_VALUE_HEADS * HEAD_WIDTH), output_weight.astype(jnp.float32).reshape(QUERY_HEADS * HEAD_WIDTH, MODEL_WIDTH), feedforward_gain.astype(jnp.float32), gate_weight.astype(jnp.float32).reshape(MODEL_WIDTH, HIDDEN_UNITS), up_weight.astype(jnp.float32).reshape(MODEL_WIDTH, HIDDEN_UNITS), down_weight.astype(jnp.float32).reshape(HIDDEN_UNITS, MODEL_WIDTH))
    span_ids = span_order.reshape(N_DP, N_SEQ, MB, SLOTS).transpose(0, 2, 1, 3).reshape(N_DP * MB, N_SEQ * SLOTS)
    offsets = jnp.arange(SPAN, dtype=jnp.int32)
    positions = (span_ids[:, :, None] * SPAN + offsets[None, None, :]).reshape(N_DP * MB, SEQ_LEN).astype(jnp.int32)

    def arrange(source):
        return source.astype(jnp.float32).reshape(N_DP, N_SEQ, MB, ROWS, MODEL_WIDTH).transpose(0, 2, 1, 3, 4).reshape(N_DP * MB, SEQ_LEN, MODEL_WIDTH)

    def restore(source):
        return source.reshape(N_DP, MB, N_SEQ, ROWS, MODEL_WIDTH).transpose(0, 2, 1, 3, 4).reshape(N_DP * N_SEQ * MB * ROWS, MODEL_WIDTH)

    def one_sequence(totals, sequence_parts):
        layer_input, places, cotangent = sequence_parts

        def layer_fn(layer_arg, *params):
            return decoder_layer(layer_arg, places, *params)
        result, pullback = jax.vjp(layer_fn, layer_input, *layer_weights)
        pulled = pullback(cotangent)
        totals = tuple((running + grad_term for running, grad_term in zip(totals, pulled[1:])))
        return (totals, (result.astype(jnp.bfloat16), pulled[0].astype(jnp.bfloat16)))
    initial = tuple((jnp.zeros_like(weight) for weight in layer_weights))
    totals, (outputs, in_grads) = lax.scan(one_sequence, initial, (arrange(hidden_in), positions, arrange(out_grad)))
    return (restore(outputs), restore(in_grads), totals[0], totals[1].reshape(-1), totals[2].reshape(-1), totals[3].reshape(-1), totals[4].reshape(-1), totals[5], totals[6].reshape(-1), totals[7].reshape(-1), totals[8].reshape(-1))
```

```python
import math

import jax
import jax.numpy as jnp
from jax import lax
from jax.experimental import pallas as pl
from jax.experimental.pallas import tpu as pltpu
from jax.sharding import PartitionSpec as P

MODEL_WIDTH = 576
QUERY_HEADS = 9
KEY_VALUE_HEADS = 3
HEAD_WIDTH = 64
HIDDEN_UNITS = 1536
SPAN = 128
MB = 4
SLOTS = 1


EPSILON = 1e-05


def angle_tables(positions, head_size):
    frequency = jnp.exp(
        jnp.arange(head_size // 2, dtype=jnp.float32) * (-2.0 * math.log(10000.0) / head_size)
    )
    angles = positions.astype(jnp.float32)[:, None] * frequency[None, :]
    angles = jnp.concatenate([angles, angles], axis=-1)[:, None, :]
    return (jnp.cos(angles), jnp.sin(angles))


def apply_rotation(value_rows, cosine_table, sine_values):
    half_size = value_rows.shape[-1] // 2
    turned = jnp.concatenate([-value_rows[..., half_size:], value_rows[..., :half_size]], axis=-1)
    return value_rows * cosine_table + turned * sine_values


def product(first_arg, second_arg):
    return jnp.dot(first_arg, second_arg, preferred_element_type=jnp.float32)


def inner_rows(first_arg, second_arg):
    return lax.dot_general(
        first_arg, second_arg, (((0,), (0,)), ((), ())), preferred_element_type=jnp.float32
    )


def inner_cols(first_arg, second_arg):
    return lax.dot_general(
        first_arg, second_arg, (((1,), (1,)), ((), ())), preferred_element_type=jnp.float32
    )


def shape_weights(flattened_rows):
    return (
        flattened_rows[0].reshape(MODEL_WIDTH, QUERY_HEADS * HEAD_WIDTH),
        flattened_rows[1].reshape(MODEL_WIDTH, KEY_VALUE_HEADS * HEAD_WIDTH),
        flattened_rows[2].reshape(MODEL_WIDTH, KEY_VALUE_HEADS * HEAD_WIDTH),
        flattened_rows[3].reshape(QUERY_HEADS * HEAD_WIDTH, MODEL_WIDTH),
        flattened_rows[4].reshape(MODEL_WIDTH, HIDDEN_UNITS),
        flattened_rows[5].reshape(MODEL_WIDTH, HIDDEN_UNITS),
        flattened_rows[6].reshape(HIDDEN_UNITS, MODEL_WIDTH),
    )


def block_scores(query_rows, key_block, query_place, key_place, factor):
    raw_scores = (
        jnp.einsum("qkgd,skd->kgqs", query_rows, key_block, preferred_element_type=jnp.float32)
        * factor
    )
    allowed = query_place[:, None] >= key_place[None, :]
    return jnp.where(allowed, raw_scores, -1e30)


def forward(layer_input, positions, span_ids, gain_pair, matrices):
    w_q, w_k, w_v, w_o, w_g, w_u, w_d = matrices
    count_of_rows = layer_input.shape[0]
    query_group_width = QUERY_HEADS // KEY_VALUE_HEADS
    factor = 1.0 / math.sqrt(HEAD_WIDTH)
    input_full = layer_input.astype(jnp.float32)
    scale_one = lax.rsqrt(jnp.mean(input_full * input_full, axis=-1, keepdims=True) + EPSILON)
    unit_one = input_full * scale_one
    normed = (unit_one * gain_pair[0]).astype(jnp.bfloat16)
    query_rows = product(normed, w_q)
    unrotated_keys = product(normed, w_k)
    value_rows = product(normed, w_v)
    cosine_table, sine_values = angle_tables(positions, HEAD_WIDTH)
    rotated_query = apply_rotation(
        query_rows.reshape(count_of_rows, QUERY_HEADS, HEAD_WIDTH), cosine_table, sine_values
    ).astype(jnp.bfloat16)
    rotated_query = rotated_query.reshape(
        count_of_rows, KEY_VALUE_HEADS, query_group_width, HEAD_WIDTH
    )
    rotated_key = apply_rotation(
        unrotated_keys.reshape(count_of_rows, KEY_VALUE_HEADS, HEAD_WIDTH),
        cosine_table,
        sine_values,
    ).astype(jnp.bfloat16)
    rotated_key = rotated_key.reshape(count_of_rows, KEY_VALUE_HEADS * HEAD_WIDTH)
    v_low = value_rows.astype(jnp.bfloat16)
    every_key, every_value, key_spans = (
        lax.all_gather(rotated_key, "seq", axis=0, tiled=True),
        lax.all_gather(v_low, "seq", axis=0, tiled=True),
        lax.all_gather(span_ids.astype(jnp.bfloat16), "seq", axis=0, tiled=True),
    )
    offsets = jnp.arange(SPAN, dtype=jnp.int32)
    key_places = (key_spans.astype(jnp.int32)[:, None] * SPAN + offsets[None, :]).reshape(-1)
    count_of_keys = every_key.shape[0]
    block_length = math.gcd(count_of_keys, 512)
    count_of_blocks = count_of_keys // block_length
    blocks_of_keys = every_key.reshape(count_of_blocks, block_length, KEY_VALUE_HEADS, HEAD_WIDTH)
    blocks_of_values = every_value.reshape(
        count_of_blocks, block_length, KEY_VALUE_HEADS, HEAD_WIDTH
    )
    place_blocks = key_places.reshape(count_of_blocks, block_length)

    def softmax_stats(carry, piece_set):
        highest, totals = carry
        key_block, key_place = piece_set
        scores = block_scores(rotated_query, key_block, positions, key_place, factor)
        new_high = jnp.maximum(highest, jnp.max(scores, axis=-1))
        totals = totals * jnp.exp(highest - new_high) + jnp.sum(
            jnp.exp(scores - new_high[..., None]), axis=-1
        )
        return ((new_high, totals), None)

    initial = (
        jnp.full((KEY_VALUE_HEADS, query_group_width, count_of_rows), -1e30, jnp.float32),
        jnp.zeros((KEY_VALUE_HEADS, query_group_width, count_of_rows), jnp.float32),
    )
    (highest, totals), _ = lax.scan(softmax_stats, initial, (blocks_of_keys, place_blocks))

    def mix_values(running, piece_set):
        key_block, value_block, key_place = piece_set
        scores = block_scores(rotated_query, key_block, positions, key_place, factor)
        layer_weights = (jnp.exp(scores - highest[..., None]) / totals[..., None]).astype(
            jnp.bfloat16
        )
        return (
            running
            + jnp.einsum(
                "kgqs,skd->qkgd", layer_weights, value_block, preferred_element_type=jnp.float32
            ),
            None,
        )

    attention_output, _ = lax.scan(
        mix_values,
        jnp.zeros((count_of_rows, KEY_VALUE_HEADS, query_group_width, HEAD_WIDTH), jnp.float32),
        (blocks_of_keys, blocks_of_values, place_blocks),
    )
    attention_output = attention_output.reshape(count_of_rows, QUERY_HEADS * HEAD_WIDTH)
    merged = attention_output.astype(jnp.bfloat16)
    middle = input_full + product(merged, w_o)
    scale_two = lax.rsqrt(jnp.mean(middle * middle, axis=-1, keepdims=True) + EPSILON)
    unit_two = middle * scale_two
    normed_two = (unit_two * gain_pair[1]).astype(jnp.bfloat16)
    gate_act = product(normed_two, w_g)
    upward = product(normed_two, w_u)
    hidden = (jax.nn.silu(gate_act) * upward).astype(jnp.bfloat16)
    result = (middle + product(hidden, w_d)).astype(jnp.bfloat16)
    stored = (
        scale_one,
        unit_one,
        normed,
        cosine_table,
        sine_values,
        rotated_query,
        blocks_of_keys,
        blocks_of_values,
        place_blocks,
        highest,
        totals,
        attention_output,
        merged,
        scale_two,
        unit_two,
        normed_two,
        gate_act,
        upward,
        hidden,
    )
    return (result, stored)


def backward(cotangent, positions, gain_pair, matrices, stored):
    w_q, w_k, w_v, w_o, w_g, w_u, w_d = matrices
    (
        scale_one,
        unit_one,
        normed,
        cosine_table,
        sine_values,
        rotated_query,
        blocks_of_keys,
        blocks_of_values,
        place_blocks,
        highest,
        totals,
        attention_output,
        merged,
        scale_two,
        unit_two,
        normed_two,
        gate_act,
        upward,
        hidden,
    ) = stored
    count_of_rows = cotangent.shape[0]
    query_group_width = QUERY_HEADS // KEY_VALUE_HEADS
    factor = 1.0 / math.sqrt(HEAD_WIDTH)
    grad_down = inner_rows(hidden, cotangent)
    back_hidden = inner_cols(cotangent, w_d)
    sigmoid_gate = jax.nn.sigmoid(gate_act)
    back_gate = (
        back_hidden * upward * sigmoid_gate * (1.0 + gate_act * (1.0 - sigmoid_gate))
    ).astype(jnp.bfloat16)
    back_up = (back_hidden * (gate_act * sigmoid_gate)).astype(jnp.bfloat16)
    grad_gate = inner_rows(normed_two, back_gate)
    grad_up = inner_rows(normed_two, back_up)
    back_norm_two = inner_cols(back_gate, w_g) + inner_cols(back_up, w_u)
    gain_two = jnp.sum(back_norm_two * unit_two, axis=0)
    back_unit = back_norm_two * gain_pair[1]
    back_middle = cotangent.astype(jnp.float32) + scale_two * (
        back_unit - unit_two * jnp.mean(back_unit * unit_two, axis=-1, keepdims=True)
    )
    middle_low = back_middle.astype(jnp.bfloat16)
    grad_out = inner_rows(merged, middle_low)
    attention_backward = inner_cols(middle_low, w_o).astype(jnp.bfloat16)
    head_gradient_rows = attention_backward.reshape(
        count_of_rows, KEY_VALUE_HEADS, query_group_width, HEAD_WIDTH
    )
    attention_head_rows = attention_output.reshape(
        count_of_rows, KEY_VALUE_HEADS, query_group_width, HEAD_WIDTH
    )
    correction = jnp.transpose(
        jnp.sum(head_gradient_rows.astype(jnp.float32) * attention_head_rows, axis=-1), (1, 2, 0)
    )

    def score_grads(running, piece_set):
        key_block, value_block, key_place = piece_set
        scores = block_scores(rotated_query, key_block, positions, key_place, factor)
        probs = jnp.exp(scores - highest[..., None]) / totals[..., None]
        back_probs = jnp.einsum(
            "qkgd,skd->kgqs", head_gradient_rows, value_block, preferred_element_type=jnp.float32
        )
        back_scores = (probs * (back_probs - correction[..., None])).astype(jnp.bfloat16)
        running = (
            running
            + jnp.einsum(
                "kgqs,skd->qkgd", back_scores, key_block, preferred_element_type=jnp.float32
            )
            * factor
        )
        key_grad = (
            jnp.einsum(
                "kgqs,qkgd->skd", back_scores, rotated_query, preferred_element_type=jnp.float32
            )
            * factor
        )
        value_grad = jnp.einsum(
            "kgqs,qkgd->skd",
            probs.astype(jnp.bfloat16),
            head_gradient_rows,
            preferred_element_type=jnp.float32,
        )
        return (running, (key_grad, value_grad))

    back_query, (gradient_of_keys, gradient_of_values) = lax.scan(
        score_grads,
        jnp.zeros((count_of_rows, KEY_VALUE_HEADS, query_group_width, HEAD_WIDTH), jnp.float32),
        (blocks_of_keys, blocks_of_values, place_blocks),
    )
    count_of_keys = gradient_of_keys.shape[0] * gradient_of_keys.shape[1]
    local_keys, value_own = (
        lax.psum_scatter(
            gradient_of_keys.reshape(count_of_keys, KEY_VALUE_HEADS * HEAD_WIDTH).astype(
                jnp.bfloat16
            ),
            "seq",
            scatter_dimension=0,
            tiled=True,
        ).astype(jnp.float32),
        lax.psum_scatter(
            gradient_of_values.reshape(count_of_keys, KEY_VALUE_HEADS * HEAD_WIDTH).astype(
                jnp.bfloat16
            ),
            "seq",
            scatter_dimension=0,
            tiled=True,
        ).astype(jnp.float32),
    )
    query_low = (
        apply_rotation(
            back_query.reshape(count_of_rows, QUERY_HEADS, HEAD_WIDTH), cosine_table, -sine_values
        )
        .astype(jnp.bfloat16)
        .reshape(count_of_rows, QUERY_HEADS * HEAD_WIDTH)
    )
    key_low = (
        apply_rotation(
            local_keys.reshape(count_of_rows, KEY_VALUE_HEADS, HEAD_WIDTH),
            cosine_table,
            -sine_values,
        )
        .astype(jnp.bfloat16)
        .reshape(count_of_rows, KEY_VALUE_HEADS * HEAD_WIDTH)
    )
    value_low = value_own.astype(jnp.bfloat16)
    grad_query = inner_rows(normed, query_low)
    grad_key = inner_rows(normed, key_low)
    grad_value = inner_rows(normed, value_low)
    back_norm_one = (
        inner_cols(query_low, w_q) + inner_cols(key_low, w_k) + inner_cols(value_low, w_v)
    )
    gain_one = jnp.sum(back_norm_one * unit_one, axis=0)
    back_unit_one = back_norm_one * gain_pair[0]
    input_back = back_middle + scale_one * (
        back_unit_one - unit_one * jnp.mean(back_unit_one * unit_one, axis=-1, keepdims=True)
    )
    weight_terms = (grad_query, grad_key, grad_value, grad_out, grad_gate, grad_up, grad_down)
    return (input_back.astype(jnp.bfloat16), weight_terms, (gain_one, gain_two))


def on_device(
    hidden_in,
    span_order,
    attention_norm_gain,
    query_weight,
    key_weight,
    value_weight,
    output_weight,
    feedforward_gain,
    gate_weight,
    up_weight,
    down_weight,
    out_grad,
):
    count_of_rows = SLOTS * SPAN
    gain_pair = (attention_norm_gain.astype(jnp.float32), feedforward_gain.astype(jnp.float32))
    offsets = jnp.arange(SPAN, dtype=jnp.int32)
    weight_totals = (
        jnp.zeros((MODEL_WIDTH, QUERY_HEADS * HEAD_WIDTH), jnp.float32),
        jnp.zeros((MODEL_WIDTH, KEY_VALUE_HEADS * HEAD_WIDTH), jnp.float32),
        jnp.zeros((MODEL_WIDTH, KEY_VALUE_HEADS * HEAD_WIDTH), jnp.float32),
        jnp.zeros((QUERY_HEADS * HEAD_WIDTH, MODEL_WIDTH), jnp.float32),
        jnp.zeros((MODEL_WIDTH, HIDDEN_UNITS), jnp.float32),
        jnp.zeros((MODEL_WIDTH, HIDDEN_UNITS), jnp.float32),
        jnp.zeros((HIDDEN_UNITS, MODEL_WIDTH), jnp.float32),
    )
    gain_totals = (jnp.zeros((MODEL_WIDTH,), jnp.float32), jnp.zeros((MODEL_WIDTH,), jnp.float32))
    outputs = []
    input_grads = []
    for micro_index in range(MB):
        layer_input = hidden_in[micro_index * count_of_rows : (micro_index + 1) * count_of_rows]
        cotangent = out_grad[micro_index * count_of_rows : (micro_index + 1) * count_of_rows]
        span_ids = span_order[micro_index * SLOTS : (micro_index + 1) * SLOTS]
        positions = (span_ids[:, None] * SPAN + offsets[None, :]).reshape(count_of_rows)
        forward_weights = shape_weights(
            (
                lax.all_gather(query_weight, ("dp", "seq"), axis=0, tiled=True),
                lax.all_gather(key_weight, ("dp", "seq"), axis=0, tiled=True),
                lax.all_gather(value_weight, ("dp", "seq"), axis=0, tiled=True),
                lax.all_gather(output_weight, ("dp", "seq"), axis=0, tiled=True),
                lax.all_gather(gate_weight, ("dp", "seq"), axis=0, tiled=True),
                lax.all_gather(up_weight, ("dp", "seq"), axis=0, tiled=True),
                lax.all_gather(down_weight, ("dp", "seq"), axis=0, tiled=True),
            )
        )
        result, stored = forward(layer_input, positions, span_ids, gain_pair, forward_weights)
        backward_weights = shape_weights(
            (
                lax.all_gather(query_weight, ("dp", "seq"), axis=0, tiled=True),
                lax.all_gather(key_weight, ("dp", "seq"), axis=0, tiled=True),
                lax.all_gather(value_weight, ("dp", "seq"), axis=0, tiled=True),
                lax.all_gather(output_weight, ("dp", "seq"), axis=0, tiled=True),
                lax.all_gather(gate_weight, ("dp", "seq"), axis=0, tiled=True),
                lax.all_gather(up_weight, ("dp", "seq"), axis=0, tiled=True),
                lax.all_gather(down_weight, ("dp", "seq"), axis=0, tiled=True),
            )
        )
        input_back, weight_terms, gain_terms = backward(
            cotangent, positions, gain_pair, backward_weights, stored
        )
        weight_totals = tuple(
            (running + term for running, term in zip(weight_totals, weight_terms))
        )
        gain_totals = tuple((running + term for running, term in zip(gain_totals, gain_terms)))
        outputs.append(result)
        input_grads.append(input_back)
    grad_query, grad_key, grad_value, grad_out, grad_gate, grad_up, grad_down = weight_totals
    owned = (
        lax.psum_scatter(grad_query.reshape(-1), ("dp", "seq"), scatter_dimension=0, tiled=True),
        lax.psum_scatter(grad_key.reshape(-1), ("dp", "seq"), scatter_dimension=0, tiled=True),
        lax.psum_scatter(grad_value.reshape(-1), ("dp", "seq"), scatter_dimension=0, tiled=True),
        lax.psum_scatter(grad_out.reshape(-1), ("dp", "seq"), scatter_dimension=0, tiled=True),
        lax.psum_scatter(grad_gate.reshape(-1), ("dp", "seq"), scatter_dimension=0, tiled=True),
        lax.psum_scatter(grad_up.reshape(-1), ("dp", "seq"), scatter_dimension=0, tiled=True),
        lax.psum_scatter(grad_down.reshape(-1), ("dp", "seq"), scatter_dimension=0, tiled=True),
    )
    gain_one, gain_two = lax.psum((gain_totals[0], gain_totals[1]), ("dp", "seq"))
    return (
        jnp.concatenate(outputs, axis=0),
        jnp.concatenate(input_grads, axis=0),
        gain_one,
        owned[0],
        owned[1],
        owned[2],
        owned[3],
        gain_two,
        owned[4],
        owned[5],
        owned[6],
    )


FACTOR = 1.0 / math.sqrt(HEAD_WIDTH)
KV_WIDTH = KEY_VALUE_HEADS * HEAD_WIDTH
Q_WIDTH = QUERY_HEADS * HEAD_WIDTH
QK_WIDTH = Q_WIDTH + KV_WIDTH
LANES = 128
HALF_FFN = HIDDEN_UNITS // 2
FFN_BLOCK = 256


def vmem_params(megabytes=48):
    return pltpu.CompilerParams(vmem_limit_bytes=megabytes * 1024 * 1024)


def dot_nn(a, b):
    return jnp.dot(a, b, preferred_element_type=jnp.float32)


def dot_tn(a, b):
    return lax.dot_general(a, b, (((0,), (0,)), ((), ())), preferred_element_type=jnp.float32)


def dot_nt(a, b):
    return lax.dot_general(a, b, (((1,), (1,)), ((), ())), preferred_element_type=jnp.float32)


def low(v):
    return v.astype(jnp.bfloat16)


def place_back(v, place):
    high = low(v)
    rest = low(v - high.astype(jnp.float32))
    return dot_nt(high, place) + dot_nt(rest, place)


def half_turn(u, lane):
    return jnp.where(
        lane % HEAD_WIDTH < HEAD_WIDTH // 2,
        pltpu.roll(u, LANES - HEAD_WIDTH // 2, 1),
        pltpu.roll(u, HEAD_WIDTH // 2, 1),
    )


def padded_heads(blocks, head, lane):
    here = blocks[head // 2]
    moved = pltpu.roll(here, HEAD_WIDTH, 1)
    low_half, high_half = (here, moved) if head % 2 == 0 else (moved, here)
    zero = jnp.zeros_like(here)
    return (
        low(jnp.where(lane < HEAD_WIDTH, low_half, zero)),
        low(jnp.where(lane >= HEAD_WIDTH, high_half, zero)),
    )


def attend_kernel(
    spans, x0, x1, x2, x3, gain_one, gain_two, place, cosine, sine, wa, wa2, wb, wb2,
    x_out, normed_out, qk_out, kpad_out, vpad_out, lse_out, attn_out, merged_out, middle_out, normed_two_out,
    wqk, wov,
):
    rows = x_out.shape[0]
    half = wa.shape[0]
    for k, block in enumerate((x0, x1, x2, x3)):
        x_out[pl.ds(pl.multiple_of(spans[k] * SPAN, SPAN), SPAN), :] = block[...]
    wqk[:half] = wa[...]
    wqk[half:] = wa2[...]
    wov[:half] = wb[...]
    wov[half:] = wb2[...]
    x = x_out[...].astype(jnp.float32)
    scale = lax.rsqrt(jnp.mean(x * x, axis=-1, keepdims=True) + EPSILON)
    normed = low(x * scale * gain_one[...])
    normed_out[...] = low(dot_nn(normed, place[...]))
    lane = lax.broadcasted_iota(jnp.int32, (rows, LANES), 1)
    cos, sin = cosine[...], sine[...]
    k_blocks = []
    for b in range(QK_WIDTH // LANES):
        u = dot_nn(normed_out[...], wqk[:, b * LANES : (b + 1) * LANES])
        turned = u * cos + half_turn(u, lane) * sin
        turned = low(turned).astype(jnp.float32)
        if (b + 1) * LANES > Q_WIDTH:
            k_blocks.append(turned)
        if (b + 1) * LANES <= Q_WIDTH:
            turned = turned * FACTOR
        elif b * LANES < Q_WIDTH:
            turned = jnp.where(lane < Q_WIDTH - b * LANES, turned * FACTOR, turned)
        qk_out[:, b * LANES : (b + 1) * LANES] = low(turned)
    first_group = QUERY_HEADS - 2 * (Q_WIDTH // LANES)
    for j in range(KEY_VALUE_HEADS):
        lo, hi = padded_heads(k_blocks, j + first_group, lane)
        kpad_out[2 * j] = lo
        kpad_out[2 * j + 1] = hi
    v = dot_nn(normed_out[...], wov[:, MODEL_WIDTH:])
    v = low(v).astype(jnp.float32)
    v = jnp.concatenate([v, jnp.zeros((rows, HEAD_WIDTH), jnp.float32)], axis=1)
    v_blocks = [v[:, :LANES], v[:, LANES:]]
    for j in range(KEY_VALUE_HEADS):
        lo, hi = padded_heads(v_blocks, j, lane)
        vpad_out[2 * j] = lo
        vpad_out[2 * j + 1] = hi
    lane_q = lax.broadcasted_iota(jnp.int32, (SPAN, LANES), 1)
    diagonal = lax.broadcasted_iota(jnp.int32, (SPAN, SPAN), 0) >= lax.broadcasted_iota(
        jnp.int32, (SPAN, SPAN), 1
    )
    groups = QUERY_HEADS // KEY_VALUE_HEADS
    for i in range(rows // SPAN):
        here = slice(i * SPAN, (i + 1) * SPAN)
        lse = jnp.zeros((SPAN, LANES), jnp.float32)
        for b in range((QUERY_HEADS + 1) // 2):
            mixed = None
            for h in range(2 * b, min(2 * b + 2, QUERY_HEADS)):
                slot = 2 * (h // groups) + h % 2
                q = qk_out[here, b * LANES : (b + 1) * LANES]
                s = dot_nt(q, kpad_out[slot, : (i + 1) * SPAN, :])
                s_last = jnp.where(diagonal, s[:, i * SPAN :], -1e30)
                s = s_last if i == 0 else jnp.concatenate([s[:, : i * SPAN], s_last], axis=1)
                top = jnp.max(s, axis=-1, keepdims=True)
                p = jnp.exp(s - top)
                total = jnp.sum(p, axis=-1, keepdims=True)
                p = low(p * (1.0 / total))
                lse = jnp.where(lane_q == h, top + jnp.log(total), lse)
                part = dot_nn(p, vpad_out[slot, : (i + 1) * SPAN, :])
                mixed = part if mixed is None else mixed + part
            attn_out[here, b * LANES : (b + 1) * LANES] = mixed
        lse_out[here, :] = lse
    merged_out[...] = low(dot_nn(low(attn_out[:, :Q_WIDTH]), place[...]))
    middle = x_out[...].astype(jnp.float32) + dot_nn(merged_out[...], wov[:, :MODEL_WIDTH])
    middle_out[...] = middle
    scale_two = lax.rsqrt(jnp.mean(middle * middle, axis=-1, keepdims=True) + EPSILON)
    normed_two_out[...] = low(dot_nn(low(middle * scale_two * gain_two[...]), place[...]))


def place_down_kernel(me, own, other, out, sems, *, order):
    count = len(order)
    rows = out.shape[0] // count
    copies = []
    for slot, relative in enumerate(order):
        source = own if slot < count // 2 else other
        at = slot % (count // 2)
        target = pl.multiple_of((me[0] ^ relative) * rows, rows)
        copies.append(
            pltpu.make_async_copy(
                source.at[pl.ds(at * rows, rows), :], out.at[pl.ds(target, rows), :], sems.at[slot]
            )
        )
    for copy in copies:
        copy.start()
    for copy in copies:
        copy.wait()


def ffn_block(n2, og, wg, wu, wd, at, result, back_norm, dg_out, du_out, dd_out):
    columns = pl.ds(pl.multiple_of(at * FFN_BLOCK, FFN_BLOCK), FFN_BLOCK)
    half = dg_out[0].shape[0]
    w_gate, w_up, w_down = wg[:, columns], wu[:, columns], wd[columns, :]
    gate = dot_nn(n2, w_gate)
    up = dot_nn(n2, w_up)
    back_hidden = dot_nt(og, w_down)
    sigmoid = jax.nn.sigmoid(gate)
    silu = gate * sigmoid
    hidden = low(silu * up)
    back_gate = low(back_hidden * up * sigmoid * (1.0 + gate * (1.0 - sigmoid)))
    back_up = low(back_hidden * silu)
    dd_out[columns, :] = low(dot_tn(hidden, og))
    dg = low(dot_tn(n2, back_gate))
    du = low(dot_tn(n2, back_up))
    dg_out[0][:, columns] = dg[:half]
    dg_out[1][:, columns] = dg[half:]
    du_out[0][:, columns] = du[:half]
    du_out[1][:, columns] = du[half:]
    result[...] += dot_nn(hidden, w_down)
    back_norm[...] += dot_nt(back_gate, w_gate) + dot_nt(back_up, w_up)


def ffn_first_kernel(
    spans, o0, o1, o2, o3, n2, wg1, wg2, wu1, wu2, wd,
    og_out, result_out, back_out, dg1, dg2, du1, du2, dd,
    wg, wu,
):
    half = wg1.shape[0]
    for k, block in enumerate((o0, o1, o2, o3)):
        og_out[pl.ds(pl.multiple_of(spans[k] * SPAN, SPAN), SPAN), :] = block[...]
    wg[:half] = wg1[...]
    wg[half:] = wg2[...]
    wu[:half] = wu1[...]
    wu[half:] = wu2[...]
    result_out[...] = jnp.zeros_like(result_out)
    back_out[...] = jnp.zeros_like(back_out)

    @pl.loop(0, HALF_FFN // FFN_BLOCK)
    def _(at):
        ffn_block(
            n2[...], og_out[...], wg, wu, wd, at, result_out, back_out, (dg1, dg2), (du1, du2), dd
        )


def ffn_second_kernel(
    me, spans, og, n2, wg1, wg2, wu1, wu2, wd, result_in, back_in, dd_in, middle, gain_two, place,
    r0, r1, r2, r3, back_middle_out, gain_out, dg1, dg2, du1, du2, dd1, dd2,
    wg, wu, dd, result, back, *, order,
):
    half = wg1.shape[0]
    wg[:half] = wg1[...]
    wg[half:] = wg2[...]
    wu[:half] = wu1[...]
    wu[half:] = wu2[...]
    result[...] = result_in[...] + middle[...]
    back[...] = back_in[...]

    @pl.loop(0, HALF_FFN // FFN_BLOCK)
    def _(at):
        ffn_block(n2[...], og[...], wg, wu, wd, at, result, back, (dg1, dg2), (du1, du2), dd)

    count = len(order)
    rows = (dd_in.shape[0] + dd.shape[0]) // count
    for slot, relative in enumerate(order):
        owner = me[0] ^ relative
        target = dd1 if slot < count // 2 else dd2
        at = (slot % (count // 2)) * rows
        first = owner < count // 2

        @pl.when(first)
        def _():
            target[at : at + rows, :] = dd_in[pl.ds(pl.multiple_of(owner * rows, 16), rows), :]

        @pl.when(jnp.logical_not(first))
        def _():
            target[at : at + rows, :] = dd[
                pl.ds(pl.multiple_of((owner - count // 2) * rows, 16), rows), :
            ]

    for k, block in enumerate((r0, r1, r2, r3)):
        block[...] = low(result[pl.ds(pl.multiple_of(spans[k] * SPAN, SPAN), SPAN), :])
    mid = middle[...]
    scale = lax.rsqrt(jnp.mean(mid * mid, axis=-1, keepdims=True) + EPSILON)
    unit = mid * scale
    back_norm = place_back(back[...], place[...])
    gain_out[...] = jnp.sum(back_norm * unit, axis=0, keepdims=True)
    back_unit = back_norm * gain_two[...]
    back_middle_out[...] = og[...].astype(jnp.float32) + scale * (
        back_unit - unit * jnp.mean(back_unit * unit, axis=-1, keepdims=True)
    )


def attend_back_kernel(
    spans, x, normed, qk, kpad, vpad, lse, attn, merged, back_middle, gain_one, place, cosine, sine,
    wa, wa2, wb, wb2,
    g0, g1, g2, g3, gain_out, da1, da2, db1, db2,
    wqk, wov, ab, dqk, dv, grad,
):
    rows = x.shape[0]
    half = wa.shape[0]
    wqk[:half] = wa[...]
    wqk[half:] = wa2[...]
    wov[:half] = wb[...]
    wov[half:] = wb2[...]
    middle_low = low(back_middle[...])
    d_out = low(dot_tn(merged[...], middle_low))
    db1[:, :MODEL_WIDTH] = d_out[:half]
    db2[:, :MODEL_WIDTH] = d_out[half:]
    ab_chunks = low(dot_nt(middle_low, wov[:, :MODEL_WIDTH]))
    ab[:, :Q_WIDTH] = low(dot_nt(ab_chunks, place[...]))
    ab[:, Q_WIDTH:] = jnp.zeros((rows, ab.shape[1] - Q_WIDTH), jnp.bfloat16)
    terms = ab[...].astype(jnp.float32) * attn[...]
    mask = low(
        (
            lax.broadcasted_iota(jnp.int32, (16, terms.shape[1]), 1) // HEAD_WIDTH
            == lax.broadcasted_iota(jnp.int32, (16, terms.shape[1]), 0)
        ).astype(jnp.float32)
    )
    high = low(terms)
    correction = dot_nt(mask, high) + dot_nt(mask, low(terms - high.astype(jnp.float32)))
    lse_rows = jnp.transpose(lse[...])
    groups = QUERY_HEADS // KEY_VALUE_HEADS
    diagonal = lax.broadcasted_iota(jnp.int32, (SPAN, SPAN), 1) >= lax.broadcasted_iota(
        jnp.int32, (SPAN, SPAN), 0
    )
    lane = lax.broadcasted_iota(jnp.int32, (SPAN, LANES), 1)
    for i in range(rows // SPAN):
        keys = slice(i * SPAN, (i + 1) * SPAN)
        first = i * SPAN
        dk_sums = [None] * (2 * KEY_VALUE_HEADS)
        dv_sums = [None] * (2 * KEY_VALUE_HEADS)
        for b in range((QUERY_HEADS + 1) // 2):
            columns = slice(b * LANES, (b + 1) * LANES)
            q = qk[first:, columns]
            a = ab[first:, columns]
            dq = None
            for h in range(2 * b, min(2 * b + 2, QUERY_HEADS)):
                slot = 2 * (h // groups) + h % 2
                s = dot_nt(kpad[slot, keys, :], q)
                s = s - lse_rows[h : h + 1, first:]
                s_first = jnp.where(diagonal, s[:, :SPAN], -1e30)
                s = (
                    s_first
                    if first + SPAN == rows
                    else jnp.concatenate([s_first, s[:, SPAN:]], axis=1)
                )
                p = jnp.exp(s)
                dp = dot_nt(vpad[slot, keys, :], a)
                ds = low(p * (dp - correction[h : h + 1, first:]))
                dk = dot_nn(ds, q)
                dvh = dot_nn(low(p), a)
                dk_sums[slot] = dk if dk_sums[slot] is None else dk_sums[slot] + dk
                dv_sums[slot] = dvh if dv_sums[slot] is None else dv_sums[slot] + dvh
                part = dot_tn(ds, kpad[slot, keys, :])
                dq = part if dq is None else dq + part
            if i == 0:
                dqk[first:, columns] = dq
            else:
                dqk[first:, columns] += dq

        def both(sums, j):
            even, odd = sums[2 * j], sums[2 * j + 1]
            return even + pltpu.roll(odd, HEAD_WIDTH, 1)

        dk_heads = [both(dk_sums, j) for j in range(KEY_VALUE_HEADS)]
        dv_heads = [both(dv_sums, j) for j in range(KEY_VALUE_HEADS)]
        key_scale = 1.0 / FACTOR
        q_tail = dqk[keys, 4 * LANES : 5 * LANES]
        dqk[keys, 4 * LANES : 5 * LANES] = jnp.where(
            lane < HEAD_WIDTH, q_tail, pltpu.roll(dk_heads[0], HEAD_WIDTH, 1) * key_scale
        )
        dqk[keys, 5 * LANES :] = (
            jnp.where(lane < HEAD_WIDTH, dk_heads[1], pltpu.roll(dk_heads[2], HEAD_WIDTH, 1))
            * key_scale
        )
        dv[keys, :LANES] = low(
            jnp.where(lane < HEAD_WIDTH, dv_heads[0], pltpu.roll(dv_heads[1], HEAD_WIDTH, 1))
        )
        dv[keys, LANES:] = low(dv_heads[2])
    lane_all = lax.broadcasted_iota(jnp.int32, (rows, LANES), 1)
    cos, sin = cosine[...], sine[...]
    for b in range(QK_WIDTH // LANES):
        u = dqk[:, b * LANES : (b + 1) * LANES] * FACTOR
        grad[:, b * LANES : (b + 1) * LANES] = low(u * cos - half_turn(u, lane_all) * sin)
    d_qk = low(dot_tn(normed[...], grad[...]))
    da1[...] = d_qk[:half]
    da2[...] = d_qk[half:]
    dv_low = dv[:, :KV_WIDTH]
    d_v = low(dot_tn(normed[...], dv_low))
    db1[:, MODEL_WIDTH:] = d_v[:half]
    db2[:, MODEL_WIDTH:] = d_v[half:]
    back_chunks = dot_nt(grad[...], wqk[...]) + dot_nt(dv_low, wov[:, MODEL_WIDTH:])
    back_norm = place_back(back_chunks, place[...])
    xf = x[...].astype(jnp.float32)
    scale = lax.rsqrt(jnp.mean(xf * xf, axis=-1, keepdims=True) + EPSILON)
    unit = xf * scale
    gain_out[...] = jnp.sum(back_norm * unit, axis=0, keepdims=True)
    back_unit = back_norm * gain_one[...]
    dqk[:, :MODEL_WIDTH] = back_middle[...] + scale * (
        back_unit - unit * jnp.mean(back_unit * unit, axis=-1, keepdims=True)
    )
    for k, block in enumerate((g0, g1, g2, g3)):
        block[...] = low(
            dqk[pl.ds(pl.multiple_of(spans[k] * SPAN, SPAN), SPAN), :MODEL_WIDTH]
        )


VMEM_SPEC = pl.BlockSpec(memory_space=pltpu.VMEM)
SMEM_SPEC = pl.BlockSpec(memory_space=pltpu.SMEM)
ANY_SPEC = pl.BlockSpec(memory_space=pl.ANY)


def shaped(rows, columns, kind):
    return jax.ShapeDtypeStruct((rows, columns), kind)


def call(body, outs, args, scalars, scratch, flops, megabytes=48):
    return pl.pallas_call(
        body,
        out_shape=outs,
        in_specs=[SMEM_SPEC] * scalars + [VMEM_SPEC] * (len(args) - scalars),
        out_specs=[VMEM_SPEC] * len(outs),
        scratch_shapes=scratch,
        compiler_params=vmem_params(megabytes),
        cost_estimate=pl.CostEstimate(
            flops=int(flops), bytes_accessed=8_000_000, transcendentals=0
        ),
    )(*args)


def whole_sequence_plan(mesh):
    axes = ("dp", "seq")
    n_dp, n_seq = mesh.shape["dp"], mesh.shape["seq"]
    count = n_dp * n_seq
    bits = count.bit_length() - 1
    seq_bits = n_seq.bit_length() - 1
    core, y_bit = 0, 1
    x_bit = seq_bits
    z_bits = tuple(range(seq_bits + 1, bits))[::-1]
    order_bits = z_bits + (x_bit, y_bit, core)

    def swap(v, bit):
        return lax.ppermute(v, axes, [(d, d ^ (1 << bit)) for d in range(count)])

    def relative(slot):
        return sum(1 << bit for at, bit in enumerate(order_bits) if slot >> at & 1)

    order = tuple(relative(slot) for slot in range(count))

    def gather_z(v):
        for bit in z_bits:
            v = jnp.concatenate([v, swap(v, bit)], axis=0)
        return v

    def gather_xy(v, x_first):
        if x_first:
            v = jnp.concatenate([v, swap(v, x_bit)], axis=0)
            v = jnp.concatenate([v, swap(v, y_bit)], axis=0)
        else:
            size = v.shape[0]
            v = jnp.concatenate([v, swap(v, y_bit)], axis=0)
            w = swap(v, x_bit)
            v = jnp.concatenate([v[:size], w[:size], v[size:], w[size:]], axis=0)
        return v, swap(v, core)

    def gather_group(v):
        v = gather_z(v)
        half = v.shape[1] // 2
        return gather_xy(v[:, :half], True) + gather_xy(v[:, half:], False)

    def scatter_xy(keep, send, x_first):
        total = keep.astype(jnp.float32) + swap(send, core).astype(jnp.float32)
        size = total.shape[0] // 4
        if x_first:
            mine = jnp.concatenate([total[:size], total[2 * size : 3 * size]], axis=0)
            theirs = jnp.concatenate([total[size : 2 * size], total[3 * size :]], axis=0)
            total = mine + swap(low(theirs), x_bit).astype(jnp.float32)
            return total[:size] + swap(low(total[size:]), y_bit).astype(jnp.float32)
        total = total[: 2 * size] + swap(low(total[2 * size :]), y_bit).astype(jnp.float32)
        return total[:size] + swap(low(total[size:]), x_bit).astype(jnp.float32)

    def scatter_z(total):
        for bit in z_bits[::-1]:
            size = total.shape[0] // 2
            total = total[:size] + swap(low(total[size:]), bit).astype(jnp.float32)
        return total

    def scatter_group(a, b):
        total = jnp.concatenate([scatter_xy(*a, False), scatter_xy(*b, True)], axis=1)
        return scatter_z(total)

    def on_sequence_device(
        hidden_in, span_order, attention_norm_gain, query_weight, key_weight, value_weight,
        output_weight, feedforward_gain, gate_weight, up_weight, down_weight, out_grad,
    ):
        seq = lax.axis_index("seq")
        me = lax.axis_index("dp") * n_seq + seq
        rows = hidden_in.shape[0]
        model_rows = MODEL_WIDTH // count
        hidden_rows = HIDDEN_UNITS // count
        gain_one = attention_norm_gain.astype(jnp.float32).reshape(1, MODEL_WIDTH)
        gain_two = feedforward_gain.astype(jnp.float32).reshape(1, MODEL_WIDTH)

        def to_sequence(blocks, size):
            parts = [lax.dynamic_slice_in_dim(blocks, seq * size, size)]
            for k in range(1, n_seq):
                part = lax.dynamic_slice_in_dim(blocks, (seq ^ k) * size, size)
                parts.append(
                    lax.ppermute(part, "seq", [(d, d ^ k) for d in range(n_seq)])
                )
            return parts

        def from_sequence(parts):
            size = parts[0].shape[0]
            out = jnp.zeros((size * n_seq,) + parts[0].shape[1:], parts[0].dtype)
            for k, part in enumerate(parts):
                if k:
                    part = lax.ppermute(part, "seq", [(d, d ^ k) for d in range(n_seq)])
                out = lax.dynamic_update_slice_in_dim(out, part, (seq ^ k) * size, 0)
            return out

        x_parts = to_sequence(hidden_in, SPAN)
        spans = jnp.concatenate(to_sequence(span_order, 1))
        def rows_of(w, columns):
            return w.reshape(model_rows, columns)
        first = jnp.concatenate(
            [
                rows_of(query_weight, Q_WIDTH),
                rows_of(key_weight, KV_WIDTH),
                rows_of(output_weight, MODEL_WIDTH),
                rows_of(value_weight, KV_WIDTH),
            ],
            axis=1,
        )
        gate = rows_of(gate_weight, HIDDEN_UNITS)
        up = rows_of(up_weight, HIDDEN_UNITS)
        wa, wa2, wb, wb2 = gather_group(first)
        down = gather_z(down_weight.reshape(hidden_rows, MODEL_WIDTH))
        down, down2 = gather_xy(down, True)
        ffn_weights = [
            gather_group(
                jnp.concatenate(
                    [
                        gate[:, c * HALF_FFN : (c + 1) * HALF_FFN],
                        up[:, c * HALF_FFN : (c + 1) * HALF_FFN],
                    ],
                    axis=1,
                )
            )
            for c in range(2)
        ]
        o_parts = to_sequence(out_grad, SPAN)

        slots = jnp.asarray(order, jnp.int32)
        natural = (
            ((slots ^ me) * model_rows)[:, None] + jnp.arange(model_rows, dtype=jnp.int32)[None, :]
        ).reshape(-1)
        place = (jnp.arange(MODEL_WIDTH, dtype=jnp.int32)[:, None] == natural[None, :]).astype(
            jnp.bfloat16
        )
        cosine, sine = angle_tables(jnp.arange(rows, dtype=jnp.int32), HEAD_WIDTH)
        sign = jnp.where(jnp.arange(HEAD_WIDTH) < HEAD_WIDTH // 2, -1.0, 1.0)
        cosine = jnp.tile(cosine[:, 0, :], (1, 2))
        sine = jnp.tile(sine[:, 0, :] * sign, (1, 2))

        bf, f4 = jnp.bfloat16, jnp.float32
        half = MODEL_WIDTH // 2
        me_scalar = me.reshape(1).astype(jnp.int32)
        x, normed, qk, kpad, vpad, lse, attn, merged, middle, normed_two = call(
            attend_kernel,
            [
                shaped(rows, MODEL_WIDTH, bf),
                shaped(rows, MODEL_WIDTH, bf),
                shaped(rows, QK_WIDTH, bf),
                jax.ShapeDtypeStruct((2 * KEY_VALUE_HEADS, rows, LANES), bf),
                jax.ShapeDtypeStruct((2 * KEY_VALUE_HEADS, rows, LANES), bf),
                shaped(rows, LANES, f4),
                shaped(rows, 5 * LANES, f4),
                shaped(rows, Q_WIDTH, bf),
                shaped(rows, MODEL_WIDTH, f4),
                shaped(rows, MODEL_WIDTH, bf),
            ],
            [spans, *x_parts, gain_one, gain_two, place, cosine, sine, wa, wa2, wb, wb2],
            1,
            [pltpu.VMEM((MODEL_WIDTH, QK_WIDTH), bf), pltpu.VMEM((MODEL_WIDTH, QK_WIDTH), bf)],
            4e9,
        )
        w_down = pl.pallas_call(
            lambda *refs: place_down_kernel(*refs, order=order),
            out_shape=shaped(HIDDEN_UNITS, MODEL_WIDTH, bf),
            in_specs=[SMEM_SPEC, ANY_SPEC, ANY_SPEC],
            out_specs=ANY_SPEC,
            scratch_shapes=[pltpu.SemaphoreType.DMA((count,))],
            cost_estimate=pl.CostEstimate(flops=0, bytes_accessed=4_000_000, transcendentals=0),
        )(me_scalar, down, down2)
        pair = [shaped(half, HALF_FFN, bf)] * 2
        weight_scratch = [pltpu.VMEM((MODEL_WIDTH, HALF_FFN), bf)] * 2
        og, result, back, dg0, dg0s, du0, du0s, dd = call(
            ffn_first_kernel,
            [
                shaped(rows, MODEL_WIDTH, bf),
                shaped(rows, MODEL_WIDTH, f4),
                shaped(rows, MODEL_WIDTH, f4),
                *pair,
                *pair,
                shaped(HALF_FFN, MODEL_WIDTH, bf),
            ],
            [spans, *o_parts, normed_two, *ffn_weights[0], w_down[:HALF_FFN]],
            1,
            weight_scratch,
            6e9,
        )
        gu0 = scatter_group((dg0, dg0s), (du0, du0s))
        r0, r1, r2, r3, back_middle, gain_two_grad, dg1, dg1s, du1, du1s, dd1, dd1s = call(
            lambda *refs: ffn_second_kernel(*refs, order=order),
            [
                *[shaped(SPAN, MODEL_WIDTH, bf)] * 4,
                shaped(rows, MODEL_WIDTH, f4),
                shaped(1, MODEL_WIDTH, f4),
                *pair,
                *pair,
                *[shaped(HIDDEN_UNITS // 2, MODEL_WIDTH, bf)] * 2,
            ],
            [
                me_scalar, spans, og, normed_two, *ffn_weights[1], w_down[HALF_FFN:],
                result, back, dd, middle, gain_two, place,
            ],
            2,
            weight_scratch
            + [
                pltpu.VMEM((HALF_FFN, MODEL_WIDTH), bf),
                pltpu.VMEM((rows, MODEL_WIDTH), f4),
                pltpu.VMEM((rows, MODEL_WIDTH), f4),
            ],
            7e9,
        )
        gu1 = scatter_group((dg1, dg1s), (du1, du1s))
        down_grad = scatter_z(scatter_xy(dd1, dd1s, True))
        hidden_out = from_sequence([r0, r1, r2, r3])
        g0, g1, g2, g3, gain_one_grad, da, das, db, dbs = call(
            attend_back_kernel,
            [
                *[shaped(SPAN, MODEL_WIDTH, bf)] * 4,
                shaped(1, MODEL_WIDTH, f4),
                *[shaped(half, QK_WIDTH, bf)] * 4,
            ],
            [
                spans, x, normed, qk, kpad, vpad, lse, attn, merged, back_middle, gain_one, place,
                cosine, sine, wa, wa2, wb, wb2,
            ],
            1,
            [
                pltpu.VMEM((MODEL_WIDTH, QK_WIDTH), bf),
                pltpu.VMEM((MODEL_WIDTH, QK_WIDTH), bf),
                pltpu.VMEM((rows, 5 * LANES), bf),
                pltpu.VMEM((rows, QK_WIDTH), f4),
                pltpu.VMEM((rows, 2 * LANES), bf),
                pltpu.VMEM((rows, QK_WIDTH), bf),
            ],
            6e9,
        )
        qkov = scatter_group((da, das), (db, dbs))
        hidden_grad = from_sequence([g0, g1, g2, g3])
        gains = lax.psum(jnp.concatenate([gain_one_grad, gain_two_grad], axis=0), axes)
        gate_grad = jnp.concatenate([gu0[:, :HALF_FFN], gu1[:, :HALF_FFN]], axis=1)
        up_grad = jnp.concatenate([gu0[:, HALF_FFN:], gu1[:, HALF_FFN:]], axis=1)
        return (
            hidden_out,
            hidden_grad,
            gains[0],
            qkov[:, :Q_WIDTH].reshape(-1),
            qkov[:, Q_WIDTH:QK_WIDTH].reshape(-1),
            qkov[:, QK_WIDTH + MODEL_WIDTH :].reshape(-1),
            qkov[:, QK_WIDTH : QK_WIDTH + MODEL_WIDTH].reshape(-1),
            gains[1],
            gate_grad.reshape(-1),
            up_grad.reshape(-1),
            down_grad.reshape(-1),
        )

    return on_sequence_device


def pick_plan(mesh):
    count = mesh.shape["dp"] * mesh.shape["seq"]
    fits = (
        mesh.shape["seq"] == MB * SLOTS
        and SLOTS == 1
        and count & (count - 1) == 0
        and MODEL_WIDTH % count == 0
        and (HIDDEN_UNITS // count) % 16 == 0
    )
    return whole_sequence_plan(mesh) if fits else on_device


def solution(mesh):
    return jax.shard_map(
        pick_plan(mesh),
        mesh=mesh,
        in_specs=(
            P(("dp", "seq"), None),
            P(("dp", "seq")),
            P(),
            P(("dp", "seq")),
            P(("dp", "seq")),
            P(("dp", "seq")),
            P(("dp", "seq")),
            P(),
            P(("dp", "seq")),
            P(("dp", "seq")),
            P(("dp", "seq")),
            P(("dp", "seq"), None),
        ),
        out_specs=(
            P(("dp", "seq"), None),
            P(("dp", "seq"), None),
            P(),
            P(("dp", "seq")),
            P(("dp", "seq")),
            P(("dp", "seq")),
            P(("dp", "seq")),
            P(),
            P(("dp", "seq")),
            P(("dp", "seq")),
            P(("dp", "seq")),
        ),
        check_vma=False,
    )
```

```python
import functools
import math

import jax
import jax.numpy as jnp
import numpy as np
from jax import lax
from jax.experimental import pallas as pl
from jax.experimental.pallas import tpu as pltpu
from jax.sharding import PartitionSpec as P

MODEL_WIDTH = 576
QUERY_HEADS = 9
KEY_VALUE_HEADS = 3
HEAD_WIDTH = 64
HIDDEN_UNITS = 1536
SPAN = 128
MB = 4
SLOTS = 1


EPSILON = 1e-05


def angle_tables(positions, head_size):
    frequency = jnp.exp(
        jnp.arange(head_size // 2, dtype=jnp.float32) * (-2.0 * math.log(10000.0) / head_size)
    )
    angles = positions.astype(jnp.float32)[:, None] * frequency[None, :]
    angles = jnp.concatenate([angles, angles], axis=-1)[:, None, :]
    return (jnp.cos(angles), jnp.sin(angles))


def apply_rotation(value_rows, cosine_table, sine_values):
    half_size = value_rows.shape[-1] // 2
    turned = jnp.concatenate([-value_rows[..., half_size:], value_rows[..., :half_size]], axis=-1)
    return value_rows * cosine_table + turned * sine_values


def product(first_arg, second_arg):
    return jnp.dot(first_arg, second_arg, preferred_element_type=jnp.float32)


def inner_rows(first_arg, second_arg):
    return lax.dot_general(
        first_arg, second_arg, (((0,), (0,)), ((), ())), preferred_element_type=jnp.float32
    )


def inner_cols(first_arg, second_arg):
    return lax.dot_general(
        first_arg, second_arg, (((1,), (1,)), ((), ())), preferred_element_type=jnp.float32
    )


def shape_weights(flattened_rows):
    return (
        flattened_rows[0].reshape(MODEL_WIDTH, QUERY_HEADS * HEAD_WIDTH),
        flattened_rows[1].reshape(MODEL_WIDTH, KEY_VALUE_HEADS * HEAD_WIDTH),
        flattened_rows[2].reshape(MODEL_WIDTH, KEY_VALUE_HEADS * HEAD_WIDTH),
        flattened_rows[3].reshape(QUERY_HEADS * HEAD_WIDTH, MODEL_WIDTH),
        flattened_rows[4].reshape(MODEL_WIDTH, HIDDEN_UNITS),
        flattened_rows[5].reshape(MODEL_WIDTH, HIDDEN_UNITS),
        flattened_rows[6].reshape(HIDDEN_UNITS, MODEL_WIDTH),
    )


def block_scores(query_rows, key_block, query_place, key_place, factor):
    raw_scores = (
        jnp.einsum("qkgd,skd->kgqs", query_rows, key_block, preferred_element_type=jnp.float32)
        * factor
    )
    allowed = query_place[:, None] >= key_place[None, :]
    return jnp.where(allowed, raw_scores, -1e30)


def forward(layer_input, positions, span_ids, gain_pair, matrices):
    w_q, w_k, w_v, w_o, w_g, w_u, w_d = matrices
    count_of_rows = layer_input.shape[0]
    query_group_width = QUERY_HEADS // KEY_VALUE_HEADS
    factor = 1.0 / math.sqrt(HEAD_WIDTH)
    input_full = layer_input.astype(jnp.float32)
    scale_one = lax.rsqrt(jnp.mean(input_full * input_full, axis=-1, keepdims=True) + EPSILON)
    unit_one = input_full * scale_one
    normed = (unit_one * gain_pair[0]).astype(jnp.bfloat16)
    query_rows = product(normed, w_q)
    unrotated_keys = product(normed, w_k)
    value_rows = product(normed, w_v)
    cosine_table, sine_values = angle_tables(positions, HEAD_WIDTH)
    rotated_query = apply_rotation(
        query_rows.reshape(count_of_rows, QUERY_HEADS, HEAD_WIDTH), cosine_table, sine_values
    ).astype(jnp.bfloat16)
    rotated_query = rotated_query.reshape(
        count_of_rows, KEY_VALUE_HEADS, query_group_width, HEAD_WIDTH
    )
    rotated_key = apply_rotation(
        unrotated_keys.reshape(count_of_rows, KEY_VALUE_HEADS, HEAD_WIDTH),
        cosine_table,
        sine_values,
    ).astype(jnp.bfloat16)
    rotated_key = rotated_key.reshape(count_of_rows, KEY_VALUE_HEADS * HEAD_WIDTH)
    v_low = value_rows.astype(jnp.bfloat16)
    every_key, every_value, key_spans = (
        lax.all_gather(rotated_key, "seq", axis=0, tiled=True),
        lax.all_gather(v_low, "seq", axis=0, tiled=True),
        lax.all_gather(span_ids.astype(jnp.bfloat16), "seq", axis=0, tiled=True),
    )
    offsets = jnp.arange(SPAN, dtype=jnp.int32)
    key_places = (key_spans.astype(jnp.int32)[:, None] * SPAN + offsets[None, :]).reshape(-1)
    count_of_keys = every_key.shape[0]
    block_length = math.gcd(count_of_keys, 512)
    count_of_blocks = count_of_keys // block_length
    blocks_of_keys = every_key.reshape(count_of_blocks, block_length, KEY_VALUE_HEADS, HEAD_WIDTH)
    blocks_of_values = every_value.reshape(
        count_of_blocks, block_length, KEY_VALUE_HEADS, HEAD_WIDTH
    )
    place_blocks = key_places.reshape(count_of_blocks, block_length)

    def softmax_stats(carry, piece_set):
        highest, totals = carry
        key_block, key_place = piece_set
        scores = block_scores(rotated_query, key_block, positions, key_place, factor)
        new_high = jnp.maximum(highest, jnp.max(scores, axis=-1))
        totals = totals * jnp.exp(highest - new_high) + jnp.sum(
            jnp.exp(scores - new_high[..., None]), axis=-1
        )
        return ((new_high, totals), None)

    initial = (
        jnp.full((KEY_VALUE_HEADS, query_group_width, count_of_rows), -1e30, jnp.float32),
        jnp.zeros((KEY_VALUE_HEADS, query_group_width, count_of_rows), jnp.float32),
    )
    (highest, totals), _ = lax.scan(softmax_stats, initial, (blocks_of_keys, place_blocks))

    def mix_values(running, piece_set):
        key_block, value_block, key_place = piece_set
        scores = block_scores(rotated_query, key_block, positions, key_place, factor)
        layer_weights = (jnp.exp(scores - highest[..., None]) / totals[..., None]).astype(
            jnp.bfloat16
        )
        return (
            running
            + jnp.einsum(
                "kgqs,skd->qkgd", layer_weights, value_block, preferred_element_type=jnp.float32
            ),
            None,
        )

    attention_output, _ = lax.scan(
        mix_values,
        jnp.zeros((count_of_rows, KEY_VALUE_HEADS, query_group_width, HEAD_WIDTH), jnp.float32),
        (blocks_of_keys, blocks_of_values, place_blocks),
    )
    attention_output = attention_output.reshape(count_of_rows, QUERY_HEADS * HEAD_WIDTH)
    merged = attention_output.astype(jnp.bfloat16)
    middle = input_full + product(merged, w_o)
    scale_two = lax.rsqrt(jnp.mean(middle * middle, axis=-1, keepdims=True) + EPSILON)
    unit_two = middle * scale_two
    normed_two = (unit_two * gain_pair[1]).astype(jnp.bfloat16)
    gate_act = product(normed_two, w_g)
    upward = product(normed_two, w_u)
    hidden = (jax.nn.silu(gate_act) * upward).astype(jnp.bfloat16)
    result = (middle + product(hidden, w_d)).astype(jnp.bfloat16)
    stored = (
        scale_one,
        unit_one,
        normed,
        cosine_table,
        sine_values,
        rotated_query,
        blocks_of_keys,
        blocks_of_values,
        place_blocks,
        highest,
        totals,
        attention_output,
        merged,
        scale_two,
        unit_two,
        normed_two,
        gate_act,
        upward,
        hidden,
    )
    return (result, stored)


def backward(cotangent, positions, gain_pair, matrices, stored):
    w_q, w_k, w_v, w_o, w_g, w_u, w_d = matrices
    (
        scale_one,
        unit_one,
        normed,
        cosine_table,
        sine_values,
        rotated_query,
        blocks_of_keys,
        blocks_of_values,
        place_blocks,
        highest,
        totals,
        attention_output,
        merged,
        scale_two,
        unit_two,
        normed_two,
        gate_act,
        upward,
        hidden,
    ) = stored
    count_of_rows = cotangent.shape[0]
    query_group_width = QUERY_HEADS // KEY_VALUE_HEADS
    factor = 1.0 / math.sqrt(HEAD_WIDTH)
    grad_down = inner_rows(hidden, cotangent)
    back_hidden = inner_cols(cotangent, w_d)
    sigmoid_gate = jax.nn.sigmoid(gate_act)
    back_gate = (
        back_hidden * upward * sigmoid_gate * (1.0 + gate_act * (1.0 - sigmoid_gate))
    ).astype(jnp.bfloat16)
    back_up = (back_hidden * (gate_act * sigmoid_gate)).astype(jnp.bfloat16)
    grad_gate = inner_rows(normed_two, back_gate)
    grad_up = inner_rows(normed_two, back_up)
    back_norm_two = inner_cols(back_gate, w_g) + inner_cols(back_up, w_u)
    gain_two = jnp.sum(back_norm_two * unit_two, axis=0)
    back_unit = back_norm_two * gain_pair[1]
    back_middle = cotangent.astype(jnp.float32) + scale_two * (
        back_unit - unit_two * jnp.mean(back_unit * unit_two, axis=-1, keepdims=True)
    )
    middle_low = back_middle.astype(jnp.bfloat16)
    grad_out = inner_rows(merged, middle_low)
    attention_backward = inner_cols(middle_low, w_o).astype(jnp.bfloat16)
    head_gradient_rows = attention_backward.reshape(
        count_of_rows, KEY_VALUE_HEADS, query_group_width, HEAD_WIDTH
    )
    attention_head_rows = attention_output.reshape(
        count_of_rows, KEY_VALUE_HEADS, query_group_width, HEAD_WIDTH
    )
    correction = jnp.transpose(
        jnp.sum(head_gradient_rows.astype(jnp.float32) * attention_head_rows, axis=-1), (1, 2, 0)
    )

    def score_grads(running, piece_set):
        key_block, value_block, key_place = piece_set
        scores = block_scores(rotated_query, key_block, positions, key_place, factor)
        probs = jnp.exp(scores - highest[..., None]) / totals[..., None]
        back_probs = jnp.einsum(
            "qkgd,skd->kgqs", head_gradient_rows, value_block, preferred_element_type=jnp.float32
        )
        back_scores = (probs * (back_probs - correction[..., None])).astype(jnp.bfloat16)
        running = (
            running
            + jnp.einsum(
                "kgqs,skd->qkgd", back_scores, key_block, preferred_element_type=jnp.float32
            )
            * factor
        )
        key_grad = (
            jnp.einsum(
                "kgqs,qkgd->skd", back_scores, rotated_query, preferred_element_type=jnp.float32
            )
            * factor
        )
        value_grad = jnp.einsum(
            "kgqs,qkgd->skd",
            probs.astype(jnp.bfloat16),
            head_gradient_rows,
            preferred_element_type=jnp.float32,
        )
        return (running, (key_grad, value_grad))

    back_query, (gradient_of_keys, gradient_of_values) = lax.scan(
        score_grads,
        jnp.zeros((count_of_rows, KEY_VALUE_HEADS, query_group_width, HEAD_WIDTH), jnp.float32),
        (blocks_of_keys, blocks_of_values, place_blocks),
    )
    count_of_keys = gradient_of_keys.shape[0] * gradient_of_keys.shape[1]
    local_keys, value_own = (
        lax.psum_scatter(
            gradient_of_keys.reshape(count_of_keys, KEY_VALUE_HEADS * HEAD_WIDTH).astype(
                jnp.bfloat16
            ),
            "seq",
            scatter_dimension=0,
            tiled=True,
        ).astype(jnp.float32),
        lax.psum_scatter(
            gradient_of_values.reshape(count_of_keys, KEY_VALUE_HEADS * HEAD_WIDTH).astype(
                jnp.bfloat16
            ),
            "seq",
            scatter_dimension=0,
            tiled=True,
        ).astype(jnp.float32),
    )
    query_low = (
        apply_rotation(
            back_query.reshape(count_of_rows, QUERY_HEADS, HEAD_WIDTH), cosine_table, -sine_values
        )
        .astype(jnp.bfloat16)
        .reshape(count_of_rows, QUERY_HEADS * HEAD_WIDTH)
    )
    key_low = (
        apply_rotation(
            local_keys.reshape(count_of_rows, KEY_VALUE_HEADS, HEAD_WIDTH),
            cosine_table,
            -sine_values,
        )
        .astype(jnp.bfloat16)
        .reshape(count_of_rows, KEY_VALUE_HEADS * HEAD_WIDTH)
    )
    value_low = value_own.astype(jnp.bfloat16)
    grad_query = inner_rows(normed, query_low)
    grad_key = inner_rows(normed, key_low)
    grad_value = inner_rows(normed, value_low)
    back_norm_one = (
        inner_cols(query_low, w_q) + inner_cols(key_low, w_k) + inner_cols(value_low, w_v)
    )
    gain_one = jnp.sum(back_norm_one * unit_one, axis=0)
    back_unit_one = back_norm_one * gain_pair[0]
    input_back = back_middle + scale_one * (
        back_unit_one - unit_one * jnp.mean(back_unit_one * unit_one, axis=-1, keepdims=True)
    )
    weight_terms = (grad_query, grad_key, grad_value, grad_out, grad_gate, grad_up, grad_down)
    return (input_back.astype(jnp.bfloat16), weight_terms, (gain_one, gain_two))


def on_device(
    hidden_in,
    span_order,
    attention_norm_gain,
    query_weight,
    key_weight,
    value_weight,
    output_weight,
    feedforward_gain,
    gate_weight,
    up_weight,
    down_weight,
    out_grad,
):
    count_of_rows = SLOTS * SPAN
    gain_pair = (attention_norm_gain.astype(jnp.float32), feedforward_gain.astype(jnp.float32))
    offsets = jnp.arange(SPAN, dtype=jnp.int32)
    weight_totals = (
        jnp.zeros((MODEL_WIDTH, QUERY_HEADS * HEAD_WIDTH), jnp.float32),
        jnp.zeros((MODEL_WIDTH, KEY_VALUE_HEADS * HEAD_WIDTH), jnp.float32),
        jnp.zeros((MODEL_WIDTH, KEY_VALUE_HEADS * HEAD_WIDTH), jnp.float32),
        jnp.zeros((QUERY_HEADS * HEAD_WIDTH, MODEL_WIDTH), jnp.float32),
        jnp.zeros((MODEL_WIDTH, HIDDEN_UNITS), jnp.float32),
        jnp.zeros((MODEL_WIDTH, HIDDEN_UNITS), jnp.float32),
        jnp.zeros((HIDDEN_UNITS, MODEL_WIDTH), jnp.float32),
    )
    gain_totals = (jnp.zeros((MODEL_WIDTH,), jnp.float32), jnp.zeros((MODEL_WIDTH,), jnp.float32))
    outputs = []
    input_grads = []
    for micro_index in range(MB):
        layer_input = hidden_in[micro_index * count_of_rows : (micro_index + 1) * count_of_rows]
        cotangent = out_grad[micro_index * count_of_rows : (micro_index + 1) * count_of_rows]
        span_ids = span_order[micro_index * SLOTS : (micro_index + 1) * SLOTS]
        positions = (span_ids[:, None] * SPAN + offsets[None, :]).reshape(count_of_rows)
        forward_weights = shape_weights(
            (
                lax.all_gather(query_weight, ("dp", "seq"), axis=0, tiled=True),
                lax.all_gather(key_weight, ("dp", "seq"), axis=0, tiled=True),
                lax.all_gather(value_weight, ("dp", "seq"), axis=0, tiled=True),
                lax.all_gather(output_weight, ("dp", "seq"), axis=0, tiled=True),
                lax.all_gather(gate_weight, ("dp", "seq"), axis=0, tiled=True),
                lax.all_gather(up_weight, ("dp", "seq"), axis=0, tiled=True),
                lax.all_gather(down_weight, ("dp", "seq"), axis=0, tiled=True),
            )
        )
        result, stored = forward(layer_input, positions, span_ids, gain_pair, forward_weights)
        backward_weights = shape_weights(
            (
                lax.all_gather(query_weight, ("dp", "seq"), axis=0, tiled=True),
                lax.all_gather(key_weight, ("dp", "seq"), axis=0, tiled=True),
                lax.all_gather(value_weight, ("dp", "seq"), axis=0, tiled=True),
                lax.all_gather(output_weight, ("dp", "seq"), axis=0, tiled=True),
                lax.all_gather(gate_weight, ("dp", "seq"), axis=0, tiled=True),
                lax.all_gather(up_weight, ("dp", "seq"), axis=0, tiled=True),
                lax.all_gather(down_weight, ("dp", "seq"), axis=0, tiled=True),
            )
        )
        input_back, weight_terms, gain_terms = backward(
            cotangent, positions, gain_pair, backward_weights, stored
        )
        weight_totals = tuple(
            (running + term for running, term in zip(weight_totals, weight_terms))
        )
        gain_totals = tuple((running + term for running, term in zip(gain_totals, gain_terms)))
        outputs.append(result)
        input_grads.append(input_back)
    grad_query, grad_key, grad_value, grad_out, grad_gate, grad_up, grad_down = weight_totals
    owned = (
        lax.psum_scatter(grad_query.reshape(-1), ("dp", "seq"), scatter_dimension=0, tiled=True),
        lax.psum_scatter(grad_key.reshape(-1), ("dp", "seq"), scatter_dimension=0, tiled=True),
        lax.psum_scatter(grad_value.reshape(-1), ("dp", "seq"), scatter_dimension=0, tiled=True),
        lax.psum_scatter(grad_out.reshape(-1), ("dp", "seq"), scatter_dimension=0, tiled=True),
        lax.psum_scatter(grad_gate.reshape(-1), ("dp", "seq"), scatter_dimension=0, tiled=True),
        lax.psum_scatter(grad_up.reshape(-1), ("dp", "seq"), scatter_dimension=0, tiled=True),
        lax.psum_scatter(grad_down.reshape(-1), ("dp", "seq"), scatter_dimension=0, tiled=True),
    )
    gain_one, gain_two = lax.psum((gain_totals[0], gain_totals[1]), ("dp", "seq"))
    return (
        jnp.concatenate(outputs, axis=0),
        jnp.concatenate(input_grads, axis=0),
        gain_one,
        owned[0],
        owned[1],
        owned[2],
        owned[3],
        gain_two,
        owned[4],
        owned[5],
        owned[6],
    )


FACTOR = 1.0 / math.sqrt(HEAD_WIDTH)
KV_WIDTH = KEY_VALUE_HEADS * HEAD_WIDTH
Q_WIDTH = QUERY_HEADS * HEAD_WIDTH
QK_WIDTH = Q_WIDTH + KV_WIDTH
LANES = 128
HALF_FFN = HIDDEN_UNITS // 2
FFN_BLOCK = 256
DOWN_PITCH = 640
DOWN_AT = HIDDEN_UNITS
DOWN_EARLY = 2
FFN_CUT = DOWN_AT + DOWN_EARLY * DOWN_PITCH
UP_AT = (3 - DOWN_EARLY) * DOWN_PITCH
SECOND_GATE_AT = 3 * DOWN_PITCH
SECOND_WIDTH = SECOND_GATE_AT + 2 * HALF_FFN
SECOND_CUT = SECOND_GATE_AT + 256


def vmem_params(megabytes=48):
    return pltpu.CompilerParams(vmem_limit_bytes=megabytes * 1024 * 1024)


def dot_nn(a, b):
    return jnp.dot(a, b, preferred_element_type=jnp.float32)


def dot_tn(a, b):
    return lax.dot_general(a, b, (((0,), (0,)), ((), ())), preferred_element_type=jnp.float32)


def dot_nt(a, b):
    return lax.dot_general(a, b, (((1,), (1,)), ((), ())), preferred_element_type=jnp.float32)


def low(v):
    return v.astype(jnp.bfloat16)


def wide(v):
    return v.astype(jnp.float32)


def place_back(v, place):
    high = low(v)
    rest = low(v - high.astype(jnp.float32))
    return dot_nt(high, place) + dot_nt(rest, place)


def half_turn(u, lane):
    return jnp.where(
        lane % HEAD_WIDTH < HEAD_WIDTH // 2,
        pltpu.roll(u, LANES - HEAD_WIDTH // 2, 1),
        pltpu.roll(u, HEAD_WIDTH // 2, 1),
    )


def padded_heads(blocks, head, lane):
    here = blocks[head // 2]
    moved = pltpu.roll(here, HEAD_WIDTH, 1)
    low_half, high_half = (here, moved) if head % 2 == 0 else (moved, here)
    zero = jnp.zeros_like(here)
    return (
        low(jnp.where(lane < HEAD_WIDTH, low_half, zero)),
        low(jnp.where(lane >= HEAD_WIDTH, high_half, zero)),
    )


def pack_kernel(
    span_order, hidden_in, out_grad, slots, offsets,
    x_mine, x_near, x_far, o_mine, o_near, o_far, place, *, n_seq,
):
    seq = lax.axis_index("seq")
    me = lax.axis_index("dp") * n_seq + seq
    tall = SPAN + 16
    for flip, x, o, at in ((0, x_mine, o_mine, 0), (1, x_near, o_near, 0), (3, x_near, o_near, 1), (2, x_far, o_far, 0)):
        origin = seq ^ flip
        block = pl.ds(pl.multiple_of(origin * SPAN, SPAN), SPAN)
        x[at * tall : at * tall + SPAN] = hidden_in[block, :]
        number = jnp.full((16, MODEL_WIDTH), span_order[origin], jnp.int32)
        x[at * tall + SPAN : (at + 1) * tall] = low(number.astype(jnp.float32))
        o[at * SPAN : (at + 1) * SPAN] = out_grad[block, :]
    natural = (slots[...] ^ me) * (MODEL_WIDTH // (n_seq * lax.axis_size("dp"))) + offsets[...]
    row = lax.broadcasted_iota(jnp.int32, place.shape, 0)
    place[...] = low((row == natural).astype(jnp.float32))


def unpack_kernel(mine, near, far, out):
    seq = lax.axis_index("seq")
    for flip, source, at in ((0, mine, 0), (1, near, 0), (2, far, 0), (3, far, 1)):
        target = pl.ds(pl.multiple_of((seq ^ flip) * SPAN, SPAN), SPAN)
        out[target, :] = source[at * SPAN : (at + 1) * SPAN]


def project_kernel(
    x_mine, x_near, x_far, gain_one, place, cosine, sine, wab, wab2,
    spans, x_out, normed_out, qk_out, kpad_out, vpad_out, wqk, wov,
):
    rows = x_out.shape[0]
    half = wab.shape[0]
    tall = SPAN + 16
    for k, (block, at) in enumerate(((x_mine, 0), (x_near, 0), (x_far, 0), (x_far, tall))):
        number = jnp.max(block[at + SPAN : at + tall, :LANES].astype(jnp.float32))
        number = number.astype(jnp.int32)
        spans[k] = number
        x_out[pl.ds(pl.multiple_of(number * SPAN, SPAN), SPAN), :] = block[at : at + SPAN]
    wa, wb = wab.at[:, :QK_WIDTH], wab.at[:, QK_WIDTH:]
    wa2, wb2 = wab2.at[:, :QK_WIDTH], wab2.at[:, QK_WIDTH:]
    wqk[:half] = wa[...]
    wqk[half:] = wa2[...]
    wov[:half] = wb[...]
    wov[half:] = wb2[...]
    x = x_out[...].astype(jnp.float32)
    scale = lax.rsqrt(jnp.mean(x * x, axis=-1, keepdims=True) + EPSILON)
    normed = low(x * scale * gain_one[...])
    normed_out[...] = low(dot_nn(normed, place[...]))
    lane = lax.broadcasted_iota(jnp.int32, (rows, LANES), 1)
    cos, sin = cosine[...], sine[...]
    k_blocks = []
    for b in range(QK_WIDTH // LANES):
        u = dot_nn(normed_out[...], wqk[:, b * LANES : (b + 1) * LANES])
        turned = u * cos + half_turn(u, lane) * sin
        turned = low(turned).astype(jnp.float32)
        if (b + 1) * LANES > Q_WIDTH:
            k_blocks.append(turned)
        if (b + 1) * LANES <= Q_WIDTH:
            turned = turned * FACTOR
        elif b * LANES < Q_WIDTH:
            turned = jnp.where(lane < Q_WIDTH - b * LANES, turned * FACTOR, turned)
        qk_out[:, b * LANES : (b + 1) * LANES] = low(turned)
    first_group = QUERY_HEADS - 2 * (Q_WIDTH // LANES)
    for j in range(KEY_VALUE_HEADS):
        lo, hi = padded_heads(k_blocks, j + first_group, lane)
        kpad_out[2 * j] = lo
        kpad_out[2 * j + 1] = hi
    v = dot_nn(normed_out[...], wov[:, MODEL_WIDTH:])
    v = low(v).astype(jnp.float32)
    v = jnp.concatenate([v, jnp.zeros((rows, HEAD_WIDTH), jnp.float32)], axis=1)
    v_blocks = [v[:, :LANES], v[:, LANES:]]
    for j in range(KEY_VALUE_HEADS):
        lo, hi = padded_heads(v_blocks, j, lane)
        vpad_out[2 * j] = lo
        vpad_out[2 * j + 1] = hi


def attend_spans(spans, qk, kpad, vpad, lse_out, attn_out):
    lane_q = lax.broadcasted_iota(jnp.int32, (SPAN, LANES), 1)
    diagonal = lax.broadcasted_iota(jnp.int32, (SPAN, SPAN), 0) >= lax.broadcasted_iota(
        jnp.int32, (SPAN, SPAN), 1
    )
    groups = QUERY_HEADS // KEY_VALUE_HEADS
    for i in spans:
        here = slice(i * SPAN, (i + 1) * SPAN)
        lse = jnp.zeros((SPAN, LANES), jnp.float32)
        for b in range((QUERY_HEADS + 1) // 2):
            mixed = None
            for h in range(2 * b, min(2 * b + 2, QUERY_HEADS)):
                slot = 2 * (h // groups) + h % 2
                q = qk[here, b * LANES : (b + 1) * LANES]
                s = dot_nt(q, kpad[slot, : (i + 1) * SPAN, :])
                s_last = jnp.where(diagonal, s[:, i * SPAN :], -1e30)
                s = s_last if i == 0 else jnp.concatenate([s[:, : i * SPAN], s_last], axis=1)
                top = jnp.max(s, axis=-1, keepdims=True)
                p = jnp.exp(s - top)
                total = jnp.sum(p, axis=-1, keepdims=True)
                p = low(p * (1.0 / total))
                lse = jnp.where(lane_q == h, top + jnp.log(total), lse)
                part = dot_nn(p, vpad[slot, : (i + 1) * SPAN, :])
                mixed = part if mixed is None else mixed + part
            attn_out[here, b * LANES : (b + 1) * LANES] = mixed
        lse_out[here, :] = lse


def attend_first_kernel(qk, kpad, vpad, lse_out, attn_out):
    attend_spans(range(qk.shape[0] // SPAN - 1), qk, kpad, vpad, lse_out, attn_out)


def attend_last_kernel(
    lse_in, attn_in, x_in, qk, kpad, vpad, gain_two, place, wab, wab2,
    lse_out, attn_out, merged_out, middle_out, normed_two_out,
):
    rows = x_in.shape[0]
    half = wab.shape[0]
    wb, wb2 = wab.at[:, QK_WIDTH:], wab2.at[:, QK_WIDTH:]
    attend_spans([rows // SPAN - 1], qk, kpad, vpad, lse_out, attn_out)
    merged = low(dot_nn(low(attn_out[:, :Q_WIDTH]), place[...]))
    merged_out[...] = merged
    middle = (
        x_in[...].astype(jnp.float32)
        + dot_nn(merged[:, :half], wb[:, :MODEL_WIDTH])
        + dot_nn(merged[:, half:], wb2[:, :MODEL_WIDTH])
    )
    middle_out[...] = middle
    scale_two = lax.rsqrt(jnp.mean(middle * middle, axis=-1, keepdims=True) + EPSILON)
    normed_two_out[...] = low(dot_nn(low(middle * scale_two * gain_two[...]), place[...]))


def ffn_block(n2, og, wg, wu, wd, at, result, back_norm, d_keep, d_send, dd_out):
    columns = pl.ds(pl.multiple_of(at * FFN_BLOCK, FFN_BLOCK), FFN_BLOCK)
    up_columns = pl.ds(pl.multiple_of(HALF_FFN + at * FFN_BLOCK, FFN_BLOCK), FFN_BLOCK)
    half = d_keep.shape[0]
    w_gate, w_up, w_down = wg[:, columns], wu[:, columns], wd[columns, :]
    gate = dot_nn(n2, w_gate)
    up = dot_nn(n2, w_up)
    back_hidden = dot_nt(og, w_down)
    sigmoid = jax.nn.sigmoid(gate)
    silu = gate * sigmoid
    hidden = low(silu * up)
    back_gate = low(back_hidden * up * sigmoid * (1.0 + gate * (1.0 - sigmoid)))
    back_up = low(back_hidden * silu)
    dd_out[columns, :] = low(dot_tn(hidden, og))
    dg = low(dot_tn(n2, back_gate))
    du = low(dot_tn(n2, back_up))
    d_keep[:, columns] = dg[:half]
    d_send[:, columns] = dg[half:]
    d_keep[:, up_columns] = du[:half]
    d_send[:, up_columns] = du[half:]
    result[...] += dot_nn(hidden, w_down)
    back_norm[...] += dot_nt(back_gate, w_gate) + dot_nt(back_up, w_up)


def ffn_first_kernel(
    spans, o_mine, o_near, o_far, n2, a0, a1, a2, a3, b0, b1, b2, b3,
    og_out, result_out, back_out, d_keep, d_send, dd, wd_out, later_out,
    wg, wu, *, order, n_seq,
):
    me = lax.axis_index("dp") * n_seq + lax.axis_index("seq")
    for k, (block, at) in enumerate(((o_mine, 0), (o_near, 0), (o_far, 0), (o_far, SPAN))):
        target = pl.ds(pl.multiple_of(spans[k] * SPAN, SPAN), SPAN)
        og_out[target, :] = block[at : at + SPAN]
    size = a0.shape[0] // 2
    places = (0, 2, 1, 3)
    for core, (first, second) in enumerate(((a0, a1), (a2, a3))):
        for at, (source, piece) in enumerate(((first, 0), (first, 1), (second, 0), (second, 1))):
            start = (4 * core + places[at]) * size
            rows = slice(start, start + size)
            part = slice(piece * size, (piece + 1) * size)
            wg[rows] = source[part, :HALF_FFN]
            later_out[rows, :HALF_FFN] = source[part, HALF_FFN:HIDDEN_UNITS]
    for core, (first, second) in enumerate(((b0, b1), (b2, b3))):
        for at, source in enumerate((first, second)):
            start = (4 * core + 2 * at) * size
            rows = slice(start, start + 2 * size)
            wu[rows] = source[:, UP_AT : UP_AT + HALF_FFN]
            later_out[rows, HALF_FFN:] = source[:, UP_AT + HALF_FFN :]
    count = len(order)
    rows, pitch = wd_out.shape[0] // count, MODEL_WIDTH // count
    each = size // pitch
    for slot, relative in enumerate(order):
        core, block, at = slot // (4 * each), slot // each % 4, slot % each
        x_side, y_side = block % 2, block // 2
        for t in range(rows // 16):
            if t < DOWN_EARLY:
                source = ((a0, a1), (a2, a3))[core][x_side]
                start = y_side * size + at * pitch
                first = DOWN_AT + t * DOWN_PITCH
            else:
                source = ((b0, b1), (b2, b3))[core][y_side]
                start = x_side * size + at * pitch
                first = (t - DOWN_EARLY) * DOWN_PITCH
            target = pl.multiple_of((me ^ relative) * rows + 16 * t, 16)
            wd_out[pl.ds(target, 16), :] = source[start : start + 16, first : first + MODEL_WIDTH]
    result_out[...] = jnp.zeros_like(result_out)
    back_out[...] = jnp.zeros_like(back_out)

    @pl.loop(0, HALF_FFN // FFN_BLOCK)
    def _(at):
        ffn_block(
            n2[...], og_out[...], wg, wu, wd_out, at, result_out, back_out, d_keep, d_send, dd
        )


def ffn_second_kernel(
    spans, og, n2, w_later, wd_in, result_in, back_in, dd_in, middle, gain_two, place,
    mine, near, far, back_middle_out, gain_out, keep_out, send_out,
    wd, dd, spread, result, back, *, order, n_seq,
):
    half = keep_out.shape[0]
    wg, wu = w_later.at[:, :HALF_FFN], w_later.at[:, HALF_FFN:]
    me = lax.axis_index("dp") * n_seq + lax.axis_index("seq")
    d_keep = keep_out.at[:, SECOND_GATE_AT : SECOND_GATE_AT + 2 * HALF_FFN]
    d_send = send_out.at[:, SECOND_GATE_AT : SECOND_GATE_AT + 2 * HALF_FFN]
    wd[...] = wd_in[HALF_FFN:, :]
    dd[:HALF_FFN] = dd_in[...]
    result[...] = result_in[...] + middle[...]
    back[...] = back_in[...]

    @pl.loop(0, HALF_FFN // FFN_BLOCK)
    def _(at):
        ffn_block(
            n2[...], og[...], wg, wu, wd, at, result, back, d_keep, d_send, dd.at[HALF_FFN:, :]
        )

    count = len(order)
    rows, pitch = HIDDEN_UNITS // count, MODEL_WIDTH // count
    spread[...] = jnp.zeros_like(spread)
    for t in range(rows // 16):
        for slot, relative in enumerate(order):
            source = pl.ds(pl.multiple_of((me ^ relative) * rows + 16 * t, 16), 16)
            spread[slot * pitch : slot * pitch + 16, :MODEL_WIDTH] = wide(dd[source, :])
        columns = slice(t * DOWN_PITCH, (t + 1) * DOWN_PITCH)
        keep_out[:, columns] = low(spread[:half])
        send_out[:, columns] = low(spread[half:])

    for k, (block, at) in enumerate(((mine, 0), (near, 0), (far, 0), (near, SPAN))):
        source = pl.ds(pl.multiple_of(spans[k] * SPAN, SPAN), SPAN)
        block[at : at + SPAN] = low(result[source, :])
    mid = middle[...]
    scale = lax.rsqrt(jnp.mean(mid * mid, axis=-1, keepdims=True) + EPSILON)
    unit = mid * scale
    back_norm = place_back(back[...], place[...])
    gain_out[...] = jnp.sum(back_norm * unit, axis=0, keepdims=True)
    back_unit = back_norm * gain_two[...]
    back_middle_out[...] = og[...].astype(jnp.float32) + scale * (
        back_unit - unit * jnp.mean(back_unit * unit, axis=-1, keepdims=True)
    )


def score_back(i, qk, kpad, vpad, ab, lse_rows, correction, dqk, dv):
    rows = qk.shape[0]
    groups = QUERY_HEADS // KEY_VALUE_HEADS
    diagonal = lax.broadcasted_iota(jnp.int32, (SPAN, SPAN), 1) >= lax.broadcasted_iota(
        jnp.int32, (SPAN, SPAN), 0
    )
    lane = lax.broadcasted_iota(jnp.int32, (SPAN, LANES), 1)
    keys = slice(i * SPAN, (i + 1) * SPAN)
    first = i * SPAN
    dk_sums = [None] * (2 * KEY_VALUE_HEADS)
    dv_sums = [None] * (2 * KEY_VALUE_HEADS)
    for b in range((QUERY_HEADS + 1) // 2):
        columns = slice(b * LANES, (b + 1) * LANES)
        q = qk[first:, columns]
        a = ab[first:, columns]
        dq = None
        for h in range(2 * b, min(2 * b + 2, QUERY_HEADS)):
            slot = 2 * (h // groups) + h % 2
            s = dot_nt(kpad[slot, keys, :], q)
            s = s - lse_rows[h : h + 1, first:]
            s_first = jnp.where(diagonal, s[:, :SPAN], -1e30)
            s = (
                s_first
                if first + SPAN == rows
                else jnp.concatenate([s_first, s[:, SPAN:]], axis=1)
            )
            p = jnp.exp(s)
            dp = dot_nt(vpad[slot, keys, :], a)
            ds = low(p * (dp - correction[h : h + 1, first:]))
            dk = dot_nn(ds, q)
            dvh = dot_nn(low(p), a)
            dk_sums[slot] = dk if dk_sums[slot] is None else dk_sums[slot] + dk
            dv_sums[slot] = dvh if dv_sums[slot] is None else dv_sums[slot] + dvh
            part = dot_tn(ds, kpad[slot, keys, :])
            dq = part if dq is None else dq + part
        if i == 0:
            dqk[first:, columns] = dq
        else:
            dqk[first:, columns] += dq

    def both(sums, j):
        return sums[2 * j] + pltpu.roll(sums[2 * j + 1], HEAD_WIDTH, 1)

    dk_heads = [both(dk_sums, j) for j in range(KEY_VALUE_HEADS)]
    dv_heads = [both(dv_sums, j) for j in range(KEY_VALUE_HEADS)]
    key_scale = 1.0 / FACTOR
    q_tail = dqk[keys, 4 * LANES : 5 * LANES]
    dqk[keys, 4 * LANES : 5 * LANES] = jnp.where(
        lane < HEAD_WIDTH, q_tail, pltpu.roll(dk_heads[0], HEAD_WIDTH, 1) * key_scale
    )
    dqk[keys, 5 * LANES :] = (
        jnp.where(lane < HEAD_WIDTH, dk_heads[1], pltpu.roll(dk_heads[2], HEAD_WIDTH, 1))
        * key_scale
    )
    dv[keys, :LANES] = low(
        jnp.where(lane < HEAD_WIDTH, dv_heads[0], pltpu.roll(dv_heads[1], HEAD_WIDTH, 1))
    )
    dv[keys, LANES:] = low(dv_heads[2])


def attend_back_first_kernel(
    qk, kpad, vpad, lse, attn, merged, back_middle, place, wab, wab2,
    keep_out, send_out, ab, lse_rows, correction, dqk, dv,
):
    rows = qk.shape[0]
    half = wab.shape[0]
    wb, wb2 = wab.at[:, QK_WIDTH:], wab2.at[:, QK_WIDTH:]
    middle_low = low(back_middle[...])
    d_out = low(dot_tn(merged[...], middle_low))
    out_columns = slice(QK_WIDTH, QK_WIDTH + MODEL_WIDTH)
    keep_out[:, out_columns] = d_out[:half]
    send_out[:, out_columns] = d_out[half:]
    ab_first = low(dot_nt(middle_low, wb[:, :MODEL_WIDTH]))
    ab_second = low(dot_nt(middle_low, wb2[:, :MODEL_WIDTH]))
    ab[:, :Q_WIDTH] = low(
        dot_nt(ab_first, place[:, :half]) + dot_nt(ab_second, place[:, half:])
    )
    ab[:, Q_WIDTH:] = jnp.zeros((rows, ab.shape[1] - Q_WIDTH), jnp.bfloat16)
    terms = ab[...].astype(jnp.float32) * attn[...]
    mask = low(
        (
            lax.broadcasted_iota(jnp.int32, (16, terms.shape[1]), 1) // HEAD_WIDTH
            == lax.broadcasted_iota(jnp.int32, (16, terms.shape[1]), 0)
        ).astype(jnp.float32)
    )
    high = low(terms)
    correction[...] = dot_nt(mask, high) + dot_nt(mask, low(terms - high.astype(jnp.float32)))
    lse_rows[...] = jnp.transpose(lse[...])
    score_back(0, qk, kpad, vpad, ab, lse_rows, correction, dqk, dv)


def attend_back_kernel(
    keep_in, send_in, spans, x, normed, qk, kpad, vpad, lse_rows, correction, ab, dqk_in, dv_in, back_middle, gain_one,
    place, cosine, sine, wab, wab2,
    mine, near, far, gain_out, d1, d2,
    dqk, dv, grad,
):
    rows = x.shape[0]
    half = wab.shape[0]
    dqk[...] = dqk_in[...]
    dv[...] = dv_in[...]
    for i in range(1, rows // SPAN):
        score_back(i, qk, kpad, vpad, ab, lse_rows, correction, dqk, dv)
    lane = lax.broadcasted_iota(jnp.int32, (rows, LANES), 1)
    cos, sin = cosine[...], sine[...]
    for b in range(QK_WIDTH // LANES):
        u = dqk[:, b * LANES : (b + 1) * LANES] * FACTOR
        grad[:, b * LANES : (b + 1) * LANES] = low(u * cos - half_turn(u, lane) * sin)
    d_qk = low(dot_tn(normed[...], grad[...]))
    d1[:, :QK_WIDTH] = d_qk[:half]
    d2[:, :QK_WIDTH] = d_qk[half:]
    dv_low = dv[:, :KV_WIDTH]
    d_v = low(dot_tn(normed[...], dv_low))
    d1[:, QK_WIDTH + MODEL_WIDTH :] = d_v[:half]
    d2[:, QK_WIDTH + MODEL_WIDTH :] = d_v[half:]
    parts = [
        dot_nt(grad[...], w[:, :QK_WIDTH]) + dot_nt(dv_low, w[:, QK_WIDTH + MODEL_WIDTH :])
        for w in (wab, wab2)
    ]
    back_norm = place_back(jnp.concatenate(parts, axis=1), place[...])
    xf = x[...].astype(jnp.float32)
    scale = lax.rsqrt(jnp.mean(xf * xf, axis=-1, keepdims=True) + EPSILON)
    unit = xf * scale
    gain_out[...] = jnp.sum(back_norm * unit, axis=0, keepdims=True)
    back_unit = back_norm * gain_one[...]
    dqk[:, :MODEL_WIDTH] = back_middle[...] + scale * (
        back_unit - unit * jnp.mean(back_unit * unit, axis=-1, keepdims=True)
    )
    for k, (block, at) in enumerate(((mine, 0), (near, 0), (far, 0), (near, SPAN))):
        source = pl.ds(pl.multiple_of(spans[k] * SPAN, SPAN), SPAN)
        block[at : at + SPAN] = low(dqk[source, :MODEL_WIDTH])


VMEM_SPEC = pl.BlockSpec(memory_space=pltpu.VMEM)
SMEM_SPEC = pl.BlockSpec(memory_space=pltpu.SMEM)
ANY_SPEC = pl.BlockSpec(memory_space=pl.ANY)


def shaped(rows, columns, kind):
    return jax.ShapeDtypeStruct((rows, columns), kind)


def call(body, outs, args, scratch, micros, scalars=(), after=(), alias=None, megabytes=16, out_specs=None):
    def run(*refs):
        body(*refs[: len(args)], *refs[len(args) + len(after) :])

    return pl.pallas_call(
        run,
        out_shape=outs,
        in_specs=[SMEM_SPEC if at in scalars else VMEM_SPEC for at in range(len(args))]
        + [ANY_SPEC] * len(after),
        out_specs=out_specs or [VMEM_SPEC] * len(outs),
        scratch_shapes=scratch,
        input_output_aliases=alias or {},
        compiler_params=vmem_params(megabytes),
        cost_estimate=pl.CostEstimate(
            flops=int(micros * 1.1e9), bytes_accessed=1_000_000, transcendentals=0
        ),
    )(*args, *after)


def whole_sequence_plan(mesh):
    axes = ("dp", "seq")
    n_dp, n_seq = mesh.shape["dp"], mesh.shape["seq"]
    count = n_dp * n_seq
    bits = count.bit_length() - 1
    seq_bits = n_seq.bit_length() - 1
    core, y_bit = 0, 1
    x_bit = seq_bits
    z_bits = tuple(range(seq_bits + 1, bits))[::-1]
    order_bits = z_bits + (x_bit, y_bit, core)

    def hold(v, *others):
        return lax.optimization_barrier((v, *others))[0] if others else v

    def swap(v, flip, until=()):
        return hold(lax.ppermute(v, axes, [(d, d ^ flip) for d in range(count)]), *until)

    def relative(slot):
        return sum(1 << bit for at, bit in enumerate(order_bits) if slot >> at & 1)

    order = tuple(relative(slot) for slot in range(count))
    z_count = 1 << len(z_bits)
    z_flips = [relative(slot) for slot in range(1, z_count)]
    flip_x, flip_y, flip_core = 1 << x_bit, 1 << y_bit, 1 << core

    def gather_z(v, until=()):
        return jnp.concatenate([v] + [swap(v, flip, until) for flip in z_flips], axis=0)

    def gather_z_stepwise(v, untils):
        for bit, until in zip(z_bits, untils):
            v = jnp.concatenate([v, swap(v, 1 << bit, until)], axis=0)
        return v

    def gather_one(v, x_first, until=()):
        return jnp.concatenate([v, swap(v, flip_x if x_first else flip_y, until)], axis=0)

    def gather_two(v, x_first, until=()):
        w = swap(v, flip_y if x_first else flip_x, until)
        size = v.shape[0] // 2
        if x_first:
            return jnp.concatenate([v, w], axis=0)
        return jnp.concatenate([v[:size], w[:size], v[size:], w[size:]], axis=0)

    def scatter_core(keep, send, until=()):
        return wide(keep) + wide(swap(send, flip_core, until))

    def scatter_one(total, x_first, until=()):
        size = total.shape[0] // 4
        if x_first:
            mine = jnp.concatenate([total[:size], total[2 * size : 3 * size]], axis=0)
            theirs = jnp.concatenate([total[size : 2 * size], total[3 * size :]], axis=0)
            return mine + wide(swap(low(theirs), flip_x, until))
        return total[: 2 * size] + wide(swap(low(total[2 * size :]), flip_y, until))

    def scatter_two(total, x_first, until=()):
        size = total.shape[0] // 2
        sent = swap(low(total[size:]), flip_y if x_first else flip_x, until)
        return total[:size] + wide(sent)

    def scatter_z(total, until=()):
        for bit in z_bits[::-1]:
            size = total.shape[0] // 2
            total = total[:size] + wide(swap(low(total[size:]), 1 << bit, until))
        return total

    def exchange(parts, near_until=(), far_until=(), far_after=()):
        mine, near, far = parts
        size = mine.shape[0]
        near = swap(near, flip_core, near_until)
        far = hold(jnp.concatenate([far, near[size:]], axis=0), *far_after)
        return mine, near[:size], swap(far, flip_y, far_until)

    def sum_everywhere(v):
        for bit in range(bits):
            v = v + swap(v, 1 << bit)
        return v

    def on_sequence_device(
        hidden_in, span_order, attention_norm_gain, query_weight, key_weight, value_weight,
        output_weight, feedforward_gain, gate_weight, up_weight, down_weight, out_grad,
    ):
        rows = hidden_in.shape[0]
        model_rows = MODEL_WIDTH // count
        hidden_rows = HIDDEN_UNITS // count
        bf, f4 = jnp.bfloat16, jnp.float32
        half = MODEL_WIDTH // 2
        gain_one = attention_norm_gain.astype(jnp.float32).reshape(1, MODEL_WIDTH)
        gain_two = feedforward_gain.astype(jnp.float32).reshape(1, MODEL_WIDTH)
        model_low, model_full = shaped(rows, MODEL_WIDTH, bf), shaped(rows, MODEL_WIDTH, f4)

        def rows_of(w, columns):
            return w.reshape(model_rows, columns)

        def unpack(parts):
            return call(unpack_kernel, [model_low], parts, [], 1, megabytes=4)[0]

        slots = np.repeat(np.asarray(order, np.int32), model_rows)[None, :]
        offsets = np.tile(np.arange(model_rows, dtype=np.int32), count)[None, :]
        packed = call(
            functools.partial(pack_kernel, n_seq=n_seq),
            [
                *[shaped(n * (SPAN + 16), MODEL_WIDTH, bf) for n in (1, 2, 1)],
                *[shaped(n * SPAN, MODEL_WIDTH, bf) for n in (1, 2, 1)],
                shaped(MODEL_WIDTH, MODEL_WIDTH, bf),
            ],
            [span_order, hidden_in, out_grad, slots, offsets],
            [],
            2,
            scalars=(0,),
        )
        place = packed[6]
        first = jnp.concatenate(
            [
                rows_of(query_weight, Q_WIDTH),
                rows_of(key_weight, KV_WIDTH),
                rows_of(output_weight, MODEL_WIDTH),
                rows_of(value_weight, KV_WIDTH),
            ],
            axis=1,
        )

        down = down_weight.reshape(3, 16, MODEL_WIDTH).swapaxes(0, 1)
        down = jnp.pad(down, ((0, model_rows - 16), (0, 0), (0, DOWN_PITCH - MODEL_WIDTH)))
        ffn = jnp.concatenate(
            [
                rows_of(gate_weight, HIDDEN_UNITS),
                down.reshape(model_rows, 3 * DOWN_PITCH),
                rows_of(up_weight, HIDDEN_UNITS),
            ],
            axis=1,
        )
        first = gather_z(hold(first, place), until=(ffn,))
        first_a, first_b = first[:, :QK_WIDTH], first[:, QK_WIDTH:]
        first_a, first_b = gather_one(first_a, False), gather_one(first_b, True)
        x_parts = exchange(packed[:3], (first,), (first_a, first_b))
        one = (first_a, first_b)
        first_a, first_b = gather_two(first_a, False), gather_two(first_b, True)
        first = jnp.concatenate([first_a, first_b], axis=1)
        ffn = gather_z_stepwise(ffn, (one, (first,)))
        o_parts = exchange(hold(tuple(packed[3:6]), *one), (first,), (), (first,))
        first_other = swap(first, flip_core)
        ffn_a, ffn_b = ffn[:, :FFN_CUT], ffn[:, FFN_CUT:]

        frequency = np.exp(np.arange(HEAD_WIDTH // 2) * (-2.0 * math.log(10000.0) / HEAD_WIDTH))
        angles = np.arange(rows)[:, None] * frequency[None, :]
        cosine = np.tile(np.cos(angles), (1, 4)).astype(np.float32)
        sine = np.sin(angles)
        sine = np.concatenate([-sine, sine, -sine, sine], axis=1).astype(np.float32)

        padded = jax.ShapeDtypeStruct((2 * KEY_VALUE_HEADS, rows, LANES), bf)
        spans, x, normed, qk, kpad, vpad = call(
            project_kernel,
            [
                jax.ShapeDtypeStruct((n_seq,), jnp.int32),
                model_low,
                model_low,
                shaped(rows, QK_WIDTH, bf),
                padded,
                padded,
            ],
            [*x_parts, gain_one, place, cosine, sine, first, first_other],
            [pltpu.VMEM((MODEL_WIDTH, QK_WIDTH), bf)] * 2,
            5,
            out_specs=[SMEM_SPEC] + [VMEM_SPEC] * 5,
        )
        stats = [shaped(rows, LANES, f4), shaped(rows, 5 * LANES, f4)]
        lse, attn = call(attend_first_kernel, stats, [qk, kpad, vpad], [], 5)
        ffn_a, ffn_b = gather_one(ffn_a, False, (lse,)), gather_one(ffn_b, True, (lse,))
        lse, attn, merged, middle, normed_two = call(
            attend_last_kernel,
            [*stats, model_low, model_full, model_low],
            [lse, attn, x, qk, kpad, vpad, gain_two, place, first, first_other],
            [],
            5,
            alias={0: 0, 1: 1},
        )
        ffn = []
        for part, flip in ((ffn_a, flip_x), (ffn_b, flip_y)):
            second = swap(part, flip, (middle,))
            ffn += [part, second, swap(part, flip_core, (middle,)), swap(second, flip_core)]
        weight_scratch = [pltpu.VMEM((MODEL_WIDTH, HALF_FFN), bf)] * 2
        og, result, back, r1, r1_send, dd, w_down, w_later = call(
            functools.partial(ffn_first_kernel, order=order, n_seq=n_seq),
            [
                model_low,
                model_full,
                model_full,
                *[shaped(half, 2 * HALF_FFN, bf)] * 2,
                shaped(HALF_FFN, MODEL_WIDTH, bf),
                shaped(HIDDEN_UNITS, MODEL_WIDTH, bf),
                shaped(MODEL_WIDTH, 2 * HALF_FFN, bf),
            ],
            [spans, *o_parts, normed_two, *ffn],
            weight_scratch,
            10,
            scalars=(0,),
        )
        r1_own = r1
        *h_parts, back_middle, gain_two_grad, r2, r2_send = call(
            functools.partial(ffn_second_kernel, order=order, n_seq=n_seq),
            [
                *[shaped(n * SPAN, MODEL_WIDTH, bf) for n in (1, 2, 1)],
                model_full,
                shaped(1, MODEL_WIDTH, f4),
                *[shaped(half, SECOND_WIDTH, bf)] * 2,
            ],
            [spans, og, normed_two, w_later, w_down, result, back, dd, middle, gain_two, place],
            [
                pltpu.VMEM((HALF_FFN, MODEL_WIDTH), bf),
                pltpu.VMEM((HIDDEN_UNITS, MODEL_WIDTH), bf),
                pltpu.VMEM((MODEL_WIDTH, DOWN_PITCH), f4),
                pltpu.VMEM((rows, MODEL_WIDTH), f4),
                pltpu.VMEM((rows, MODEL_WIDTH), f4),
            ],
            13,
            scalars=(0,),
            megabytes=18,
        )
        r1 = scatter_core(r1_own, r1_send, (back_middle,))
        r3, r3_send, ab, lse_rows, correction, dqk, dv = call(
            attend_back_first_kernel,
            [
                *[shaped(half, 2 * HALF_FFN, bf)] * 2,
                shaped(rows, 5 * LANES, bf),
                shaped(LANES, rows, f4),
                shaped(16, rows, f4),
                shaped(rows, QK_WIDTH, f4),
                shaped(rows, 2 * LANES, bf),
            ],
            [qk, kpad, vpad, lse, attn, merged, back_middle, place, first, first_other],
            [],
            7,
            after=[r1],
        )
        r1 = scatter_one(r1, False, (ab,))
        r2 = scatter_core(r2, r2_send, (ab,))
        *g_parts, gain_one_grad, r3, r3_send = call(
            attend_back_kernel,
            [
                *[shaped(n * SPAN, MODEL_WIDTH, bf) for n in (1, 2, 1)],
                shaped(1, MODEL_WIDTH, f4),
                *[shaped(half, 2 * HALF_FFN, bf)] * 2,
            ],
            [
                r3, r3_send, spans, x, normed, qk, kpad, vpad, lse_rows, correction, ab, dqk, dv, back_middle,
                gain_one, place, cosine, sine, first, first_other,
            ],
            [
                pltpu.VMEM((rows, QK_WIDTH), f4),
                pltpu.VMEM((rows, 2 * LANES), bf),
                pltpu.VMEM((rows, QK_WIDTH), bf),
            ],
            10,
            scalars=(2,),
            after=[r2],
            alias={0: 3 + 1, 1: 3 + 2},
        )
        r1 = scatter_two(r1, False, (gain_one_grad,))
        r3 = scatter_core(r3, r3_send, (r1,))
        r2_a = scatter_one(r2[:, :SECOND_CUT], True, (r3,))
        r2_b = scatter_one(r2[:, SECOND_CUT:], False, (r3,))
        h_parts = exchange(h_parts, (ab,), (r3,))
        r3 = scatter_one(r3, False, (r2_a, r2_b))
        r2_a, r2_b = scatter_two(r2_a, True, (r3,)), scatter_two(r2_b, False, (r3,))
        g_parts = exchange(g_parts, (r2_a,), (r2_a,))
        r1 = scatter_z(r1, (r2_a, r2_b))
        hidden_out = unpack([hold(p, r2_a) for p in h_parts])
        r3 = scatter_two(r3, False, (r2_a, r2_b))
        r2 = scatter_z(jnp.concatenate([r2_a, r2_b], axis=1), (r3,))
        r3 = scatter_z(r3)
        hidden_grad = unpack(g_parts)
        gains = sum_everywhere(jnp.concatenate([gain_one_grad, gain_two_grad], axis=0))
        gu1 = r2[:, SECOND_GATE_AT:]
        gate_grad = jnp.concatenate([r1[:, :HALF_FFN], gu1[:, :HALF_FFN]], axis=1)
        up_grad = jnp.concatenate([r1[:, HALF_FFN:], gu1[:, HALF_FFN : 2 * HALF_FFN]], axis=1)
        down_grad = r2[:16, :SECOND_GATE_AT].reshape(16, 3, DOWN_PITCH)[:, :, :MODEL_WIDTH]
        return (
            hidden_out,
            hidden_grad,
            gains[0],
            r3[:, :Q_WIDTH].reshape(-1),
            r3[:, Q_WIDTH:QK_WIDTH].reshape(-1),
            r3[:, QK_WIDTH + MODEL_WIDTH :].reshape(-1),
            r3[:, QK_WIDTH : QK_WIDTH + MODEL_WIDTH].reshape(-1),
            gains[1],
            gate_grad.reshape(-1),
            up_grad.reshape(-1),
            down_grad.swapaxes(0, 1).reshape(-1),
        )

    return on_sequence_device


def pick_plan(mesh):
    count = mesh.shape["dp"] * mesh.shape["seq"]
    fits = (
        mesh.shape["seq"] == MB * SLOTS
        and SLOTS == 1
        and count & (count - 1) == 0
        and MODEL_WIDTH % count == 0
        and (HIDDEN_UNITS // count) % 16 == 0
    )
    return whole_sequence_plan(mesh) if fits else on_device


def solution(mesh):
    return jax.shard_map(
        pick_plan(mesh),
        mesh=mesh,
        in_specs=(
            P(("dp", "seq"), None),
            P(("dp", "seq")),
            P(),
            P(("dp", "seq")),
            P(("dp", "seq")),
            P(("dp", "seq")),
            P(("dp", "seq")),
            P(),
            P(("dp", "seq")),
            P(("dp", "seq")),
            P(("dp", "seq")),
            P(("dp", "seq"), None),
        ),
        out_specs=(
            P(("dp", "seq"), None),
            P(("dp", "seq"), None),
            P(),
            P(("dp", "seq")),
            P(("dp", "seq")),
            P(("dp", "seq")),
            P(("dp", "seq")),
            P(),
            P(("dp", "seq")),
            P(("dp", "seq")),
            P(("dp", "seq")),
        ),
        check_vma=False,
    )
```

```python
import functools
import math

import jax
import jax.numpy as jnp
import numpy as np
from jax import lax
from jax.experimental import pallas as pl
from jax.experimental.pallas import tpu as pltpu
from jax.sharding import PartitionSpec as P

MODEL_WIDTH = 576
QUERY_HEADS = 9
KEY_VALUE_HEADS = 3
HEAD_WIDTH = 64
HIDDEN_UNITS = 1536
SPAN = 128
MB = 4
SLOTS = 1


EPSILON = 1e-05


def angle_tables(positions, head_size):
    frequency = jnp.exp(
        jnp.arange(head_size // 2, dtype=jnp.float32) * (-2.0 * math.log(10000.0) / head_size)
    )
    angles = positions.astype(jnp.float32)[:, None] * frequency[None, :]
    angles = jnp.concatenate([angles, angles], axis=-1)[:, None, :]
    return (jnp.cos(angles), jnp.sin(angles))


def apply_rotation(value_rows, cosine_table, sine_values):
    half_size = value_rows.shape[-1] // 2
    turned = jnp.concatenate([-value_rows[..., half_size:], value_rows[..., :half_size]], axis=-1)
    return value_rows * cosine_table + turned * sine_values


def product(first_arg, second_arg):
    return jnp.dot(first_arg, second_arg, preferred_element_type=jnp.float32)


def inner_rows(first_arg, second_arg):
    return lax.dot_general(
        first_arg, second_arg, (((0,), (0,)), ((), ())), preferred_element_type=jnp.float32
    )


def inner_cols(first_arg, second_arg):
    return lax.dot_general(
        first_arg, second_arg, (((1,), (1,)), ((), ())), preferred_element_type=jnp.float32
    )


def shape_weights(flattened_rows):
    return (
        flattened_rows[0].reshape(MODEL_WIDTH, QUERY_HEADS * HEAD_WIDTH),
        flattened_rows[1].reshape(MODEL_WIDTH, KEY_VALUE_HEADS * HEAD_WIDTH),
        flattened_rows[2].reshape(MODEL_WIDTH, KEY_VALUE_HEADS * HEAD_WIDTH),
        flattened_rows[3].reshape(QUERY_HEADS * HEAD_WIDTH, MODEL_WIDTH),
        flattened_rows[4].reshape(MODEL_WIDTH, HIDDEN_UNITS),
        flattened_rows[5].reshape(MODEL_WIDTH, HIDDEN_UNITS),
        flattened_rows[6].reshape(HIDDEN_UNITS, MODEL_WIDTH),
    )


def block_scores(query_rows, key_block, query_place, key_place, factor):
    raw_scores = (
        jnp.einsum("qkgd,skd->kgqs", query_rows, key_block, preferred_element_type=jnp.float32)
        * factor
    )
    allowed = query_place[:, None] >= key_place[None, :]
    return jnp.where(allowed, raw_scores, -1e30)


def forward(layer_input, positions, span_ids, gain_pair, matrices):
    w_q, w_k, w_v, w_o, w_g, w_u, w_d = matrices
    count_of_rows = layer_input.shape[0]
    query_group_width = QUERY_HEADS // KEY_VALUE_HEADS
    factor = 1.0 / math.sqrt(HEAD_WIDTH)
    input_full = layer_input.astype(jnp.float32)
    scale_one = lax.rsqrt(jnp.mean(input_full * input_full, axis=-1, keepdims=True) + EPSILON)
    unit_one = input_full * scale_one
    normed = (unit_one * gain_pair[0]).astype(jnp.bfloat16)
    query_rows = product(normed, w_q)
    unrotated_keys = product(normed, w_k)
    value_rows = product(normed, w_v)
    cosine_table, sine_values = angle_tables(positions, HEAD_WIDTH)
    rotated_query = apply_rotation(
        query_rows.reshape(count_of_rows, QUERY_HEADS, HEAD_WIDTH), cosine_table, sine_values
    ).astype(jnp.bfloat16)
    rotated_query = rotated_query.reshape(
        count_of_rows, KEY_VALUE_HEADS, query_group_width, HEAD_WIDTH
    )
    rotated_key = apply_rotation(
        unrotated_keys.reshape(count_of_rows, KEY_VALUE_HEADS, HEAD_WIDTH),
        cosine_table,
        sine_values,
    ).astype(jnp.bfloat16)
    rotated_key = rotated_key.reshape(count_of_rows, KEY_VALUE_HEADS * HEAD_WIDTH)
    v_low = value_rows.astype(jnp.bfloat16)
    every_key, every_value, key_spans = (
        lax.all_gather(rotated_key, "seq", axis=0, tiled=True),
        lax.all_gather(v_low, "seq", axis=0, tiled=True),
        lax.all_gather(span_ids.astype(jnp.bfloat16), "seq", axis=0, tiled=True),
    )
    offsets = jnp.arange(SPAN, dtype=jnp.int32)
    key_places = (key_spans.astype(jnp.int32)[:, None] * SPAN + offsets[None, :]).reshape(-1)
    count_of_keys = every_key.shape[0]
    block_length = math.gcd(count_of_keys, 512)
    count_of_blocks = count_of_keys // block_length
    blocks_of_keys = every_key.reshape(count_of_blocks, block_length, KEY_VALUE_HEADS, HEAD_WIDTH)
    blocks_of_values = every_value.reshape(
        count_of_blocks, block_length, KEY_VALUE_HEADS, HEAD_WIDTH
    )
    place_blocks = key_places.reshape(count_of_blocks, block_length)

    def softmax_stats(carry, piece_set):
        highest, totals = carry
        key_block, key_place = piece_set
        scores = block_scores(rotated_query, key_block, positions, key_place, factor)
        new_high = jnp.maximum(highest, jnp.max(scores, axis=-1))
        totals = totals * jnp.exp(highest - new_high) + jnp.sum(
            jnp.exp(scores - new_high[..., None]), axis=-1
        )
        return ((new_high, totals), None)

    initial = (
        jnp.full((KEY_VALUE_HEADS, query_group_width, count_of_rows), -1e30, jnp.float32),
        jnp.zeros((KEY_VALUE_HEADS, query_group_width, count_of_rows), jnp.float32),
    )
    (highest, totals), _ = lax.scan(softmax_stats, initial, (blocks_of_keys, place_blocks))

    def mix_values(running, piece_set):
        key_block, value_block, key_place = piece_set
        scores = block_scores(rotated_query, key_block, positions, key_place, factor)
        layer_weights = (jnp.exp(scores - highest[..., None]) / totals[..., None]).astype(
            jnp.bfloat16
        )
        return (
            running
            + jnp.einsum(
                "kgqs,skd->qkgd", layer_weights, value_block, preferred_element_type=jnp.float32
            ),
            None,
        )

    attention_output, _ = lax.scan(
        mix_values,
        jnp.zeros((count_of_rows, KEY_VALUE_HEADS, query_group_width, HEAD_WIDTH), jnp.float32),
        (blocks_of_keys, blocks_of_values, place_blocks),
    )
    attention_output = attention_output.reshape(count_of_rows, QUERY_HEADS * HEAD_WIDTH)
    merged = attention_output.astype(jnp.bfloat16)
    middle = input_full + product(merged, w_o)
    scale_two = lax.rsqrt(jnp.mean(middle * middle, axis=-1, keepdims=True) + EPSILON)
    unit_two = middle * scale_two
    normed_two = (unit_two * gain_pair[1]).astype(jnp.bfloat16)
    gate_act = product(normed_two, w_g)
    upward = product(normed_two, w_u)
    hidden = (jax.nn.silu(gate_act) * upward).astype(jnp.bfloat16)
    result = (middle + product(hidden, w_d)).astype(jnp.bfloat16)
    stored = (
        scale_one,
        unit_one,
        normed,
        cosine_table,
        sine_values,
        rotated_query,
        blocks_of_keys,
        blocks_of_values,
        place_blocks,
        highest,
        totals,
        attention_output,
        merged,
        scale_two,
        unit_two,
        normed_two,
        gate_act,
        upward,
        hidden,
    )
    return (result, stored)


def backward(cotangent, positions, gain_pair, matrices, stored):
    w_q, w_k, w_v, w_o, w_g, w_u, w_d = matrices
    (
        scale_one,
        unit_one,
        normed,
        cosine_table,
        sine_values,
        rotated_query,
        blocks_of_keys,
        blocks_of_values,
        place_blocks,
        highest,
        totals,
        attention_output,
        merged,
        scale_two,
        unit_two,
        normed_two,
        gate_act,
        upward,
        hidden,
    ) = stored
    count_of_rows = cotangent.shape[0]
    query_group_width = QUERY_HEADS // KEY_VALUE_HEADS
    factor = 1.0 / math.sqrt(HEAD_WIDTH)
    grad_down = inner_rows(hidden, cotangent)
    back_hidden = inner_cols(cotangent, w_d)
    sigmoid_gate = jax.nn.sigmoid(gate_act)
    back_gate = (
        back_hidden * upward * sigmoid_gate * (1.0 + gate_act * (1.0 - sigmoid_gate))
    ).astype(jnp.bfloat16)
    back_up = (back_hidden * (gate_act * sigmoid_gate)).astype(jnp.bfloat16)
    grad_gate = inner_rows(normed_two, back_gate)
    grad_up = inner_rows(normed_two, back_up)
    back_norm_two = inner_cols(back_gate, w_g) + inner_cols(back_up, w_u)
    gain_two = jnp.sum(back_norm_two * unit_two, axis=0)
    back_unit = back_norm_two * gain_pair[1]
    back_middle = cotangent.astype(jnp.float32) + scale_two * (
        back_unit - unit_two * jnp.mean(back_unit * unit_two, axis=-1, keepdims=True)
    )
    middle_low = back_middle.astype(jnp.bfloat16)
    grad_out = inner_rows(merged, middle_low)
    attention_backward = inner_cols(middle_low, w_o).astype(jnp.bfloat16)
    head_gradient_rows = attention_backward.reshape(
        count_of_rows, KEY_VALUE_HEADS, query_group_width, HEAD_WIDTH
    )
    attention_head_rows = attention_output.reshape(
        count_of_rows, KEY_VALUE_HEADS, query_group_width, HEAD_WIDTH
    )
    correction = jnp.transpose(
        jnp.sum(head_gradient_rows.astype(jnp.float32) * attention_head_rows, axis=-1), (1, 2, 0)
    )

    def score_grads(running, piece_set):
        key_block, value_block, key_place = piece_set
        scores = block_scores(rotated_query, key_block, positions, key_place, factor)
        probs = jnp.exp(scores - highest[..., None]) / totals[..., None]
        back_probs = jnp.einsum(
            "qkgd,skd->kgqs", head_gradient_rows, value_block, preferred_element_type=jnp.float32
        )
        back_scores = (probs * (back_probs - correction[..., None])).astype(jnp.bfloat16)
        running = (
            running
            + jnp.einsum(
                "kgqs,skd->qkgd", back_scores, key_block, preferred_element_type=jnp.float32
            )
            * factor
        )
        key_grad = (
            jnp.einsum(
                "kgqs,qkgd->skd", back_scores, rotated_query, preferred_element_type=jnp.float32
            )
            * factor
        )
        value_grad = jnp.einsum(
            "kgqs,qkgd->skd",
            probs.astype(jnp.bfloat16),
            head_gradient_rows,
            preferred_element_type=jnp.float32,
        )
        return (running, (key_grad, value_grad))

    back_query, (gradient_of_keys, gradient_of_values) = lax.scan(
        score_grads,
        jnp.zeros((count_of_rows, KEY_VALUE_HEADS, query_group_width, HEAD_WIDTH), jnp.float32),
        (blocks_of_keys, blocks_of_values, place_blocks),
    )
    count_of_keys = gradient_of_keys.shape[0] * gradient_of_keys.shape[1]
    local_keys, value_own = (
        lax.psum_scatter(
            gradient_of_keys.reshape(count_of_keys, KEY_VALUE_HEADS * HEAD_WIDTH).astype(
                jnp.bfloat16
            ),
            "seq",
            scatter_dimension=0,
            tiled=True,
        ).astype(jnp.float32),
        lax.psum_scatter(
            gradient_of_values.reshape(count_of_keys, KEY_VALUE_HEADS * HEAD_WIDTH).astype(
                jnp.bfloat16
            ),
            "seq",
            scatter_dimension=0,
            tiled=True,
        ).astype(jnp.float32),
    )
    query_low = (
        apply_rotation(
            back_query.reshape(count_of_rows, QUERY_HEADS, HEAD_WIDTH), cosine_table, -sine_values
        )
        .astype(jnp.bfloat16)
        .reshape(count_of_rows, QUERY_HEADS * HEAD_WIDTH)
    )
    key_low = (
        apply_rotation(
            local_keys.reshape(count_of_rows, KEY_VALUE_HEADS, HEAD_WIDTH),
            cosine_table,
            -sine_values,
        )
        .astype(jnp.bfloat16)
        .reshape(count_of_rows, KEY_VALUE_HEADS * HEAD_WIDTH)
    )
    value_low = value_own.astype(jnp.bfloat16)
    grad_query = inner_rows(normed, query_low)
    grad_key = inner_rows(normed, key_low)
    grad_value = inner_rows(normed, value_low)
    back_norm_one = (
        inner_cols(query_low, w_q) + inner_cols(key_low, w_k) + inner_cols(value_low, w_v)
    )
    gain_one = jnp.sum(back_norm_one * unit_one, axis=0)
    back_unit_one = back_norm_one * gain_pair[0]
    input_back = back_middle + scale_one * (
        back_unit_one - unit_one * jnp.mean(back_unit_one * unit_one, axis=-1, keepdims=True)
    )
    weight_terms = (grad_query, grad_key, grad_value, grad_out, grad_gate, grad_up, grad_down)
    return (input_back.astype(jnp.bfloat16), weight_terms, (gain_one, gain_two))


def on_device(
    hidden_in,
    span_order,
    attention_norm_gain,
    query_weight,
    key_weight,
    value_weight,
    output_weight,
    feedforward_gain,
    gate_weight,
    up_weight,
    down_weight,
    out_grad,
):
    count_of_rows = SLOTS * SPAN
    gain_pair = (attention_norm_gain.astype(jnp.float32), feedforward_gain.astype(jnp.float32))
    offsets = jnp.arange(SPAN, dtype=jnp.int32)
    weight_totals = (
        jnp.zeros((MODEL_WIDTH, QUERY_HEADS * HEAD_WIDTH), jnp.float32),
        jnp.zeros((MODEL_WIDTH, KEY_VALUE_HEADS * HEAD_WIDTH), jnp.float32),
        jnp.zeros((MODEL_WIDTH, KEY_VALUE_HEADS * HEAD_WIDTH), jnp.float32),
        jnp.zeros((QUERY_HEADS * HEAD_WIDTH, MODEL_WIDTH), jnp.float32),
        jnp.zeros((MODEL_WIDTH, HIDDEN_UNITS), jnp.float32),
        jnp.zeros((MODEL_WIDTH, HIDDEN_UNITS), jnp.float32),
        jnp.zeros((HIDDEN_UNITS, MODEL_WIDTH), jnp.float32),
    )
    gain_totals = (jnp.zeros((MODEL_WIDTH,), jnp.float32), jnp.zeros((MODEL_WIDTH,), jnp.float32))
    outputs = []
    input_grads = []
    for micro_index in range(MB):
        layer_input = hidden_in[micro_index * count_of_rows : (micro_index + 1) * count_of_rows]
        cotangent = out_grad[micro_index * count_of_rows : (micro_index + 1) * count_of_rows]
        span_ids = span_order[micro_index * SLOTS : (micro_index + 1) * SLOTS]
        positions = (span_ids[:, None] * SPAN + offsets[None, :]).reshape(count_of_rows)
        forward_weights = shape_weights(
            (
                lax.all_gather(query_weight, ("dp", "seq"), axis=0, tiled=True),
                lax.all_gather(key_weight, ("dp", "seq"), axis=0, tiled=True),
                lax.all_gather(value_weight, ("dp", "seq"), axis=0, tiled=True),
                lax.all_gather(output_weight, ("dp", "seq"), axis=0, tiled=True),
                lax.all_gather(gate_weight, ("dp", "seq"), axis=0, tiled=True),
                lax.all_gather(up_weight, ("dp", "seq"), axis=0, tiled=True),
                lax.all_gather(down_weight, ("dp", "seq"), axis=0, tiled=True),
            )
        )
        result, stored = forward(layer_input, positions, span_ids, gain_pair, forward_weights)
        backward_weights = shape_weights(
            (
                lax.all_gather(query_weight, ("dp", "seq"), axis=0, tiled=True),
                lax.all_gather(key_weight, ("dp", "seq"), axis=0, tiled=True),
                lax.all_gather(value_weight, ("dp", "seq"), axis=0, tiled=True),
                lax.all_gather(output_weight, ("dp", "seq"), axis=0, tiled=True),
                lax.all_gather(gate_weight, ("dp", "seq"), axis=0, tiled=True),
                lax.all_gather(up_weight, ("dp", "seq"), axis=0, tiled=True),
                lax.all_gather(down_weight, ("dp", "seq"), axis=0, tiled=True),
            )
        )
        input_back, weight_terms, gain_terms = backward(
            cotangent, positions, gain_pair, backward_weights, stored
        )
        weight_totals = tuple(
            (running + term for running, term in zip(weight_totals, weight_terms))
        )
        gain_totals = tuple((running + term for running, term in zip(gain_totals, gain_terms)))
        outputs.append(result)
        input_grads.append(input_back)
    grad_query, grad_key, grad_value, grad_out, grad_gate, grad_up, grad_down = weight_totals
    owned = (
        lax.psum_scatter(grad_query.reshape(-1), ("dp", "seq"), scatter_dimension=0, tiled=True),
        lax.psum_scatter(grad_key.reshape(-1), ("dp", "seq"), scatter_dimension=0, tiled=True),
        lax.psum_scatter(grad_value.reshape(-1), ("dp", "seq"), scatter_dimension=0, tiled=True),
        lax.psum_scatter(grad_out.reshape(-1), ("dp", "seq"), scatter_dimension=0, tiled=True),
        lax.psum_scatter(grad_gate.reshape(-1), ("dp", "seq"), scatter_dimension=0, tiled=True),
        lax.psum_scatter(grad_up.reshape(-1), ("dp", "seq"), scatter_dimension=0, tiled=True),
        lax.psum_scatter(grad_down.reshape(-1), ("dp", "seq"), scatter_dimension=0, tiled=True),
    )
    gain_one, gain_two = lax.psum((gain_totals[0], gain_totals[1]), ("dp", "seq"))
    return (
        jnp.concatenate(outputs, axis=0),
        jnp.concatenate(input_grads, axis=0),
        gain_one,
        owned[0],
        owned[1],
        owned[2],
        owned[3],
        gain_two,
        owned[4],
        owned[5],
        owned[6],
    )


FACTOR = 1.0 / math.sqrt(HEAD_WIDTH)
KV_WIDTH = KEY_VALUE_HEADS * HEAD_WIDTH
Q_WIDTH = QUERY_HEADS * HEAD_WIDTH
QK_WIDTH = Q_WIDTH + KV_WIDTH
LANES = 128
HALF_FFN = HIDDEN_UNITS // 2
FFN_BLOCK = 256
DOWN_PITCH = 640
DOWN_AT = HALF_FFN
DOWN_EARLY = 2
FFN_CUT = DOWN_AT + DOWN_EARLY * DOWN_PITCH
UP_AT = (3 - DOWN_EARLY) * DOWN_PITCH
SECOND_GATE_AT = 3 * DOWN_PITCH
SECOND_WIDTH = SECOND_GATE_AT + 2 * HALF_FFN
SECOND_CUT = SECOND_WIDTH // 3


def vmem_params(megabytes=48):
    return pltpu.CompilerParams(vmem_limit_bytes=megabytes * 1024 * 1024)


def dot_nn(a, b):
    return jnp.dot(a, b, preferred_element_type=jnp.float32)


def dot_tn(a, b):
    return lax.dot_general(a, b, (((0,), (0,)), ((), ())), preferred_element_type=jnp.float32)


def dot_nt(a, b):
    return lax.dot_general(a, b, (((1,), (1,)), ((), ())), preferred_element_type=jnp.float32)


def low(v):
    return v.astype(jnp.bfloat16)


def wide(v):
    return v.astype(jnp.float32)


def place_back(v, place):
    high = low(v)
    rest = low(v - high.astype(jnp.float32))
    return dot_nt(high, place) + dot_nt(rest, place)


def half_turn(u, lane):
    return jnp.where(
        lane % HEAD_WIDTH < HEAD_WIDTH // 2,
        pltpu.roll(u, LANES - HEAD_WIDTH // 2, 1),
        pltpu.roll(u, HEAD_WIDTH // 2, 1),
    )


def padded_heads(blocks, head, lane):
    here = blocks[head // 2]
    moved = pltpu.roll(here, HEAD_WIDTH, 1)
    low_half, high_half = (here, moved) if head % 2 == 0 else (moved, here)
    zero = jnp.zeros_like(here)
    return (
        low(jnp.where(lane < HEAD_WIDTH, low_half, zero)),
        low(jnp.where(lane >= HEAD_WIDTH, high_half, zero)),
    )


def pack_kernel(
    span_order, hidden_in, out_grad, slots, offsets,
    x_mine, x_near, x_far, o_mine, o_near, o_far, place, *, n_seq,
):
    seq = lax.axis_index("seq")
    me = lax.axis_index("dp") * n_seq + seq
    tall = SPAN + 16
    for flip, x, o, at in ((0, x_mine, o_mine, 0), (1, x_near, o_near, 0), (3, x_near, o_near, 1), (2, x_far, o_far, 0)):
        origin = seq ^ flip
        block = pl.ds(pl.multiple_of(origin * SPAN, SPAN), SPAN)
        x[at * tall : at * tall + SPAN] = hidden_in[block, :]
        number = jnp.full((16, MODEL_WIDTH), span_order[origin], jnp.int32)
        x[at * tall + SPAN : (at + 1) * tall] = low(number.astype(jnp.float32))
        o[at * SPAN : (at + 1) * SPAN] = out_grad[block, :]
    natural = (slots[...] ^ me) * (MODEL_WIDTH // (n_seq * lax.axis_size("dp"))) + offsets[...]
    row = lax.broadcasted_iota(jnp.int32, place.shape, 0)
    place[...] = low((row == natural).astype(jnp.float32))


def unpack_kernel(mine, near, far, out):
    seq = lax.axis_index("seq")
    for flip, source, at in ((0, mine, 0), (1, near, 0), (2, far, 0), (3, far, 1)):
        target = pl.ds(pl.multiple_of((seq ^ flip) * SPAN, SPAN), SPAN)
        out[target, :] = source[at * SPAN : (at + 1) * SPAN]


def project_kernel(
    x_mine, x_near, x_far, gain_one, place, cosine, sine, wab, wab2,
    spans, x_out, normed_out, qk_out, kpad_out, vpad_out, wqk, wov,
):
    rows = x_out.shape[0]
    half = wab.shape[0]
    tall = SPAN + 16
    for k, (block, at) in enumerate(((x_mine, 0), (x_near, 0), (x_far, 0), (x_far, tall))):
        number = jnp.max(block[at + SPAN : at + tall, :LANES].astype(jnp.float32))
        number = number.astype(jnp.int32)
        spans[k] = number
        x_out[pl.ds(pl.multiple_of(number * SPAN, SPAN), SPAN), :] = block[at : at + SPAN]
    wa, wb = wab.at[:, :QK_WIDTH], wab.at[:, QK_WIDTH:]
    wa2, wb2 = wab2.at[:, :QK_WIDTH], wab2.at[:, QK_WIDTH:]
    wqk[:half] = wa[...]
    wqk[half:] = wa2[...]
    wov[:half] = wb[...]
    wov[half:] = wb2[...]
    x = x_out[...].astype(jnp.float32)
    scale = lax.rsqrt(jnp.mean(x * x, axis=-1, keepdims=True) + EPSILON)
    normed = low(x * scale * gain_one[...])
    normed_out[...] = low(dot_nn(normed, place[...]))
    lane = lax.broadcasted_iota(jnp.int32, (rows, LANES), 1)
    cos, sin = cosine[...], sine[...]
    k_blocks = []
    for b in range(QK_WIDTH // LANES):
        u = dot_nn(normed_out[...], wqk[:, b * LANES : (b + 1) * LANES])
        turned = u * cos + half_turn(u, lane) * sin
        turned = low(turned).astype(jnp.float32)
        if (b + 1) * LANES > Q_WIDTH:
            k_blocks.append(turned)
        if (b + 1) * LANES <= Q_WIDTH:
            turned = turned * FACTOR
        elif b * LANES < Q_WIDTH:
            turned = jnp.where(lane < Q_WIDTH - b * LANES, turned * FACTOR, turned)
        qk_out[:, b * LANES : (b + 1) * LANES] = low(turned)
    first_group = QUERY_HEADS - 2 * (Q_WIDTH // LANES)
    for j in range(KEY_VALUE_HEADS):
        lo, hi = padded_heads(k_blocks, j + first_group, lane)
        kpad_out[2 * j] = lo
        kpad_out[2 * j + 1] = hi
    v = dot_nn(normed_out[...], wov[:, MODEL_WIDTH:])
    v = low(v).astype(jnp.float32)
    v = jnp.concatenate([v, jnp.zeros((rows, HEAD_WIDTH), jnp.float32)], axis=1)
    v_blocks = [v[:, :LANES], v[:, LANES:]]
    for j in range(KEY_VALUE_HEADS):
        lo, hi = padded_heads(v_blocks, j, lane)
        vpad_out[2 * j] = lo
        vpad_out[2 * j + 1] = hi


def attend_spans(spans, qk, kpad, vpad, lse_out, attn_out):
    lane_q = lax.broadcasted_iota(jnp.int32, (SPAN, LANES), 1)
    diagonal = lax.broadcasted_iota(jnp.int32, (SPAN, SPAN), 0) >= lax.broadcasted_iota(
        jnp.int32, (SPAN, SPAN), 1
    )
    groups = QUERY_HEADS // KEY_VALUE_HEADS
    for i in spans:
        here = slice(i * SPAN, (i + 1) * SPAN)
        lse = jnp.zeros((SPAN, LANES), jnp.float32)
        for b in range((QUERY_HEADS + 1) // 2):
            mixed = None
            for h in range(2 * b, min(2 * b + 2, QUERY_HEADS)):
                slot = 2 * (h // groups) + h % 2
                q = qk[here, b * LANES : (b + 1) * LANES]
                s = dot_nt(q, kpad[slot, : (i + 1) * SPAN, :])
                s_last = jnp.where(diagonal, s[:, i * SPAN :], -1e30)
                s = s_last if i == 0 else jnp.concatenate([s[:, : i * SPAN], s_last], axis=1)
                top = jnp.max(s, axis=-1, keepdims=True)
                p = jnp.exp(s - top)
                total = jnp.sum(p, axis=-1, keepdims=True)
                p = low(p * (1.0 / total))
                lse = jnp.where(lane_q == h, top + jnp.log(total), lse)
                part = dot_nn(p, vpad[slot, : (i + 1) * SPAN, :])
                mixed = part if mixed is None else mixed + part
            attn_out[here, b * LANES : (b + 1) * LANES] = mixed
        lse_out[here, :] = lse


def attend_first_kernel(qk, kpad, vpad, lse_out, attn_out):
    attend_spans(range(qk.shape[0] // SPAN - 1), qk, kpad, vpad, lse_out, attn_out)


def attend_last_kernel(
    lse_in, attn_in, x_in, qk, kpad, vpad, gain_two, place, wab, wab2,
    lse_out, attn_out, merged_out, middle_out, normed_two_out,
):
    rows = x_in.shape[0]
    half = wab.shape[0]
    wb, wb2 = wab.at[:, QK_WIDTH:], wab2.at[:, QK_WIDTH:]
    attend_spans([rows // SPAN - 1], qk, kpad, vpad, lse_out, attn_out)
    merged = low(dot_nn(low(attn_out[:, :Q_WIDTH]), place[...]))
    merged_out[...] = merged
    middle = (
        x_in[...].astype(jnp.float32)
        + dot_nn(merged[:, :half], wb[:, :MODEL_WIDTH])
        + dot_nn(merged[:, half:], wb2[:, :MODEL_WIDTH])
    )
    middle_out[...] = middle
    scale_two = lax.rsqrt(jnp.mean(middle * middle, axis=-1, keepdims=True) + EPSILON)
    normed_two_out[...] = low(dot_nn(low(middle * scale_two * gain_two[...]), place[...]))


def ffn_block(n2, og, wg, wu, wd, at, result, back_norm, d_keep, d_send, dd_out):
    columns = pl.ds(pl.multiple_of(at * FFN_BLOCK, FFN_BLOCK), FFN_BLOCK)
    up_columns = pl.ds(pl.multiple_of(HALF_FFN + at * FFN_BLOCK, FFN_BLOCK), FFN_BLOCK)
    half = d_keep.shape[0]
    w_gate, w_up, w_down = wg[:, columns], wu[:, columns], wd[columns, :]
    gate = dot_nn(n2, w_gate)
    up = dot_nn(n2, w_up)
    back_hidden = dot_nt(og, w_down)
    sigmoid = jax.nn.sigmoid(gate)
    silu = gate * sigmoid
    hidden = low(silu * up)
    back_gate = low(back_hidden * up * sigmoid * (1.0 + gate * (1.0 - sigmoid)))
    back_up = low(back_hidden * silu)
    dd_out[columns, :] = low(dot_tn(hidden, og))
    dg = low(dot_tn(n2, back_gate))
    du = low(dot_tn(n2, back_up))
    d_keep[:, columns] = dg[:half]
    d_send[:, columns] = dg[half:]
    d_keep[:, up_columns] = du[:half]
    d_send[:, up_columns] = du[half:]
    result[...] += dot_nn(hidden, w_down)
    back_norm[...] += dot_nt(back_gate, w_gate) + dot_nt(back_up, w_up)


def fill_gate(target, a0, a1, a2, a3):
    size = a0.shape[0] // 2
    for core, (first, second) in enumerate(((a0, a1), (a2, a3))):
        for at, source in enumerate((first, second, first, second)):
            start = (4 * core + at) * size
            piece = slice(at // 2 * size, (at // 2 + 1) * size)
            target[start : start + size] = source[piece, :HALF_FFN]


def fill_up(target, column, b0, b1, b2, b3):
    for at, source in enumerate((b0, b1, b2, b3)):
        size = source.shape[0]
        target[at * size : (at + 1) * size] = source[:, column : column + HALF_FFN]


def ffn_first_kernel(
    spans, o_mine, o_near, o_far, n2, a0, a1, a2, a3, b0, b1, b2, b3,
    og_out, result_out, back_out, d_keep, d_send, dd, wd_out,
    wg, wu, *, order, n_seq,
):
    me = lax.axis_index("dp") * n_seq + lax.axis_index("seq")
    for k, (block, at) in enumerate(((o_mine, 0), (o_near, 0), (o_far, 0), (o_far, SPAN))):
        target = pl.ds(pl.multiple_of(spans[k] * SPAN, SPAN), SPAN)
        og_out[target, :] = block[at : at + SPAN]
    size = a0.shape[0] // 2
    fill_gate(wg, a0, a1, a2, a3)
    fill_up(wu, UP_AT, b0, b1, b2, b3)
    count = len(order)
    rows, pitch = wd_out.shape[0] // count, MODEL_WIDTH // count
    each = size // pitch
    for slot, relative in enumerate(order):
        core, block, at = slot // (4 * each), slot // each % 4, slot % each
        x_side, y_side = block % 2, block // 2
        for t in range(rows // 16):
            if t < DOWN_EARLY:
                source = ((a0, a1), (a2, a3))[core][x_side]
                start = y_side * size + at * pitch
                first = DOWN_AT + t * DOWN_PITCH
            else:
                source = ((b0, b1), (b2, b3))[core][y_side]
                start = x_side * size + at * pitch
                first = (t - DOWN_EARLY) * DOWN_PITCH
            target = pl.multiple_of((me ^ relative) * rows + 16 * t, 16)
            wd_out[pl.ds(target, 16), :] = source[start : start + 16, first : first + MODEL_WIDTH]
    result_out[...] = jnp.zeros_like(result_out)
    back_out[...] = jnp.zeros_like(back_out)

    @pl.loop(0, HALF_FFN // FFN_BLOCK)
    def _(at):
        ffn_block(
            n2[...], og_out[...], wg, wu, wd_out, at, result_out, back_out, d_keep, d_send, dd
        )


def ffn_second_kernel(
    spans, og, n2, a0, a1, a2, a3, b0, b1, b2, b3,
    wd_in, result_in, back_in, dd_in, middle, gain_two, place,
    mine, near, far, back_middle_out, gain_out, keep_out, send_out,
    wg, wu, wd, dd, spread, result, back, *, order, n_seq,
):
    half = keep_out.shape[0]
    fill_gate(wg, a0, a1, a2, a3)
    fill_up(wu, 0, b0, b1, b2, b3)
    me = lax.axis_index("dp") * n_seq + lax.axis_index("seq")
    d_keep = keep_out.at[:, SECOND_GATE_AT : SECOND_GATE_AT + 2 * HALF_FFN]
    d_send = send_out.at[:, SECOND_GATE_AT : SECOND_GATE_AT + 2 * HALF_FFN]
    wd[...] = wd_in[HALF_FFN:, :]
    dd[:HALF_FFN] = dd_in[...]
    result[...] = result_in[...] + middle[...]
    back[...] = back_in[...]

    @pl.loop(0, HALF_FFN // FFN_BLOCK)
    def _(at):
        ffn_block(
            n2[...], og[...], wg, wu, wd, at, result, back, d_keep, d_send, dd.at[HALF_FFN:, :]
        )

    count = len(order)
    rows, pitch = HIDDEN_UNITS // count, MODEL_WIDTH // count
    spread[...] = jnp.zeros_like(spread)
    for t in range(rows // 16):
        for slot, relative in enumerate(order):
            source = pl.ds(pl.multiple_of((me ^ relative) * rows + 16 * t, 16), 16)
            spread[slot * pitch : slot * pitch + 16, :MODEL_WIDTH] = wide(dd[source, :])
        columns = slice(t * DOWN_PITCH, (t + 1) * DOWN_PITCH)
        keep_out[:, columns] = low(spread[:half])
        send_out[:, columns] = low(spread[half:])

    for k, (block, at) in enumerate(((mine, 0), (near, 0), (far, 0), (near, SPAN))):
        source = pl.ds(pl.multiple_of(spans[k] * SPAN, SPAN), SPAN)
        block[at : at + SPAN] = low(result[source, :])
    mid = middle[...]
    scale = lax.rsqrt(jnp.mean(mid * mid, axis=-1, keepdims=True) + EPSILON)
    unit = mid * scale
    back_norm = place_back(back[...], place[...])
    gain_out[...] = jnp.sum(back_norm * unit, axis=0, keepdims=True)
    back_unit = back_norm * gain_two[...]
    back_middle_out[...] = og[...].astype(jnp.float32) + scale * (
        back_unit - unit * jnp.mean(back_unit * unit, axis=-1, keepdims=True)
    )


def score_back(i, qk, kpad, vpad, ab, lse_rows, correction, dqk, dv):
    rows = qk.shape[0]
    groups = QUERY_HEADS // KEY_VALUE_HEADS
    diagonal = lax.broadcasted_iota(jnp.int32, (SPAN, SPAN), 1) >= lax.broadcasted_iota(
        jnp.int32, (SPAN, SPAN), 0
    )
    lane = lax.broadcasted_iota(jnp.int32, (SPAN, LANES), 1)
    keys = slice(i * SPAN, (i + 1) * SPAN)
    first = i * SPAN
    dk_sums = [None] * (2 * KEY_VALUE_HEADS)
    dv_sums = [None] * (2 * KEY_VALUE_HEADS)
    for b in range((QUERY_HEADS + 1) // 2):
        columns = slice(b * LANES, (b + 1) * LANES)
        q = qk[first:, columns]
        a = ab[first:, columns]
        dq = None
        for h in range(2 * b, min(2 * b + 2, QUERY_HEADS)):
            slot = 2 * (h // groups) + h % 2
            s = dot_nt(kpad[slot, keys, :], q)
            s = s - lse_rows[h : h + 1, first:]
            s_first = jnp.where(diagonal, s[:, :SPAN], -1e30)
            s = (
                s_first
                if first + SPAN == rows
                else jnp.concatenate([s_first, s[:, SPAN:]], axis=1)
            )
            p = jnp.exp(s)
            dp = dot_nt(vpad[slot, keys, :], a)
            ds = low(p * (dp - correction[h : h + 1, first:]))
            dk = dot_nn(ds, q)
            dvh = dot_nn(low(p), a)
            dk_sums[slot] = dk if dk_sums[slot] is None else dk_sums[slot] + dk
            dv_sums[slot] = dvh if dv_sums[slot] is None else dv_sums[slot] + dvh
            part = dot_tn(ds, kpad[slot, keys, :])
            dq = part if dq is None else dq + part
        if i == 0:
            dqk[first:, columns] = dq
        else:
            dqk[first:, columns] += dq

    def both(sums, j):
        return sums[2 * j] + pltpu.roll(sums[2 * j + 1], HEAD_WIDTH, 1)

    dk_heads = [both(dk_sums, j) for j in range(KEY_VALUE_HEADS)]
    dv_heads = [both(dv_sums, j) for j in range(KEY_VALUE_HEADS)]
    key_scale = 1.0 / FACTOR
    q_tail = dqk[keys, 4 * LANES : 5 * LANES]
    dqk[keys, 4 * LANES : 5 * LANES] = jnp.where(
        lane < HEAD_WIDTH, q_tail, pltpu.roll(dk_heads[0], HEAD_WIDTH, 1) * key_scale
    )
    dqk[keys, 5 * LANES :] = (
        jnp.where(lane < HEAD_WIDTH, dk_heads[1], pltpu.roll(dk_heads[2], HEAD_WIDTH, 1))
        * key_scale
    )
    dv[keys, :LANES] = low(
        jnp.where(lane < HEAD_WIDTH, dv_heads[0], pltpu.roll(dv_heads[1], HEAD_WIDTH, 1))
    )
    dv[keys, LANES:] = low(dv_heads[2])


def attend_back_first_kernel(
    qk, kpad, vpad, lse, attn, merged, back_middle, place, wab, wab2,
    keep_out, send_out, ab, lse_rows, correction, dqk, dv,
):
    rows = qk.shape[0]
    half = wab.shape[0]
    wb, wb2 = wab.at[:, QK_WIDTH:], wab2.at[:, QK_WIDTH:]
    middle_low = low(back_middle[...])
    d_out = low(dot_tn(merged[...], middle_low))
    out_columns = slice(QK_WIDTH, QK_WIDTH + MODEL_WIDTH)
    keep_out[:half, out_columns] = d_out[:half]
    send_out[:half, out_columns] = d_out[half:]
    ab_first = low(dot_nt(middle_low, wb[:, :MODEL_WIDTH]))
    ab_second = low(dot_nt(middle_low, wb2[:, :MODEL_WIDTH]))
    ab[:, :Q_WIDTH] = low(
        dot_nt(ab_first, place[:, :half]) + dot_nt(ab_second, place[:, half:])
    )
    ab[:, Q_WIDTH:] = jnp.zeros((rows, ab.shape[1] - Q_WIDTH), jnp.bfloat16)
    terms = ab[...].astype(jnp.float32) * attn[...]
    mask = low(
        (
            lax.broadcasted_iota(jnp.int32, (16, terms.shape[1]), 1) // HEAD_WIDTH
            == lax.broadcasted_iota(jnp.int32, (16, terms.shape[1]), 0)
        ).astype(jnp.float32)
    )
    high = low(terms)
    correction[...] = dot_nt(mask, high) + dot_nt(mask, low(terms - high.astype(jnp.float32)))
    lse_rows[...] = jnp.transpose(lse[...])
    score_back(0, qk, kpad, vpad, ab, lse_rows, correction, dqk, dv)


def attend_back_second_kernel(
    dqk_in, dv_in, qk, kpad, vpad, lse_rows, correction, ab, dqk, dv,
):
    for i in range(1, qk.shape[0] // SPAN):
        score_back(i, qk, kpad, vpad, ab, lse_rows, correction, dqk, dv)


def project_back_kernel(
    keep_in, send_in, gain_two_in, spans, x, normed, dqk, dv, back_middle, gain_one,
    place, cosine, sine, wab, wab2,
    mine, near, far, d1, d2,
    grad, grad_full,
):
    rows = x.shape[0]
    half = wab.shape[0]
    lane = lax.broadcasted_iota(jnp.int32, (rows, LANES), 1)
    cos, sin = cosine[...], sine[...]
    for b in range(QK_WIDTH // LANES):
        u = dqk[:, b * LANES : (b + 1) * LANES] * FACTOR
        grad[:, b * LANES : (b + 1) * LANES] = low(u * cos - half_turn(u, lane) * sin)
    d_qk = low(dot_tn(normed[...], grad[...]))
    d1[:half, :QK_WIDTH] = d_qk[:half]
    d2[:half, :QK_WIDTH] = d_qk[half:]
    dv_low = dv[:, :KV_WIDTH]
    d_v = low(dot_tn(normed[...], dv_low))
    d1[:half, QK_WIDTH + MODEL_WIDTH :] = d_v[:half]
    d2[:half, QK_WIDTH + MODEL_WIDTH :] = d_v[half:]
    parts = [
        dot_nt(grad[...], w[:, :QK_WIDTH]) + dot_nt(dv_low, w[:, QK_WIDTH + MODEL_WIDTH :])
        for w in (wab, wab2)
    ]
    back_norm = place_back(jnp.concatenate(parts, axis=1), place[...])
    xf = x[...].astype(jnp.float32)
    scale = lax.rsqrt(jnp.mean(xf * xf, axis=-1, keepdims=True) + EPSILON)
    unit = xf * scale
    gain_row = lax.broadcasted_iota(jnp.int32, (16, MODEL_WIDTH), 0)
    gains = jnp.where(
        gain_row == 0, jnp.sum(back_norm * unit, axis=0, keepdims=True), gain_two_in[...]
    )
    for d in (d1, d2):
        d[half:, :MODEL_WIDTH] = low(gains)
        d[half:, MODEL_WIDTH:] = jnp.zeros((16, d.shape[1] - MODEL_WIDTH), jnp.bfloat16)
    back_unit = back_norm * gain_one[...]
    grad_full[...] = back_middle[...] + scale * (
        back_unit - unit * jnp.mean(back_unit * unit, axis=-1, keepdims=True)
    )
    for k, (block, at) in enumerate(((mine, 0), (near, 0), (far, 0), (near, SPAN))):
        source = pl.ds(pl.multiple_of(spans[k] * SPAN, SPAN), SPAN)
        block[at : at + SPAN] = low(grad_full[source, :])


VMEM_SPEC = pl.BlockSpec(memory_space=pltpu.VMEM)
SMEM_SPEC = pl.BlockSpec(memory_space=pltpu.SMEM)
ANY_SPEC = pl.BlockSpec(memory_space=pl.ANY)


def shaped(rows, columns, kind):
    return jax.ShapeDtypeStruct((rows, columns), kind)


def call(body, outs, args, scratch, micros, scalars=(), after=(), alias=None, megabytes=16, out_specs=None):
    def run(*refs):
        body(*refs[: len(args)], *refs[len(args) + len(after) :])

    return pl.pallas_call(
        run,
        out_shape=outs,
        in_specs=[SMEM_SPEC if at in scalars else VMEM_SPEC for at in range(len(args))]
        + [ANY_SPEC] * len(after),
        out_specs=out_specs or [VMEM_SPEC] * len(outs),
        scratch_shapes=scratch,
        input_output_aliases=alias or {},
        compiler_params=vmem_params(megabytes),
        cost_estimate=pl.CostEstimate(
            flops=int(micros * 1.1e9), bytes_accessed=1_000_000, transcendentals=0
        ),
    )(*args, *after)


def whole_sequence_plan(mesh):
    axes = ("dp", "seq")
    n_dp, n_seq = mesh.shape["dp"], mesh.shape["seq"]
    count = n_dp * n_seq
    bits = count.bit_length() - 1
    seq_bits = n_seq.bit_length() - 1
    core, y_bit = 0, 1
    x_bit = seq_bits
    z_bits = tuple(range(seq_bits + 1, bits))[::-1]
    order_bits = z_bits + (x_bit, y_bit, core)

    def hold(v, *others):
        return lax.optimization_barrier((v, *others))[0] if others else v

    def together(*arrays):
        return lax.optimization_barrier(arrays)

    def swap(v, flip, until=()):
        return hold(lax.ppermute(v, axes, [(d, d ^ flip) for d in range(count)]), *until)

    def relative(slot):
        return sum(1 << bit for at, bit in enumerate(order_bits) if slot >> at & 1)

    order = tuple(relative(slot) for slot in range(count))
    z_count = 1 << len(z_bits)
    z_flips = [relative(slot) for slot in range(1, z_count)]
    flip_x, flip_y, flip_core = 1 << x_bit, 1 << y_bit, 1 << core

    def gather_z(v, until=()):
        return jnp.concatenate([v] + [swap(v, flip, until) for flip in z_flips], axis=0)

    def gather_z_stepwise(v, untils):
        for bit, until in zip(z_bits, untils):
            v = jnp.concatenate([v, swap(v, 1 << bit, until)], axis=0)
        return v

    def gather_one(v, x_first, until=()):
        return jnp.concatenate([v, swap(v, flip_x if x_first else flip_y, until)], axis=0)

    def gather_two(v, x_first, until=()):
        w = swap(v, flip_y if x_first else flip_x, until)
        size = v.shape[0] // 2
        if x_first:
            return jnp.concatenate([v, w], axis=0)
        return jnp.concatenate([v[:size], w[:size], v[size:], w[size:]], axis=0)

    def scatter_core(keep, send, until=()):
        return wide(keep) + wide(swap(send, flip_core, until))

    def scatter_one(total, x_first, until=()):
        size = total.shape[0] // 4
        if x_first:
            mine = jnp.concatenate([total[:size], total[2 * size : 3 * size]], axis=0)
            theirs = jnp.concatenate([total[size : 2 * size], total[3 * size :]], axis=0)
            return mine + wide(swap(low(theirs), flip_x, until))
        return total[: 2 * size] + wide(swap(low(total[2 * size :]), flip_y, until))

    def scatter_two(total, x_first, until=()):
        size = total.shape[0] // 2
        sent = swap(low(total[size:]), flip_y if x_first else flip_x, until)
        return total[:size] + wide(sent)

    def scatter_bit(total, bit):
        size = total.shape[0] // 2
        return total[:size] + wide(swap(low(total[size:]), 1 << bit))

    def scatter_z_with_sums(total, sums):
        size = total.shape[0] // z_count
        sums = lax.reduce_precision(sums.reshape(size, -1), 8, 7)
        width, wanted = total.shape[1], sums.shape[1]
        beside = jnp.pad(low(sums), ((0, 0), (0, -wanted % LANES)))
        out, terms = total[:size], [sums]
        for at, flip in enumerate(z_flips):
            theirs = low(total[(at + 1) * size : (at + 2) * size])
            sent = swap(jnp.concatenate([theirs, beside], axis=1), flip)
            out = out + wide(sent[:, :width])
            terms.append(wide(sent[:, width : width + wanted]))
        while len(terms) > 1:
            terms = [a + b for a, b in zip(terms[::2], terms[1::2])]
        return out, terms[0].reshape(-1)

    def exchange(parts, near_until=(), far_until=(), far_after=()):
        mine, near, far = parts
        size = mine.shape[0]
        near = swap(near, flip_core, near_until)
        far = hold(jnp.concatenate([far, near[size:]], axis=0), *far_after)
        return mine, near[:size], swap(far, flip_y, far_until)

    def scatter_with_sums(mine, theirs, sums, flip, until=()):
        sums = lax.reduce_precision(sums, 8, 7)
        sent = swap(jnp.concatenate([low(theirs), low(sums)], axis=0), flip, until)
        return mine + wide(sent[: mine.shape[0]]), sums + wide(sent[mine.shape[0] :])

    def on_sequence_device(
        hidden_in, span_order, attention_norm_gain, query_weight, key_weight, value_weight,
        output_weight, feedforward_gain, gate_weight, up_weight, down_weight, out_grad,
    ):
        rows = hidden_in.shape[0]
        model_rows = MODEL_WIDTH // count
        hidden_rows = HIDDEN_UNITS // count
        bf, f4 = jnp.bfloat16, jnp.float32
        half = MODEL_WIDTH // 2
        gain_one = attention_norm_gain.astype(jnp.float32).reshape(1, MODEL_WIDTH)
        gain_two = feedforward_gain.astype(jnp.float32).reshape(1, MODEL_WIDTH)
        model_low, model_full = shaped(rows, MODEL_WIDTH, bf), shaped(rows, MODEL_WIDTH, f4)

        def rows_of(w, columns):
            return w.reshape(model_rows, columns)

        def unpack(parts):
            return call(unpack_kernel, [model_low], parts, [], 1, megabytes=4)[0]

        slots = np.repeat(np.asarray(order, np.int32), model_rows)[None, :]
        offsets = np.tile(np.arange(model_rows, dtype=np.int32), count)[None, :]
        packed = call(
            functools.partial(pack_kernel, n_seq=n_seq),
            [
                *[shaped(n * (SPAN + 16), MODEL_WIDTH, bf) for n in (1, 2, 1)],
                *[shaped(n * SPAN, MODEL_WIDTH, bf) for n in (1, 2, 1)],
                shaped(MODEL_WIDTH, MODEL_WIDTH, bf),
            ],
            [span_order, hidden_in, out_grad, slots, offsets],
            [],
            2,
            scalars=(0,),
        )
        place = packed[6]
        first = jnp.concatenate(
            [
                rows_of(query_weight, Q_WIDTH),
                rows_of(key_weight, KV_WIDTH),
                rows_of(output_weight, MODEL_WIDTH),
                rows_of(value_weight, KV_WIDTH),
            ],
            axis=1,
        )

        down = down_weight.reshape(3, 16, MODEL_WIDTH).swapaxes(0, 1)
        down = jnp.pad(down, ((0, model_rows - 16), (0, 0), (0, DOWN_PITCH - MODEL_WIDTH)))
        gate, up = rows_of(gate_weight, HIDDEN_UNITS), rows_of(up_weight, HIDDEN_UNITS)
        ffn = jnp.concatenate(
            [gate[:, :HALF_FFN], down.reshape(model_rows, 3 * DOWN_PITCH), up[:, :HALF_FFN]], axis=1
        )
        later = jnp.concatenate([gate[:, HALF_FFN:], up[:, HALF_FFN:]], axis=1)
        first = gather_z(hold(first, place), until=(ffn,))
        first_a, first_b = first[:, :QK_WIDTH], first[:, QK_WIDTH:]
        first_a, first_b = gather_one(first_a, False), gather_one(first_b, True)
        x_parts = exchange(packed[:3], (first,), (first_a, first_b))
        one = (first_a, first_b)
        first_a, first_b = gather_two(first_a, False), gather_two(first_b, True)
        first = jnp.concatenate([first_a, first_b], axis=1)
        ffn = gather_z_stepwise(ffn, (one, (first,)))
        o_parts = exchange(hold(tuple(packed[3:6]), *one), (first,), (ffn,), (first,))
        first_other = swap(first, flip_core)
        ffn_a, ffn_b = ffn[:, :FFN_CUT], ffn[:, FFN_CUT:]

        frequency = np.exp(np.arange(HEAD_WIDTH // 2) * (-2.0 * math.log(10000.0) / HEAD_WIDTH))
        angles = np.arange(rows)[:, None] * frequency[None, :]
        cosine = np.tile(np.cos(angles), (1, 4)).astype(np.float32)
        sine = np.sin(angles)
        sine = np.concatenate([-sine, sine, -sine, sine], axis=1).astype(np.float32)

        padded = jax.ShapeDtypeStruct((2 * KEY_VALUE_HEADS, rows, LANES), bf)
        spans, x, normed, qk, kpad, vpad = call(
            project_kernel,
            [
                jax.ShapeDtypeStruct((n_seq,), jnp.int32),
                model_low,
                model_low,
                shaped(rows, QK_WIDTH, bf),
                padded,
                padded,
            ],
            [*x_parts, gain_one, place, cosine, sine, first, first_other],
            [pltpu.VMEM((MODEL_WIDTH, QK_WIDTH), bf)] * 2,
            5,
            out_specs=[SMEM_SPEC] + [VMEM_SPEC] * 5,
        )
        stats = [shaped(rows, LANES, f4), shaped(rows, 5 * LANES, f4)]
        lse, attn = call(attend_first_kernel, stats, [qk, kpad, vpad], [], 5)
        ffn_a, ffn_b = gather_one(ffn_a, False, (x,)), gather_one(ffn_b, True, (x,))
        later = gather_z_stepwise(hold(later, ffn), ((ffn_a, ffn_b), (lse,)))
        lse, attn, merged, middle, normed_two = call(
            attend_last_kernel,
            [*stats, model_low, model_full, model_low],
            [lse, attn, x, qk, kpad, vpad, gain_two, place, first, first_other],
            [],
            5,
            alias={0: 0, 1: 1},
        )
        ffn = []
        for part, flip in ((ffn_a, flip_x), (ffn_b, flip_y)):
            second = swap(part, flip, (middle,))
            ffn += [part, second, swap(part, flip_core, (middle,)), swap(second, flip_core)]
        later_a = gather_one(later[:, :HALF_FFN], False, (ffn[1],))
        later_b = gather_one(later[:, HALF_FFN:], True, (ffn[5],))
        weight_scratch = [pltpu.VMEM((MODEL_WIDTH, HALF_FFN), bf)] * 2
        og, result, back, r1, r1_send, dd, w_down = call(
            functools.partial(ffn_first_kernel, order=order, n_seq=n_seq),
            [
                model_low,
                model_full,
                model_full,
                *[shaped(half, 2 * HALF_FFN, bf)] * 2,
                shaped(HALF_FFN, MODEL_WIDTH, bf),
                shaped(HIDDEN_UNITS, MODEL_WIDTH, bf),
            ],
            [spans, *o_parts, normed_two, *ffn],
            weight_scratch,
            10,
            scalars=(0,),
        )
        r1_own = r1
        later = []
        for part, flip in ((later_a, flip_x), (later_b, flip_y)):
            second = swap(part, flip, (og,))
            later += [part, second, swap(part, flip_core, (og,)), swap(second, flip_core)]
        *h_parts, back_middle, gain_two_grad, r2, r2_send = call(
            functools.partial(ffn_second_kernel, order=order, n_seq=n_seq),
            [
                *[shaped(n * SPAN, MODEL_WIDTH, bf) for n in (1, 2, 1)],
                model_full,
                shaped(1, MODEL_WIDTH, f4),
                *[shaped(half, SECOND_WIDTH, bf)] * 2,
            ],
            [spans, og, normed_two, *later, w_down, result, back, dd, middle, gain_two, place],
            weight_scratch
            + [
                pltpu.VMEM((HALF_FFN, MODEL_WIDTH), bf),
                pltpu.VMEM((HIDDEN_UNITS, MODEL_WIDTH), bf),
                pltpu.VMEM((MODEL_WIDTH, DOWN_PITCH), f4),
                pltpu.VMEM((rows, MODEL_WIDTH), f4),
                pltpu.VMEM((rows, MODEL_WIDTH), f4),
            ],
            13,
            scalars=(0,),
            megabytes=18,
        )
        r1 = scatter_core(r1_own, r1_send, (back_middle,))
        r3, r3_send, ab, lse_rows, correction, dqk, dv = call(
            attend_back_first_kernel,
            [
                *[shaped(half + 16, 2 * HALF_FFN, bf)] * 2,
                shaped(rows, 5 * LANES, bf),
                shaped(LANES, rows, f4),
                shaped(16, rows, f4),
                shaped(rows, QK_WIDTH, f4),
                shaped(rows, 2 * LANES, bf),
            ],
            [qk, kpad, vpad, lse, attn, merged, back_middle, place, first, first_other],
            [],
            7,
            after=[r1],
        )
        r2 = scatter_core(r2, r2_send, (ab,))
        h_near = swap(h_parts[1], flip_core, (ab,))
        dqk, dv = call(
            attend_back_second_kernel,
            [shaped(rows, QK_WIDTH, f4), shaped(rows, 2 * LANES, bf)],
            [dqk, dv, qk, kpad, vpad, lse_rows, correction, ab],
            [],
            6,
            after=[r2],
            alias={0: 0, 1: 1},
        )
        p1 = scatter_one(r2[:, :SECOND_CUT], True, (dqk,))
        p2 = scatter_one(r2[:, SECOND_CUT : 2 * SECOND_CUT], False, (dqk,))
        *g_parts, r3, r3_send = call(
            project_back_kernel,
            [
                *[shaped(n * SPAN, MODEL_WIDTH, bf) for n in (1, 2, 1)],
                *[shaped(half + 16, 2 * HALF_FFN, bf)] * 2,
            ],
            [
                r3, r3_send, gain_two_grad, spans, x, normed, dqk, dv, back_middle,
                gain_one, place, cosine, sine, first, first_other,
            ],
            [pltpu.VMEM((rows, QK_WIDTH), bf), pltpu.VMEM((rows, MODEL_WIDTH), f4)],
            5,
            scalars=(3,),
            after=[p1, p2],
            alias={0: 3, 1: 4},
        )
        p1, p2 = scatter_two(p1, True, (r3,)), scatter_two(p2, False, (r3,))
        p3 = scatter_one(r2[:, 2 * SECOND_CUT :], True, (r3,))
        r1 = scatter_one(r1, False, (r3,))
        sent = wide(swap(r3_send, flip_core))
        r3 = wide(r3)
        r1, p3 = scatter_two(r1, False), scatter_two(p3, True)
        total, sums, r1, p1, p2, p3 = together(
            r3[:half] + sent[:half], r3[half:] + sent[half:], r1, p1, p2, p3
        )
        size = half // 4
        r3_a, r3_b = total[:, :QK_WIDTH], total[:, QK_WIDTH:]
        r3_a, sums = scatter_with_sums(
            jnp.concatenate([r3_a[:size], r3_a[2 * size : 3 * size]], axis=0),
            jnp.concatenate([r3_a[size : 2 * size], r3_a[3 * size :]], axis=0),
            sums[:, :QK_WIDTH],
            flip_x,
        )
        r3_b = scatter_one(r3_b, False)
        early = jnp.concatenate([p1, p2, r1], axis=1)
        early = scatter_bit(early, z_bits[-1])
        g_near = swap(g_parts[1], flip_core)
        r3_a, r3_b, sums, early, g_near, h_near = together(
            r3_a, r3_b, sums, early, g_near, h_near
        )
        r3_a, sums = scatter_with_sums(r3_a[:size], r3_a[size:], sums, flip_y)
        r3_b = scatter_two(r3_b, False)
        for bit in z_bits[-2::-1]:
            early = scatter_bit(early, bit)
        h_far = swap(jnp.concatenate([h_parts[2], h_near[SPAN:]], axis=0), flip_y)
        r3_a, r3_b, sums, early, h_far, g_near = together(
            r3_a, r3_b, sums, early, h_far, g_near
        )
        g_far = swap(jnp.concatenate([g_parts[2], g_near[SPAN:]], axis=0), flip_y)
        late = jnp.concatenate([r3_a, r3_b, p3], axis=1)
        late, sums = scatter_z_with_sums(late, sums[:2, :MODEL_WIDTH])
        hidden_out = unpack([h_parts[0], h_near[:SPAN], h_far])
        r1 = early[:, 2 * SECOND_CUT :]
        r2 = jnp.concatenate([early[:, : 2 * SECOND_CUT], late[:, 2 * HALF_FFN :]], axis=1)
        r3 = late
        hidden_grad = unpack([g_parts[0], g_near[:SPAN], g_far])
        gu1 = r2[:, SECOND_GATE_AT:]
        gate_grad = jnp.concatenate([r1[:, :HALF_FFN], gu1[:, :HALF_FFN]], axis=1)
        up_grad = jnp.concatenate([r1[:, HALF_FFN:], gu1[:, HALF_FFN : 2 * HALF_FFN]], axis=1)
        down_grad = r2[:16, :SECOND_GATE_AT].reshape(16, 3, DOWN_PITCH)[:, :, :MODEL_WIDTH]
        return (
            hidden_out,
            hidden_grad,
            sums[:MODEL_WIDTH],
            r3[:, :Q_WIDTH].reshape(-1),
            r3[:, Q_WIDTH:QK_WIDTH].reshape(-1),
            r3[:, QK_WIDTH + MODEL_WIDTH : 2 * HALF_FFN].reshape(-1),
            r3[:, QK_WIDTH : QK_WIDTH + MODEL_WIDTH].reshape(-1),
            sums[MODEL_WIDTH:],
            gate_grad.reshape(-1),
            up_grad.reshape(-1),
            down_grad.swapaxes(0, 1).reshape(-1),
        )

    return on_sequence_device


def pick_plan(mesh):
    count = mesh.shape["dp"] * mesh.shape["seq"]
    fits = (
        mesh.shape["seq"] == MB * SLOTS
        and SLOTS == 1
        and count & (count - 1) == 0
        and MODEL_WIDTH % count == 0
        and (HIDDEN_UNITS // count) % 16 == 0
    )
    return whole_sequence_plan(mesh) if fits else on_device


def solution(mesh):
    return jax.shard_map(
        pick_plan(mesh),
        mesh=mesh,
        in_specs=(
            P(("dp", "seq"), None),
            P(("dp", "seq")),
            P(),
            P(("dp", "seq")),
            P(("dp", "seq")),
            P(("dp", "seq")),
            P(("dp", "seq")),
            P(),
            P(("dp", "seq")),
            P(("dp", "seq")),
            P(("dp", "seq")),
            P(("dp", "seq"), None),
        ),
        out_specs=(
            P(("dp", "seq"), None),
            P(("dp", "seq"), None),
            P(),
            P(("dp", "seq")),
            P(("dp", "seq")),
            P(("dp", "seq")),
            P(("dp", "seq")),
            P(),
            P(("dp", "seq")),
            P(("dp", "seq")),
            P(("dp", "seq")),
        ),
        check_vma=False,
    )
```

```python
import functools
import math

import jax
import jax.numpy as jnp
import numpy as np
from jax import lax
from jax.experimental import pallas as pl
from jax.experimental.pallas import tpu as pltpu
from jax.sharding import PartitionSpec as P

MODEL_WIDTH = 576
QUERY_HEADS = 9
KEY_VALUE_HEADS = 3
HEAD_WIDTH = 64
HIDDEN_UNITS = 1536
SPAN = 128
MB = 4
SLOTS = 1


EPSILON = 1e-05


def angle_tables(positions, head_size):
    frequency = jnp.exp(
        jnp.arange(head_size // 2, dtype=jnp.float32) * (-2.0 * math.log(10000.0) / head_size)
    )
    angles = positions.astype(jnp.float32)[:, None] * frequency[None, :]
    angles = jnp.concatenate([angles, angles], axis=-1)[:, None, :]
    return (jnp.cos(angles), jnp.sin(angles))


def apply_rotation(value_rows, cosine_table, sine_values):
    half_size = value_rows.shape[-1] // 2
    turned = jnp.concatenate([-value_rows[..., half_size:], value_rows[..., :half_size]], axis=-1)
    return value_rows * cosine_table + turned * sine_values


def product(first_arg, second_arg):
    return jnp.dot(first_arg, second_arg, preferred_element_type=jnp.float32)


def inner_rows(first_arg, second_arg):
    return lax.dot_general(
        first_arg, second_arg, (((0,), (0,)), ((), ())), preferred_element_type=jnp.float32
    )


def inner_cols(first_arg, second_arg):
    return lax.dot_general(
        first_arg, second_arg, (((1,), (1,)), ((), ())), preferred_element_type=jnp.float32
    )


def shape_weights(flattened_rows):
    return (
        flattened_rows[0].reshape(MODEL_WIDTH, QUERY_HEADS * HEAD_WIDTH),
        flattened_rows[1].reshape(MODEL_WIDTH, KEY_VALUE_HEADS * HEAD_WIDTH),
        flattened_rows[2].reshape(MODEL_WIDTH, KEY_VALUE_HEADS * HEAD_WIDTH),
        flattened_rows[3].reshape(QUERY_HEADS * HEAD_WIDTH, MODEL_WIDTH),
        flattened_rows[4].reshape(MODEL_WIDTH, HIDDEN_UNITS),
        flattened_rows[5].reshape(MODEL_WIDTH, HIDDEN_UNITS),
        flattened_rows[6].reshape(HIDDEN_UNITS, MODEL_WIDTH),
    )


def block_scores(query_rows, key_block, query_place, key_place, factor):
    raw_scores = (
        jnp.einsum("qkgd,skd->kgqs", query_rows, key_block, preferred_element_type=jnp.float32)
        * factor
    )
    allowed = query_place[:, None] >= key_place[None, :]
    return jnp.where(allowed, raw_scores, -1e30)


def forward(layer_input, positions, span_ids, gain_pair, matrices):
    w_q, w_k, w_v, w_o, w_g, w_u, w_d = matrices
    count_of_rows = layer_input.shape[0]
    query_group_width = QUERY_HEADS // KEY_VALUE_HEADS
    factor = 1.0 / math.sqrt(HEAD_WIDTH)
    input_full = layer_input.astype(jnp.float32)
    scale_one = lax.rsqrt(jnp.mean(input_full * input_full, axis=-1, keepdims=True) + EPSILON)
    unit_one = input_full * scale_one
    normed = (unit_one * gain_pair[0]).astype(jnp.bfloat16)
    query_rows = product(normed, w_q)
    unrotated_keys = product(normed, w_k)
    value_rows = product(normed, w_v)
    cosine_table, sine_values = angle_tables(positions, HEAD_WIDTH)
    rotated_query = apply_rotation(
        query_rows.reshape(count_of_rows, QUERY_HEADS, HEAD_WIDTH), cosine_table, sine_values
    ).astype(jnp.bfloat16)
    rotated_query = rotated_query.reshape(
        count_of_rows, KEY_VALUE_HEADS, query_group_width, HEAD_WIDTH
    )
    rotated_key = apply_rotation(
        unrotated_keys.reshape(count_of_rows, KEY_VALUE_HEADS, HEAD_WIDTH),
        cosine_table,
        sine_values,
    ).astype(jnp.bfloat16)
    rotated_key = rotated_key.reshape(count_of_rows, KEY_VALUE_HEADS * HEAD_WIDTH)
    v_low = value_rows.astype(jnp.bfloat16)
    every_key, every_value, key_spans = (
        lax.all_gather(rotated_key, "seq", axis=0, tiled=True),
        lax.all_gather(v_low, "seq", axis=0, tiled=True),
        lax.all_gather(span_ids.astype(jnp.bfloat16), "seq", axis=0, tiled=True),
    )
    offsets = jnp.arange(SPAN, dtype=jnp.int32)
    key_places = (key_spans.astype(jnp.int32)[:, None] * SPAN + offsets[None, :]).reshape(-1)
    count_of_keys = every_key.shape[0]
    block_length = math.gcd(count_of_keys, 512)
    count_of_blocks = count_of_keys // block_length
    blocks_of_keys = every_key.reshape(count_of_blocks, block_length, KEY_VALUE_HEADS, HEAD_WIDTH)
    blocks_of_values = every_value.reshape(
        count_of_blocks, block_length, KEY_VALUE_HEADS, HEAD_WIDTH
    )
    place_blocks = key_places.reshape(count_of_blocks, block_length)

    def softmax_stats(carry, piece_set):
        highest, totals = carry
        key_block, key_place = piece_set
        scores = block_scores(rotated_query, key_block, positions, key_place, factor)
        new_high = jnp.maximum(highest, jnp.max(scores, axis=-1))
        totals = totals * jnp.exp(highest - new_high) + jnp.sum(
            jnp.exp(scores - new_high[..., None]), axis=-1
        )
        return ((new_high, totals), None)

    initial = (
        jnp.full((KEY_VALUE_HEADS, query_group_width, count_of_rows), -1e30, jnp.float32),
        jnp.zeros((KEY_VALUE_HEADS, query_group_width, count_of_rows), jnp.float32),
    )
    (highest, totals), _ = lax.scan(softmax_stats, initial, (blocks_of_keys, place_blocks))

    def mix_values(running, piece_set):
        key_block, value_block, key_place = piece_set
        scores = block_scores(rotated_query, key_block, positions, key_place, factor)
        layer_weights = (jnp.exp(scores - highest[..., None]) / totals[..., None]).astype(
            jnp.bfloat16
        )
        return (
            running
            + jnp.einsum(
                "kgqs,skd->qkgd", layer_weights, value_block, preferred_element_type=jnp.float32
            ),
            None,
        )

    attention_output, _ = lax.scan(
        mix_values,
        jnp.zeros((count_of_rows, KEY_VALUE_HEADS, query_group_width, HEAD_WIDTH), jnp.float32),
        (blocks_of_keys, blocks_of_values, place_blocks),
    )
    attention_output = attention_output.reshape(count_of_rows, QUERY_HEADS * HEAD_WIDTH)
    merged = attention_output.astype(jnp.bfloat16)
    middle = input_full + product(merged, w_o)
    scale_two = lax.rsqrt(jnp.mean(middle * middle, axis=-1, keepdims=True) + EPSILON)
    unit_two = middle * scale_two
    normed_two = (unit_two * gain_pair[1]).astype(jnp.bfloat16)
    gate_act = product(normed_two, w_g)
    upward = product(normed_two, w_u)
    hidden = (jax.nn.silu(gate_act) * upward).astype(jnp.bfloat16)
    result = (middle + product(hidden, w_d)).astype(jnp.bfloat16)
    stored = (
        scale_one,
        unit_one,
        normed,
        cosine_table,
        sine_values,
        rotated_query,
        blocks_of_keys,
        blocks_of_values,
        place_blocks,
        highest,
        totals,
        attention_output,
        merged,
        scale_two,
        unit_two,
        normed_two,
        gate_act,
        upward,
        hidden,
    )
    return (result, stored)


def backward(cotangent, positions, gain_pair, matrices, stored):
    w_q, w_k, w_v, w_o, w_g, w_u, w_d = matrices
    (
        scale_one,
        unit_one,
        normed,
        cosine_table,
        sine_values,
        rotated_query,
        blocks_of_keys,
        blocks_of_values,
        place_blocks,
        highest,
        totals,
        attention_output,
        merged,
        scale_two,
        unit_two,
        normed_two,
        gate_act,
        upward,
        hidden,
    ) = stored
    count_of_rows = cotangent.shape[0]
    query_group_width = QUERY_HEADS // KEY_VALUE_HEADS
    factor = 1.0 / math.sqrt(HEAD_WIDTH)
    grad_down = inner_rows(hidden, cotangent)
    back_hidden = inner_cols(cotangent, w_d)
    sigmoid_gate = jax.nn.sigmoid(gate_act)
    back_gate = (
        back_hidden * upward * sigmoid_gate * (1.0 + gate_act * (1.0 - sigmoid_gate))
    ).astype(jnp.bfloat16)
    back_up = (back_hidden * (gate_act * sigmoid_gate)).astype(jnp.bfloat16)
    grad_gate = inner_rows(normed_two, back_gate)
    grad_up = inner_rows(normed_two, back_up)
    back_norm_two = inner_cols(back_gate, w_g) + inner_cols(back_up, w_u)
    gain_two = jnp.sum(back_norm_two * unit_two, axis=0)
    back_unit = back_norm_two * gain_pair[1]
    back_middle = cotangent.astype(jnp.float32) + scale_two * (
        back_unit - unit_two * jnp.mean(back_unit * unit_two, axis=-1, keepdims=True)
    )
    middle_low = back_middle.astype(jnp.bfloat16)
    grad_out = inner_rows(merged, middle_low)
    attention_backward = inner_cols(middle_low, w_o).astype(jnp.bfloat16)
    head_gradient_rows = attention_backward.reshape(
        count_of_rows, KEY_VALUE_HEADS, query_group_width, HEAD_WIDTH
    )
    attention_head_rows = attention_output.reshape(
        count_of_rows, KEY_VALUE_HEADS, query_group_width, HEAD_WIDTH
    )
    correction = jnp.transpose(
        jnp.sum(head_gradient_rows.astype(jnp.float32) * attention_head_rows, axis=-1), (1, 2, 0)
    )

    def score_grads(running, piece_set):
        key_block, value_block, key_place = piece_set
        scores = block_scores(rotated_query, key_block, positions, key_place, factor)
        probs = jnp.exp(scores - highest[..., None]) / totals[..., None]
        back_probs = jnp.einsum(
            "qkgd,skd->kgqs", head_gradient_rows, value_block, preferred_element_type=jnp.float32
        )
        back_scores = (probs * (back_probs - correction[..., None])).astype(jnp.bfloat16)
        running = (
            running
            + jnp.einsum(
                "kgqs,skd->qkgd", back_scores, key_block, preferred_element_type=jnp.float32
            )
            * factor
        )
        key_grad = (
            jnp.einsum(
                "kgqs,qkgd->skd", back_scores, rotated_query, preferred_element_type=jnp.float32
            )
            * factor
        )
        value_grad = jnp.einsum(
            "kgqs,qkgd->skd",
            probs.astype(jnp.bfloat16),
            head_gradient_rows,
            preferred_element_type=jnp.float32,
        )
        return (running, (key_grad, value_grad))

    back_query, (gradient_of_keys, gradient_of_values) = lax.scan(
        score_grads,
        jnp.zeros((count_of_rows, KEY_VALUE_HEADS, query_group_width, HEAD_WIDTH), jnp.float32),
        (blocks_of_keys, blocks_of_values, place_blocks),
    )
    count_of_keys = gradient_of_keys.shape[0] * gradient_of_keys.shape[1]
    local_keys, value_own = (
        lax.psum_scatter(
            gradient_of_keys.reshape(count_of_keys, KEY_VALUE_HEADS * HEAD_WIDTH).astype(
                jnp.bfloat16
            ),
            "seq",
            scatter_dimension=0,
            tiled=True,
        ).astype(jnp.float32),
        lax.psum_scatter(
            gradient_of_values.reshape(count_of_keys, KEY_VALUE_HEADS * HEAD_WIDTH).astype(
                jnp.bfloat16
            ),
            "seq",
            scatter_dimension=0,
            tiled=True,
        ).astype(jnp.float32),
    )
    query_low = (
        apply_rotation(
            back_query.reshape(count_of_rows, QUERY_HEADS, HEAD_WIDTH), cosine_table, -sine_values
        )
        .astype(jnp.bfloat16)
        .reshape(count_of_rows, QUERY_HEADS * HEAD_WIDTH)
    )
    key_low = (
        apply_rotation(
            local_keys.reshape(count_of_rows, KEY_VALUE_HEADS, HEAD_WIDTH),
            cosine_table,
            -sine_values,
        )
        .astype(jnp.bfloat16)
        .reshape(count_of_rows, KEY_VALUE_HEADS * HEAD_WIDTH)
    )
    value_low = value_own.astype(jnp.bfloat16)
    grad_query = inner_rows(normed, query_low)
    grad_key = inner_rows(normed, key_low)
    grad_value = inner_rows(normed, value_low)
    back_norm_one = (
        inner_cols(query_low, w_q) + inner_cols(key_low, w_k) + inner_cols(value_low, w_v)
    )
    gain_one = jnp.sum(back_norm_one * unit_one, axis=0)
    back_unit_one = back_norm_one * gain_pair[0]
    input_back = back_middle + scale_one * (
        back_unit_one - unit_one * jnp.mean(back_unit_one * unit_one, axis=-1, keepdims=True)
    )
    weight_terms = (grad_query, grad_key, grad_value, grad_out, grad_gate, grad_up, grad_down)
    return (input_back.astype(jnp.bfloat16), weight_terms, (gain_one, gain_two))


def on_device(
    hidden_in,
    span_order,
    attention_norm_gain,
    query_weight,
    key_weight,
    value_weight,
    output_weight,
    feedforward_gain,
    gate_weight,
    up_weight,
    down_weight,
    out_grad,
):
    count_of_rows = SLOTS * SPAN
    gain_pair = (attention_norm_gain.astype(jnp.float32), feedforward_gain.astype(jnp.float32))
    offsets = jnp.arange(SPAN, dtype=jnp.int32)
    weight_totals = (
        jnp.zeros((MODEL_WIDTH, QUERY_HEADS * HEAD_WIDTH), jnp.float32),
        jnp.zeros((MODEL_WIDTH, KEY_VALUE_HEADS * HEAD_WIDTH), jnp.float32),
        jnp.zeros((MODEL_WIDTH, KEY_VALUE_HEADS * HEAD_WIDTH), jnp.float32),
        jnp.zeros((QUERY_HEADS * HEAD_WIDTH, MODEL_WIDTH), jnp.float32),
        jnp.zeros((MODEL_WIDTH, HIDDEN_UNITS), jnp.float32),
        jnp.zeros((MODEL_WIDTH, HIDDEN_UNITS), jnp.float32),
        jnp.zeros((HIDDEN_UNITS, MODEL_WIDTH), jnp.float32),
    )
    gain_totals = (jnp.zeros((MODEL_WIDTH,), jnp.float32), jnp.zeros((MODEL_WIDTH,), jnp.float32))
    outputs = []
    input_grads = []
    for micro_index in range(MB):
        layer_input = hidden_in[micro_index * count_of_rows : (micro_index + 1) * count_of_rows]
        cotangent = out_grad[micro_index * count_of_rows : (micro_index + 1) * count_of_rows]
        span_ids = span_order[micro_index * SLOTS : (micro_index + 1) * SLOTS]
        positions = (span_ids[:, None] * SPAN + offsets[None, :]).reshape(count_of_rows)
        forward_weights = shape_weights(
            (
                lax.all_gather(query_weight, ("dp", "seq"), axis=0, tiled=True),
                lax.all_gather(key_weight, ("dp", "seq"), axis=0, tiled=True),
                lax.all_gather(value_weight, ("dp", "seq"), axis=0, tiled=True),
                lax.all_gather(output_weight, ("dp", "seq"), axis=0, tiled=True),
                lax.all_gather(gate_weight, ("dp", "seq"), axis=0, tiled=True),
                lax.all_gather(up_weight, ("dp", "seq"), axis=0, tiled=True),
                lax.all_gather(down_weight, ("dp", "seq"), axis=0, tiled=True),
            )
        )
        result, stored = forward(layer_input, positions, span_ids, gain_pair, forward_weights)
        backward_weights = shape_weights(
            (
                lax.all_gather(query_weight, ("dp", "seq"), axis=0, tiled=True),
                lax.all_gather(key_weight, ("dp", "seq"), axis=0, tiled=True),
                lax.all_gather(value_weight, ("dp", "seq"), axis=0, tiled=True),
                lax.all_gather(output_weight, ("dp", "seq"), axis=0, tiled=True),
                lax.all_gather(gate_weight, ("dp", "seq"), axis=0, tiled=True),
                lax.all_gather(up_weight, ("dp", "seq"), axis=0, tiled=True),
                lax.all_gather(down_weight, ("dp", "seq"), axis=0, tiled=True),
            )
        )
        input_back, weight_terms, gain_terms = backward(
            cotangent, positions, gain_pair, backward_weights, stored
        )
        weight_totals = tuple(
            (running + term for running, term in zip(weight_totals, weight_terms))
        )
        gain_totals = tuple((running + term for running, term in zip(gain_totals, gain_terms)))
        outputs.append(result)
        input_grads.append(input_back)
    grad_query, grad_key, grad_value, grad_out, grad_gate, grad_up, grad_down = weight_totals
    owned = (
        lax.psum_scatter(grad_query.reshape(-1), ("dp", "seq"), scatter_dimension=0, tiled=True),
        lax.psum_scatter(grad_key.reshape(-1), ("dp", "seq"), scatter_dimension=0, tiled=True),
        lax.psum_scatter(grad_value.reshape(-1), ("dp", "seq"), scatter_dimension=0, tiled=True),
        lax.psum_scatter(grad_out.reshape(-1), ("dp", "seq"), scatter_dimension=0, tiled=True),
        lax.psum_scatter(grad_gate.reshape(-1), ("dp", "seq"), scatter_dimension=0, tiled=True),
        lax.psum_scatter(grad_up.reshape(-1), ("dp", "seq"), scatter_dimension=0, tiled=True),
        lax.psum_scatter(grad_down.reshape(-1), ("dp", "seq"), scatter_dimension=0, tiled=True),
    )
    gain_one, gain_two = lax.psum((gain_totals[0], gain_totals[1]), ("dp", "seq"))
    return (
        jnp.concatenate(outputs, axis=0),
        jnp.concatenate(input_grads, axis=0),
        gain_one,
        owned[0],
        owned[1],
        owned[2],
        owned[3],
        gain_two,
        owned[4],
        owned[5],
        owned[6],
    )


FACTOR = 1.0 / math.sqrt(HEAD_WIDTH)
KV_WIDTH = KEY_VALUE_HEADS * HEAD_WIDTH
Q_WIDTH = QUERY_HEADS * HEAD_WIDTH
QK_WIDTH = Q_WIDTH + KV_WIDTH
LANES = 128
HALF_FFN = HIDDEN_UNITS // 2
FFN_BLOCK = 256
DOWN_PITCH = 640
DOWN_AT = HALF_FFN
DOWN_EARLY = 2
FFN_CUT = DOWN_AT + DOWN_EARLY * DOWN_PITCH
UP_AT = (3 - DOWN_EARLY) * DOWN_PITCH
SECOND_GATE_AT = 3 * DOWN_PITCH
SECOND_WIDTH = SECOND_GATE_AT + 2 * HALF_FFN
SECOND_CUT = SECOND_WIDTH // 3


def vmem_params(megabytes=48):
    return pltpu.CompilerParams(vmem_limit_bytes=megabytes * 1024 * 1024)


def dot_nn(a, b):
    return jnp.dot(a, b, preferred_element_type=jnp.float32)


def dot_tn(a, b):
    return lax.dot_general(a, b, (((0,), (0,)), ((), ())), preferred_element_type=jnp.float32)


def dot_nt(a, b):
    return lax.dot_general(a, b, (((1,), (1,)), ((), ())), preferred_element_type=jnp.float32)


def low(v):
    return v.astype(jnp.bfloat16)


def wide(v):
    return v.astype(jnp.float32)


def place_back(v, place):
    high = low(v)
    rest = low(v - high.astype(jnp.float32))
    return dot_nt(high, place) + dot_nt(rest, place)


def half_turn(u, lane):
    return jnp.where(
        lane % HEAD_WIDTH < HEAD_WIDTH // 2,
        pltpu.roll(u, LANES - HEAD_WIDTH // 2, 1),
        pltpu.roll(u, HEAD_WIDTH // 2, 1),
    )


def padded_heads(blocks, head, lane):
    here = blocks[head // 2]
    moved = pltpu.roll(here, HEAD_WIDTH, 1)
    low_half, high_half = (here, moved) if head % 2 == 0 else (moved, here)
    zero = jnp.zeros_like(here)
    return (
        low(jnp.where(lane < HEAD_WIDTH, low_half, zero)),
        low(jnp.where(lane >= HEAD_WIDTH, high_half, zero)),
    )


def pack_kernel(
    span_order, hidden_in, out_grad, slots, offsets,
    x_mine, x_near, x_far, o_mine, o_near, o_far, place, *, n_seq,
):
    seq = lax.axis_index("seq")
    me = lax.axis_index("dp") * n_seq + seq
    tall = SPAN + 16
    for flip, x, o, at in ((0, x_mine, o_mine, 0), (1, x_near, o_near, 0), (3, x_near, o_near, 1), (2, x_far, o_far, 0)):
        origin = seq ^ flip
        block = pl.ds(pl.multiple_of(origin * SPAN, SPAN), SPAN)
        x[at * tall : at * tall + SPAN] = hidden_in[block, :]
        number = jnp.full((16, MODEL_WIDTH), span_order[origin], jnp.int32)
        x[at * tall + SPAN : (at + 1) * tall] = low(number.astype(jnp.float32))
        o[at * SPAN : (at + 1) * SPAN] = out_grad[block, :]
    natural = (slots[...] ^ me) * (MODEL_WIDTH // (n_seq * lax.axis_size("dp"))) + offsets[...]
    row = lax.broadcasted_iota(jnp.int32, place.shape, 0)
    place[...] = low((row == natural).astype(jnp.float32))


def unpack_kernel(mine, near, far, out):
    seq = lax.axis_index("seq")
    for flip, source, at in ((0, mine, 0), (1, near, 0), (2, far, 0), (3, far, 1)):
        target = pl.ds(pl.multiple_of((seq ^ flip) * SPAN, SPAN), SPAN)
        out[target, :] = source[at * SPAN : (at + 1) * SPAN]


def project_kernel(
    x_mine, x_near, x_far, gain_one, place, cosine, sine, wab, wab2,
    spans, x_out, normed_out, qk_out, kpad_out, vpad_out, wqk, wov,
):
    rows = x_out.shape[0]
    half = wab.shape[0]
    tall = SPAN + 16
    for k, (block, at) in enumerate(((x_mine, 0), (x_near, 0), (x_far, 0), (x_far, tall))):
        number = jnp.max(block[at + SPAN : at + tall, :LANES].astype(jnp.float32))
        number = number.astype(jnp.int32)
        spans[k] = number
        x_out[pl.ds(pl.multiple_of(number * SPAN, SPAN), SPAN), :] = block[at : at + SPAN]
    wa, wb = wab.at[:, :QK_WIDTH], wab.at[:, QK_WIDTH:]
    wa2, wb2 = wab2.at[:, :QK_WIDTH], wab2.at[:, QK_WIDTH:]
    wqk[:half] = wa[...]
    wqk[half:] = wa2[...]
    wov[:half] = wb[...]
    wov[half:] = wb2[...]
    x = x_out[...].astype(jnp.float32)
    scale = lax.rsqrt(jnp.mean(x * x, axis=-1, keepdims=True) + EPSILON)
    normed = low(x * scale * gain_one[...])
    normed_out[...] = low(dot_nn(normed, place[...]))
    lane = lax.broadcasted_iota(jnp.int32, (rows, LANES), 1)
    cos, sin = cosine[...], sine[...]
    k_blocks = []
    for b in range(QK_WIDTH // LANES):
        u = dot_nn(normed_out[...], wqk[:, b * LANES : (b + 1) * LANES])
        turned = u * cos + half_turn(u, lane) * sin
        turned = low(turned).astype(jnp.float32)
        if (b + 1) * LANES > Q_WIDTH:
            k_blocks.append(turned)
        if (b + 1) * LANES <= Q_WIDTH:
            turned = turned * FACTOR
        elif b * LANES < Q_WIDTH:
            turned = jnp.where(lane < Q_WIDTH - b * LANES, turned * FACTOR, turned)
        qk_out[:, b * LANES : (b + 1) * LANES] = low(turned)
    first_group = QUERY_HEADS - 2 * (Q_WIDTH // LANES)
    for j in range(KEY_VALUE_HEADS):
        lo, hi = padded_heads(k_blocks, j + first_group, lane)
        kpad_out[2 * j] = lo
        kpad_out[2 * j + 1] = hi
    v = dot_nn(normed_out[...], wov[:, MODEL_WIDTH:])
    v = low(v).astype(jnp.float32)
    v = jnp.concatenate([v, jnp.zeros((rows, HEAD_WIDTH), jnp.float32)], axis=1)
    v_blocks = [v[:, :LANES], v[:, LANES:]]
    for j in range(KEY_VALUE_HEADS):
        lo, hi = padded_heads(v_blocks, j, lane)
        vpad_out[2 * j] = lo
        vpad_out[2 * j + 1] = hi


def head_slot(head):
    group = head // (QUERY_HEADS // KEY_VALUE_HEADS) if isinstance(head, int) else (head * 11) >> 5
    return 2 * group + head % 2


def head_blocks(body):
    @pl.loop(0, QUERY_HEADS // 2)
    def _(b):
        body(2 * b, pl.ds(pl.multiple_of(b * LANES, LANES), LANES), 2)

    if QUERY_HEADS % 2:
        last = QUERY_HEADS // 2
        body(2 * last, slice(last * LANES, (last + 1) * LANES), 1)


def attend_spans(count, qk, kpad, vpad, lse_out, attn_out):
    lane = lax.broadcasted_iota(jnp.int32, (SPAN, LANES), 1)
    diagonal = lax.broadcasted_iota(jnp.int32, (SPAN, SPAN), 0) >= lax.broadcasted_iota(
        jnp.int32, (SPAN, SPAN), 1
    )
    lse_out[...] = jnp.zeros_like(lse_out)

    def block(first_head, columns, heads):
        for i in range(count):
            here = slice(i * SPAN, (i + 1) * SPAN)
            q = qk[here, columns]
            lse = lse_out[here, :]
            mixed = None
            for side in range(heads):
                h = first_head + side
                slot = head_slot(h)
                s = dot_nt(q, kpad[slot, : (i + 1) * SPAN, :])
                s_last = jnp.where(diagonal, s[:, i * SPAN :], -1e30)
                s = s_last if i == 0 else jnp.concatenate([s[:, : i * SPAN], s_last], axis=1)
                top = jnp.max(s, axis=-1, keepdims=True)
                p = jnp.exp(s - top)
                total = jnp.sum(p, axis=-1, keepdims=True)
                p = low(p * (1.0 / total))
                lse = jnp.where(lane == h, top + jnp.log(total), lse)
                part = dot_nn(p, vpad[slot, : (i + 1) * SPAN, :])
                mixed = part if mixed is None else mixed + part
            attn_out[here, columns] = mixed
            lse_out[here, :] = lse

    head_blocks(block)


def attend_kernel(
    x_in, qk, kpad, vpad, gain_two, place, wab, wab2,
    lse_out, attn_out, merged_out, middle_out, normed_two_out,
):
    rows = x_in.shape[0]
    half = wab.shape[0]
    wb, wb2 = wab.at[:, QK_WIDTH:], wab2.at[:, QK_WIDTH:]
    attend_spans(rows // SPAN, qk, kpad, vpad, lse_out, attn_out)
    merged = low(dot_nn(low(attn_out[:, :Q_WIDTH]), place[...]))
    merged_out[...] = merged
    middle = (
        x_in[...].astype(jnp.float32)
        + dot_nn(merged[:, :half], wb[:, :MODEL_WIDTH])
        + dot_nn(merged[:, half:], wb2[:, :MODEL_WIDTH])
    )
    middle_out[...] = middle
    scale_two = lax.rsqrt(jnp.mean(middle * middle, axis=-1, keepdims=True) + EPSILON)
    normed_two_out[...] = low(dot_nn(low(middle * scale_two * gain_two[...]), place[...]))


def ffn_block(n2, og, wg, wu, wd, at, result, back_norm, d_keep, d_send, dd_out):
    columns = pl.ds(pl.multiple_of(at * FFN_BLOCK, FFN_BLOCK), FFN_BLOCK)
    up_columns = pl.ds(pl.multiple_of(HALF_FFN + at * FFN_BLOCK, FFN_BLOCK), FFN_BLOCK)
    half = d_keep.shape[0]
    w_gate, w_up, w_down = wg[:, columns], wu[:, columns], wd[columns, :]
    gate = dot_nn(n2, w_gate)
    up = dot_nn(n2, w_up)
    back_hidden = dot_nt(og, w_down)
    sigmoid = jax.nn.sigmoid(gate)
    silu = gate * sigmoid
    hidden = low(silu * up)
    back_gate = low(back_hidden * up * sigmoid * (1.0 + gate * (1.0 - sigmoid)))
    back_up = low(back_hidden * silu)
    dd_out[columns, :] = low(dot_tn(hidden, og))
    dg = low(dot_tn(n2, back_gate))
    du = low(dot_tn(n2, back_up))
    d_keep[:, columns] = dg[:half]
    d_send[:, columns] = dg[half:]
    d_keep[:, up_columns] = du[:half]
    d_send[:, up_columns] = du[half:]
    result[...] += dot_nn(hidden, w_down)
    back_norm[...] += dot_nt(back_gate, w_gate) + dot_nt(back_up, w_up)


def fill_gate(target, a0, a1, a2, a3):
    size = a0.shape[0] // 2
    for core, (first, second) in enumerate(((a0, a1), (a2, a3))):
        for at, source in enumerate((first, second, first, second)):
            start = (4 * core + at) * size
            piece = slice(at // 2 * size, (at // 2 + 1) * size)
            target[start : start + size] = source[piece, :HALF_FFN]


def fill_up(target, column, b0, b1, b2, b3):
    for at, source in enumerate((b0, b1, b2, b3)):
        size = source.shape[0]
        target[at * size : (at + 1) * size] = source[:, column : column + HALF_FFN]


def ffn_first_kernel(
    spans, o_mine, o_near, o_far, n2, a0, a1, a2, a3, b0, b1, b2, b3,
    og_out, result_out, back_out, d_keep, d_send, dd, wd_out,
    wg, wu, *, order, n_seq,
):
    me = lax.axis_index("dp") * n_seq + lax.axis_index("seq")
    for k, (block, at) in enumerate(((o_mine, 0), (o_near, 0), (o_far, 0), (o_far, SPAN))):
        target = pl.ds(pl.multiple_of(spans[k] * SPAN, SPAN), SPAN)
        og_out[target, :] = block[at : at + SPAN]
    size = a0.shape[0] // 2
    fill_gate(wg, a0, a1, a2, a3)
    fill_up(wu, UP_AT, b0, b1, b2, b3)
    count = len(order)
    rows, pitch = wd_out.shape[0] // count, MODEL_WIDTH // count
    each = size // pitch
    for slot, relative in enumerate(order):
        core, block, at = slot // (4 * each), slot // each % 4, slot % each
        x_side, y_side = block % 2, block // 2
        for t in range(rows // 16):
            if t < DOWN_EARLY:
                source = ((a0, a1), (a2, a3))[core][x_side]
                start = y_side * size + at * pitch
                first = DOWN_AT + t * DOWN_PITCH
            else:
                source = ((b0, b1), (b2, b3))[core][y_side]
                start = x_side * size + at * pitch
                first = (t - DOWN_EARLY) * DOWN_PITCH
            target = pl.multiple_of((me ^ relative) * rows + 16 * t, 16)
            wd_out[pl.ds(target, 16), :] = source[start : start + 16, first : first + MODEL_WIDTH]
    result_out[...] = jnp.zeros_like(result_out)
    back_out[...] = jnp.zeros_like(back_out)

    @pl.loop(0, HALF_FFN // FFN_BLOCK)
    def _(at):
        ffn_block(
            n2[...], og_out[...], wg, wu, wd_out, at, result_out, back_out, d_keep, d_send, dd
        )


def ffn_second_kernel(
    spans, og, n2, a0, a1, a2, a3, b0, b1, b2, b3,
    wd_in, result_in, back_in, dd_in, middle, gain_two, place,
    mine, near, far, back_middle_out, gain_out, keep_out, send_out,
    wg, wu, wd, dd, spread, result, back, *, order, n_seq,
):
    half = keep_out.shape[0]
    fill_gate(wg, a0, a1, a2, a3)
    fill_up(wu, 0, b0, b1, b2, b3)
    me = lax.axis_index("dp") * n_seq + lax.axis_index("seq")
    d_keep = keep_out.at[:, SECOND_GATE_AT : SECOND_GATE_AT + 2 * HALF_FFN]
    d_send = send_out.at[:, SECOND_GATE_AT : SECOND_GATE_AT + 2 * HALF_FFN]
    wd[...] = wd_in[HALF_FFN:, :]
    dd[:HALF_FFN] = dd_in[...]
    result[...] = result_in[...] + middle[...]
    back[...] = back_in[...]

    @pl.loop(0, HALF_FFN // FFN_BLOCK)
    def _(at):
        ffn_block(
            n2[...], og[...], wg, wu, wd, at, result, back, d_keep, d_send, dd.at[HALF_FFN:, :]
        )

    count = len(order)
    rows, pitch = HIDDEN_UNITS // count, MODEL_WIDTH // count
    spread[...] = jnp.zeros_like(spread)
    for t in range(rows // 16):
        for slot, relative in enumerate(order):
            source = pl.ds(pl.multiple_of((me ^ relative) * rows + 16 * t, 16), 16)
            spread[slot * pitch : slot * pitch + 16, :MODEL_WIDTH] = wide(dd[source, :])
        columns = slice(t * DOWN_PITCH, (t + 1) * DOWN_PITCH)
        keep_out[:, columns] = low(spread[:half])
        send_out[:, columns] = low(spread[half:])

    for k, (block, at) in enumerate(((mine, 0), (near, 0), (far, 0), (near, SPAN))):
        source = pl.ds(pl.multiple_of(spans[k] * SPAN, SPAN), SPAN)
        block[at : at + SPAN] = low(result[source, :])
    mid = middle[...]
    scale = lax.rsqrt(jnp.mean(mid * mid, axis=-1, keepdims=True) + EPSILON)
    unit = mid * scale
    back_norm = place_back(back[...], place[...])
    gain_out[...] = jnp.sum(back_norm * unit, axis=0, keepdims=True)
    back_unit = back_norm * gain_two[...]
    back_middle_out[...] = og[...].astype(jnp.float32) + scale * (
        back_unit - unit * jnp.mean(back_unit * unit, axis=-1, keepdims=True)
    )


def score_back(i, qk, kpad, vpad, ab, lse_rows, correction, dqk, dv):
    rows = qk.shape[0]
    groups = QUERY_HEADS // KEY_VALUE_HEADS
    diagonal = lax.broadcasted_iota(jnp.int32, (SPAN, SPAN), 1) >= lax.broadcasted_iota(
        jnp.int32, (SPAN, SPAN), 0
    )
    lane = lax.broadcasted_iota(jnp.int32, (SPAN, LANES), 1)
    keys = slice(i * SPAN, (i + 1) * SPAN)
    first = i * SPAN
    dk_sums = [None] * (2 * KEY_VALUE_HEADS)
    dv_sums = [None] * (2 * KEY_VALUE_HEADS)
    for b in range((QUERY_HEADS + 1) // 2):
        columns = slice(b * LANES, (b + 1) * LANES)
        q = qk[first:, columns]
        a = ab[first:, columns]
        dq = None
        for h in range(2 * b, min(2 * b + 2, QUERY_HEADS)):
            slot = 2 * (h // groups) + h % 2
            s = dot_nt(kpad[slot, keys, :], q)
            s = s - lse_rows[h : h + 1, first:]
            s_first = jnp.where(diagonal, s[:, :SPAN], -1e30)
            s = (
                s_first
                if first + SPAN == rows
                else jnp.concatenate([s_first, s[:, SPAN:]], axis=1)
            )
            p = jnp.exp(s)
            dp = dot_nt(vpad[slot, keys, :], a)
            ds = low(p * (dp - correction[h : h + 1, first:]))
            dk = dot_nn(ds, q)
            dvh = dot_nn(low(p), a)
            dk_sums[slot] = dk if dk_sums[slot] is None else dk_sums[slot] + dk
            dv_sums[slot] = dvh if dv_sums[slot] is None else dv_sums[slot] + dvh
            part = dot_tn(ds, kpad[slot, keys, :])
            dq = part if dq is None else dq + part
        if i == 0:
            dqk[first:, columns] = dq
        else:
            dqk[first:, columns] += dq

    def both(sums, j):
        return sums[2 * j] + pltpu.roll(sums[2 * j + 1], HEAD_WIDTH, 1)

    dk_heads = [both(dk_sums, j) for j in range(KEY_VALUE_HEADS)]
    dv_heads = [both(dv_sums, j) for j in range(KEY_VALUE_HEADS)]
    key_scale = 1.0 / FACTOR
    q_tail = dqk[keys, 4 * LANES : 5 * LANES]
    dqk[keys, 4 * LANES : 5 * LANES] = jnp.where(
        lane < HEAD_WIDTH, q_tail, pltpu.roll(dk_heads[0], HEAD_WIDTH, 1) * key_scale
    )
    dqk[keys, 5 * LANES :] = (
        jnp.where(lane < HEAD_WIDTH, dk_heads[1], pltpu.roll(dk_heads[2], HEAD_WIDTH, 1))
        * key_scale
    )
    dv[keys, :LANES] = low(
        jnp.where(lane < HEAD_WIDTH, dv_heads[0], pltpu.roll(dv_heads[1], HEAD_WIDTH, 1))
    )
    dv[keys, LANES:] = low(dv_heads[2])


def attend_back_first_kernel(
    qk, kpad, vpad, lse, attn, merged, back_middle, place, wab, wab2,
    keep_out, send_out, ab, lse_rows, correction, dqk, dv,
):
    rows = qk.shape[0]
    half = wab.shape[0]
    wb, wb2 = wab.at[:, QK_WIDTH:], wab2.at[:, QK_WIDTH:]
    middle_low = low(back_middle[...])
    d_out = low(dot_tn(merged[...], middle_low))
    out_columns = slice(QK_WIDTH, QK_WIDTH + MODEL_WIDTH)
    keep_out[:half, out_columns] = d_out[:half]
    send_out[:half, out_columns] = d_out[half:]
    ab_first = low(dot_nt(middle_low, wb[:, :MODEL_WIDTH]))
    ab_second = low(dot_nt(middle_low, wb2[:, :MODEL_WIDTH]))
    ab[:, :Q_WIDTH] = low(
        dot_nt(ab_first, place[:, :half]) + dot_nt(ab_second, place[:, half:])
    )
    ab[:, Q_WIDTH:] = jnp.zeros((rows, ab.shape[1] - Q_WIDTH), jnp.bfloat16)
    terms = ab[...].astype(jnp.float32) * attn[...]
    mask = low(
        (
            lax.broadcasted_iota(jnp.int32, (16, terms.shape[1]), 1) // HEAD_WIDTH
            == lax.broadcasted_iota(jnp.int32, (16, terms.shape[1]), 0)
        ).astype(jnp.float32)
    )
    high = low(terms)
    correction[...] = dot_nt(mask, high) + dot_nt(mask, low(terms - high.astype(jnp.float32)))
    lse_rows[...] = jnp.transpose(lse[...])
    score_back(0, qk, kpad, vpad, ab, lse_rows, correction, dqk, dv)


def attend_back_second_kernel(
    dqk_in, dv_in, qk, kpad, vpad, lse_rows, correction, ab, dqk, dv,
):
    for i in range(1, qk.shape[0] // SPAN):
        score_back(i, qk, kpad, vpad, ab, lse_rows, correction, dqk, dv)


def project_back_kernel(
    keep_in, send_in, gain_two_in, spans, x, normed, dqk, dv, back_middle, gain_one,
    place, cosine, sine, wab, wab2,
    mine, near, far, d1, d2,
    grad, grad_full,
):
    rows = x.shape[0]
    half = wab.shape[0]
    lane = lax.broadcasted_iota(jnp.int32, (rows, LANES), 1)
    cos, sin = cosine[...], sine[...]
    for b in range(QK_WIDTH // LANES):
        u = dqk[:, b * LANES : (b + 1) * LANES] * FACTOR
        grad[:, b * LANES : (b + 1) * LANES] = low(u * cos - half_turn(u, lane) * sin)
    d_qk = low(dot_tn(normed[...], grad[...]))
    d1[:half, :QK_WIDTH] = d_qk[:half]
    d2[:half, :QK_WIDTH] = d_qk[half:]
    dv_low = dv[:, :KV_WIDTH]
    d_v = low(dot_tn(normed[...], dv_low))
    d1[:half, QK_WIDTH + MODEL_WIDTH :] = d_v[:half]
    d2[:half, QK_WIDTH + MODEL_WIDTH :] = d_v[half:]
    parts = [
        dot_nt(grad[...], w[:, :QK_WIDTH]) + dot_nt(dv_low, w[:, QK_WIDTH + MODEL_WIDTH :])
        for w in (wab, wab2)
    ]
    back_norm = place_back(jnp.concatenate(parts, axis=1), place[...])
    xf = x[...].astype(jnp.float32)
    scale = lax.rsqrt(jnp.mean(xf * xf, axis=-1, keepdims=True) + EPSILON)
    unit = xf * scale
    gain_row = lax.broadcasted_iota(jnp.int32, (16, MODEL_WIDTH), 0)
    gains = jnp.where(
        gain_row == 0, jnp.sum(back_norm * unit, axis=0, keepdims=True), gain_two_in[...]
    )
    for d in (d1, d2):
        d[half:, :MODEL_WIDTH] = low(gains)
        d[half:, MODEL_WIDTH:] = jnp.zeros((16, d.shape[1] - MODEL_WIDTH), jnp.bfloat16)
    back_unit = back_norm * gain_one[...]
    grad_full[...] = back_middle[...] + scale * (
        back_unit - unit * jnp.mean(back_unit * unit, axis=-1, keepdims=True)
    )
    for k, (block, at) in enumerate(((mine, 0), (near, 0), (far, 0), (near, SPAN))):
        source = pl.ds(pl.multiple_of(spans[k] * SPAN, SPAN), SPAN)
        block[at : at + SPAN] = low(grad_full[source, :])


VMEM_SPEC = pl.BlockSpec(memory_space=pltpu.VMEM)
SMEM_SPEC = pl.BlockSpec(memory_space=pltpu.SMEM)
ANY_SPEC = pl.BlockSpec(memory_space=pl.ANY)


def shaped(rows, columns, kind):
    return jax.ShapeDtypeStruct((rows, columns), kind)


def call(body, outs, args, scratch, micros, scalars=(), after=(), alias=None, megabytes=16, out_specs=None):
    def run(*refs):
        body(*refs[: len(args)], *refs[len(args) + len(after) :])

    return pl.pallas_call(
        run,
        out_shape=outs,
        in_specs=[SMEM_SPEC if at in scalars else VMEM_SPEC for at in range(len(args))]
        + [ANY_SPEC] * len(after),
        out_specs=out_specs or [VMEM_SPEC] * len(outs),
        scratch_shapes=scratch,
        input_output_aliases=alias or {},
        compiler_params=vmem_params(megabytes),
        cost_estimate=pl.CostEstimate(
            flops=int(micros * 1.1e9), bytes_accessed=1_000_000, transcendentals=0
        ),
    )(*args, *after)


def whole_sequence_plan(mesh):
    axes = ("dp", "seq")
    n_dp, n_seq = mesh.shape["dp"], mesh.shape["seq"]
    count = n_dp * n_seq
    bits = count.bit_length() - 1
    seq_bits = n_seq.bit_length() - 1
    core, y_bit = 0, 1
    x_bit = seq_bits
    z_bits = tuple(range(seq_bits + 1, bits))[::-1]
    order_bits = z_bits + (x_bit, y_bit, core)

    def hold(v, *others):
        return lax.optimization_barrier((v, *others))[0] if others else v

    def together(*arrays):
        return lax.optimization_barrier(arrays)

    def swap(v, flip, until=()):
        return hold(lax.ppermute(v, axes, [(d, d ^ flip) for d in range(count)]), *until)

    def relative(slot):
        return sum(1 << bit for at, bit in enumerate(order_bits) if slot >> at & 1)

    order = tuple(relative(slot) for slot in range(count))
    z_count = 1 << len(z_bits)
    z_flips = [relative(slot) for slot in range(1, z_count)]
    flip_x, flip_y, flip_core = 1 << x_bit, 1 << y_bit, 1 << core

    def gather_z(v, until=()):
        return jnp.concatenate([v] + [swap(v, flip, until) for flip in z_flips], axis=0)

    def gather_z_stepwise(v, untils):
        for bit, until in zip(z_bits, untils):
            v = jnp.concatenate([v, swap(v, 1 << bit, until)], axis=0)
        return v

    def gather_one(v, x_first, until=()):
        return jnp.concatenate([v, swap(v, flip_x if x_first else flip_y, until)], axis=0)

    def gather_two(v, x_first, until=()):
        w = swap(v, flip_y if x_first else flip_x, until)
        size = v.shape[0] // 2
        if x_first:
            return jnp.concatenate([v, w], axis=0)
        return jnp.concatenate([v[:size], w[:size], v[size:], w[size:]], axis=0)

    def scatter_core(keep, send, until=()):
        return wide(keep) + wide(swap(send, flip_core, until))

    def scatter_one(total, x_first, until=()):
        size = total.shape[0] // 4
        if x_first:
            mine = jnp.concatenate([total[:size], total[2 * size : 3 * size]], axis=0)
            theirs = jnp.concatenate([total[size : 2 * size], total[3 * size :]], axis=0)
            return mine + wide(swap(low(theirs), flip_x, until))
        return total[: 2 * size] + wide(swap(low(total[2 * size :]), flip_y, until))

    def scatter_two(total, x_first, until=()):
        size = total.shape[0] // 2
        sent = swap(low(total[size:]), flip_y if x_first else flip_x, until)
        return total[:size] + wide(sent)

    def scatter_bit(total, bit):
        size = total.shape[0] // 2
        return total[:size] + wide(swap(low(total[size:]), 1 << bit))

    def scatter_z_with_sums(total, sums):
        size = total.shape[0] // z_count
        sums = lax.reduce_precision(sums.reshape(size, -1), 8, 7)
        width, wanted = total.shape[1], sums.shape[1]
        beside = jnp.pad(low(sums), ((0, 0), (0, -wanted % LANES)))
        out, terms = total[:size], [sums]
        for at, flip in enumerate(z_flips):
            theirs = low(total[(at + 1) * size : (at + 2) * size])
            sent = swap(jnp.concatenate([theirs, beside], axis=1), flip)
            out = out + wide(sent[:, :width])
            terms.append(wide(sent[:, width : width + wanted]))
        while len(terms) > 1:
            terms = [a + b for a, b in zip(terms[::2], terms[1::2])]
        return out, terms[0].reshape(-1)

    def exchange(parts, near_until=(), far_until=(), far_after=()):
        mine, near, far = parts
        size = mine.shape[0]
        near = swap(near, flip_core, near_until)
        far = hold(jnp.concatenate([far, near[size:]], axis=0), *far_after)
        return mine, near[:size], swap(far, flip_y, far_until)

    def scatter_with_sums(mine, theirs, sums, flip, until=()):
        sums = lax.reduce_precision(sums, 8, 7)
        sent = swap(jnp.concatenate([low(theirs), low(sums)], axis=0), flip, until)
        return mine + wide(sent[: mine.shape[0]]), sums + wide(sent[mine.shape[0] :])

    def on_sequence_device(
        hidden_in, span_order, attention_norm_gain, query_weight, key_weight, value_weight,
        output_weight, feedforward_gain, gate_weight, up_weight, down_weight, out_grad,
    ):
        rows = hidden_in.shape[0]
        model_rows = MODEL_WIDTH // count
        hidden_rows = HIDDEN_UNITS // count
        bf, f4 = jnp.bfloat16, jnp.float32
        half = MODEL_WIDTH // 2
        gain_one = attention_norm_gain.astype(jnp.float32).reshape(1, MODEL_WIDTH)
        gain_two = feedforward_gain.astype(jnp.float32).reshape(1, MODEL_WIDTH)
        model_low, model_full = shaped(rows, MODEL_WIDTH, bf), shaped(rows, MODEL_WIDTH, f4)

        def rows_of(w, columns):
            return w.reshape(model_rows, columns)

        def unpack(parts):
            return call(unpack_kernel, [model_low], parts, [], 1, megabytes=4)[0]

        slots = np.repeat(np.asarray(order, np.int32), model_rows)[None, :]
        offsets = np.tile(np.arange(model_rows, dtype=np.int32), count)[None, :]
        packed = call(
            functools.partial(pack_kernel, n_seq=n_seq),
            [
                *[shaped(n * (SPAN + 16), MODEL_WIDTH, bf) for n in (1, 2, 1)],
                *[shaped(n * SPAN, MODEL_WIDTH, bf) for n in (1, 2, 1)],
                shaped(MODEL_WIDTH, MODEL_WIDTH, bf),
            ],
            [span_order, hidden_in, out_grad, slots, offsets],
            [],
            2,
            scalars=(0,),
        )
        place = packed[6]
        first = jnp.concatenate(
            [
                rows_of(query_weight, Q_WIDTH),
                rows_of(key_weight, KV_WIDTH),
                rows_of(output_weight, MODEL_WIDTH),
                rows_of(value_weight, KV_WIDTH),
            ],
            axis=1,
        )

        down = down_weight.reshape(3, 16, MODEL_WIDTH).swapaxes(0, 1)
        down = jnp.pad(down, ((0, model_rows - 16), (0, 0), (0, DOWN_PITCH - MODEL_WIDTH)))
        gate, up = rows_of(gate_weight, HIDDEN_UNITS), rows_of(up_weight, HIDDEN_UNITS)
        ffn = jnp.concatenate(
            [gate[:, :HALF_FFN], down.reshape(model_rows, 3 * DOWN_PITCH), up[:, :HALF_FFN]], axis=1
        )
        later = jnp.concatenate([gate[:, HALF_FFN:], up[:, HALF_FFN:]], axis=1)
        first = gather_z(hold(first, place), until=(ffn,))
        first_a, first_b = first[:, :QK_WIDTH], first[:, QK_WIDTH:]
        first_a, first_b = gather_one(first_a, False), gather_one(first_b, True)
        x_parts = exchange(packed[:3], (first,), (first_a, first_b))
        one = (first_a, first_b)
        first_a, first_b = gather_two(first_a, False), gather_two(first_b, True)
        first = jnp.concatenate([first_a, first_b], axis=1)
        ffn = gather_z_stepwise(ffn, (one, (first,)))
        o_parts = exchange(hold(tuple(packed[3:6]), *one), (first,), (ffn,), (first,))
        first_other = swap(first, flip_core)
        ffn_a, ffn_b = ffn[:, :FFN_CUT], ffn[:, FFN_CUT:]

        frequency = np.exp(np.arange(HEAD_WIDTH // 2) * (-2.0 * math.log(10000.0) / HEAD_WIDTH))
        angles = np.arange(rows)[:, None] * frequency[None, :]
        cosine = np.tile(np.cos(angles), (1, 4)).astype(np.float32)
        sine = np.sin(angles)
        sine = np.concatenate([-sine, sine, -sine, sine], axis=1).astype(np.float32)

        padded = jax.ShapeDtypeStruct((2 * KEY_VALUE_HEADS, rows, LANES), bf)
        spans, x, normed, qk, kpad, vpad = call(
            project_kernel,
            [
                jax.ShapeDtypeStruct((n_seq,), jnp.int32),
                model_low,
                model_low,
                shaped(rows, QK_WIDTH, bf),
                padded,
                padded,
            ],
            [*x_parts, gain_one, place, cosine, sine, first, first_other],
            [pltpu.VMEM((MODEL_WIDTH, QK_WIDTH), bf)] * 2,
            5,
            out_specs=[SMEM_SPEC] + [VMEM_SPEC] * 5,
        )
        stats = [shaped(rows, LANES, f4), shaped(rows, 5 * LANES, f4)]
        ffn_a, ffn_b = gather_one(ffn_a, False, (x,)), gather_one(ffn_b, True, (x,))
        lse, attn, merged, middle, normed_two = call(
            attend_kernel,
            [*stats, model_low, model_full, model_low],
            [x, qk, kpad, vpad, gain_two, place, first, first_other],
            [],
            10,
        )
        later = gather_z_stepwise(hold(later, ffn), ((ffn_a, ffn_b), (middle,)))
        ffn = []
        for part, flip in ((ffn_a, flip_x), (ffn_b, flip_y)):
            second = swap(part, flip, (middle,))
            ffn += [part, second, swap(part, flip_core, (middle,)), swap(second, flip_core)]
        later_a = gather_one(later[:, :HALF_FFN], False, (ffn[1],))
        later_b = gather_one(later[:, HALF_FFN:], True, (ffn[5],))
        weight_scratch = [pltpu.VMEM((MODEL_WIDTH, HALF_FFN), bf)] * 2
        og, result, back, r1, r1_send, dd, w_down = call(
            functools.partial(ffn_first_kernel, order=order, n_seq=n_seq),
            [
                model_low,
                model_full,
                model_full,
                *[shaped(half, 2 * HALF_FFN, bf)] * 2,
                shaped(HALF_FFN, MODEL_WIDTH, bf),
                shaped(HIDDEN_UNITS, MODEL_WIDTH, bf),
            ],
            [spans, *o_parts, normed_two, *ffn],
            weight_scratch,
            10,
            scalars=(0,),
        )
        r1_own = r1
        later = []
        for part, flip in ((later_a, flip_x), (later_b, flip_y)):
            second = swap(part, flip, (og,))
            later += [part, second, swap(part, flip_core, (og,)), swap(second, flip_core)]
        *h_parts, back_middle, gain_two_grad, r2, r2_send = call(
            functools.partial(ffn_second_kernel, order=order, n_seq=n_seq),
            [
                *[shaped(n * SPAN, MODEL_WIDTH, bf) for n in (1, 2, 1)],
                model_full,
                shaped(1, MODEL_WIDTH, f4),
                *[shaped(half, SECOND_WIDTH, bf)] * 2,
            ],
            [spans, og, normed_two, *later, w_down, result, back, dd, middle, gain_two, place],
            weight_scratch
            + [
                pltpu.VMEM((HALF_FFN, MODEL_WIDTH), bf),
                pltpu.VMEM((HIDDEN_UNITS, MODEL_WIDTH), bf),
                pltpu.VMEM((MODEL_WIDTH, DOWN_PITCH), f4),
                pltpu.VMEM((rows, MODEL_WIDTH), f4),
                pltpu.VMEM((rows, MODEL_WIDTH), f4),
            ],
            13,
            scalars=(0,),
            megabytes=18,
        )
        r1 = scatter_core(r1_own, r1_send, (back_middle,))
        r3, r3_send, ab, lse_rows, correction, dqk, dv = call(
            attend_back_first_kernel,
            [
                *[shaped(half + 16, 2 * HALF_FFN, bf)] * 2,
                shaped(rows, 5 * LANES, bf),
                shaped(LANES, rows, f4),
                shaped(16, rows, f4),
                shaped(rows, QK_WIDTH, f4),
                shaped(rows, 2 * LANES, bf),
            ],
            [qk, kpad, vpad, lse, attn, merged, back_middle, place, first, first_other],
            [],
            7,
            after=[r1],
        )
        r2 = scatter_core(r2, r2_send, (ab,))
        h_near = swap(h_parts[1], flip_core, (ab,))
        dqk, dv = call(
            attend_back_second_kernel,
            [shaped(rows, QK_WIDTH, f4), shaped(rows, 2 * LANES, bf)],
            [dqk, dv, qk, kpad, vpad, lse_rows, correction, ab],
            [],
            6,
            after=[r2],
            alias={0: 0, 1: 1},
        )
        p1 = scatter_one(r2[:, :SECOND_CUT], True, (dqk,))
        p2 = scatter_one(r2[:, SECOND_CUT : 2 * SECOND_CUT], False, (dqk,))
        *g_parts, r3, r3_send = call(
            project_back_kernel,
            [
                *[shaped(n * SPAN, MODEL_WIDTH, bf) for n in (1, 2, 1)],
                *[shaped(half + 16, 2 * HALF_FFN, bf)] * 2,
            ],
            [
                r3, r3_send, gain_two_grad, spans, x, normed, dqk, dv, back_middle,
                gain_one, place, cosine, sine, first, first_other,
            ],
            [pltpu.VMEM((rows, QK_WIDTH), bf), pltpu.VMEM((rows, MODEL_WIDTH), f4)],
            5,
            scalars=(3,),
            after=[p1, p2],
            alias={0: 3, 1: 4},
        )
        p1, p2 = scatter_two(p1, True, (r3,)), scatter_two(p2, False, (r3,))
        p3 = scatter_one(r2[:, 2 * SECOND_CUT :], True, (r3,))
        r1 = scatter_one(r1, False, (r3,))
        sent = wide(swap(r3_send, flip_core))
        r3 = wide(r3)
        r1, p3 = scatter_two(r1, False), scatter_two(p3, True)
        total, sums, r1, p1, p2, p3 = together(
            r3[:half] + sent[:half], r3[half:] + sent[half:], r1, p1, p2, p3
        )
        size = half // 4
        r3_a, r3_b = total[:, :QK_WIDTH], total[:, QK_WIDTH:]
        r3_a, sums = scatter_with_sums(
            jnp.concatenate([r3_a[:size], r3_a[2 * size : 3 * size]], axis=0),
            jnp.concatenate([r3_a[size : 2 * size], r3_a[3 * size :]], axis=0),
            sums[:, :QK_WIDTH],
            flip_x,
        )
        r3_b = scatter_one(r3_b, False)
        early = jnp.concatenate([p1, p2, r1], axis=1)
        early = scatter_bit(early, z_bits[-1])
        g_near = swap(g_parts[1], flip_core)
        r3_a, r3_b, sums, early, g_near, h_near = together(
            r3_a, r3_b, sums, early, g_near, h_near
        )
        r3_a, sums = scatter_with_sums(r3_a[:size], r3_a[size:], sums, flip_y)
        r3_b = scatter_two(r3_b, False)
        for bit in z_bits[-2::-1]:
            early = scatter_bit(early, bit)
        h_far = swap(jnp.concatenate([h_parts[2], h_near[SPAN:]], axis=0), flip_y)
        r3_a, r3_b, sums, early, h_far, g_near = together(
            r3_a, r3_b, sums, early, h_far, g_near
        )
        g_far = swap(jnp.concatenate([g_parts[2], g_near[SPAN:]], axis=0), flip_y)
        late = jnp.concatenate([r3_a, r3_b, p3], axis=1)
        late, sums = scatter_z_with_sums(late, sums[:2, :MODEL_WIDTH])
        hidden_out = unpack([h_parts[0], h_near[:SPAN], h_far])
        r1 = early[:, 2 * SECOND_CUT :]
        r2 = jnp.concatenate([early[:, : 2 * SECOND_CUT], late[:, 2 * HALF_FFN :]], axis=1)
        r3 = late
        hidden_grad = unpack([g_parts[0], g_near[:SPAN], g_far])
        gu1 = r2[:, SECOND_GATE_AT:]
        gate_grad = jnp.concatenate([r1[:, :HALF_FFN], gu1[:, :HALF_FFN]], axis=1)
        up_grad = jnp.concatenate([r1[:, HALF_FFN:], gu1[:, HALF_FFN : 2 * HALF_FFN]], axis=1)
        down_grad = r2[:16, :SECOND_GATE_AT].reshape(16, 3, DOWN_PITCH)[:, :, :MODEL_WIDTH]
        return (
            hidden_out,
            hidden_grad,
            sums[:MODEL_WIDTH],
            r3[:, :Q_WIDTH].reshape(-1),
            r3[:, Q_WIDTH:QK_WIDTH].reshape(-1),
            r3[:, QK_WIDTH + MODEL_WIDTH : 2 * HALF_FFN].reshape(-1),
            r3[:, QK_WIDTH : QK_WIDTH + MODEL_WIDTH].reshape(-1),
            sums[MODEL_WIDTH:],
            gate_grad.reshape(-1),
            up_grad.reshape(-1),
            down_grad.swapaxes(0, 1).reshape(-1),
        )

    return on_sequence_device


def pick_plan(mesh):
    count = mesh.shape["dp"] * mesh.shape["seq"]
    fits = (
        mesh.shape["seq"] == MB * SLOTS
        and SLOTS == 1
        and count & (count - 1) == 0
        and MODEL_WIDTH % count == 0
        and (HIDDEN_UNITS // count) % 16 == 0
    )
    return whole_sequence_plan(mesh) if fits else on_device


def solution(mesh):
    return jax.shard_map(
        pick_plan(mesh),
        mesh=mesh,
        in_specs=(
            P(("dp", "seq"), None),
            P(("dp", "seq")),
            P(),
            P(("dp", "seq")),
            P(("dp", "seq")),
            P(("dp", "seq")),
            P(("dp", "seq")),
            P(),
            P(("dp", "seq")),
            P(("dp", "seq")),
            P(("dp", "seq")),
            P(("dp", "seq"), None),
        ),
        out_specs=(
            P(("dp", "seq"), None),
            P(("dp", "seq"), None),
            P(),
            P(("dp", "seq")),
            P(("dp", "seq")),
            P(("dp", "seq")),
            P(("dp", "seq")),
            P(),
            P(("dp", "seq")),
            P(("dp", "seq")),
            P(("dp", "seq")),
        ),
        check_vma=False,
    )
```

```python
import functools
import math

import jax
import jax.numpy as jnp
import numpy as np
from jax import lax
from jax.experimental import pallas as pl
from jax.experimental.pallas import tpu as pltpu
from jax.sharding import PartitionSpec as P

MODEL_WIDTH = 576
QUERY_HEADS = 9
KEY_VALUE_HEADS = 3
HEAD_WIDTH = 64
HIDDEN_UNITS = 1536
SPAN = 128
MB = 4
SLOTS = 1


EPSILON = 1e-05


def angle_tables(positions, head_size):
    frequency = jnp.exp(
        jnp.arange(head_size // 2, dtype=jnp.float32) * (-2.0 * math.log(10000.0) / head_size)
    )
    angles = positions.astype(jnp.float32)[:, None] * frequency[None, :]
    angles = jnp.concatenate([angles, angles], axis=-1)[:, None, :]
    return (jnp.cos(angles), jnp.sin(angles))


def apply_rotation(value_rows, cosine_table, sine_values):
    half_size = value_rows.shape[-1] // 2
    turned = jnp.concatenate([-value_rows[..., half_size:], value_rows[..., :half_size]], axis=-1)
    return value_rows * cosine_table + turned * sine_values


def product(first_arg, second_arg):
    return jnp.dot(first_arg, second_arg, preferred_element_type=jnp.float32)


def inner_rows(first_arg, second_arg):
    return lax.dot_general(
        first_arg, second_arg, (((0,), (0,)), ((), ())), preferred_element_type=jnp.float32
    )


def inner_cols(first_arg, second_arg):
    return lax.dot_general(
        first_arg, second_arg, (((1,), (1,)), ((), ())), preferred_element_type=jnp.float32
    )


def shape_weights(flattened_rows):
    return (
        flattened_rows[0].reshape(MODEL_WIDTH, QUERY_HEADS * HEAD_WIDTH),
        flattened_rows[1].reshape(MODEL_WIDTH, KEY_VALUE_HEADS * HEAD_WIDTH),
        flattened_rows[2].reshape(MODEL_WIDTH, KEY_VALUE_HEADS * HEAD_WIDTH),
        flattened_rows[3].reshape(QUERY_HEADS * HEAD_WIDTH, MODEL_WIDTH),
        flattened_rows[4].reshape(MODEL_WIDTH, HIDDEN_UNITS),
        flattened_rows[5].reshape(MODEL_WIDTH, HIDDEN_UNITS),
        flattened_rows[6].reshape(HIDDEN_UNITS, MODEL_WIDTH),
    )


def block_scores(query_rows, key_block, query_place, key_place, factor):
    raw_scores = (
        jnp.einsum("qkgd,skd->kgqs", query_rows, key_block, preferred_element_type=jnp.float32)
        * factor
    )
    allowed = query_place[:, None] >= key_place[None, :]
    return jnp.where(allowed, raw_scores, -1e30)


def forward(layer_input, positions, span_ids, gain_pair, matrices):
    w_q, w_k, w_v, w_o, w_g, w_u, w_d = matrices
    count_of_rows = layer_input.shape[0]
    query_group_width = QUERY_HEADS // KEY_VALUE_HEADS
    factor = 1.0 / math.sqrt(HEAD_WIDTH)
    input_full = layer_input.astype(jnp.float32)
    scale_one = lax.rsqrt(jnp.mean(input_full * input_full, axis=-1, keepdims=True) + EPSILON)
    unit_one = input_full * scale_one
    normed = (unit_one * gain_pair[0]).astype(jnp.bfloat16)
    query_rows = product(normed, w_q)
    unrotated_keys = product(normed, w_k)
    value_rows = product(normed, w_v)
    cosine_table, sine_values = angle_tables(positions, HEAD_WIDTH)
    rotated_query = apply_rotation(
        query_rows.reshape(count_of_rows, QUERY_HEADS, HEAD_WIDTH), cosine_table, sine_values
    ).astype(jnp.bfloat16)
    rotated_query = rotated_query.reshape(
        count_of_rows, KEY_VALUE_HEADS, query_group_width, HEAD_WIDTH
    )
    rotated_key = apply_rotation(
        unrotated_keys.reshape(count_of_rows, KEY_VALUE_HEADS, HEAD_WIDTH),
        cosine_table,
        sine_values,
    ).astype(jnp.bfloat16)
    rotated_key = rotated_key.reshape(count_of_rows, KEY_VALUE_HEADS * HEAD_WIDTH)
    v_low = value_rows.astype(jnp.bfloat16)
    every_key, every_value, key_spans = (
        lax.all_gather(rotated_key, "seq", axis=0, tiled=True),
        lax.all_gather(v_low, "seq", axis=0, tiled=True),
        lax.all_gather(span_ids.astype(jnp.bfloat16), "seq", axis=0, tiled=True),
    )
    offsets = jnp.arange(SPAN, dtype=jnp.int32)
    key_places = (key_spans.astype(jnp.int32)[:, None] * SPAN + offsets[None, :]).reshape(-1)
    count_of_keys = every_key.shape[0]
    block_length = math.gcd(count_of_keys, 512)
    count_of_blocks = count_of_keys // block_length
    blocks_of_keys = every_key.reshape(count_of_blocks, block_length, KEY_VALUE_HEADS, HEAD_WIDTH)
    blocks_of_values = every_value.reshape(
        count_of_blocks, block_length, KEY_VALUE_HEADS, HEAD_WIDTH
    )
    place_blocks = key_places.reshape(count_of_blocks, block_length)

    def softmax_stats(carry, piece_set):
        highest, totals = carry
        key_block, key_place = piece_set
        scores = block_scores(rotated_query, key_block, positions, key_place, factor)
        new_high = jnp.maximum(highest, jnp.max(scores, axis=-1))
        totals = totals * jnp.exp(highest - new_high) + jnp.sum(
            jnp.exp(scores - new_high[..., None]), axis=-1
        )
        return ((new_high, totals), None)

    initial = (
        jnp.full((KEY_VALUE_HEADS, query_group_width, count_of_rows), -1e30, jnp.float32),
        jnp.zeros((KEY_VALUE_HEADS, query_group_width, count_of_rows), jnp.float32),
    )
    (highest, totals), _ = lax.scan(softmax_stats, initial, (blocks_of_keys, place_blocks))

    def mix_values(running, piece_set):
        key_block, value_block, key_place = piece_set
        scores = block_scores(rotated_query, key_block, positions, key_place, factor)
        layer_weights = (jnp.exp(scores - highest[..., None]) / totals[..., None]).astype(
            jnp.bfloat16
        )
        return (
            running
            + jnp.einsum(
                "kgqs,skd->qkgd", layer_weights, value_block, preferred_element_type=jnp.float32
            ),
            None,
        )

    attention_output, _ = lax.scan(
        mix_values,
        jnp.zeros((count_of_rows, KEY_VALUE_HEADS, query_group_width, HEAD_WIDTH), jnp.float32),
        (blocks_of_keys, blocks_of_values, place_blocks),
    )
    attention_output = attention_output.reshape(count_of_rows, QUERY_HEADS * HEAD_WIDTH)
    merged = attention_output.astype(jnp.bfloat16)
    middle = input_full + product(merged, w_o)
    scale_two = lax.rsqrt(jnp.mean(middle * middle, axis=-1, keepdims=True) + EPSILON)
    unit_two = middle * scale_two
    normed_two = (unit_two * gain_pair[1]).astype(jnp.bfloat16)
    gate_act = product(normed_two, w_g)
    upward = product(normed_two, w_u)
    hidden = (jax.nn.silu(gate_act) * upward).astype(jnp.bfloat16)
    result = (middle + product(hidden, w_d)).astype(jnp.bfloat16)
    stored = (
        scale_one,
        unit_one,
        normed,
        cosine_table,
        sine_values,
        rotated_query,
        blocks_of_keys,
        blocks_of_values,
        place_blocks,
        highest,
        totals,
        attention_output,
        merged,
        scale_two,
        unit_two,
        normed_two,
        gate_act,
        upward,
        hidden,
    )
    return (result, stored)


def backward(cotangent, positions, gain_pair, matrices, stored):
    w_q, w_k, w_v, w_o, w_g, w_u, w_d = matrices
    (
        scale_one,
        unit_one,
        normed,
        cosine_table,
        sine_values,
        rotated_query,
        blocks_of_keys,
        blocks_of_values,
        place_blocks,
        highest,
        totals,
        attention_output,
        merged,
        scale_two,
        unit_two,
        normed_two,
        gate_act,
        upward,
        hidden,
    ) = stored
    count_of_rows = cotangent.shape[0]
    query_group_width = QUERY_HEADS // KEY_VALUE_HEADS
    factor = 1.0 / math.sqrt(HEAD_WIDTH)
    grad_down = inner_rows(hidden, cotangent)
    back_hidden = inner_cols(cotangent, w_d)
    sigmoid_gate = jax.nn.sigmoid(gate_act)
    back_gate = (
        back_hidden * upward * sigmoid_gate * (1.0 + gate_act * (1.0 - sigmoid_gate))
    ).astype(jnp.bfloat16)
    back_up = (back_hidden * (gate_act * sigmoid_gate)).astype(jnp.bfloat16)
    grad_gate = inner_rows(normed_two, back_gate)
    grad_up = inner_rows(normed_two, back_up)
    back_norm_two = inner_cols(back_gate, w_g) + inner_cols(back_up, w_u)
    gain_two = jnp.sum(back_norm_two * unit_two, axis=0)
    back_unit = back_norm_two * gain_pair[1]
    back_middle = cotangent.astype(jnp.float32) + scale_two * (
        back_unit - unit_two * jnp.mean(back_unit * unit_two, axis=-1, keepdims=True)
    )
    middle_low = back_middle.astype(jnp.bfloat16)
    grad_out = inner_rows(merged, middle_low)
    attention_backward = inner_cols(middle_low, w_o).astype(jnp.bfloat16)
    head_gradient_rows = attention_backward.reshape(
        count_of_rows, KEY_VALUE_HEADS, query_group_width, HEAD_WIDTH
    )
    attention_head_rows = attention_output.reshape(
        count_of_rows, KEY_VALUE_HEADS, query_group_width, HEAD_WIDTH
    )
    correction = jnp.transpose(
        jnp.sum(head_gradient_rows.astype(jnp.float32) * attention_head_rows, axis=-1), (1, 2, 0)
    )

    def score_grads(running, piece_set):
        key_block, value_block, key_place = piece_set
        scores = block_scores(rotated_query, key_block, positions, key_place, factor)
        probs = jnp.exp(scores - highest[..., None]) / totals[..., None]
        back_probs = jnp.einsum(
            "qkgd,skd->kgqs", head_gradient_rows, value_block, preferred_element_type=jnp.float32
        )
        back_scores = (probs * (back_probs - correction[..., None])).astype(jnp.bfloat16)
        running = (
            running
            + jnp.einsum(
                "kgqs,skd->qkgd", back_scores, key_block, preferred_element_type=jnp.float32
            )
            * factor
        )
        key_grad = (
            jnp.einsum(
                "kgqs,qkgd->skd", back_scores, rotated_query, preferred_element_type=jnp.float32
            )
            * factor
        )
        value_grad = jnp.einsum(
            "kgqs,qkgd->skd",
            probs.astype(jnp.bfloat16),
            head_gradient_rows,
            preferred_element_type=jnp.float32,
        )
        return (running, (key_grad, value_grad))

    back_query, (gradient_of_keys, gradient_of_values) = lax.scan(
        score_grads,
        jnp.zeros((count_of_rows, KEY_VALUE_HEADS, query_group_width, HEAD_WIDTH), jnp.float32),
        (blocks_of_keys, blocks_of_values, place_blocks),
    )
    count_of_keys = gradient_of_keys.shape[0] * gradient_of_keys.shape[1]
    local_keys, value_own = (
        lax.psum_scatter(
            gradient_of_keys.reshape(count_of_keys, KEY_VALUE_HEADS * HEAD_WIDTH).astype(
                jnp.bfloat16
            ),
            "seq",
            scatter_dimension=0,
            tiled=True,
        ).astype(jnp.float32),
        lax.psum_scatter(
            gradient_of_values.reshape(count_of_keys, KEY_VALUE_HEADS * HEAD_WIDTH).astype(
                jnp.bfloat16
            ),
            "seq",
            scatter_dimension=0,
            tiled=True,
        ).astype(jnp.float32),
    )
    query_low = (
        apply_rotation(
            back_query.reshape(count_of_rows, QUERY_HEADS, HEAD_WIDTH), cosine_table, -sine_values
        )
        .astype(jnp.bfloat16)
        .reshape(count_of_rows, QUERY_HEADS * HEAD_WIDTH)
    )
    key_low = (
        apply_rotation(
            local_keys.reshape(count_of_rows, KEY_VALUE_HEADS, HEAD_WIDTH),
            cosine_table,
            -sine_values,
        )
        .astype(jnp.bfloat16)
        .reshape(count_of_rows, KEY_VALUE_HEADS * HEAD_WIDTH)
    )
    value_low = value_own.astype(jnp.bfloat16)
    grad_query = inner_rows(normed, query_low)
    grad_key = inner_rows(normed, key_low)
    grad_value = inner_rows(normed, value_low)
    back_norm_one = (
        inner_cols(query_low, w_q) + inner_cols(key_low, w_k) + inner_cols(value_low, w_v)
    )
    gain_one = jnp.sum(back_norm_one * unit_one, axis=0)
    back_unit_one = back_norm_one * gain_pair[0]
    input_back = back_middle + scale_one * (
        back_unit_one - unit_one * jnp.mean(back_unit_one * unit_one, axis=-1, keepdims=True)
    )
    weight_terms = (grad_query, grad_key, grad_value, grad_out, grad_gate, grad_up, grad_down)
    return (input_back.astype(jnp.bfloat16), weight_terms, (gain_one, gain_two))


def on_device(
    hidden_in,
    span_order,
    attention_norm_gain,
    query_weight,
    key_weight,
    value_weight,
    output_weight,
    feedforward_gain,
    gate_weight,
    up_weight,
    down_weight,
    out_grad,
):
    count_of_rows = SLOTS * SPAN
    gain_pair = (attention_norm_gain.astype(jnp.float32), feedforward_gain.astype(jnp.float32))
    offsets = jnp.arange(SPAN, dtype=jnp.int32)
    weight_totals = (
        jnp.zeros((MODEL_WIDTH, QUERY_HEADS * HEAD_WIDTH), jnp.float32),
        jnp.zeros((MODEL_WIDTH, KEY_VALUE_HEADS * HEAD_WIDTH), jnp.float32),
        jnp.zeros((MODEL_WIDTH, KEY_VALUE_HEADS * HEAD_WIDTH), jnp.float32),
        jnp.zeros((QUERY_HEADS * HEAD_WIDTH, MODEL_WIDTH), jnp.float32),
        jnp.zeros((MODEL_WIDTH, HIDDEN_UNITS), jnp.float32),
        jnp.zeros((MODEL_WIDTH, HIDDEN_UNITS), jnp.float32),
        jnp.zeros((HIDDEN_UNITS, MODEL_WIDTH), jnp.float32),
    )
    gain_totals = (jnp.zeros((MODEL_WIDTH,), jnp.float32), jnp.zeros((MODEL_WIDTH,), jnp.float32))
    outputs = []
    input_grads = []
    for micro_index in range(MB):
        layer_input = hidden_in[micro_index * count_of_rows : (micro_index + 1) * count_of_rows]
        cotangent = out_grad[micro_index * count_of_rows : (micro_index + 1) * count_of_rows]
        span_ids = span_order[micro_index * SLOTS : (micro_index + 1) * SLOTS]
        positions = (span_ids[:, None] * SPAN + offsets[None, :]).reshape(count_of_rows)
        forward_weights = shape_weights(
            (
                lax.all_gather(query_weight, ("dp", "seq"), axis=0, tiled=True),
                lax.all_gather(key_weight, ("dp", "seq"), axis=0, tiled=True),
                lax.all_gather(value_weight, ("dp", "seq"), axis=0, tiled=True),
                lax.all_gather(output_weight, ("dp", "seq"), axis=0, tiled=True),
                lax.all_gather(gate_weight, ("dp", "seq"), axis=0, tiled=True),
                lax.all_gather(up_weight, ("dp", "seq"), axis=0, tiled=True),
                lax.all_gather(down_weight, ("dp", "seq"), axis=0, tiled=True),
            )
        )
        result, stored = forward(layer_input, positions, span_ids, gain_pair, forward_weights)
        backward_weights = shape_weights(
            (
                lax.all_gather(query_weight, ("dp", "seq"), axis=0, tiled=True),
                lax.all_gather(key_weight, ("dp", "seq"), axis=0, tiled=True),
                lax.all_gather(value_weight, ("dp", "seq"), axis=0, tiled=True),
                lax.all_gather(output_weight, ("dp", "seq"), axis=0, tiled=True),
                lax.all_gather(gate_weight, ("dp", "seq"), axis=0, tiled=True),
                lax.all_gather(up_weight, ("dp", "seq"), axis=0, tiled=True),
                lax.all_gather(down_weight, ("dp", "seq"), axis=0, tiled=True),
            )
        )
        input_back, weight_terms, gain_terms = backward(
            cotangent, positions, gain_pair, backward_weights, stored
        )
        weight_totals = tuple(
            (running + term for running, term in zip(weight_totals, weight_terms))
        )
        gain_totals = tuple((running + term for running, term in zip(gain_totals, gain_terms)))
        outputs.append(result)
        input_grads.append(input_back)
    grad_query, grad_key, grad_value, grad_out, grad_gate, grad_up, grad_down = weight_totals
    owned = (
        lax.psum_scatter(grad_query.reshape(-1), ("dp", "seq"), scatter_dimension=0, tiled=True),
        lax.psum_scatter(grad_key.reshape(-1), ("dp", "seq"), scatter_dimension=0, tiled=True),
        lax.psum_scatter(grad_value.reshape(-1), ("dp", "seq"), scatter_dimension=0, tiled=True),
        lax.psum_scatter(grad_out.reshape(-1), ("dp", "seq"), scatter_dimension=0, tiled=True),
        lax.psum_scatter(grad_gate.reshape(-1), ("dp", "seq"), scatter_dimension=0, tiled=True),
        lax.psum_scatter(grad_up.reshape(-1), ("dp", "seq"), scatter_dimension=0, tiled=True),
        lax.psum_scatter(grad_down.reshape(-1), ("dp", "seq"), scatter_dimension=0, tiled=True),
    )
    gain_one, gain_two = lax.psum((gain_totals[0], gain_totals[1]), ("dp", "seq"))
    return (
        jnp.concatenate(outputs, axis=0),
        jnp.concatenate(input_grads, axis=0),
        gain_one,
        owned[0],
        owned[1],
        owned[2],
        owned[3],
        gain_two,
        owned[4],
        owned[5],
        owned[6],
    )


FACTOR = 1.0 / math.sqrt(HEAD_WIDTH)
KV_WIDTH = KEY_VALUE_HEADS * HEAD_WIDTH
Q_WIDTH = QUERY_HEADS * HEAD_WIDTH
QK_WIDTH = Q_WIDTH + KV_WIDTH
LANES = 128
HALF_FFN = HIDDEN_UNITS // 2
FFN_BLOCK = 768
DOWN_PITCH = 640
DOWN_AT = HALF_FFN
DOWN_EARLY = 2
FFN_CUT = DOWN_AT + DOWN_EARLY * DOWN_PITCH
UP_AT = (3 - DOWN_EARLY) * DOWN_PITCH
SECOND_GATE_AT = 3 * DOWN_PITCH
SECOND_WIDTH = SECOND_GATE_AT + 2 * HALF_FFN
SECOND_CUT = SECOND_WIDTH // 3


def vmem_params(megabytes=48):
    return pltpu.CompilerParams(vmem_limit_bytes=megabytes * 1024 * 1024)


def dot_nn(a, b):
    return jnp.dot(a, b, preferred_element_type=jnp.float32)


def dot_tn(a, b):
    return lax.dot_general(a, b, (((0,), (0,)), ((), ())), preferred_element_type=jnp.float32)


def dot_nt(a, b):
    return lax.dot_general(a, b, (((1,), (1,)), ((), ())), preferred_element_type=jnp.float32)


def low(v):
    return v.astype(jnp.bfloat16)


def wide(v):
    return v.astype(jnp.float32)


def place_back(v, place):
    high = low(v)
    rest = low(v - high.astype(jnp.float32))
    return dot_nt(high, place) + dot_nt(rest, place)


def half_turn(u, lane):
    return jnp.where(
        lane % HEAD_WIDTH < HEAD_WIDTH // 2,
        pltpu.roll(u, LANES - HEAD_WIDTH // 2, 1),
        pltpu.roll(u, HEAD_WIDTH // 2, 1),
    )


def padded_heads(blocks, head, lane):
    here = blocks[head // 2]
    moved = pltpu.roll(here, HEAD_WIDTH, 1)
    low_half, high_half = (here, moved) if head % 2 == 0 else (moved, here)
    zero = jnp.zeros_like(here)
    return (
        low(jnp.where(lane < HEAD_WIDTH, low_half, zero)),
        low(jnp.where(lane >= HEAD_WIDTH, high_half, zero)),
    )


def pack_kernel(
    span_order, hidden_in, out_grad, slots, offsets,
    x_mine, x_near, x_far, o_mine, o_near, o_far, place, *, n_seq,
):
    seq = lax.axis_index("seq")
    me = lax.axis_index("dp") * n_seq + seq
    tall = SPAN + 16
    for flip, x, o, at in ((0, x_mine, o_mine, 0), (1, x_near, o_near, 0), (3, x_near, o_near, 1), (2, x_far, o_far, 0)):
        origin = seq ^ flip
        block = pl.ds(pl.multiple_of(origin * SPAN, SPAN), SPAN)
        x[at * tall : at * tall + SPAN] = hidden_in[block, :]
        number = jnp.full((16, MODEL_WIDTH), span_order[origin], jnp.int32)
        x[at * tall + SPAN : (at + 1) * tall] = low(number.astype(jnp.float32))
        o[at * SPAN : (at + 1) * SPAN] = out_grad[block, :]
    natural = (slots[...] ^ me) * (MODEL_WIDTH // (n_seq * lax.axis_size("dp"))) + offsets[...]
    row = lax.broadcasted_iota(jnp.int32, place.shape, 0)
    place[...] = low((row == natural).astype(jnp.float32))


def unpack_kernel(mine, near, far, out):
    seq = lax.axis_index("seq")
    for flip, source, at in ((0, mine, 0), (1, near, 0), (2, far, 0), (3, far, 1)):
        target = pl.ds(pl.multiple_of((seq ^ flip) * SPAN, SPAN), SPAN)
        out[target, :] = source[at * SPAN : (at + 1) * SPAN]


def project_kernel(
    x_mine, x_near, x_far, gain_one, place, cosine, sine, wab, wab2,
    spans, x_out, normed_out, qk_out, kpad_out, vpad_out, wqk, wov,
):
    rows = x_out.shape[0]
    half = wab.shape[0]
    tall = SPAN + 16
    for k, (block, at) in enumerate(((x_mine, 0), (x_near, 0), (x_far, 0), (x_far, tall))):
        number = jnp.max(block[at + SPAN : at + tall, :LANES].astype(jnp.float32))
        number = number.astype(jnp.int32)
        spans[k] = number
        x_out[pl.ds(pl.multiple_of(number * SPAN, SPAN), SPAN), :] = block[at : at + SPAN]
    wa, wb = wab.at[:, :QK_WIDTH], wab.at[:, QK_WIDTH:]
    wa2, wb2 = wab2.at[:, :QK_WIDTH], wab2.at[:, QK_WIDTH:]
    wqk[:half] = wa[...]
    wqk[half:] = wa2[...]
    wov[:half] = wb[...]
    wov[half:] = wb2[...]
    x = x_out[...].astype(jnp.float32)
    scale = lax.rsqrt(jnp.mean(x * x, axis=-1, keepdims=True) + EPSILON)
    normed = low(x * scale * gain_one[...])
    normed_out[...] = low(dot_nn(normed, place[...]))
    lane = lax.broadcasted_iota(jnp.int32, (rows, LANES), 1)
    cos, sin = cosine[...], sine[...]
    k_blocks = []
    for b in range(QK_WIDTH // LANES):
        u = dot_nn(normed_out[...], wqk[:, b * LANES : (b + 1) * LANES])
        turned = u * cos + half_turn(u, lane) * sin
        turned = low(turned).astype(jnp.float32)
        if (b + 1) * LANES > Q_WIDTH:
            k_blocks.append(turned)
        if (b + 1) * LANES <= Q_WIDTH:
            turned = turned * FACTOR
        elif b * LANES < Q_WIDTH:
            turned = jnp.where(lane < Q_WIDTH - b * LANES, turned * FACTOR, turned)
        qk_out[:, b * LANES : (b + 1) * LANES] = low(turned)
    first_group = QUERY_HEADS - 2 * (Q_WIDTH // LANES)
    for j in range(KEY_VALUE_HEADS):
        lo, hi = padded_heads(k_blocks, j + first_group, lane)
        kpad_out[2 * j] = lo
        kpad_out[2 * j + 1] = hi
    v = dot_nn(normed_out[...], wov[:, MODEL_WIDTH:])
    v = low(v).astype(jnp.float32)
    v = jnp.concatenate([v, jnp.zeros((rows, HEAD_WIDTH), jnp.float32)], axis=1)
    v_blocks = [v[:, :LANES], v[:, LANES:]]
    for j in range(KEY_VALUE_HEADS):
        lo, hi = padded_heads(v_blocks, j, lane)
        vpad_out[2 * j] = lo
        vpad_out[2 * j + 1] = hi


def head_slot(head):
    group = head // (QUERY_HEADS // KEY_VALUE_HEADS) if isinstance(head, int) else (head * 11) >> 5
    return 2 * group + head % 2


def head_blocks(body):
    @pl.loop(0, QUERY_HEADS // 2)
    def _(b):
        body(2 * b, pl.ds(pl.multiple_of(b * LANES, LANES), LANES), 2)

    if QUERY_HEADS % 2:
        last = QUERY_HEADS // 2
        body(2 * last, slice(last * LANES, (last + 1) * LANES), 1)


def attend_spans(count, qk, kpad, vpad, lse_out, attn_out):
    lane = lax.broadcasted_iota(jnp.int32, (SPAN, LANES), 1)
    diagonal = lax.broadcasted_iota(jnp.int32, (SPAN, SPAN), 0) >= lax.broadcasted_iota(
        jnp.int32, (SPAN, SPAN), 1
    )
    lse_out[...] = jnp.zeros_like(lse_out)

    def block(first_head, columns, heads):
        for i in range(count):
            here = slice(i * SPAN, (i + 1) * SPAN)
            q = qk[here, columns]
            lse = lse_out[here, :]
            mixed = None
            for side in range(heads):
                h = first_head + side
                slot = head_slot(h)
                s = dot_nt(q, kpad[slot, : (i + 1) * SPAN, :])
                s_last = jnp.where(diagonal, s[:, i * SPAN :], -1e30)
                s = s_last if i == 0 else jnp.concatenate([s[:, : i * SPAN], s_last], axis=1)
                top = jnp.max(s, axis=-1, keepdims=True)
                p = jnp.exp(s - top)
                total = jnp.sum(p, axis=-1, keepdims=True)
                p = low(p * (1.0 / total))
                lse = jnp.where(lane == h, top + jnp.log(total), lse)
                part = dot_nn(p, vpad[slot, : (i + 1) * SPAN, :])
                mixed = part if mixed is None else mixed + part
            attn_out[here, columns] = mixed
            lse_out[here, :] = lse

    head_blocks(block)


def attend_kernel(
    x_in, qk, kpad, vpad, gain_two, place, wab, wab2,
    lse_out, attn_out, merged_out, middle_out, normed_two_out,
):
    rows = x_in.shape[0]
    half = wab.shape[0]
    wb, wb2 = wab.at[:, QK_WIDTH:], wab2.at[:, QK_WIDTH:]
    attend_spans(rows // SPAN, qk, kpad, vpad, lse_out, attn_out)
    merged = low(dot_nn(low(attn_out[:, :Q_WIDTH]), place[...]))
    merged_out[...] = merged
    middle = (
        x_in[...].astype(jnp.float32)
        + dot_nn(merged[:, :half], wb[:, :MODEL_WIDTH])
        + dot_nn(merged[:, half:], wb2[:, :MODEL_WIDTH])
    )
    middle_out[...] = middle
    scale_two = lax.rsqrt(jnp.mean(middle * middle, axis=-1, keepdims=True) + EPSILON)
    normed_two_out[...] = low(dot_nn(low(middle * scale_two * gain_two[...]), place[...]))


def ffn_block(n2, og, wg, wu, wd, at, result, back_norm, d_keep, d_send, dd_out):
    columns = pl.ds(pl.multiple_of(at * FFN_BLOCK, FFN_BLOCK), FFN_BLOCK)
    up_columns = pl.ds(pl.multiple_of(HALF_FFN + at * FFN_BLOCK, FFN_BLOCK), FFN_BLOCK)
    half = d_keep.shape[0]
    w_gate, w_up, w_down = wg[:, columns], wu[:, columns], wd[columns, :]
    gate = dot_nn(n2, w_gate)
    up = dot_nn(n2, w_up)
    back_hidden = dot_nt(og, w_down)
    sigmoid = jax.nn.sigmoid(gate)
    silu = gate * sigmoid
    hidden = low(silu * up)
    back_gate = low(back_hidden * up * sigmoid * (1.0 + gate * (1.0 - sigmoid)))
    back_up = low(back_hidden * silu)
    dd_out[columns, :] = low(dot_tn(hidden, og))
    dg = low(dot_tn(n2, back_gate))
    du = low(dot_tn(n2, back_up))
    d_keep[:, columns] = dg[:half]
    d_send[:, columns] = dg[half:]
    d_keep[:, up_columns] = du[:half]
    d_send[:, up_columns] = du[half:]
    result[...] += dot_nn(hidden, w_down)
    back_norm[...] += dot_nt(back_gate, w_gate) + dot_nt(back_up, w_up)


def fill_gate(target, a0, a1, a2, a3):
    size = a0.shape[0] // 2
    for core, (first, second) in enumerate(((a0, a1), (a2, a3))):
        for at, source in enumerate((first, second, first, second)):
            start = (4 * core + at) * size
            piece = slice(at // 2 * size, (at // 2 + 1) * size)
            target[start : start + size] = source[piece, :HALF_FFN]


def fill_up(target, column, b0, b1, b2, b3):
    for at, source in enumerate((b0, b1, b2, b3)):
        size = source.shape[0]
        target[at * size : (at + 1) * size] = source[:, column : column + HALF_FFN]


def ffn_first_kernel(
    spans, o_mine, o_near, o_far, n2, a0, a1, a2, a3, b0, b1, b2, b3,
    og_out, result_out, back_out, d_keep, d_send, dd, wd_out,
    wg, wu, *, order, n_seq,
):
    me = lax.axis_index("dp") * n_seq + lax.axis_index("seq")
    for k, (block, at) in enumerate(((o_mine, 0), (o_near, 0), (o_far, 0), (o_far, SPAN))):
        target = pl.ds(pl.multiple_of(spans[k] * SPAN, SPAN), SPAN)
        og_out[target, :] = block[at : at + SPAN]
    size = a0.shape[0] // 2
    fill_gate(wg, a0, a1, a2, a3)
    fill_up(wu, UP_AT, b0, b1, b2, b3)
    count = len(order)
    rows, pitch = wd_out.shape[0] // count, MODEL_WIDTH // count
    each = size // pitch
    for slot, relative in enumerate(order):
        core, block, at = slot // (4 * each), slot // each % 4, slot % each
        x_side, y_side = block % 2, block // 2
        for t in range(rows // 16):
            if t < DOWN_EARLY:
                source = ((a0, a1), (a2, a3))[core][x_side]
                start = y_side * size + at * pitch
                first = DOWN_AT + t * DOWN_PITCH
            else:
                source = ((b0, b1), (b2, b3))[core][y_side]
                start = x_side * size + at * pitch
                first = (t - DOWN_EARLY) * DOWN_PITCH
            target = pl.multiple_of((me ^ relative) * rows + 16 * t, 16)
            wd_out[pl.ds(target, 16), :] = source[start : start + 16, first : first + MODEL_WIDTH]
    result_out[...] = jnp.zeros_like(result_out)
    back_out[...] = jnp.zeros_like(back_out)

    @pl.loop(0, HALF_FFN // FFN_BLOCK)
    def _(at):
        ffn_block(
            n2[...], og_out[...], wg, wu, wd_out, at, result_out, back_out, d_keep, d_send, dd
        )


def ffn_second_kernel(
    spans, og, n2, a0, a1, a2, a3, b0, b1, b2, b3,
    wd_in, result_in, back_in, dd_in, middle, gain_two, place,
    mine, near, far, back_middle_out, gain_out, keep_out, send_out,
    wg, wu, wd, dd, spread, result, back, *, order, n_seq,
):
    half = keep_out.shape[0]
    fill_gate(wg, a0, a1, a2, a3)
    fill_up(wu, 0, b0, b1, b2, b3)
    me = lax.axis_index("dp") * n_seq + lax.axis_index("seq")
    d_keep = keep_out.at[:, SECOND_GATE_AT : SECOND_GATE_AT + 2 * HALF_FFN]
    d_send = send_out.at[:, SECOND_GATE_AT : SECOND_GATE_AT + 2 * HALF_FFN]
    wd[...] = wd_in[HALF_FFN:, :]
    dd[:HALF_FFN] = dd_in[...]
    result[...] = result_in[...] + middle[...]
    back[...] = back_in[...]

    @pl.loop(0, HALF_FFN // FFN_BLOCK)
    def _(at):
        ffn_block(
            n2[...], og[...], wg, wu, wd, at, result, back, d_keep, d_send, dd.at[HALF_FFN:, :]
        )

    count = len(order)
    rows, pitch = HIDDEN_UNITS // count, MODEL_WIDTH // count
    spread[...] = jnp.zeros_like(spread)
    for t in range(rows // 16):
        for slot, relative in enumerate(order):
            source = pl.ds(pl.multiple_of((me ^ relative) * rows + 16 * t, 16), 16)
            spread[slot * pitch : slot * pitch + 16, :MODEL_WIDTH] = wide(dd[source, :])
        columns = slice(t * DOWN_PITCH, (t + 1) * DOWN_PITCH)
        keep_out[:, columns] = low(spread[:half])
        send_out[:, columns] = low(spread[half:])

    for k, (block, at) in enumerate(((mine, 0), (near, 0), (far, 0), (near, SPAN))):
        source = pl.ds(pl.multiple_of(spans[k] * SPAN, SPAN), SPAN)
        block[at : at + SPAN] = low(result[source, :])
    mid = middle[...]
    scale = lax.rsqrt(jnp.mean(mid * mid, axis=-1, keepdims=True) + EPSILON)
    unit = mid * scale
    back_norm = place_back(back[...], place[...])
    gain_out[...] = jnp.sum(back_norm * unit, axis=0, keepdims=True)
    back_unit = back_norm * gain_two[...]
    back_middle_out[...] = og[...].astype(jnp.float32) + scale * (
        back_unit - unit * jnp.mean(back_unit * unit, axis=-1, keepdims=True)
    )


def score_back(i, qk, kpad, vpad, ab, lse_rows, correction, dqk, dv):
    rows = qk.shape[0]
    groups = QUERY_HEADS // KEY_VALUE_HEADS
    diagonal = lax.broadcasted_iota(jnp.int32, (SPAN, SPAN), 1) >= lax.broadcasted_iota(
        jnp.int32, (SPAN, SPAN), 0
    )
    lane = lax.broadcasted_iota(jnp.int32, (SPAN, LANES), 1)
    keys = slice(i * SPAN, (i + 1) * SPAN)
    first = i * SPAN
    dk_sums = [None] * (2 * KEY_VALUE_HEADS)
    dv_sums = [None] * (2 * KEY_VALUE_HEADS)
    for b in range((QUERY_HEADS + 1) // 2):
        columns = slice(b * LANES, (b + 1) * LANES)
        q = qk[first:, columns]
        a = ab[first:, columns]
        dq = None
        for h in range(2 * b, min(2 * b + 2, QUERY_HEADS)):
            slot = 2 * (h // groups) + h % 2
            s = dot_nt(kpad[slot, keys, :], q)
            s = s - lse_rows[h : h + 1, first:]
            s_first = jnp.where(diagonal, s[:, :SPAN], -1e30)
            s = (
                s_first
                if first + SPAN == rows
                else jnp.concatenate([s_first, s[:, SPAN:]], axis=1)
            )
            p = jnp.exp(s)
            dp = dot_nt(vpad[slot, keys, :], a)
            ds = low(p * (dp - correction[h : h + 1, first:]))
            dk = dot_nn(ds, q)
            dvh = dot_nn(low(p), a)
            dk_sums[slot] = dk if dk_sums[slot] is None else dk_sums[slot] + dk
            dv_sums[slot] = dvh if dv_sums[slot] is None else dv_sums[slot] + dvh
            part = dot_tn(ds, kpad[slot, keys, :])
            dq = part if dq is None else dq + part
        if i == 0:
            dqk[first:, columns] = dq
        else:
            dqk[first:, columns] += dq

    def both(sums, j):
        return sums[2 * j] + pltpu.roll(sums[2 * j + 1], HEAD_WIDTH, 1)

    dk_heads = [both(dk_sums, j) for j in range(KEY_VALUE_HEADS)]
    dv_heads = [both(dv_sums, j) for j in range(KEY_VALUE_HEADS)]
    key_scale = 1.0 / FACTOR
    q_tail = dqk[keys, 4 * LANES : 5 * LANES]
    dqk[keys, 4 * LANES : 5 * LANES] = jnp.where(
        lane < HEAD_WIDTH, q_tail, pltpu.roll(dk_heads[0], HEAD_WIDTH, 1) * key_scale
    )
    dqk[keys, 5 * LANES :] = (
        jnp.where(lane < HEAD_WIDTH, dk_heads[1], pltpu.roll(dk_heads[2], HEAD_WIDTH, 1))
        * key_scale
    )
    dv[keys, :LANES] = low(
        jnp.where(lane < HEAD_WIDTH, dv_heads[0], pltpu.roll(dv_heads[1], HEAD_WIDTH, 1))
    )
    dv[keys, LANES:] = low(dv_heads[2])


def attend_back_first_kernel(
    qk, kpad, vpad, lse, attn, merged, back_middle, place, wab, wab2,
    keep_out, send_out, ab, lse_rows, correction, dqk, dv,
):
    rows = qk.shape[0]
    half = wab.shape[0]
    wb, wb2 = wab.at[:, QK_WIDTH:], wab2.at[:, QK_WIDTH:]
    middle_low = low(back_middle[...])
    d_out = low(dot_tn(merged[...], middle_low))
    out_columns = slice(QK_WIDTH, QK_WIDTH + MODEL_WIDTH)
    keep_out[:half, out_columns] = d_out[:half]
    send_out[:half, out_columns] = d_out[half:]
    ab_first = low(dot_nt(middle_low, wb[:, :MODEL_WIDTH]))
    ab_second = low(dot_nt(middle_low, wb2[:, :MODEL_WIDTH]))
    ab[:, :Q_WIDTH] = low(
        dot_nt(ab_first, place[:, :half]) + dot_nt(ab_second, place[:, half:])
    )
    ab[:, Q_WIDTH:] = jnp.zeros((rows, ab.shape[1] - Q_WIDTH), jnp.bfloat16)
    terms = ab[...].astype(jnp.float32) * attn[...]
    mask = low(
        (
            lax.broadcasted_iota(jnp.int32, (16, terms.shape[1]), 1) // HEAD_WIDTH
            == lax.broadcasted_iota(jnp.int32, (16, terms.shape[1]), 0)
        ).astype(jnp.float32)
    )
    high = low(terms)
    correction[...] = dot_nt(mask, high) + dot_nt(mask, low(terms - high.astype(jnp.float32)))
    lse_rows[...] = jnp.transpose(lse[...])
    score_back(0, qk, kpad, vpad, ab, lse_rows, correction, dqk, dv)


def attend_back_second_kernel(
    dqk_in, dv_in, qk, kpad, vpad, lse_rows, correction, ab, dqk, dv,
):
    for i in range(1, qk.shape[0] // SPAN):
        score_back(i, qk, kpad, vpad, ab, lse_rows, correction, dqk, dv)


def project_back_kernel(
    keep_in, send_in, gain_two_in, spans, x, normed, dqk, dv, back_middle, gain_one,
    place, cosine, sine, wab, wab2,
    mine, near, far, d1, d2,
    grad, grad_full,
):
    rows = x.shape[0]
    half = wab.shape[0]
    lane = lax.broadcasted_iota(jnp.int32, (rows, LANES), 1)
    cos, sin = cosine[...], sine[...]
    for b in range(QK_WIDTH // LANES):
        u = dqk[:, b * LANES : (b + 1) * LANES] * FACTOR
        grad[:, b * LANES : (b + 1) * LANES] = low(u * cos - half_turn(u, lane) * sin)
    d_qk = low(dot_tn(normed[...], grad[...]))
    d1[:half, :QK_WIDTH] = d_qk[:half]
    d2[:half, :QK_WIDTH] = d_qk[half:]
    dv_low = dv[:, :KV_WIDTH]
    d_v = low(dot_tn(normed[...], dv_low))
    d1[:half, QK_WIDTH + MODEL_WIDTH :] = d_v[:half]
    d2[:half, QK_WIDTH + MODEL_WIDTH :] = d_v[half:]
    parts = [
        dot_nt(grad[...], w[:, :QK_WIDTH]) + dot_nt(dv_low, w[:, QK_WIDTH + MODEL_WIDTH :])
        for w in (wab, wab2)
    ]
    back_norm = place_back(jnp.concatenate(parts, axis=1), place[...])
    xf = x[...].astype(jnp.float32)
    scale = lax.rsqrt(jnp.mean(xf * xf, axis=-1, keepdims=True) + EPSILON)
    unit = xf * scale
    gain_row = lax.broadcasted_iota(jnp.int32, (16, MODEL_WIDTH), 0)
    gains = jnp.where(
        gain_row == 0, jnp.sum(back_norm * unit, axis=0, keepdims=True), gain_two_in[...]
    )
    for d in (d1, d2):
        d[half:, :MODEL_WIDTH] = low(gains)
        d[half:, MODEL_WIDTH:] = jnp.zeros((16, d.shape[1] - MODEL_WIDTH), jnp.bfloat16)
    back_unit = back_norm * gain_one[...]
    grad_full[...] = back_middle[...] + scale * (
        back_unit - unit * jnp.mean(back_unit * unit, axis=-1, keepdims=True)
    )
    for k, (block, at) in enumerate(((mine, 0), (near, 0), (far, 0), (near, SPAN))):
        source = pl.ds(pl.multiple_of(spans[k] * SPAN, SPAN), SPAN)
        block[at : at + SPAN] = low(grad_full[source, :])


VMEM_SPEC = pl.BlockSpec(memory_space=pltpu.VMEM)
SMEM_SPEC = pl.BlockSpec(memory_space=pltpu.SMEM)
ANY_SPEC = pl.BlockSpec(memory_space=pl.ANY)


def shaped(rows, columns, kind):
    return jax.ShapeDtypeStruct((rows, columns), kind)


def call(body, outs, args, scratch, micros, scalars=(), after=(), alias=None, megabytes=16, out_specs=None):
    def run(*refs):
        body(*refs[: len(args)], *refs[len(args) + len(after) :])

    return pl.pallas_call(
        run,
        out_shape=outs,
        in_specs=[SMEM_SPEC if at in scalars else VMEM_SPEC for at in range(len(args))]
        + [ANY_SPEC] * len(after),
        out_specs=out_specs or [VMEM_SPEC] * len(outs),
        scratch_shapes=scratch,
        input_output_aliases=alias or {},
        compiler_params=vmem_params(megabytes),
        cost_estimate=pl.CostEstimate(
            flops=int(micros * 1.1e9), bytes_accessed=1_000_000, transcendentals=0
        ),
    )(*args, *after)


def whole_sequence_plan(mesh):
    axes = ("dp", "seq")
    n_dp, n_seq = mesh.shape["dp"], mesh.shape["seq"]
    count = n_dp * n_seq
    bits = count.bit_length() - 1
    seq_bits = n_seq.bit_length() - 1
    core, y_bit = 0, 1
    x_bit = seq_bits
    z_bits = tuple(range(seq_bits + 1, bits))[::-1]
    order_bits = z_bits + (x_bit, y_bit, core)

    def hold(v, *others):
        return lax.optimization_barrier((v, *others))[0] if others else v

    def together(*arrays):
        return lax.optimization_barrier(arrays)

    def swap(v, flip, until=()):
        return hold(lax.ppermute(v, axes, [(d, d ^ flip) for d in range(count)]), *until)

    def relative(slot):
        return sum(1 << bit for at, bit in enumerate(order_bits) if slot >> at & 1)

    order = tuple(relative(slot) for slot in range(count))
    z_count = 1 << len(z_bits)
    z_flips = [relative(slot) for slot in range(1, z_count)]
    flip_x, flip_y, flip_core = 1 << x_bit, 1 << y_bit, 1 << core

    def gather_z(v, until=()):
        return jnp.concatenate([v] + [swap(v, flip, until) for flip in z_flips], axis=0)

    def gather_z_stepwise(v, untils):
        for bit, until in zip(z_bits, untils):
            v = jnp.concatenate([v, swap(v, 1 << bit, until)], axis=0)
        return v

    def gather_one(v, x_first, until=()):
        return jnp.concatenate([v, swap(v, flip_x if x_first else flip_y, until)], axis=0)

    def gather_two(v, x_first, until=()):
        w = swap(v, flip_y if x_first else flip_x, until)
        size = v.shape[0] // 2
        if x_first:
            return jnp.concatenate([v, w], axis=0)
        return jnp.concatenate([v[:size], w[:size], v[size:], w[size:]], axis=0)

    def scatter_core(keep, send, until=()):
        return wide(keep) + wide(swap(send, flip_core, until))

    def scatter_one(total, x_first, until=()):
        size = total.shape[0] // 4
        if x_first:
            mine = jnp.concatenate([total[:size], total[2 * size : 3 * size]], axis=0)
            theirs = jnp.concatenate([total[size : 2 * size], total[3 * size :]], axis=0)
            return mine + wide(swap(low(theirs), flip_x, until))
        return total[: 2 * size] + wide(swap(low(total[2 * size :]), flip_y, until))

    def scatter_two(total, x_first, until=()):
        size = total.shape[0] // 2
        sent = swap(low(total[size:]), flip_y if x_first else flip_x, until)
        return total[:size] + wide(sent)

    def scatter_bit(total, bit):
        size = total.shape[0] // 2
        return total[:size] + wide(swap(low(total[size:]), 1 << bit))

    def scatter_z_with_sums(total, sums):
        size = total.shape[0] // z_count
        sums = lax.reduce_precision(sums.reshape(size, -1), 8, 7)
        width, wanted = total.shape[1], sums.shape[1]
        beside = jnp.pad(low(sums), ((0, 0), (0, -wanted % LANES)))
        out, terms = total[:size], [sums]
        for at, flip in enumerate(z_flips):
            theirs = low(total[(at + 1) * size : (at + 2) * size])
            sent = swap(jnp.concatenate([theirs, beside], axis=1), flip)
            out = out + wide(sent[:, :width])
            terms.append(wide(sent[:, width : width + wanted]))
        while len(terms) > 1:
            terms = [a + b for a, b in zip(terms[::2], terms[1::2])]
        return out, terms[0].reshape(-1)

    def exchange(parts, near_until=(), far_until=(), far_after=()):
        mine, near, far = parts
        size = mine.shape[0]
        near = swap(near, flip_core, near_until)
        far = hold(jnp.concatenate([far, near[size:]], axis=0), *far_after)
        return mine, near[:size], swap(far, flip_y, far_until)

    def scatter_with_sums(mine, theirs, sums, flip, until=()):
        sums = lax.reduce_precision(sums, 8, 7)
        sent = swap(jnp.concatenate([low(theirs), low(sums)], axis=0), flip, until)
        return mine + wide(sent[: mine.shape[0]]), sums + wide(sent[mine.shape[0] :])

    def on_sequence_device(
        hidden_in, span_order, attention_norm_gain, query_weight, key_weight, value_weight,
        output_weight, feedforward_gain, gate_weight, up_weight, down_weight, out_grad,
    ):
        rows = hidden_in.shape[0]
        model_rows = MODEL_WIDTH // count
        hidden_rows = HIDDEN_UNITS // count
        bf, f4 = jnp.bfloat16, jnp.float32
        half = MODEL_WIDTH // 2
        gain_one = attention_norm_gain.astype(jnp.float32).reshape(1, MODEL_WIDTH)
        gain_two = feedforward_gain.astype(jnp.float32).reshape(1, MODEL_WIDTH)
        model_low, model_full = shaped(rows, MODEL_WIDTH, bf), shaped(rows, MODEL_WIDTH, f4)

        def rows_of(w, columns):
            return w.reshape(model_rows, columns)

        def unpack(parts):
            return call(unpack_kernel, [model_low], parts, [], 1, megabytes=4)[0]

        slots = np.repeat(np.asarray(order, np.int32), model_rows)[None, :]
        offsets = np.tile(np.arange(model_rows, dtype=np.int32), count)[None, :]
        packed = call(
            functools.partial(pack_kernel, n_seq=n_seq),
            [
                *[shaped(n * (SPAN + 16), MODEL_WIDTH, bf) for n in (1, 2, 1)],
                *[shaped(n * SPAN, MODEL_WIDTH, bf) for n in (1, 2, 1)],
                shaped(MODEL_WIDTH, MODEL_WIDTH, bf),
            ],
            [span_order, hidden_in, out_grad, slots, offsets],
            [],
            2,
            scalars=(0,),
        )
        place = packed[6]
        first = jnp.concatenate(
            [
                rows_of(query_weight, Q_WIDTH),
                rows_of(key_weight, KV_WIDTH),
                rows_of(output_weight, MODEL_WIDTH),
                rows_of(value_weight, KV_WIDTH),
            ],
            axis=1,
        )

        down = down_weight.reshape(3, 16, MODEL_WIDTH).swapaxes(0, 1)
        down = jnp.pad(down, ((0, model_rows - 16), (0, 0), (0, DOWN_PITCH - MODEL_WIDTH)))
        gate, up = rows_of(gate_weight, HIDDEN_UNITS), rows_of(up_weight, HIDDEN_UNITS)
        ffn = jnp.concatenate(
            [gate[:, :HALF_FFN], down.reshape(model_rows, 3 * DOWN_PITCH), up[:, :HALF_FFN]], axis=1
        )
        later = jnp.concatenate([gate[:, HALF_FFN:], up[:, HALF_FFN:]], axis=1)
        first = gather_z(hold(first, place), until=(ffn,))
        first_a, first_b = first[:, :QK_WIDTH], first[:, QK_WIDTH:]
        first_a, first_b = gather_one(first_a, False), gather_one(first_b, True)
        x_parts = exchange(packed[:3], (first,), (first_a, first_b))
        one = (first_a, first_b)
        first_a, first_b = gather_two(first_a, False), gather_two(first_b, True)
        first = jnp.concatenate([first_a, first_b], axis=1)
        ffn = gather_z_stepwise(ffn, (one, (first,)))
        o_mine, o_near, o_far = hold(tuple(packed[3:6]), *one)
        o_near = swap(o_near, flip_core, (first,))
        o_far = jnp.concatenate([o_far, o_near[SPAN:]], axis=0)
        first_other = swap(first, flip_core)
        ffn_a, ffn_b = ffn[:, :FFN_CUT], ffn[:, FFN_CUT:]

        frequency = np.exp(np.arange(HEAD_WIDTH // 2) * (-2.0 * math.log(10000.0) / HEAD_WIDTH))
        angles = np.arange(rows)[:, None] * frequency[None, :]
        cosine = np.tile(np.cos(angles), (1, 4)).astype(np.float32)
        sine = np.sin(angles)
        sine = np.concatenate([-sine, sine, -sine, sine], axis=1).astype(np.float32)

        padded = jax.ShapeDtypeStruct((2 * KEY_VALUE_HEADS, rows, LANES), bf)
        spans, x, normed, qk, kpad, vpad = call(
            project_kernel,
            [
                jax.ShapeDtypeStruct((n_seq,), jnp.int32),
                model_low,
                model_low,
                shaped(rows, QK_WIDTH, bf),
                padded,
                padded,
            ],
            [*x_parts, gain_one, place, cosine, sine, first, first_other],
            [pltpu.VMEM((MODEL_WIDTH, QK_WIDTH), bf)] * 2,
            5,
            out_specs=[SMEM_SPEC] + [VMEM_SPEC] * 5,
        )
        stats = [shaped(rows, LANES, f4), shaped(rows, 5 * LANES, f4)]
        ffn_a, ffn_b = gather_one(ffn_a, False, (x,)), gather_one(ffn_b, True, (x,))
        later = gather_z_stepwise(hold(later, ffn), ((first,), (x,)))
        lse, attn, merged, middle, normed_two = call(
            attend_kernel,
            [*stats, model_low, model_full, model_low],
            [x, qk, kpad, vpad, gain_two, place, first, first_other],
            [],
            10,
        )
        o_far, second_a, second_b, later_y, later_x, middle = together(
            swap(o_far, flip_y),
            swap(ffn_a, flip_x),
            swap(ffn_b, flip_y),
            swap(later[:, :HALF_FFN], flip_y),
            swap(later[:, HALF_FFN:], flip_x),
            middle,
        )
        o_parts = (o_mine, o_near[:SPAN], o_far)
        ffn = []
        for part, second in ((ffn_a, second_a), (ffn_b, second_b)):
            ffn += [part, second, swap(part, flip_core), swap(second, flip_core)]
        later_a = jnp.concatenate([later[:, :HALF_FFN], later_y], axis=0)
        later_b = jnp.concatenate([later[:, HALF_FFN:], later_x], axis=0)
        weight_scratch = [pltpu.VMEM((MODEL_WIDTH, HALF_FFN), bf)] * 2
        og, result, back, r1, r1_send, dd, w_down = call(
            functools.partial(ffn_first_kernel, order=order, n_seq=n_seq),
            [
                model_low,
                model_full,
                model_full,
                *[shaped(half, 2 * HALF_FFN, bf)] * 2,
                shaped(HALF_FFN, MODEL_WIDTH, bf),
                shaped(HIDDEN_UNITS, MODEL_WIDTH, bf),
            ],
            [spans, *o_parts, normed_two, *ffn],
            weight_scratch,
            10,
            scalars=(0,),
        )
        r1_own = r1
        later = []
        for part, flip in ((later_a, flip_x), (later_b, flip_y)):
            second = swap(part, flip, (og,))
            later += [part, second, swap(part, flip_core, (og,)), swap(second, flip_core)]
        *h_parts, back_middle, gain_two_grad, r2, r2_send = call(
            functools.partial(ffn_second_kernel, order=order, n_seq=n_seq),
            [
                *[shaped(n * SPAN, MODEL_WIDTH, bf) for n in (1, 2, 1)],
                model_full,
                shaped(1, MODEL_WIDTH, f4),
                *[shaped(half, SECOND_WIDTH, bf)] * 2,
            ],
            [spans, og, normed_two, *later, w_down, result, back, dd, middle, gain_two, place],
            weight_scratch
            + [
                pltpu.VMEM((HALF_FFN, MODEL_WIDTH), bf),
                pltpu.VMEM((HIDDEN_UNITS, MODEL_WIDTH), bf),
                pltpu.VMEM((MODEL_WIDTH, DOWN_PITCH), f4),
                pltpu.VMEM((rows, MODEL_WIDTH), f4),
                pltpu.VMEM((rows, MODEL_WIDTH), f4),
            ],
            13,
            scalars=(0,),
            megabytes=18,
        )
        r1 = scatter_core(r1_own, r1_send, (back_middle,))
        r3, r3_send, ab, lse_rows, correction, dqk, dv = call(
            attend_back_first_kernel,
            [
                *[shaped(half + 16, 2 * HALF_FFN, bf)] * 2,
                shaped(rows, 5 * LANES, bf),
                shaped(LANES, rows, f4),
                shaped(16, rows, f4),
                shaped(rows, QK_WIDTH, f4),
                shaped(rows, 2 * LANES, bf),
            ],
            [qk, kpad, vpad, lse, attn, merged, back_middle, place, first, first_other],
            [],
            7,
            after=[r1],
        )
        r2 = scatter_core(r2, r2_send, (ab,))
        h_near = swap(h_parts[1], flip_core, (ab,))
        dqk, dv = call(
            attend_back_second_kernel,
            [shaped(rows, QK_WIDTH, f4), shaped(rows, 2 * LANES, bf)],
            [dqk, dv, qk, kpad, vpad, lse_rows, correction, ab],
            [],
            6,
            after=[r2],
            alias={0: 0, 1: 1},
        )
        p1 = scatter_one(r2[:, :SECOND_CUT], True, (dqk,))
        p2 = scatter_one(r2[:, SECOND_CUT : 2 * SECOND_CUT], False, (dqk,))
        *g_parts, r3, r3_send = call(
            project_back_kernel,
            [
                *[shaped(n * SPAN, MODEL_WIDTH, bf) for n in (1, 2, 1)],
                *[shaped(half + 16, 2 * HALF_FFN, bf)] * 2,
            ],
            [
                r3, r3_send, gain_two_grad, spans, x, normed, dqk, dv, back_middle,
                gain_one, place, cosine, sine, first, first_other,
            ],
            [pltpu.VMEM((rows, QK_WIDTH), bf), pltpu.VMEM((rows, MODEL_WIDTH), f4)],
            5,
            scalars=(3,),
            after=[p1, p2],
            alias={0: 3, 1: 4},
        )
        p1, p2 = scatter_two(p1, True, (r3,)), scatter_two(p2, False, (r3,))
        p3 = scatter_one(r2[:, 2 * SECOND_CUT :], True, (r3,))
        r1 = scatter_one(r1, False, (r3,))
        sent = wide(swap(r3_send, flip_core))
        r3 = wide(r3)
        r1, p3 = scatter_two(r1, False), scatter_two(p3, True)
        total, sums, r1, p1, p2, p3 = together(
            r3[:half] + sent[:half], r3[half:] + sent[half:], r1, p1, p2, p3
        )
        size = half // 4
        r3_a, r3_b = total[:, :QK_WIDTH], total[:, QK_WIDTH:]
        r3_a, sums = scatter_with_sums(
            jnp.concatenate([r3_a[:size], r3_a[2 * size : 3 * size]], axis=0),
            jnp.concatenate([r3_a[size : 2 * size], r3_a[3 * size :]], axis=0),
            sums[:, :QK_WIDTH],
            flip_x,
        )
        r3_b = scatter_one(r3_b, False)
        early = jnp.concatenate([p1, p2, r1], axis=1)
        early = scatter_bit(early, z_bits[-1])
        g_near = swap(g_parts[1], flip_core)
        r3_a, r3_b, sums, early, g_near, h_near = together(
            r3_a, r3_b, sums, early, g_near, h_near
        )
        r3_a, sums = scatter_with_sums(r3_a[:size], r3_a[size:], sums, flip_y)
        r3_b = scatter_two(r3_b, False)
        for bit in z_bits[-2::-1]:
            early = scatter_bit(early, bit)
        h_far = swap(jnp.concatenate([h_parts[2], h_near[SPAN:]], axis=0), flip_y)
        r3_a, r3_b, sums, early, h_far, g_near = together(
            r3_a, r3_b, sums, early, h_far, g_near
        )
        g_far = swap(jnp.concatenate([g_parts[2], g_near[SPAN:]], axis=0), flip_y)
        late = jnp.concatenate([r3_a, r3_b, p3], axis=1)
        late, sums = scatter_z_with_sums(late, sums[:2, :MODEL_WIDTH])
        hidden_out = unpack([h_parts[0], h_near[:SPAN], h_far])
        r1 = early[:, 2 * SECOND_CUT :]
        r2 = jnp.concatenate([early[:, : 2 * SECOND_CUT], late[:, 2 * HALF_FFN :]], axis=1)
        r3 = late
        hidden_grad = unpack([g_parts[0], g_near[:SPAN], g_far])
        gu1 = r2[:, SECOND_GATE_AT:]
        gate_grad = jnp.concatenate([r1[:, :HALF_FFN], gu1[:, :HALF_FFN]], axis=1)
        up_grad = jnp.concatenate([r1[:, HALF_FFN:], gu1[:, HALF_FFN : 2 * HALF_FFN]], axis=1)
        down_grad = r2[:16, :SECOND_GATE_AT].reshape(16, 3, DOWN_PITCH)[:, :, :MODEL_WIDTH]
        return (
            hidden_out,
            hidden_grad,
            sums[:MODEL_WIDTH],
            r3[:, :Q_WIDTH].reshape(-1),
            r3[:, Q_WIDTH:QK_WIDTH].reshape(-1),
            r3[:, QK_WIDTH + MODEL_WIDTH : 2 * HALF_FFN].reshape(-1),
            r3[:, QK_WIDTH : QK_WIDTH + MODEL_WIDTH].reshape(-1),
            sums[MODEL_WIDTH:],
            gate_grad.reshape(-1),
            up_grad.reshape(-1),
            down_grad.swapaxes(0, 1).reshape(-1),
        )

    return on_sequence_device


def pick_plan(mesh):
    count = mesh.shape["dp"] * mesh.shape["seq"]
    fits = (
        mesh.shape["seq"] == MB * SLOTS
        and SLOTS == 1
        and count & (count - 1) == 0
        and MODEL_WIDTH % count == 0
        and (HIDDEN_UNITS // count) % 16 == 0
    )
    return whole_sequence_plan(mesh) if fits else on_device


def solution(mesh):
    return jax.shard_map(
        pick_plan(mesh),
        mesh=mesh,
        in_specs=(
            P(("dp", "seq"), None),
            P(("dp", "seq")),
            P(),
            P(("dp", "seq")),
            P(("dp", "seq")),
            P(("dp", "seq")),
            P(("dp", "seq")),
            P(),
            P(("dp", "seq")),
            P(("dp", "seq")),
            P(("dp", "seq")),
            P(("dp", "seq"), None),
        ),
        out_specs=(
            P(("dp", "seq"), None),
            P(("dp", "seq"), None),
            P(),
            P(("dp", "seq")),
            P(("dp", "seq")),
            P(("dp", "seq")),
            P(("dp", "seq")),
            P(),
            P(("dp", "seq")),
            P(("dp", "seq")),
            P(("dp", "seq")),
        ),
        check_vma=False,
    )
```

```python
import functools
import math

import jax
import jax.numpy as jnp
import numpy as np
from jax import lax
from jax.experimental import pallas as pl
from jax.experimental.pallas import tpu as pltpu
from jax.sharding import PartitionSpec as P

MODEL_WIDTH = 576
QUERY_HEADS = 9
KEY_VALUE_HEADS = 3
HEAD_WIDTH = 64
HIDDEN_UNITS = 1536
SPAN = 128
MB = 4
SLOTS = 1


EPSILON = 1e-05


def angle_tables(positions, head_size):
    frequency = jnp.exp(
        jnp.arange(head_size // 2, dtype=jnp.float32) * (-2.0 * math.log(10000.0) / head_size)
    )
    angles = positions.astype(jnp.float32)[:, None] * frequency[None, :]
    angles = jnp.concatenate([angles, angles], axis=-1)[:, None, :]
    return (jnp.cos(angles), jnp.sin(angles))


def apply_rotation(value_rows, cosine_table, sine_values):
    half_size = value_rows.shape[-1] // 2
    turned = jnp.concatenate([-value_rows[..., half_size:], value_rows[..., :half_size]], axis=-1)
    return value_rows * cosine_table + turned * sine_values


def product(first_arg, second_arg):
    return jnp.dot(first_arg, second_arg, preferred_element_type=jnp.float32)


def inner_rows(first_arg, second_arg):
    return lax.dot_general(
        first_arg, second_arg, (((0,), (0,)), ((), ())), preferred_element_type=jnp.float32
    )


def inner_cols(first_arg, second_arg):
    return lax.dot_general(
        first_arg, second_arg, (((1,), (1,)), ((), ())), preferred_element_type=jnp.float32
    )


def shape_weights(flattened_rows):
    return (
        flattened_rows[0].reshape(MODEL_WIDTH, QUERY_HEADS * HEAD_WIDTH),
        flattened_rows[1].reshape(MODEL_WIDTH, KEY_VALUE_HEADS * HEAD_WIDTH),
        flattened_rows[2].reshape(MODEL_WIDTH, KEY_VALUE_HEADS * HEAD_WIDTH),
        flattened_rows[3].reshape(QUERY_HEADS * HEAD_WIDTH, MODEL_WIDTH),
        flattened_rows[4].reshape(MODEL_WIDTH, HIDDEN_UNITS),
        flattened_rows[5].reshape(MODEL_WIDTH, HIDDEN_UNITS),
        flattened_rows[6].reshape(HIDDEN_UNITS, MODEL_WIDTH),
    )


def block_scores(query_rows, key_block, query_place, key_place, factor):
    raw_scores = (
        jnp.einsum("qkgd,skd->kgqs", query_rows, key_block, preferred_element_type=jnp.float32)
        * factor
    )
    allowed = query_place[:, None] >= key_place[None, :]
    return jnp.where(allowed, raw_scores, -1e30)


def forward(layer_input, positions, span_ids, gain_pair, matrices):
    w_q, w_k, w_v, w_o, w_g, w_u, w_d = matrices
    count_of_rows = layer_input.shape[0]
    query_group_width = QUERY_HEADS // KEY_VALUE_HEADS
    factor = 1.0 / math.sqrt(HEAD_WIDTH)
    input_full = layer_input.astype(jnp.float32)
    scale_one = lax.rsqrt(jnp.mean(input_full * input_full, axis=-1, keepdims=True) + EPSILON)
    unit_one = input_full * scale_one
    normed = (unit_one * gain_pair[0]).astype(jnp.bfloat16)
    query_rows = product(normed, w_q)
    unrotated_keys = product(normed, w_k)
    value_rows = product(normed, w_v)
    cosine_table, sine_values = angle_tables(positions, HEAD_WIDTH)
    rotated_query = apply_rotation(
        query_rows.reshape(count_of_rows, QUERY_HEADS, HEAD_WIDTH), cosine_table, sine_values
    ).astype(jnp.bfloat16)
    rotated_query = rotated_query.reshape(
        count_of_rows, KEY_VALUE_HEADS, query_group_width, HEAD_WIDTH
    )
    rotated_key = apply_rotation(
        unrotated_keys.reshape(count_of_rows, KEY_VALUE_HEADS, HEAD_WIDTH),
        cosine_table,
        sine_values,
    ).astype(jnp.bfloat16)
    rotated_key = rotated_key.reshape(count_of_rows, KEY_VALUE_HEADS * HEAD_WIDTH)
    v_low = value_rows.astype(jnp.bfloat16)
    every_key, every_value, key_spans = (
        lax.all_gather(rotated_key, "seq", axis=0, tiled=True),
        lax.all_gather(v_low, "seq", axis=0, tiled=True),
        lax.all_gather(span_ids.astype(jnp.bfloat16), "seq", axis=0, tiled=True),
    )
    offsets = jnp.arange(SPAN, dtype=jnp.int32)
    key_places = (key_spans.astype(jnp.int32)[:, None] * SPAN + offsets[None, :]).reshape(-1)
    count_of_keys = every_key.shape[0]
    block_length = math.gcd(count_of_keys, 512)
    count_of_blocks = count_of_keys // block_length
    blocks_of_keys = every_key.reshape(count_of_blocks, block_length, KEY_VALUE_HEADS, HEAD_WIDTH)
    blocks_of_values = every_value.reshape(
        count_of_blocks, block_length, KEY_VALUE_HEADS, HEAD_WIDTH
    )
    place_blocks = key_places.reshape(count_of_blocks, block_length)

    def softmax_stats(carry, piece_set):
        highest, totals = carry
        key_block, key_place = piece_set
        scores = block_scores(rotated_query, key_block, positions, key_place, factor)
        new_high = jnp.maximum(highest, jnp.max(scores, axis=-1))
        totals = totals * jnp.exp(highest - new_high) + jnp.sum(
            jnp.exp(scores - new_high[..., None]), axis=-1
        )
        return ((new_high, totals), None)

    initial = (
        jnp.full((KEY_VALUE_HEADS, query_group_width, count_of_rows), -1e30, jnp.float32),
        jnp.zeros((KEY_VALUE_HEADS, query_group_width, count_of_rows), jnp.float32),
    )
    (highest, totals), _ = lax.scan(softmax_stats, initial, (blocks_of_keys, place_blocks))

    def mix_values(running, piece_set):
        key_block, value_block, key_place = piece_set
        scores = block_scores(rotated_query, key_block, positions, key_place, factor)
        layer_weights = (jnp.exp(scores - highest[..., None]) / totals[..., None]).astype(
            jnp.bfloat16
        )
        return (
            running
            + jnp.einsum(
                "kgqs,skd->qkgd", layer_weights, value_block, preferred_element_type=jnp.float32
            ),
            None,
        )

    attention_output, _ = lax.scan(
        mix_values,
        jnp.zeros((count_of_rows, KEY_VALUE_HEADS, query_group_width, HEAD_WIDTH), jnp.float32),
        (blocks_of_keys, blocks_of_values, place_blocks),
    )
    attention_output = attention_output.reshape(count_of_rows, QUERY_HEADS * HEAD_WIDTH)
    merged = attention_output.astype(jnp.bfloat16)
    middle = input_full + product(merged, w_o)
    scale_two = lax.rsqrt(jnp.mean(middle * middle, axis=-1, keepdims=True) + EPSILON)
    unit_two = middle * scale_two
    normed_two = (unit_two * gain_pair[1]).astype(jnp.bfloat16)
    gate_act = product(normed_two, w_g)
    upward = product(normed_two, w_u)
    hidden = (jax.nn.silu(gate_act) * upward).astype(jnp.bfloat16)
    result = (middle + product(hidden, w_d)).astype(jnp.bfloat16)
    stored = (
        scale_one,
        unit_one,
        normed,
        cosine_table,
        sine_values,
        rotated_query,
        blocks_of_keys,
        blocks_of_values,
        place_blocks,
        highest,
        totals,
        attention_output,
        merged,
        scale_two,
        unit_two,
        normed_two,
        gate_act,
        upward,
        hidden,
    )
    return (result, stored)


def backward(cotangent, positions, gain_pair, matrices, stored):
    w_q, w_k, w_v, w_o, w_g, w_u, w_d = matrices
    (
        scale_one,
        unit_one,
        normed,
        cosine_table,
        sine_values,
        rotated_query,
        blocks_of_keys,
        blocks_of_values,
        place_blocks,
        highest,
        totals,
        attention_output,
        merged,
        scale_two,
        unit_two,
        normed_two,
        gate_act,
        upward,
        hidden,
    ) = stored
    count_of_rows = cotangent.shape[0]
    query_group_width = QUERY_HEADS // KEY_VALUE_HEADS
    factor = 1.0 / math.sqrt(HEAD_WIDTH)
    grad_down = inner_rows(hidden, cotangent)
    back_hidden = inner_cols(cotangent, w_d)
    sigmoid_gate = jax.nn.sigmoid(gate_act)
    back_gate = (
        back_hidden * upward * sigmoid_gate * (1.0 + gate_act * (1.0 - sigmoid_gate))
    ).astype(jnp.bfloat16)
    back_up = (back_hidden * (gate_act * sigmoid_gate)).astype(jnp.bfloat16)
    grad_gate = inner_rows(normed_two, back_gate)
    grad_up = inner_rows(normed_two, back_up)
    back_norm_two = inner_cols(back_gate, w_g) + inner_cols(back_up, w_u)
    gain_two = jnp.sum(back_norm_two * unit_two, axis=0)
    back_unit = back_norm_two * gain_pair[1]
    back_middle = cotangent.astype(jnp.float32) + scale_two * (
        back_unit - unit_two * jnp.mean(back_unit * unit_two, axis=-1, keepdims=True)
    )
    middle_low = back_middle.astype(jnp.bfloat16)
    grad_out = inner_rows(merged, middle_low)
    attention_backward = inner_cols(middle_low, w_o).astype(jnp.bfloat16)
    head_gradient_rows = attention_backward.reshape(
        count_of_rows, KEY_VALUE_HEADS, query_group_width, HEAD_WIDTH
    )
    attention_head_rows = attention_output.reshape(
        count_of_rows, KEY_VALUE_HEADS, query_group_width, HEAD_WIDTH
    )
    correction = jnp.transpose(
        jnp.sum(head_gradient_rows.astype(jnp.float32) * attention_head_rows, axis=-1), (1, 2, 0)
    )

    def score_grads(running, piece_set):
        key_block, value_block, key_place = piece_set
        scores = block_scores(rotated_query, key_block, positions, key_place, factor)
        probs = jnp.exp(scores - highest[..., None]) / totals[..., None]
        back_probs = jnp.einsum(
            "qkgd,skd->kgqs", head_gradient_rows, value_block, preferred_element_type=jnp.float32
        )
        back_scores = (probs * (back_probs - correction[..., None])).astype(jnp.bfloat16)
        running = (
            running
            + jnp.einsum(
                "kgqs,skd->qkgd", back_scores, key_block, preferred_element_type=jnp.float32
            )
            * factor
        )
        key_grad = (
            jnp.einsum(
                "kgqs,qkgd->skd", back_scores, rotated_query, preferred_element_type=jnp.float32
            )
            * factor
        )
        value_grad = jnp.einsum(
            "kgqs,qkgd->skd",
            probs.astype(jnp.bfloat16),
            head_gradient_rows,
            preferred_element_type=jnp.float32,
        )
        return (running, (key_grad, value_grad))

    back_query, (gradient_of_keys, gradient_of_values) = lax.scan(
        score_grads,
        jnp.zeros((count_of_rows, KEY_VALUE_HEADS, query_group_width, HEAD_WIDTH), jnp.float32),
        (blocks_of_keys, blocks_of_values, place_blocks),
    )
    count_of_keys = gradient_of_keys.shape[0] * gradient_of_keys.shape[1]
    local_keys, value_own = (
        lax.psum_scatter(
            gradient_of_keys.reshape(count_of_keys, KEY_VALUE_HEADS * HEAD_WIDTH).astype(
                jnp.bfloat16
            ),
            "seq",
            scatter_dimension=0,
            tiled=True,
        ).astype(jnp.float32),
        lax.psum_scatter(
            gradient_of_values.reshape(count_of_keys, KEY_VALUE_HEADS * HEAD_WIDTH).astype(
                jnp.bfloat16
            ),
            "seq",
            scatter_dimension=0,
            tiled=True,
        ).astype(jnp.float32),
    )
    query_low = (
        apply_rotation(
            back_query.reshape(count_of_rows, QUERY_HEADS, HEAD_WIDTH), cosine_table, -sine_values
        )
        .astype(jnp.bfloat16)
        .reshape(count_of_rows, QUERY_HEADS * HEAD_WIDTH)
    )
    key_low = (
        apply_rotation(
            local_keys.reshape(count_of_rows, KEY_VALUE_HEADS, HEAD_WIDTH),
            cosine_table,
            -sine_values,
        )
        .astype(jnp.bfloat16)
        .reshape(count_of_rows, KEY_VALUE_HEADS * HEAD_WIDTH)
    )
    value_low = value_own.astype(jnp.bfloat16)
    grad_query = inner_rows(normed, query_low)
    grad_key = inner_rows(normed, key_low)
    grad_value = inner_rows(normed, value_low)
    back_norm_one = (
        inner_cols(query_low, w_q) + inner_cols(key_low, w_k) + inner_cols(value_low, w_v)
    )
    gain_one = jnp.sum(back_norm_one * unit_one, axis=0)
    back_unit_one = back_norm_one * gain_pair[0]
    input_back = back_middle + scale_one * (
        back_unit_one - unit_one * jnp.mean(back_unit_one * unit_one, axis=-1, keepdims=True)
    )
    weight_terms = (grad_query, grad_key, grad_value, grad_out, grad_gate, grad_up, grad_down)
    return (input_back.astype(jnp.bfloat16), weight_terms, (gain_one, gain_two))


def on_device(
    hidden_in,
    span_order,
    attention_norm_gain,
    query_weight,
    key_weight,
    value_weight,
    output_weight,
    feedforward_gain,
    gate_weight,
    up_weight,
    down_weight,
    out_grad,
):
    count_of_rows = SLOTS * SPAN
    gain_pair = (attention_norm_gain.astype(jnp.float32), feedforward_gain.astype(jnp.float32))
    offsets = jnp.arange(SPAN, dtype=jnp.int32)
    weight_totals = (
        jnp.zeros((MODEL_WIDTH, QUERY_HEADS * HEAD_WIDTH), jnp.float32),
        jnp.zeros((MODEL_WIDTH, KEY_VALUE_HEADS * HEAD_WIDTH), jnp.float32),
        jnp.zeros((MODEL_WIDTH, KEY_VALUE_HEADS * HEAD_WIDTH), jnp.float32),
        jnp.zeros((QUERY_HEADS * HEAD_WIDTH, MODEL_WIDTH), jnp.float32),
        jnp.zeros((MODEL_WIDTH, HIDDEN_UNITS), jnp.float32),
        jnp.zeros((MODEL_WIDTH, HIDDEN_UNITS), jnp.float32),
        jnp.zeros((HIDDEN_UNITS, MODEL_WIDTH), jnp.float32),
    )
    gain_totals = (jnp.zeros((MODEL_WIDTH,), jnp.float32), jnp.zeros((MODEL_WIDTH,), jnp.float32))
    outputs = []
    input_grads = []
    for micro_index in range(MB):
        layer_input = hidden_in[micro_index * count_of_rows : (micro_index + 1) * count_of_rows]
        cotangent = out_grad[micro_index * count_of_rows : (micro_index + 1) * count_of_rows]
        span_ids = span_order[micro_index * SLOTS : (micro_index + 1) * SLOTS]
        positions = (span_ids[:, None] * SPAN + offsets[None, :]).reshape(count_of_rows)
        forward_weights = shape_weights(
            (
                lax.all_gather(query_weight, ("dp", "seq"), axis=0, tiled=True),
                lax.all_gather(key_weight, ("dp", "seq"), axis=0, tiled=True),
                lax.all_gather(value_weight, ("dp", "seq"), axis=0, tiled=True),
                lax.all_gather(output_weight, ("dp", "seq"), axis=0, tiled=True),
                lax.all_gather(gate_weight, ("dp", "seq"), axis=0, tiled=True),
                lax.all_gather(up_weight, ("dp", "seq"), axis=0, tiled=True),
                lax.all_gather(down_weight, ("dp", "seq"), axis=0, tiled=True),
            )
        )
        result, stored = forward(layer_input, positions, span_ids, gain_pair, forward_weights)
        backward_weights = shape_weights(
            (
                lax.all_gather(query_weight, ("dp", "seq"), axis=0, tiled=True),
                lax.all_gather(key_weight, ("dp", "seq"), axis=0, tiled=True),
                lax.all_gather(value_weight, ("dp", "seq"), axis=0, tiled=True),
                lax.all_gather(output_weight, ("dp", "seq"), axis=0, tiled=True),
                lax.all_gather(gate_weight, ("dp", "seq"), axis=0, tiled=True),
                lax.all_gather(up_weight, ("dp", "seq"), axis=0, tiled=True),
                lax.all_gather(down_weight, ("dp", "seq"), axis=0, tiled=True),
            )
        )
        input_back, weight_terms, gain_terms = backward(
            cotangent, positions, gain_pair, backward_weights, stored
        )
        weight_totals = tuple(
            (running + term for running, term in zip(weight_totals, weight_terms))
        )
        gain_totals = tuple((running + term for running, term in zip(gain_totals, gain_terms)))
        outputs.append(result)
        input_grads.append(input_back)
    grad_query, grad_key, grad_value, grad_out, grad_gate, grad_up, grad_down = weight_totals
    owned = (
        lax.psum_scatter(grad_query.reshape(-1), ("dp", "seq"), scatter_dimension=0, tiled=True),
        lax.psum_scatter(grad_key.reshape(-1), ("dp", "seq"), scatter_dimension=0, tiled=True),
        lax.psum_scatter(grad_value.reshape(-1), ("dp", "seq"), scatter_dimension=0, tiled=True),
        lax.psum_scatter(grad_out.reshape(-1), ("dp", "seq"), scatter_dimension=0, tiled=True),
        lax.psum_scatter(grad_gate.reshape(-1), ("dp", "seq"), scatter_dimension=0, tiled=True),
        lax.psum_scatter(grad_up.reshape(-1), ("dp", "seq"), scatter_dimension=0, tiled=True),
        lax.psum_scatter(grad_down.reshape(-1), ("dp", "seq"), scatter_dimension=0, tiled=True),
    )
    gain_one, gain_two = lax.psum((gain_totals[0], gain_totals[1]), ("dp", "seq"))
    return (
        jnp.concatenate(outputs, axis=0),
        jnp.concatenate(input_grads, axis=0),
        gain_one,
        owned[0],
        owned[1],
        owned[2],
        owned[3],
        gain_two,
        owned[4],
        owned[5],
        owned[6],
    )


FACTOR = 1.0 / math.sqrt(HEAD_WIDTH)
KV_WIDTH = KEY_VALUE_HEADS * HEAD_WIDTH
Q_WIDTH = QUERY_HEADS * HEAD_WIDTH
QK_WIDTH = Q_WIDTH + KV_WIDTH
LANES = 128
HALF_FFN = HIDDEN_UNITS // 2
FFN_BLOCK = 768
DOWN_PITCH = 640
DOWN_AT = HALF_FFN
DOWN_EARLY = 2
FFN_CUT = DOWN_AT + DOWN_EARLY * DOWN_PITCH
UP_AT = (3 - DOWN_EARLY) * DOWN_PITCH
SECOND_GATE_AT = 3 * DOWN_PITCH
SECOND_WIDTH = SECOND_GATE_AT + 2 * HALF_FFN
SECOND_CUT = SECOND_WIDTH // 3


def vmem_params(megabytes=48):
    return pltpu.CompilerParams(vmem_limit_bytes=megabytes * 1024 * 1024)


def dot_nn(a, b):
    return jnp.dot(a, b, preferred_element_type=jnp.float32)


def dot_tn(a, b):
    return lax.dot_general(a, b, (((0,), (0,)), ((), ())), preferred_element_type=jnp.float32)


def dot_nt(a, b):
    return lax.dot_general(a, b, (((1,), (1,)), ((), ())), preferred_element_type=jnp.float32)


def low(v):
    return v.astype(jnp.bfloat16)


def wide(v):
    return v.astype(jnp.float32)


def place_back(v, place):
    high = low(v)
    rest = low(v - high.astype(jnp.float32))
    return dot_nt(high, place) + dot_nt(rest, place)


def half_turn(u, lane):
    return jnp.where(
        lane % HEAD_WIDTH < HEAD_WIDTH // 2,
        pltpu.roll(u, LANES - HEAD_WIDTH // 2, 1),
        pltpu.roll(u, HEAD_WIDTH // 2, 1),
    )


def padded_heads(blocks, head, lane):
    here = blocks[head // 2]
    moved = pltpu.roll(here, HEAD_WIDTH, 1)
    low_half, high_half = (here, moved) if head % 2 == 0 else (moved, here)
    zero = jnp.zeros_like(here)
    return (
        low(jnp.where(lane < HEAD_WIDTH, low_half, zero)),
        low(jnp.where(lane >= HEAD_WIDTH, high_half, zero)),
    )


def pack_kernel(
    span_order, hidden_in, out_grad, slots, offsets,
    x_mine, x_near, x_far, o_mine, o_near, o_far, place, *, n_seq,
):
    seq = lax.axis_index("seq")
    me = lax.axis_index("dp") * n_seq + seq
    tall = SPAN + 16
    for flip, x, o, at in ((0, x_mine, o_mine, 0), (1, x_near, o_near, 0), (3, x_near, o_near, 1), (2, x_far, o_far, 0)):
        origin = seq ^ flip
        block = pl.ds(pl.multiple_of(origin * SPAN, SPAN), SPAN)
        x[at * tall : at * tall + SPAN] = hidden_in[block, :]
        number = jnp.full((16, MODEL_WIDTH), span_order[origin], jnp.int32)
        x[at * tall + SPAN : (at + 1) * tall] = low(number.astype(jnp.float32))
        o[at * SPAN : (at + 1) * SPAN] = out_grad[block, :]
    natural = (slots[...] ^ me) * (MODEL_WIDTH // (n_seq * lax.axis_size("dp"))) + offsets[...]
    row = lax.broadcasted_iota(jnp.int32, place.shape, 0)
    place[...] = low((row == natural).astype(jnp.float32))


def unpack_kernel(mine, near, far, out):
    seq = lax.axis_index("seq")
    for flip, source, at in ((0, mine, 0), (1, near, 0), (2, far, 0), (3, far, 1)):
        target = pl.ds(pl.multiple_of((seq ^ flip) * SPAN, SPAN), SPAN)
        out[target, :] = source[at * SPAN : (at + 1) * SPAN]


def project_kernel(
    x_mine, x_near, x_far, gain_one, place, cosine, sine, wab, wab2,
    spans, x_out, normed_out, qk_out, kpad_out, vpad_out, wqk, wov,
):
    rows = x_out.shape[0]
    half = wab.shape[0]
    tall = SPAN + 16
    for k, (block, at) in enumerate(((x_mine, 0), (x_near, 0), (x_far, 0), (x_far, tall))):
        number = jnp.max(block[at + SPAN : at + tall, :LANES].astype(jnp.float32))
        number = number.astype(jnp.int32)
        spans[k] = number
        x_out[pl.ds(pl.multiple_of(number * SPAN, SPAN), SPAN), :] = block[at : at + SPAN]
    wa, wb = wab.at[:, :QK_WIDTH], wab.at[:, QK_WIDTH:]
    wa2, wb2 = wab2.at[:, :QK_WIDTH], wab2.at[:, QK_WIDTH:]
    wqk[:half] = wa[...]
    wqk[half:] = wa2[...]
    wov[:half] = wb[...]
    wov[half:] = wb2[...]
    x = x_out[...].astype(jnp.float32)
    scale = lax.rsqrt(jnp.mean(x * x, axis=-1, keepdims=True) + EPSILON)
    normed = low(x * scale * gain_one[...])
    normed_out[...] = low(dot_nn(normed, place[...]))
    lane = lax.broadcasted_iota(jnp.int32, (rows, LANES), 1)
    cos, sin = cosine[...], sine[...]
    k_blocks = []
    for b in range(QK_WIDTH // LANES):
        u = dot_nn(normed_out[...], wqk[:, b * LANES : (b + 1) * LANES])
        turned = u * cos + half_turn(u, lane) * sin
        turned = low(turned).astype(jnp.float32)
        if (b + 1) * LANES > Q_WIDTH:
            k_blocks.append(turned)
        if (b + 1) * LANES <= Q_WIDTH:
            turned = turned * FACTOR
        elif b * LANES < Q_WIDTH:
            turned = jnp.where(lane < Q_WIDTH - b * LANES, turned * FACTOR, turned)
        qk_out[:, b * LANES : (b + 1) * LANES] = low(turned)
    first_group = QUERY_HEADS - 2 * (Q_WIDTH // LANES)
    for j in range(KEY_VALUE_HEADS):
        lo, hi = padded_heads(k_blocks, j + first_group, lane)
        kpad_out[2 * j] = lo
        kpad_out[2 * j + 1] = hi
    v = dot_nn(normed_out[...], wov[:, MODEL_WIDTH:])
    v = low(v).astype(jnp.float32)
    v = jnp.concatenate([v, jnp.zeros((rows, HEAD_WIDTH), jnp.float32)], axis=1)
    v_blocks = [v[:, :LANES], v[:, LANES:]]
    for j in range(KEY_VALUE_HEADS):
        lo, hi = padded_heads(v_blocks, j, lane)
        vpad_out[2 * j] = lo
        vpad_out[2 * j + 1] = hi


def head_slot(head):
    group = head // (QUERY_HEADS // KEY_VALUE_HEADS) if isinstance(head, int) else (head * 11) >> 5
    return 2 * group + head % 2


def head_blocks(body):
    @pl.loop(0, QUERY_HEADS // 2)
    def _(b):
        body(2 * b, pl.ds(pl.multiple_of(b * LANES, LANES), LANES), 2)

    if QUERY_HEADS % 2:
        last = QUERY_HEADS // 2
        body(2 * last, slice(last * LANES, (last + 1) * LANES), 1)


def attend_spans(count, qk, kpad, vpad, lse_out, attn_out):
    lane = lax.broadcasted_iota(jnp.int32, (SPAN, LANES), 1)
    diagonal = lax.broadcasted_iota(jnp.int32, (SPAN, SPAN), 0) >= lax.broadcasted_iota(
        jnp.int32, (SPAN, SPAN), 1
    )
    lse_out[...] = jnp.zeros_like(lse_out)

    def block(first_head, columns, heads):
        for i in range(count):
            here = slice(i * SPAN, (i + 1) * SPAN)
            q = qk[here, columns]
            lse = lse_out[here, :]
            mixed = None
            for side in range(heads):
                h = first_head + side
                slot = head_slot(h)
                s = dot_nt(q, kpad[slot, : (i + 1) * SPAN, :])
                s_last = jnp.where(diagonal, s[:, i * SPAN :], -1e30)
                s = s_last if i == 0 else jnp.concatenate([s[:, : i * SPAN], s_last], axis=1)
                top = jnp.max(s, axis=-1, keepdims=True)
                p = jnp.exp(s - top)
                total = jnp.sum(p, axis=-1, keepdims=True)
                p = low(p * (1.0 / total))
                lse = jnp.where(lane == h, top + jnp.log(total), lse)
                part = dot_nn(p, vpad[slot, : (i + 1) * SPAN, :])
                mixed = part if mixed is None else mixed + part
            attn_out[here, columns] = mixed
            lse_out[here, :] = lse

    head_blocks(block)


def attend_kernel(
    x_in, qk, kpad, vpad, gain_two, place, wab, wab2,
    lse_out, attn_out, merged_out, middle_out, normed_two_out,
):
    rows = x_in.shape[0]
    half = wab.shape[0]
    wb, wb2 = wab.at[:, QK_WIDTH:], wab2.at[:, QK_WIDTH:]
    attend_spans(rows // SPAN, qk, kpad, vpad, lse_out, attn_out)
    merged = low(dot_nn(low(attn_out[:, :Q_WIDTH]), place[...]))
    merged_out[...] = merged
    middle = (
        x_in[...].astype(jnp.float32)
        + dot_nn(merged[:, :half], wb[:, :MODEL_WIDTH])
        + dot_nn(merged[:, half:], wb2[:, :MODEL_WIDTH])
    )
    middle_out[...] = middle
    scale_two = lax.rsqrt(jnp.mean(middle * middle, axis=-1, keepdims=True) + EPSILON)
    normed_two_out[...] = low(dot_nn(low(middle * scale_two * gain_two[...]), place[...]))


def ffn_block(n2, og, wg, wu, wd, at, result, back_norm, d_keep, d_send, dd_out):
    columns = pl.ds(pl.multiple_of(at * FFN_BLOCK, FFN_BLOCK), FFN_BLOCK)
    up_columns = pl.ds(pl.multiple_of(HALF_FFN + at * FFN_BLOCK, FFN_BLOCK), FFN_BLOCK)
    half = d_keep.shape[0]
    w_gate, w_up, w_down = wg[:, columns], wu[:, columns], wd[columns, :]
    gate = dot_nn(n2, w_gate)
    up = dot_nn(n2, w_up)
    back_hidden = dot_nt(og, w_down)
    sigmoid = jax.nn.sigmoid(gate)
    silu = gate * sigmoid
    hidden = low(silu * up)
    back_gate = low(back_hidden * up * sigmoid * (1.0 + gate * (1.0 - sigmoid)))
    back_up = low(back_hidden * silu)
    dd_out[columns, :] = low(dot_tn(hidden, og))
    dg = low(dot_tn(n2, back_gate))
    du = low(dot_tn(n2, back_up))
    d_keep[:, columns] = dg[:half]
    d_send[:, columns] = dg[half:]
    d_keep[:, up_columns] = du[:half]
    d_send[:, up_columns] = du[half:]
    result[...] += dot_nn(hidden, w_down)
    back_norm[...] += dot_nt(back_gate, w_gate) + dot_nt(back_up, w_up)


def fill_gate(target, a0, a1, a2, a3):
    size = a0.shape[0] // 2
    for core, (first, second) in enumerate(((a0, a1), (a2, a3))):
        for at, source in enumerate((first, second, first, second)):
            start = (4 * core + at) * size
            piece = slice(at // 2 * size, (at // 2 + 1) * size)
            target[start : start + size] = source[piece, :HALF_FFN]


def fill_up(target, column, b0, b1, b2, b3):
    for at, source in enumerate((b0, b1, b2, b3)):
        size = source.shape[0]
        target[at * size : (at + 1) * size] = source[:, column : column + HALF_FFN]


def ffn_first_kernel(
    spans, o_mine, o_near, o_far, n2, a0, a1, a2, a3, b0, b1, b2, b3,
    og_out, result_out, back_out, d_keep, d_send, dd, wd_out,
    wg, wu, *, order, n_seq,
):
    me = lax.axis_index("dp") * n_seq + lax.axis_index("seq")
    for k, (block, at) in enumerate(((o_mine, 0), (o_near, 0), (o_far, 0), (o_far, SPAN))):
        target = pl.ds(pl.multiple_of(spans[k] * SPAN, SPAN), SPAN)
        og_out[target, :] = block[at : at + SPAN]
    size = a0.shape[0] // 2
    fill_gate(wg, a0, a1, a2, a3)
    fill_up(wu, UP_AT, b0, b1, b2, b3)
    count = len(order)
    rows, pitch = wd_out.shape[0] // count, MODEL_WIDTH // count
    each = size // pitch
    for slot, relative in enumerate(order):
        core, block, at = slot // (4 * each), slot // each % 4, slot % each
        x_side, y_side = block % 2, block // 2
        for t in range(rows // 16):
            if t < DOWN_EARLY:
                source = ((a0, a1), (a2, a3))[core][x_side]
                start = y_side * size + at * pitch
                first = DOWN_AT + t * DOWN_PITCH
            else:
                source = ((b0, b1), (b2, b3))[core][y_side]
                start = x_side * size + at * pitch
                first = (t - DOWN_EARLY) * DOWN_PITCH
            target = pl.multiple_of((me ^ relative) * rows + 16 * t, 16)
            wd_out[pl.ds(target, 16), :] = source[start : start + 16, first : first + MODEL_WIDTH]
    result_out[...] = jnp.zeros_like(result_out)
    back_out[...] = jnp.zeros_like(back_out)

    @pl.loop(0, HALF_FFN // FFN_BLOCK)
    def _(at):
        ffn_block(
            n2[...], og_out[...], wg, wu, wd_out, at, result_out, back_out, d_keep, d_send, dd
        )


def ffn_second_kernel(
    spans, og, n2, a0, a1, a2, a3, b0, b1, b2, b3,
    wd_in, result_in, back_in, dd_in, middle, gain_two, place,
    mine, near, far, back_middle_out, gain_out, keep_out, send_out,
    wg, wu, wd, dd, spread, result, back, *, order, n_seq,
):
    half = keep_out.shape[0]
    fill_gate(wg, a0, a1, a2, a3)
    fill_up(wu, 0, b0, b1, b2, b3)
    me = lax.axis_index("dp") * n_seq + lax.axis_index("seq")
    d_keep = keep_out.at[:, SECOND_GATE_AT : SECOND_GATE_AT + 2 * HALF_FFN]
    d_send = send_out.at[:, SECOND_GATE_AT : SECOND_GATE_AT + 2 * HALF_FFN]
    wd[...] = wd_in[HALF_FFN:, :]
    dd[:HALF_FFN] = dd_in[...]
    result[...] = result_in[...] + middle[...]
    back[...] = back_in[...]

    @pl.loop(0, HALF_FFN // FFN_BLOCK)
    def _(at):
        ffn_block(
            n2[...], og[...], wg, wu, wd, at, result, back, d_keep, d_send, dd.at[HALF_FFN:, :]
        )

    count = len(order)
    rows, pitch = HIDDEN_UNITS // count, MODEL_WIDTH // count
    spread[...] = jnp.zeros_like(spread)
    for t in range(rows // 16):
        for slot, relative in enumerate(order):
            source = pl.ds(pl.multiple_of((me ^ relative) * rows + 16 * t, 16), 16)
            spread[slot * pitch : slot * pitch + 16, :MODEL_WIDTH] = wide(dd[source, :])
        columns = slice(t * DOWN_PITCH, (t + 1) * DOWN_PITCH)
        keep_out[:, columns] = low(spread[:half])
        send_out[:, columns] = low(spread[half:])

    for k, (block, at) in enumerate(((mine, 0), (near, 0), (far, 0), (near, SPAN))):
        source = pl.ds(pl.multiple_of(spans[k] * SPAN, SPAN), SPAN)
        block[at : at + SPAN] = low(result[source, :])
    mid = middle[...]
    scale = lax.rsqrt(jnp.mean(mid * mid, axis=-1, keepdims=True) + EPSILON)
    unit = mid * scale
    back_norm = place_back(back[...], place[...])
    gain_out[...] = jnp.sum(back_norm * unit, axis=0, keepdims=True)
    back_unit = back_norm * gain_two[...]
    back_middle_out[...] = og[...].astype(jnp.float32) + scale * (
        back_unit - unit * jnp.mean(back_unit * unit, axis=-1, keepdims=True)
    )


def score_back(i, qk, kpad, vpad, ab, lse_rows, correction, dqk, dv):
    rows = qk.shape[0]
    groups = QUERY_HEADS // KEY_VALUE_HEADS
    diagonal = lax.broadcasted_iota(jnp.int32, (SPAN, SPAN), 1) >= lax.broadcasted_iota(
        jnp.int32, (SPAN, SPAN), 0
    )
    lane = lax.broadcasted_iota(jnp.int32, (SPAN, LANES), 1)
    keys = slice(i * SPAN, (i + 1) * SPAN)
    first = i * SPAN
    dk_sums = [None] * (2 * KEY_VALUE_HEADS)
    dv_sums = [None] * (2 * KEY_VALUE_HEADS)
    for b in range((QUERY_HEADS + 1) // 2):
        columns = slice(b * LANES, (b + 1) * LANES)
        q = qk[first:, columns]
        a = ab[first:, columns]
        dq = None
        for h in range(2 * b, min(2 * b + 2, QUERY_HEADS)):
            slot = 2 * (h // groups) + h % 2
            s = dot_nt(kpad[slot, keys, :], q)
            s = s - lse_rows[h : h + 1, first:]
            s_first = jnp.where(diagonal, s[:, :SPAN], -1e30)
            s = (
                s_first
                if first + SPAN == rows
                else jnp.concatenate([s_first, s[:, SPAN:]], axis=1)
            )
            p = jnp.exp(s)
            dp = dot_nt(vpad[slot, keys, :], a)
            ds = low(p * (dp - correction[h : h + 1, first:]))
            dk = dot_nn(ds, q)
            dvh = dot_nn(low(p), a)
            dk_sums[slot] = dk if dk_sums[slot] is None else dk_sums[slot] + dk
            dv_sums[slot] = dvh if dv_sums[slot] is None else dv_sums[slot] + dvh
            part = dot_tn(ds, kpad[slot, keys, :])
            dq = part if dq is None else dq + part
        if i == 0:
            dqk[first:, columns] = dq
        else:
            dqk[first:, columns] += dq

    def both(sums, j):
        return sums[2 * j] + pltpu.roll(sums[2 * j + 1], HEAD_WIDTH, 1)

    dk_heads = [both(dk_sums, j) for j in range(KEY_VALUE_HEADS)]
    dv_heads = [both(dv_sums, j) for j in range(KEY_VALUE_HEADS)]
    key_scale = 1.0 / FACTOR
    q_tail = dqk[keys, 4 * LANES : 5 * LANES]
    dqk[keys, 4 * LANES : 5 * LANES] = jnp.where(
        lane < HEAD_WIDTH, q_tail, pltpu.roll(dk_heads[0], HEAD_WIDTH, 1) * key_scale
    )
    dqk[keys, 5 * LANES :] = (
        jnp.where(lane < HEAD_WIDTH, dk_heads[1], pltpu.roll(dk_heads[2], HEAD_WIDTH, 1))
        * key_scale
    )
    dv[keys, :LANES] = low(
        jnp.where(lane < HEAD_WIDTH, dv_heads[0], pltpu.roll(dv_heads[1], HEAD_WIDTH, 1))
    )
    dv[keys, LANES:] = low(dv_heads[2])


def attend_back_first_kernel(
    qk, kpad, vpad, lse, attn, merged, back_middle, place, wab, wab2,
    keep_out, send_out, ab, lse_rows, correction, dqk, dv,
):
    rows = qk.shape[0]
    half = wab.shape[0]
    wb, wb2 = wab.at[:, QK_WIDTH:], wab2.at[:, QK_WIDTH:]
    middle_low = low(back_middle[...])
    d_out = low(dot_tn(merged[...], middle_low))
    out_columns = slice(QK_WIDTH, QK_WIDTH + MODEL_WIDTH)
    keep_out[:half, out_columns] = d_out[:half]
    send_out[:half, out_columns] = d_out[half:]
    ab_first = low(dot_nt(middle_low, wb[:, :MODEL_WIDTH]))
    ab_second = low(dot_nt(middle_low, wb2[:, :MODEL_WIDTH]))
    ab[:, :Q_WIDTH] = low(
        dot_nt(ab_first, place[:, :half]) + dot_nt(ab_second, place[:, half:])
    )
    ab[:, Q_WIDTH:] = jnp.zeros((rows, ab.shape[1] - Q_WIDTH), jnp.bfloat16)
    terms = ab[...].astype(jnp.float32) * attn[...]
    mask = low(
        (
            lax.broadcasted_iota(jnp.int32, (16, terms.shape[1]), 1) // HEAD_WIDTH
            == lax.broadcasted_iota(jnp.int32, (16, terms.shape[1]), 0)
        ).astype(jnp.float32)
    )
    high = low(terms)
    correction[...] = dot_nt(mask, high) + dot_nt(mask, low(terms - high.astype(jnp.float32)))
    lse_rows[...] = jnp.transpose(lse[...])
    score_back(0, qk, kpad, vpad, ab, lse_rows, correction, dqk, dv)


def attend_back_second_kernel(
    dqk_in, dv_in, qk, kpad, vpad, lse_rows, correction, ab, dqk, dv,
):
    for i in range(1, qk.shape[0] // SPAN):
        score_back(i, qk, kpad, vpad, ab, lse_rows, correction, dqk, dv)


def project_back_kernel(
    keep_in, send_in, gain_two_in, spans, x, normed, dqk, dv, back_middle, gain_one,
    place, cosine, sine, wab, wab2,
    mine, near, far, d1, d2,
    grad, grad_full,
):
    rows = x.shape[0]
    half = wab.shape[0]
    lane = lax.broadcasted_iota(jnp.int32, (rows, LANES), 1)
    cos, sin = cosine[...], sine[...]
    for b in range(QK_WIDTH // LANES):
        u = dqk[:, b * LANES : (b + 1) * LANES] * FACTOR
        grad[:, b * LANES : (b + 1) * LANES] = low(u * cos - half_turn(u, lane) * sin)
    d_qk = low(dot_tn(normed[...], grad[...]))
    d1[:half, :QK_WIDTH] = d_qk[:half]
    d2[:half, :QK_WIDTH] = d_qk[half:]
    dv_low = dv[:, :KV_WIDTH]
    d_v = low(dot_tn(normed[...], dv_low))
    d1[:half, QK_WIDTH + MODEL_WIDTH :] = d_v[:half]
    d2[:half, QK_WIDTH + MODEL_WIDTH :] = d_v[half:]
    parts = [
        dot_nt(grad[...], w[:, :QK_WIDTH]) + dot_nt(dv_low, w[:, QK_WIDTH + MODEL_WIDTH :])
        for w in (wab, wab2)
    ]
    back_norm = place_back(jnp.concatenate(parts, axis=1), place[...])
    xf = x[...].astype(jnp.float32)
    scale = lax.rsqrt(jnp.mean(xf * xf, axis=-1, keepdims=True) + EPSILON)
    unit = xf * scale
    gain_row = lax.broadcasted_iota(jnp.int32, (16, MODEL_WIDTH), 0)
    gains = jnp.where(
        gain_row == 0, jnp.sum(back_norm * unit, axis=0, keepdims=True), gain_two_in[...]
    )
    for d in (d1, d2):
        d[half:, :MODEL_WIDTH] = low(gains)
        d[half:, MODEL_WIDTH:] = jnp.zeros((16, d.shape[1] - MODEL_WIDTH), jnp.bfloat16)
    back_unit = back_norm * gain_one[...]
    grad_full[...] = back_middle[...] + scale * (
        back_unit - unit * jnp.mean(back_unit * unit, axis=-1, keepdims=True)
    )
    for k, (block, at) in enumerate(((mine, 0), (near, 0), (far, 0), (near, SPAN))):
        source = pl.ds(pl.multiple_of(spans[k] * SPAN, SPAN), SPAN)
        block[at : at + SPAN] = low(grad_full[source, :])


VMEM_SPEC = pl.BlockSpec(memory_space=pltpu.VMEM)
SMEM_SPEC = pl.BlockSpec(memory_space=pltpu.SMEM)
ANY_SPEC = pl.BlockSpec(memory_space=pl.ANY)


def shaped(rows, columns, kind):
    return jax.ShapeDtypeStruct((rows, columns), kind)


def call(body, outs, args, scratch, micros, scalars=(), after=(), alias=None, megabytes=16, out_specs=None):
    def run(*refs):
        body(*refs[: len(args)], *refs[len(args) + len(after) :])

    return pl.pallas_call(
        run,
        out_shape=outs,
        in_specs=[SMEM_SPEC if at in scalars else VMEM_SPEC for at in range(len(args))]
        + [ANY_SPEC] * len(after),
        out_specs=out_specs or [VMEM_SPEC] * len(outs),
        scratch_shapes=scratch,
        input_output_aliases=alias or {},
        compiler_params=vmem_params(megabytes),
        cost_estimate=pl.CostEstimate(
            flops=int(micros * 1.1e9), bytes_accessed=1_000_000, transcendentals=0
        ),
    )(*args, *after)


def whole_sequence_plan(mesh):
    axes = ("dp", "seq")
    n_dp, n_seq = mesh.shape["dp"], mesh.shape["seq"]
    count = n_dp * n_seq
    bits = count.bit_length() - 1
    seq_bits = n_seq.bit_length() - 1
    core, y_bit = 0, 1
    x_bit = seq_bits
    z_bits = tuple(range(seq_bits + 1, bits))[::-1]
    order_bits = z_bits + (x_bit, y_bit, core)

    def hold(v, *others):
        return lax.optimization_barrier((v, *others))[0] if others else v

    def together(*arrays):
        return lax.optimization_barrier(arrays)

    def swap(v, flip, until=()):
        return hold(lax.ppermute(v, axes, [(d, d ^ flip) for d in range(count)]), *until)

    def relative(slot):
        return sum(1 << bit for at, bit in enumerate(order_bits) if slot >> at & 1)

    order = tuple(relative(slot) for slot in range(count))
    z_count = 1 << len(z_bits)
    z_flips = [relative(slot) for slot in range(1, z_count)]
    flip_x, flip_y, flip_core = 1 << x_bit, 1 << y_bit, 1 << core

    def gather_z(v, until=()):
        return jnp.concatenate([v] + [swap(v, flip, until) for flip in z_flips], axis=0)

    def gather_z_stepwise(v, untils):
        for bit, until in zip(z_bits, untils):
            v = jnp.concatenate([v, swap(v, 1 << bit, until)], axis=0)
        return v

    def gather_one(v, x_first, until=()):
        return jnp.concatenate([v, swap(v, flip_x if x_first else flip_y, until)], axis=0)

    def gather_two(v, x_first, until=()):
        w = swap(v, flip_y if x_first else flip_x, until)
        size = v.shape[0] // 2
        if x_first:
            return jnp.concatenate([v, w], axis=0)
        return jnp.concatenate([v[:size], w[:size], v[size:], w[size:]], axis=0)

    def scatter_core(keep, send, until=()):
        return wide(keep) + wide(swap(send, flip_core, until))

    def scatter_one(total, x_first, until=()):
        size = total.shape[0] // 4
        if x_first:
            mine = jnp.concatenate([total[:size], total[2 * size : 3 * size]], axis=0)
            theirs = jnp.concatenate([total[size : 2 * size], total[3 * size :]], axis=0)
            return mine + wide(swap(low(theirs), flip_x, until))
        return total[: 2 * size] + wide(swap(low(total[2 * size :]), flip_y, until))

    def scatter_two(total, x_first, until=()):
        size = total.shape[0] // 2
        sent = swap(low(total[size:]), flip_y if x_first else flip_x, until)
        return total[:size] + wide(sent)

    def scatter_bit(total, bit):
        size = total.shape[0] // 2
        return total[:size] + wide(swap(low(total[size:]), 1 << bit))

    def scatter_z_with_sums(total, sums):
        size = total.shape[0] // z_count
        sums = lax.reduce_precision(sums.reshape(size, -1), 8, 7)
        width, wanted = total.shape[1], sums.shape[1]
        beside = jnp.pad(low(sums), ((0, 0), (0, -wanted % LANES)))
        out, terms = total[:size], [sums]
        for at, flip in enumerate(z_flips):
            theirs = low(total[(at + 1) * size : (at + 2) * size])
            sent = swap(jnp.concatenate([theirs, beside], axis=1), flip)
            out = out + wide(sent[:, :width])
            terms.append(wide(sent[:, width : width + wanted]))
        while len(terms) > 1:
            terms = [a + b for a, b in zip(terms[::2], terms[1::2])]
        return out, terms[0].reshape(-1)

    def exchange(parts, near_until=(), far_until=(), far_after=()):
        mine, near, far = parts
        size = mine.shape[0]
        near = swap(near, flip_core, near_until)
        far = hold(jnp.concatenate([far, near[size:]], axis=0), *far_after)
        return mine, near[:size], swap(far, flip_y, far_until)

    def scatter_with_sums(mine, theirs, sums, flip, until=()):
        sums = lax.reduce_precision(sums, 8, 7)
        sent = swap(jnp.concatenate([low(theirs), low(sums)], axis=0), flip, until)
        return mine + wide(sent[: mine.shape[0]]), sums + wide(sent[mine.shape[0] :])

    def on_sequence_device(
        hidden_in, span_order, attention_norm_gain, query_weight, key_weight, value_weight,
        output_weight, feedforward_gain, gate_weight, up_weight, down_weight, out_grad,
    ):
        rows = hidden_in.shape[0]
        model_rows = MODEL_WIDTH // count
        hidden_rows = HIDDEN_UNITS // count
        bf, f4 = jnp.bfloat16, jnp.float32
        half = MODEL_WIDTH // 2
        gain_one = attention_norm_gain.astype(jnp.float32).reshape(1, MODEL_WIDTH)
        gain_two = feedforward_gain.astype(jnp.float32).reshape(1, MODEL_WIDTH)
        model_low, model_full = shaped(rows, MODEL_WIDTH, bf), shaped(rows, MODEL_WIDTH, f4)

        def rows_of(w, columns):
            return w.reshape(model_rows, columns)

        def unpack(parts):
            return call(unpack_kernel, [model_low], parts, [], 1, megabytes=4)[0]

        slots = np.repeat(np.asarray(order, np.int32), model_rows)[None, :]
        offsets = np.tile(np.arange(model_rows, dtype=np.int32), count)[None, :]
        packed = call(
            functools.partial(pack_kernel, n_seq=n_seq),
            [
                *[shaped(n * (SPAN + 16), MODEL_WIDTH, bf) for n in (1, 2, 1)],
                *[shaped(n * SPAN, MODEL_WIDTH, bf) for n in (1, 2, 1)],
                shaped(MODEL_WIDTH, MODEL_WIDTH, bf),
            ],
            [span_order, hidden_in, out_grad, slots, offsets],
            [],
            2,
            scalars=(0,),
        )
        place = packed[6]
        first = jnp.concatenate(
            [
                rows_of(query_weight, Q_WIDTH),
                rows_of(key_weight, KV_WIDTH),
                rows_of(output_weight, MODEL_WIDTH),
                rows_of(value_weight, KV_WIDTH),
            ],
            axis=1,
        )

        down = down_weight.reshape(3, 16, MODEL_WIDTH).swapaxes(0, 1)
        down = jnp.pad(down, ((0, model_rows - 16), (0, 0), (0, DOWN_PITCH - MODEL_WIDTH)))
        gate, up = rows_of(gate_weight, HIDDEN_UNITS), rows_of(up_weight, HIDDEN_UNITS)
        ffn = jnp.concatenate(
            [gate[:, :HALF_FFN], down.reshape(model_rows, 3 * DOWN_PITCH), up[:, :HALF_FFN]], axis=1
        )
        later = jnp.concatenate([gate[:, HALF_FFN:], up[:, HALF_FFN:]], axis=1)
        first = gather_z(first, until=(ffn, place))
        first_a, first_b = first[:, :QK_WIDTH], first[:, QK_WIDTH:]
        first_a, first_b = gather_one(first_a, False), gather_one(first_b, True)
        x_parts = exchange(packed[:3], (first,), (first_a, first_b))
        one = (first_a, first_b)
        first_a, first_b = gather_two(first_a, False), gather_two(first_b, True)
        first = jnp.concatenate([first_a, first_b], axis=1)
        ffn = gather_z_stepwise(ffn, (one, (first,)))
        o_mine, o_near, o_far = hold(tuple(packed[3:6]), *one)
        o_near = swap(o_near, flip_core, (first,))
        o_far = jnp.concatenate([o_far, o_near[SPAN:]], axis=0)
        first_other = swap(first, flip_core)
        ffn_a, ffn_b = ffn[:, :FFN_CUT], ffn[:, FFN_CUT:]

        frequency = np.exp(np.arange(HEAD_WIDTH // 2) * (-2.0 * math.log(10000.0) / HEAD_WIDTH))
        angles = np.arange(rows)[:, None] * frequency[None, :]
        cosine = np.tile(np.cos(angles), (1, 4)).astype(np.float32)
        sine = np.sin(angles)
        sine = np.concatenate([-sine, sine, -sine, sine], axis=1).astype(np.float32)

        padded = jax.ShapeDtypeStruct((2 * KEY_VALUE_HEADS, rows, LANES), bf)
        spans, x, normed, qk, kpad, vpad = call(
            project_kernel,
            [
                jax.ShapeDtypeStruct((n_seq,), jnp.int32),
                model_low,
                model_low,
                shaped(rows, QK_WIDTH, bf),
                padded,
                padded,
            ],
            [*x_parts, gain_one, place, cosine, sine, first, first_other],
            [pltpu.VMEM((MODEL_WIDTH, QK_WIDTH), bf)] * 2,
            5,
            out_specs=[SMEM_SPEC] + [VMEM_SPEC] * 5,
        )
        stats = [shaped(rows, LANES, f4), shaped(rows, 5 * LANES, f4)]
        ffn_a, ffn_b = gather_one(ffn_a, False, (x,)), gather_one(ffn_b, True, (x,))
        later = gather_z_stepwise(hold(later, ffn), ((first,), (x,)))
        lse, attn, merged, middle, normed_two = call(
            attend_kernel,
            [*stats, model_low, model_full, model_low],
            [x, qk, kpad, vpad, gain_two, place, first, first_other],
            [],
            10,
        )
        o_far, second_a, second_b, later_y, later_x, middle = together(
            swap(o_far, flip_y),
            swap(ffn_a, flip_x),
            swap(ffn_b, flip_y),
            swap(later[:, :HALF_FFN], flip_y),
            swap(later[:, HALF_FFN:], flip_x),
            middle,
        )
        o_parts = (o_mine, o_near[:SPAN], o_far)
        ffn = []
        for part, second in ((ffn_a, second_a), (ffn_b, second_b)):
            ffn += [part, second, swap(part, flip_core), swap(second, flip_core)]
        later_a = jnp.concatenate([later[:, :HALF_FFN], later_y], axis=0)
        later_b = jnp.concatenate([later[:, HALF_FFN:], later_x], axis=0)
        weight_scratch = [pltpu.VMEM((MODEL_WIDTH, HALF_FFN), bf)] * 2
        og, result, back, r1, r1_send, dd, w_down = call(
            functools.partial(ffn_first_kernel, order=order, n_seq=n_seq),
            [
                model_low,
                model_full,
                model_full,
                *[shaped(half, 2 * HALF_FFN, bf)] * 2,
                shaped(HALF_FFN, MODEL_WIDTH, bf),
                shaped(HIDDEN_UNITS, MODEL_WIDTH, bf),
            ],
            [spans, *o_parts, normed_two, *ffn],
            weight_scratch,
            10,
            scalars=(0,),
        )
        r1_own = r1
        later = []
        for part, flip in ((later_a, flip_x), (later_b, flip_y)):
            second = swap(part, flip, (og,))
            later += [part, second, swap(part, flip_core, (og,)), swap(second, flip_core)]
        *h_parts, back_middle, gain_two_grad, r2, r2_send = call(
            functools.partial(ffn_second_kernel, order=order, n_seq=n_seq),
            [
                *[shaped(n * SPAN, MODEL_WIDTH, bf) for n in (1, 2, 1)],
                model_full,
                shaped(1, MODEL_WIDTH, f4),
                *[shaped(half, SECOND_WIDTH, bf)] * 2,
            ],
            [spans, og, normed_two, *later, w_down, result, back, dd, middle, gain_two, place],
            weight_scratch
            + [
                pltpu.VMEM((HALF_FFN, MODEL_WIDTH), bf),
                pltpu.VMEM((HIDDEN_UNITS, MODEL_WIDTH), bf),
                pltpu.VMEM((MODEL_WIDTH, DOWN_PITCH), f4),
                pltpu.VMEM((rows, MODEL_WIDTH), f4),
                pltpu.VMEM((rows, MODEL_WIDTH), f4),
            ],
            13,
            scalars=(0,),
            megabytes=18,
        )
        r1 = scatter_core(r1_own, r1_send, (back_middle,))
        r3, r3_send, ab, lse_rows, correction, dqk, dv = call(
            attend_back_first_kernel,
            [
                *[shaped(half + 16, 2 * HALF_FFN, bf)] * 2,
                shaped(rows, 5 * LANES, bf),
                shaped(LANES, rows, f4),
                shaped(16, rows, f4),
                shaped(rows, QK_WIDTH, f4),
                shaped(rows, 2 * LANES, bf),
            ],
            [qk, kpad, vpad, lse, attn, merged, back_middle, place, first, first_other],
            [],
            7,
            after=[r1],
        )
        r2 = scatter_core(r2, r2_send, (ab,))
        h_near = swap(h_parts[1], flip_core, (ab,))
        dqk, dv = call(
            attend_back_second_kernel,
            [shaped(rows, QK_WIDTH, f4), shaped(rows, 2 * LANES, bf)],
            [dqk, dv, qk, kpad, vpad, lse_rows, correction, ab],
            [],
            6,
            after=[r2],
            alias={0: 0, 1: 1},
        )
        p1 = scatter_one(r2[:, :SECOND_CUT], True, (dqk,))
        p2 = scatter_one(r2[:, SECOND_CUT : 2 * SECOND_CUT], False, (dqk,))
        *g_parts, r3, r3_send = call(
            project_back_kernel,
            [
                *[shaped(n * SPAN, MODEL_WIDTH, bf) for n in (1, 2, 1)],
                *[shaped(half + 16, 2 * HALF_FFN, bf)] * 2,
            ],
            [
                r3, r3_send, gain_two_grad, spans, x, normed, dqk, dv, back_middle,
                gain_one, place, cosine, sine, first, first_other,
            ],
            [pltpu.VMEM((rows, QK_WIDTH), bf), pltpu.VMEM((rows, MODEL_WIDTH), f4)],
            5,
            scalars=(3,),
            after=[p1, p2],
            alias={0: 3, 1: 4},
        )
        p1, p2 = scatter_two(p1, True, (r3,)), scatter_two(p2, False, (r3,))
        p3 = scatter_one(r2[:, 2 * SECOND_CUT :], True, (r3,))
        r1 = scatter_one(r1, False, (r3,))
        sent = wide(swap(r3_send, flip_core))
        r3 = wide(r3)
        r1, p3 = scatter_two(r1, False), scatter_two(p3, True)
        total, sums, r1, p1, p2, p3 = together(
            r3[:half] + sent[:half], r3[half:] + sent[half:], r1, p1, p2, p3
        )
        size = half // 4
        r3_a, r3_b = total[:, :QK_WIDTH], total[:, QK_WIDTH:]
        r3_a, sums = scatter_with_sums(
            jnp.concatenate([r3_a[:size], r3_a[2 * size : 3 * size]], axis=0),
            jnp.concatenate([r3_a[size : 2 * size], r3_a[3 * size :]], axis=0),
            sums[:, :QK_WIDTH],
            flip_x,
        )
        r3_b = scatter_one(r3_b, False)
        early = jnp.concatenate([p1, p2, r1], axis=1)
        early = scatter_bit(early, z_bits[-1])
        g_near = swap(g_parts[1], flip_core)
        r3_a, r3_b, sums, early, g_near, h_near = together(
            r3_a, r3_b, sums, early, g_near, h_near
        )
        r3_a, sums = scatter_with_sums(r3_a[:size], r3_a[size:], sums, flip_y)
        r3_b = scatter_two(r3_b, False)
        for bit in z_bits[-2::-1]:
            early = scatter_bit(early, bit)
        h_far = swap(jnp.concatenate([h_parts[2], h_near[SPAN:]], axis=0), flip_y)
        r3_a, r3_b, sums, early, h_far, g_near = together(
            r3_a, r3_b, sums, early, h_far, g_near
        )
        g_far = swap(jnp.concatenate([g_parts[2], g_near[SPAN:]], axis=0), flip_y)
        late = jnp.concatenate([r3_a, r3_b, p3], axis=1)
        late, sums = scatter_z_with_sums(late, sums[:2, :MODEL_WIDTH])
        hidden_out = unpack([h_parts[0], h_near[:SPAN], h_far])
        r1 = early[:, 2 * SECOND_CUT :]
        r2 = jnp.concatenate([early[:, : 2 * SECOND_CUT], late[:, 2 * HALF_FFN :]], axis=1)
        r3 = late
        hidden_grad = unpack([g_parts[0], g_near[:SPAN], g_far])
        gu1 = r2[:, SECOND_GATE_AT:]
        gate_grad = jnp.concatenate([r1[:, :HALF_FFN], gu1[:, :HALF_FFN]], axis=1)
        up_grad = jnp.concatenate([r1[:, HALF_FFN:], gu1[:, HALF_FFN : 2 * HALF_FFN]], axis=1)
        down_grad = r2[:16, :SECOND_GATE_AT].reshape(16, 3, DOWN_PITCH)[:, :, :MODEL_WIDTH]
        return (
            hidden_out,
            hidden_grad,
            sums[:MODEL_WIDTH],
            r3[:, :Q_WIDTH].reshape(-1),
            r3[:, Q_WIDTH:QK_WIDTH].reshape(-1),
            r3[:, QK_WIDTH + MODEL_WIDTH : 2 * HALF_FFN].reshape(-1),
            r3[:, QK_WIDTH : QK_WIDTH + MODEL_WIDTH].reshape(-1),
            sums[MODEL_WIDTH:],
            gate_grad.reshape(-1),
            up_grad.reshape(-1),
            down_grad.swapaxes(0, 1).reshape(-1),
        )

    return on_sequence_device


def pick_plan(mesh):
    count = mesh.shape["dp"] * mesh.shape["seq"]
    fits = (
        mesh.shape["seq"] == MB * SLOTS
        and SLOTS == 1
        and count & (count - 1) == 0
        and MODEL_WIDTH % count == 0
        and (HIDDEN_UNITS // count) % 16 == 0
    )
    return whole_sequence_plan(mesh) if fits else on_device


def solution(mesh):
    return jax.shard_map(
        pick_plan(mesh),
        mesh=mesh,
        in_specs=(
            P(("dp", "seq"), None),
            P(("dp", "seq")),
            P(),
            P(("dp", "seq")),
            P(("dp", "seq")),
            P(("dp", "seq")),
            P(("dp", "seq")),
            P(),
            P(("dp", "seq")),
            P(("dp", "seq")),
            P(("dp", "seq")),
            P(("dp", "seq"), None),
        ),
        out_specs=(
            P(("dp", "seq"), None),
            P(("dp", "seq"), None),
            P(),
            P(("dp", "seq")),
            P(("dp", "seq")),
            P(("dp", "seq")),
            P(("dp", "seq")),
            P(),
            P(("dp", "seq")),
            P(("dp", "seq")),
            P(("dp", "seq")),
        ),
        check_vma=False,
    )
```

```python
import functools
import math

import jax
import jax.numpy as jnp
import numpy as np
from jax import lax
from jax.experimental import pallas as pl
from jax.experimental.pallas import tpu as pltpu
from jax.sharding import PartitionSpec as P

MODEL_WIDTH = 576
QUERY_HEADS = 9
KEY_VALUE_HEADS = 3
HEAD_WIDTH = 64
HIDDEN_UNITS = 1536
SPAN = 128
MB = 4
SLOTS = 1


EPSILON = 1e-05


def angle_tables(positions, head_size):
    frequency = jnp.exp(
        jnp.arange(head_size // 2, dtype=jnp.float32) * (-2.0 * math.log(10000.0) / head_size)
    )
    angles = positions.astype(jnp.float32)[:, None] * frequency[None, :]
    angles = jnp.concatenate([angles, angles], axis=-1)[:, None, :]
    return (jnp.cos(angles), jnp.sin(angles))


def apply_rotation(value_rows, cosine_table, sine_values):
    half_size = value_rows.shape[-1] // 2
    turned = jnp.concatenate([-value_rows[..., half_size:], value_rows[..., :half_size]], axis=-1)
    return value_rows * cosine_table + turned * sine_values


def product(first_arg, second_arg):
    return jnp.dot(first_arg, second_arg, preferred_element_type=jnp.float32)


def inner_rows(first_arg, second_arg):
    return lax.dot_general(
        first_arg, second_arg, (((0,), (0,)), ((), ())), preferred_element_type=jnp.float32
    )


def inner_cols(first_arg, second_arg):
    return lax.dot_general(
        first_arg, second_arg, (((1,), (1,)), ((), ())), preferred_element_type=jnp.float32
    )


def shape_weights(flattened_rows):
    return (
        flattened_rows[0].reshape(MODEL_WIDTH, QUERY_HEADS * HEAD_WIDTH),
        flattened_rows[1].reshape(MODEL_WIDTH, KEY_VALUE_HEADS * HEAD_WIDTH),
        flattened_rows[2].reshape(MODEL_WIDTH, KEY_VALUE_HEADS * HEAD_WIDTH),
        flattened_rows[3].reshape(QUERY_HEADS * HEAD_WIDTH, MODEL_WIDTH),
        flattened_rows[4].reshape(MODEL_WIDTH, HIDDEN_UNITS),
        flattened_rows[5].reshape(MODEL_WIDTH, HIDDEN_UNITS),
        flattened_rows[6].reshape(HIDDEN_UNITS, MODEL_WIDTH),
    )


def block_scores(query_rows, key_block, query_place, key_place, factor):
    raw_scores = (
        jnp.einsum("qkgd,skd->kgqs", query_rows, key_block, preferred_element_type=jnp.float32)
        * factor
    )
    allowed = query_place[:, None] >= key_place[None, :]
    return jnp.where(allowed, raw_scores, -1e30)


def forward(layer_input, positions, span_ids, gain_pair, matrices):
    w_q, w_k, w_v, w_o, w_g, w_u, w_d = matrices
    count_of_rows = layer_input.shape[0]
    query_group_width = QUERY_HEADS // KEY_VALUE_HEADS
    factor = 1.0 / math.sqrt(HEAD_WIDTH)
    input_full = layer_input.astype(jnp.float32)
    scale_one = lax.rsqrt(jnp.mean(input_full * input_full, axis=-1, keepdims=True) + EPSILON)
    unit_one = input_full * scale_one
    normed = (unit_one * gain_pair[0]).astype(jnp.bfloat16)
    query_rows = product(normed, w_q)
    unrotated_keys = product(normed, w_k)
    value_rows = product(normed, w_v)
    cosine_table, sine_values = angle_tables(positions, HEAD_WIDTH)
    rotated_query = apply_rotation(
        query_rows.reshape(count_of_rows, QUERY_HEADS, HEAD_WIDTH), cosine_table, sine_values
    ).astype(jnp.bfloat16)
    rotated_query = rotated_query.reshape(
        count_of_rows, KEY_VALUE_HEADS, query_group_width, HEAD_WIDTH
    )
    rotated_key = apply_rotation(
        unrotated_keys.reshape(count_of_rows, KEY_VALUE_HEADS, HEAD_WIDTH),
        cosine_table,
        sine_values,
    ).astype(jnp.bfloat16)
    rotated_key = rotated_key.reshape(count_of_rows, KEY_VALUE_HEADS * HEAD_WIDTH)
    v_low = value_rows.astype(jnp.bfloat16)
    every_key, every_value, key_spans = (
        lax.all_gather(rotated_key, "seq", axis=0, tiled=True),
        lax.all_gather(v_low, "seq", axis=0, tiled=True),
        lax.all_gather(span_ids.astype(jnp.bfloat16), "seq", axis=0, tiled=True),
    )
    offsets = jnp.arange(SPAN, dtype=jnp.int32)
    key_places = (key_spans.astype(jnp.int32)[:, None] * SPAN + offsets[None, :]).reshape(-1)
    count_of_keys = every_key.shape[0]
    block_length = math.gcd(count_of_keys, 512)
    count_of_blocks = count_of_keys // block_length
    blocks_of_keys = every_key.reshape(count_of_blocks, block_length, KEY_VALUE_HEADS, HEAD_WIDTH)
    blocks_of_values = every_value.reshape(
        count_of_blocks, block_length, KEY_VALUE_HEADS, HEAD_WIDTH
    )
    place_blocks = key_places.reshape(count_of_blocks, block_length)

    def softmax_stats(carry, piece_set):
        highest, totals = carry
        key_block, key_place = piece_set
        scores = block_scores(rotated_query, key_block, positions, key_place, factor)
        new_high = jnp.maximum(highest, jnp.max(scores, axis=-1))
        totals = totals * jnp.exp(highest - new_high) + jnp.sum(
            jnp.exp(scores - new_high[..., None]), axis=-1
        )
        return ((new_high, totals), None)

    initial = (
        jnp.full((KEY_VALUE_HEADS, query_group_width, count_of_rows), -1e30, jnp.float32),
        jnp.zeros((KEY_VALUE_HEADS, query_group_width, count_of_rows), jnp.float32),
    )
    (highest, totals), _ = lax.scan(softmax_stats, initial, (blocks_of_keys, place_blocks))

    def mix_values(running, piece_set):
        key_block, value_block, key_place = piece_set
        scores = block_scores(rotated_query, key_block, positions, key_place, factor)
        layer_weights = (jnp.exp(scores - highest[..., None]) / totals[..., None]).astype(
            jnp.bfloat16
        )
        return (
            running
            + jnp.einsum(
                "kgqs,skd->qkgd", layer_weights, value_block, preferred_element_type=jnp.float32
            ),
            None,
        )

    attention_output, _ = lax.scan(
        mix_values,
        jnp.zeros((count_of_rows, KEY_VALUE_HEADS, query_group_width, HEAD_WIDTH), jnp.float32),
        (blocks_of_keys, blocks_of_values, place_blocks),
    )
    attention_output = attention_output.reshape(count_of_rows, QUERY_HEADS * HEAD_WIDTH)
    merged = attention_output.astype(jnp.bfloat16)
    middle = input_full + product(merged, w_o)
    scale_two = lax.rsqrt(jnp.mean(middle * middle, axis=-1, keepdims=True) + EPSILON)
    unit_two = middle * scale_two
    normed_two = (unit_two * gain_pair[1]).astype(jnp.bfloat16)
    gate_act = product(normed_two, w_g)
    upward = product(normed_two, w_u)
    hidden = (jax.nn.silu(gate_act) * upward).astype(jnp.bfloat16)
    result = (middle + product(hidden, w_d)).astype(jnp.bfloat16)
    stored = (
        scale_one,
        unit_one,
        normed,
        cosine_table,
        sine_values,
        rotated_query,
        blocks_of_keys,
        blocks_of_values,
        place_blocks,
        highest,
        totals,
        attention_output,
        merged,
        scale_two,
        unit_two,
        normed_two,
        gate_act,
        upward,
        hidden,
    )
    return (result, stored)


def backward(cotangent, positions, gain_pair, matrices, stored):
    w_q, w_k, w_v, w_o, w_g, w_u, w_d = matrices
    (
        scale_one,
        unit_one,
        normed,
        cosine_table,
        sine_values,
        rotated_query,
        blocks_of_keys,
        blocks_of_values,
        place_blocks,
        highest,
        totals,
        attention_output,
        merged,
        scale_two,
        unit_two,
        normed_two,
        gate_act,
        upward,
        hidden,
    ) = stored
    count_of_rows = cotangent.shape[0]
    query_group_width = QUERY_HEADS // KEY_VALUE_HEADS
    factor = 1.0 / math.sqrt(HEAD_WIDTH)
    grad_down = inner_rows(hidden, cotangent)
    back_hidden = inner_cols(cotangent, w_d)
    sigmoid_gate = jax.nn.sigmoid(gate_act)
    back_gate = (
        back_hidden * upward * sigmoid_gate * (1.0 + gate_act * (1.0 - sigmoid_gate))
    ).astype(jnp.bfloat16)
    back_up = (back_hidden * (gate_act * sigmoid_gate)).astype(jnp.bfloat16)
    grad_gate = inner_rows(normed_two, back_gate)
    grad_up = inner_rows(normed_two, back_up)
    back_norm_two = inner_cols(back_gate, w_g) + inner_cols(back_up, w_u)
    gain_two = jnp.sum(back_norm_two * unit_two, axis=0)
    back_unit = back_norm_two * gain_pair[1]
    back_middle = cotangent.astype(jnp.float32) + scale_two * (
        back_unit - unit_two * jnp.mean(back_unit * unit_two, axis=-1, keepdims=True)
    )
    middle_low = back_middle.astype(jnp.bfloat16)
    grad_out = inner_rows(merged, middle_low)
    attention_backward = inner_cols(middle_low, w_o).astype(jnp.bfloat16)
    head_gradient_rows = attention_backward.reshape(
        count_of_rows, KEY_VALUE_HEADS, query_group_width, HEAD_WIDTH
    )
    attention_head_rows = attention_output.reshape(
        count_of_rows, KEY_VALUE_HEADS, query_group_width, HEAD_WIDTH
    )
    correction = jnp.transpose(
        jnp.sum(head_gradient_rows.astype(jnp.float32) * attention_head_rows, axis=-1), (1, 2, 0)
    )

    def score_grads(running, piece_set):
        key_block, value_block, key_place = piece_set
        scores = block_scores(rotated_query, key_block, positions, key_place, factor)
        probs = jnp.exp(scores - highest[..., None]) / totals[..., None]
        back_probs = jnp.einsum(
            "qkgd,skd->kgqs", head_gradient_rows, value_block, preferred_element_type=jnp.float32
        )
        back_scores = (probs * (back_probs - correction[..., None])).astype(jnp.bfloat16)
        running = (
            running
            + jnp.einsum(
                "kgqs,skd->qkgd", back_scores, key_block, preferred_element_type=jnp.float32
            )
            * factor
        )
        key_grad = (
            jnp.einsum(
                "kgqs,qkgd->skd", back_scores, rotated_query, preferred_element_type=jnp.float32
            )
            * factor
        )
        value_grad = jnp.einsum(
            "kgqs,qkgd->skd",
            probs.astype(jnp.bfloat16),
            head_gradient_rows,
            preferred_element_type=jnp.float32,
        )
        return (running, (key_grad, value_grad))

    back_query, (gradient_of_keys, gradient_of_values) = lax.scan(
        score_grads,
        jnp.zeros((count_of_rows, KEY_VALUE_HEADS, query_group_width, HEAD_WIDTH), jnp.float32),
        (blocks_of_keys, blocks_of_values, place_blocks),
    )
    count_of_keys = gradient_of_keys.shape[0] * gradient_of_keys.shape[1]
    local_keys, value_own = (
        lax.psum_scatter(
            gradient_of_keys.reshape(count_of_keys, KEY_VALUE_HEADS * HEAD_WIDTH).astype(
                jnp.bfloat16
            ),
            "seq",
            scatter_dimension=0,
            tiled=True,
        ).astype(jnp.float32),
        lax.psum_scatter(
            gradient_of_values.reshape(count_of_keys, KEY_VALUE_HEADS * HEAD_WIDTH).astype(
                jnp.bfloat16
            ),
            "seq",
            scatter_dimension=0,
            tiled=True,
        ).astype(jnp.float32),
    )
    query_low = (
        apply_rotation(
            back_query.reshape(count_of_rows, QUERY_HEADS, HEAD_WIDTH), cosine_table, -sine_values
        )
        .astype(jnp.bfloat16)
        .reshape(count_of_rows, QUERY_HEADS * HEAD_WIDTH)
    )
    key_low = (
        apply_rotation(
            local_keys.reshape(count_of_rows, KEY_VALUE_HEADS, HEAD_WIDTH),
            cosine_table,
            -sine_values,
        )
        .astype(jnp.bfloat16)
        .reshape(count_of_rows, KEY_VALUE_HEADS * HEAD_WIDTH)
    )
    value_low = value_own.astype(jnp.bfloat16)
    grad_query = inner_rows(normed, query_low)
    grad_key = inner_rows(normed, key_low)
    grad_value = inner_rows(normed, value_low)
    back_norm_one = (
        inner_cols(query_low, w_q) + inner_cols(key_low, w_k) + inner_cols(value_low, w_v)
    )
    gain_one = jnp.sum(back_norm_one * unit_one, axis=0)
    back_unit_one = back_norm_one * gain_pair[0]
    input_back = back_middle + scale_one * (
        back_unit_one - unit_one * jnp.mean(back_unit_one * unit_one, axis=-1, keepdims=True)
    )
    weight_terms = (grad_query, grad_key, grad_value, grad_out, grad_gate, grad_up, grad_down)
    return (input_back.astype(jnp.bfloat16), weight_terms, (gain_one, gain_two))


def on_device(
    hidden_in,
    span_order,
    attention_norm_gain,
    query_weight,
    key_weight,
    value_weight,
    output_weight,
    feedforward_gain,
    gate_weight,
    up_weight,
    down_weight,
    out_grad,
):
    count_of_rows = SLOTS * SPAN
    gain_pair = (attention_norm_gain.astype(jnp.float32), feedforward_gain.astype(jnp.float32))
    offsets = jnp.arange(SPAN, dtype=jnp.int32)
    weight_totals = (
        jnp.zeros((MODEL_WIDTH, QUERY_HEADS * HEAD_WIDTH), jnp.float32),
        jnp.zeros((MODEL_WIDTH, KEY_VALUE_HEADS * HEAD_WIDTH), jnp.float32),
        jnp.zeros((MODEL_WIDTH, KEY_VALUE_HEADS * HEAD_WIDTH), jnp.float32),
        jnp.zeros((QUERY_HEADS * HEAD_WIDTH, MODEL_WIDTH), jnp.float32),
        jnp.zeros((MODEL_WIDTH, HIDDEN_UNITS), jnp.float32),
        jnp.zeros((MODEL_WIDTH, HIDDEN_UNITS), jnp.float32),
        jnp.zeros((HIDDEN_UNITS, MODEL_WIDTH), jnp.float32),
    )
    gain_totals = (jnp.zeros((MODEL_WIDTH,), jnp.float32), jnp.zeros((MODEL_WIDTH,), jnp.float32))
    outputs = []
    input_grads = []
    for micro_index in range(MB):
        layer_input = hidden_in[micro_index * count_of_rows : (micro_index + 1) * count_of_rows]
        cotangent = out_grad[micro_index * count_of_rows : (micro_index + 1) * count_of_rows]
        span_ids = span_order[micro_index * SLOTS : (micro_index + 1) * SLOTS]
        positions = (span_ids[:, None] * SPAN + offsets[None, :]).reshape(count_of_rows)
        forward_weights = shape_weights(
            (
                lax.all_gather(query_weight, ("dp", "seq"), axis=0, tiled=True),
                lax.all_gather(key_weight, ("dp", "seq"), axis=0, tiled=True),
                lax.all_gather(value_weight, ("dp", "seq"), axis=0, tiled=True),
                lax.all_gather(output_weight, ("dp", "seq"), axis=0, tiled=True),
                lax.all_gather(gate_weight, ("dp", "seq"), axis=0, tiled=True),
                lax.all_gather(up_weight, ("dp", "seq"), axis=0, tiled=True),
                lax.all_gather(down_weight, ("dp", "seq"), axis=0, tiled=True),
            )
        )
        result, stored = forward(layer_input, positions, span_ids, gain_pair, forward_weights)
        backward_weights = shape_weights(
            (
                lax.all_gather(query_weight, ("dp", "seq"), axis=0, tiled=True),
                lax.all_gather(key_weight, ("dp", "seq"), axis=0, tiled=True),
                lax.all_gather(value_weight, ("dp", "seq"), axis=0, tiled=True),
                lax.all_gather(output_weight, ("dp", "seq"), axis=0, tiled=True),
                lax.all_gather(gate_weight, ("dp", "seq"), axis=0, tiled=True),
                lax.all_gather(up_weight, ("dp", "seq"), axis=0, tiled=True),
                lax.all_gather(down_weight, ("dp", "seq"), axis=0, tiled=True),
            )
        )
        input_back, weight_terms, gain_terms = backward(
            cotangent, positions, gain_pair, backward_weights, stored
        )
        weight_totals = tuple(
            (running + term for running, term in zip(weight_totals, weight_terms))
        )
        gain_totals = tuple((running + term for running, term in zip(gain_totals, gain_terms)))
        outputs.append(result)
        input_grads.append(input_back)
    grad_query, grad_key, grad_value, grad_out, grad_gate, grad_up, grad_down = weight_totals
    owned = (
        lax.psum_scatter(grad_query.reshape(-1), ("dp", "seq"), scatter_dimension=0, tiled=True),
        lax.psum_scatter(grad_key.reshape(-1), ("dp", "seq"), scatter_dimension=0, tiled=True),
        lax.psum_scatter(grad_value.reshape(-1), ("dp", "seq"), scatter_dimension=0, tiled=True),
        lax.psum_scatter(grad_out.reshape(-1), ("dp", "seq"), scatter_dimension=0, tiled=True),
        lax.psum_scatter(grad_gate.reshape(-1), ("dp", "seq"), scatter_dimension=0, tiled=True),
        lax.psum_scatter(grad_up.reshape(-1), ("dp", "seq"), scatter_dimension=0, tiled=True),
        lax.psum_scatter(grad_down.reshape(-1), ("dp", "seq"), scatter_dimension=0, tiled=True),
    )
    gain_one, gain_two = lax.psum((gain_totals[0], gain_totals[1]), ("dp", "seq"))
    return (
        jnp.concatenate(outputs, axis=0),
        jnp.concatenate(input_grads, axis=0),
        gain_one,
        owned[0],
        owned[1],
        owned[2],
        owned[3],
        gain_two,
        owned[4],
        owned[5],
        owned[6],
    )


FACTOR = 1.0 / math.sqrt(HEAD_WIDTH)
KV_WIDTH = KEY_VALUE_HEADS * HEAD_WIDTH
Q_WIDTH = QUERY_HEADS * HEAD_WIDTH
QK_WIDTH = Q_WIDTH + KV_WIDTH
LANES = 128
HALF_FFN = HIDDEN_UNITS // 2
FFN_BLOCK = 768
DOWN_PITCH = 640
DOWN_AT = HALF_FFN
DOWN_EARLY = 2
FFN_CUT = DOWN_AT + DOWN_EARLY * DOWN_PITCH
UP_AT = (3 - DOWN_EARLY) * DOWN_PITCH
SECOND_GATE_AT = 3 * DOWN_PITCH
SECOND_WIDTH = SECOND_GATE_AT + 2 * HALF_FFN
SECOND_CUT = SECOND_WIDTH // 3


def vmem_params(megabytes=48):
    return pltpu.CompilerParams(vmem_limit_bytes=megabytes * 1024 * 1024)


def dot_nn(a, b):
    return jnp.dot(a, b, preferred_element_type=jnp.float32)


def dot_tn(a, b):
    return lax.dot_general(a, b, (((0,), (0,)), ((), ())), preferred_element_type=jnp.float32)


def dot_nt(a, b):
    return lax.dot_general(a, b, (((1,), (1,)), ((), ())), preferred_element_type=jnp.float32)


def low(v):
    return v.astype(jnp.bfloat16)


def wide(v):
    return v.astype(jnp.float32)


def place_back(v, place):
    high = low(v)
    rest = low(v - high.astype(jnp.float32))
    return dot_nt(high, place) + dot_nt(rest, place)


def half_turn(u, lane):
    return jnp.where(
        lane % HEAD_WIDTH < HEAD_WIDTH // 2,
        pltpu.roll(u, LANES - HEAD_WIDTH // 2, 1),
        pltpu.roll(u, HEAD_WIDTH // 2, 1),
    )


def padded_heads(blocks, head, lane):
    here = blocks[head // 2]
    moved = pltpu.roll(here, HEAD_WIDTH, 1)
    low_half, high_half = (here, moved) if head % 2 == 0 else (moved, here)
    zero = jnp.zeros_like(here)
    return (
        low(jnp.where(lane < HEAD_WIDTH, low_half, zero)),
        low(jnp.where(lane >= HEAD_WIDTH, high_half, zero)),
    )


def pack_kernel(
    span_order, hidden_in, out_grad, slots, offsets,
    x_mine, x_near, x_far, o_mine, o_near, o_far, place, *, n_seq,
):
    seq = lax.axis_index("seq")
    me = lax.axis_index("dp") * n_seq + seq
    tall = SPAN + 16
    for flip, x, o, at in ((0, x_mine, o_mine, 0), (1, x_near, o_near, 0), (3, x_near, o_near, 1), (2, x_far, o_far, 0)):
        origin = seq ^ flip
        block = pl.ds(pl.multiple_of(origin * SPAN, SPAN), SPAN)
        x[at * tall : at * tall + SPAN] = hidden_in[block, :]
        number = jnp.full((16, MODEL_WIDTH), span_order[origin], jnp.int32)
        x[at * tall + SPAN : (at + 1) * tall] = low(number.astype(jnp.float32))
        o[at * SPAN : (at + 1) * SPAN] = out_grad[block, :]
    natural = (slots[...] ^ me) * (MODEL_WIDTH // (n_seq * lax.axis_size("dp"))) + offsets[...]
    row = lax.broadcasted_iota(jnp.int32, place.shape, 0)
    place[...] = low((row == natural).astype(jnp.float32))


def unpack_kernel(mine, near, far, out):
    seq = lax.axis_index("seq")
    for flip, source, at in ((0, mine, 0), (1, near, 0), (2, far, 0), (3, far, 1)):
        target = pl.ds(pl.multiple_of((seq ^ flip) * SPAN, SPAN), SPAN)
        out[target, :] = source[at * SPAN : (at + 1) * SPAN]


def project_kernel(
    x_mine, x_near, x_far, gain_one, place, cosine, sine, wab, wab2,
    spans, x_out, normed_out, qk_out, kpad_out, vpad_out, wqk, wov,
):
    rows = x_out.shape[0]
    half = wab.shape[0]
    tall = SPAN + 16
    for k, (block, at) in enumerate(((x_mine, 0), (x_near, 0), (x_far, 0), (x_far, tall))):
        number = jnp.max(block[at + SPAN : at + tall, :LANES].astype(jnp.float32))
        number = number.astype(jnp.int32)
        spans[k] = number
        x_out[pl.ds(pl.multiple_of(number * SPAN, SPAN), SPAN), :] = block[at : at + SPAN]
    wa, wb = wab.at[:, :QK_WIDTH], wab.at[:, QK_WIDTH:]
    wa2, wb2 = wab2.at[:, :QK_WIDTH], wab2.at[:, QK_WIDTH:]
    wqk[:half] = wa[...]
    wqk[half:] = wa2[...]
    wov[:half] = wb[...]
    wov[half:] = wb2[...]
    x = x_out[...].astype(jnp.float32)
    scale = lax.rsqrt(jnp.mean(x * x, axis=-1, keepdims=True) + EPSILON)
    normed = low(x * scale * gain_one[...])
    normed_out[...] = low(dot_nn(normed, place[...]))
    lane = lax.broadcasted_iota(jnp.int32, (rows, LANES), 1)
    cos, sin = cosine[...], sine[...]
    k_blocks = []
    for b in range(QK_WIDTH // LANES):
        u = dot_nn(normed_out[...], wqk[:, b * LANES : (b + 1) * LANES])
        turned = u * cos + half_turn(u, lane) * sin
        turned = low(turned).astype(jnp.float32)
        if (b + 1) * LANES > Q_WIDTH:
            k_blocks.append(turned)
        if (b + 1) * LANES <= Q_WIDTH:
            turned = turned * FACTOR
        elif b * LANES < Q_WIDTH:
            turned = jnp.where(lane < Q_WIDTH - b * LANES, turned * FACTOR, turned)
        qk_out[:, b * LANES : (b + 1) * LANES] = low(turned)
    first_group = QUERY_HEADS - 2 * (Q_WIDTH // LANES)
    for j in range(KEY_VALUE_HEADS):
        lo, hi = padded_heads(k_blocks, j + first_group, lane)
        kpad_out[2 * j] = lo
        kpad_out[2 * j + 1] = hi
    v = dot_nn(normed_out[...], wov[:, MODEL_WIDTH:])
    v = low(v).astype(jnp.float32)
    v = jnp.concatenate([v, jnp.zeros((rows, HEAD_WIDTH), jnp.float32)], axis=1)
    v_blocks = [v[:, :LANES], v[:, LANES:]]
    for j in range(KEY_VALUE_HEADS):
        lo, hi = padded_heads(v_blocks, j, lane)
        vpad_out[2 * j] = lo
        vpad_out[2 * j + 1] = hi


def head_slot(head):
    group = head // (QUERY_HEADS // KEY_VALUE_HEADS) if isinstance(head, int) else (head * 11) >> 5
    return 2 * group + head % 2


def head_blocks(body):
    @pl.loop(0, QUERY_HEADS // 2)
    def _(b):
        body(2 * b, pl.ds(pl.multiple_of(b * LANES, LANES), LANES), 2)

    if QUERY_HEADS % 2:
        last = QUERY_HEADS // 2
        body(2 * last, slice(last * LANES, (last + 1) * LANES), 1)


def attend_spans(count, qk, kpad, vpad, lse_out, attn_out):
    lane = lax.broadcasted_iota(jnp.int32, (SPAN, LANES), 1)
    diagonal = lax.broadcasted_iota(jnp.int32, (SPAN, SPAN), 0) >= lax.broadcasted_iota(
        jnp.int32, (SPAN, SPAN), 1
    )
    lse_out[...] = jnp.zeros_like(lse_out)

    def block(first_head, columns, heads):
        for i in range(count):
            here = slice(i * SPAN, (i + 1) * SPAN)
            q = qk[here, columns]
            lse = lse_out[here, :]
            mixed = None
            for side in range(heads):
                h = first_head + side
                slot = head_slot(h)
                s = dot_nt(q, kpad[slot, : (i + 1) * SPAN, :])
                s_last = jnp.where(diagonal, s[:, i * SPAN :], -1e30)
                s = s_last if i == 0 else jnp.concatenate([s[:, : i * SPAN], s_last], axis=1)
                top = jnp.max(s, axis=-1, keepdims=True)
                p = jnp.exp(s - top)
                total = jnp.sum(p, axis=-1, keepdims=True)
                p = low(p * (1.0 / total))
                lse = jnp.where(lane == h, top + jnp.log(total), lse)
                part = dot_nn(p, vpad[slot, : (i + 1) * SPAN, :])
                mixed = part if mixed is None else mixed + part
            attn_out[here, columns] = mixed
            lse_out[here, :] = lse

    head_blocks(block)


def attend_kernel(
    x_in, qk, kpad, vpad, gain_two, place, wab, wab2,
    lse_out, attn_out, merged_out, middle_out, normed_two_out,
):
    rows = x_in.shape[0]
    half = wab.shape[0]
    wb, wb2 = wab.at[:, QK_WIDTH:], wab2.at[:, QK_WIDTH:]
    attend_spans(rows // SPAN, qk, kpad, vpad, lse_out, attn_out)
    merged = low(dot_nn(low(attn_out[:, :Q_WIDTH]), place[...]))
    merged_out[...] = merged
    middle = (
        x_in[...].astype(jnp.float32)
        + dot_nn(merged[:, :half], wb[:, :MODEL_WIDTH])
        + dot_nn(merged[:, half:], wb2[:, :MODEL_WIDTH])
    )
    middle_out[...] = middle
    scale_two = lax.rsqrt(jnp.mean(middle * middle, axis=-1, keepdims=True) + EPSILON)
    normed_two_out[...] = low(dot_nn(low(middle * scale_two * gain_two[...]), place[...]))


def ffn_block(n2, og, wg, wu, wd, at, result, back_norm, d_keep, d_send, dd_out):
    columns = pl.ds(pl.multiple_of(at * FFN_BLOCK, FFN_BLOCK), FFN_BLOCK)
    up_columns = pl.ds(pl.multiple_of(HALF_FFN + at * FFN_BLOCK, FFN_BLOCK), FFN_BLOCK)
    half = d_keep.shape[0]
    w_gate, w_up, w_down = wg[:, columns], wu[:, columns], wd[columns, :]
    gate = dot_nn(n2, w_gate)
    up = dot_nn(n2, w_up)
    back_hidden = dot_nt(og, w_down)
    sigmoid = jax.nn.sigmoid(gate)
    silu = gate * sigmoid
    hidden = low(silu * up)
    back_gate = low(back_hidden * up * sigmoid * (1.0 + gate * (1.0 - sigmoid)))
    back_up = low(back_hidden * silu)
    dd_out[columns, :] = low(dot_tn(hidden, og))
    dg = low(dot_tn(n2, back_gate))
    du = low(dot_tn(n2, back_up))
    d_keep[:, columns] = dg[:half]
    d_send[:, columns] = dg[half:]
    d_keep[:, up_columns] = du[:half]
    d_send[:, up_columns] = du[half:]
    result[...] += dot_nn(hidden, w_down)
    back_norm[...] += dot_nt(back_gate, w_gate) + dot_nt(back_up, w_up)


def fill_gate(target, a0, a1, a2, a3):
    size = a0.shape[0] // 2
    for core, (first, second) in enumerate(((a0, a1), (a2, a3))):
        for at, source in enumerate((first, second, first, second)):
            start = (4 * core + at) * size
            piece = slice(at // 2 * size, (at // 2 + 1) * size)
            target[start : start + size] = source[piece, :HALF_FFN]


def fill_up(target, column, b0, b1, b2, b3):
    for at, source in enumerate((b0, b1, b2, b3)):
        size = source.shape[0]
        target[at * size : (at + 1) * size] = source[:, column : column + HALF_FFN]


def ffn_first_kernel(
    spans, o_mine, o_near, o_far, n2, a0, a1, a2, a3, b0, b1, b2, b3,
    og_out, result_out, back_out, d_keep, d_send, dd, wd_out,
    wg, wu, *, order, n_seq,
):
    me = lax.axis_index("dp") * n_seq + lax.axis_index("seq")
    for k, (block, at) in enumerate(((o_mine, 0), (o_near, 0), (o_far, 0), (o_far, SPAN))):
        target = pl.ds(pl.multiple_of(spans[k] * SPAN, SPAN), SPAN)
        og_out[target, :] = block[at : at + SPAN]
    size = a0.shape[0] // 2
    fill_gate(wg, a0, a1, a2, a3)
    fill_up(wu, UP_AT, b0, b1, b2, b3)
    count = len(order)
    rows, pitch = wd_out.shape[0] // count, MODEL_WIDTH // count
    each = size // pitch
    for slot, relative in enumerate(order):
        core, block, at = slot // (4 * each), slot // each % 4, slot % each
        x_side, y_side = block % 2, block // 2
        for t in range(rows // 16):
            if t < DOWN_EARLY:
                source = ((a0, a1), (a2, a3))[core][x_side]
                start = y_side * size + at * pitch
                first = DOWN_AT + t * DOWN_PITCH
            else:
                source = ((b0, b1), (b2, b3))[core][y_side]
                start = x_side * size + at * pitch
                first = (t - DOWN_EARLY) * DOWN_PITCH
            target = pl.multiple_of((me ^ relative) * rows + 16 * t, 16)
            wd_out[pl.ds(target, 16), :] = source[start : start + 16, first : first + MODEL_WIDTH]
    result_out[...] = jnp.zeros_like(result_out)
    back_out[...] = jnp.zeros_like(back_out)

    @pl.loop(0, HALF_FFN // FFN_BLOCK)
    def _(at):
        ffn_block(
            n2[...], og_out[...], wg, wu, wd_out, at, result_out, back_out, d_keep, d_send, dd
        )


def ffn_second_kernel(
    spans, og, n2, a0, a1, a2, a3, b0, b1, b2, b3,
    wd_in, result_in, back_in, dd_in, middle, gain_two, place,
    mine, near, far, back_middle_out, gain_out, keep_out, send_out,
    wg, wu, wd, dd, spread, result, back, *, order, n_seq,
):
    half = keep_out.shape[0]
    fill_gate(wg, a0, a1, a2, a3)
    fill_up(wu, 0, b0, b1, b2, b3)
    me = lax.axis_index("dp") * n_seq + lax.axis_index("seq")
    d_keep = keep_out.at[:, SECOND_GATE_AT : SECOND_GATE_AT + 2 * HALF_FFN]
    d_send = send_out.at[:, SECOND_GATE_AT : SECOND_GATE_AT + 2 * HALF_FFN]
    wd[...] = wd_in[HALF_FFN:, :]
    dd[:HALF_FFN] = dd_in[...]
    result[...] = result_in[...] + middle[...]
    back[...] = back_in[...]

    @pl.loop(0, HALF_FFN // FFN_BLOCK)
    def _(at):
        ffn_block(
            n2[...], og[...], wg, wu, wd, at, result, back, d_keep, d_send, dd.at[HALF_FFN:, :]
        )

    count = len(order)
    rows, pitch = HIDDEN_UNITS // count, MODEL_WIDTH // count
    spread[...] = jnp.zeros_like(spread)
    for t in range(rows // 16):
        for slot, relative in enumerate(order):
            source = pl.ds(pl.multiple_of((me ^ relative) * rows + 16 * t, 16), 16)
            spread[slot * pitch : slot * pitch + 16, :MODEL_WIDTH] = wide(dd[source, :])
        columns = slice(t * DOWN_PITCH, (t + 1) * DOWN_PITCH)
        keep_out[:, columns] = low(spread[:half])
        send_out[:, columns] = low(spread[half:])

    for k, (block, at) in enumerate(((mine, 0), (near, 0), (far, 0), (near, SPAN))):
        source = pl.ds(pl.multiple_of(spans[k] * SPAN, SPAN), SPAN)
        block[at : at + SPAN] = low(result[source, :])
    mid = middle[...]
    scale = lax.rsqrt(jnp.mean(mid * mid, axis=-1, keepdims=True) + EPSILON)
    unit = mid * scale
    back_norm = place_back(back[...], place[...])
    gain_out[...] = jnp.sum(back_norm * unit, axis=0, keepdims=True)
    back_unit = back_norm * gain_two[...]
    back_middle_out[...] = og[...].astype(jnp.float32) + scale * (
        back_unit - unit * jnp.mean(back_unit * unit, axis=-1, keepdims=True)
    )


def score_back(i, qk, kpad, vpad, ab, lse_rows, correction, dqk, dv):
    rows = qk.shape[0]
    groups = QUERY_HEADS // KEY_VALUE_HEADS
    diagonal = lax.broadcasted_iota(jnp.int32, (SPAN, SPAN), 1) >= lax.broadcasted_iota(
        jnp.int32, (SPAN, SPAN), 0
    )
    lane = lax.broadcasted_iota(jnp.int32, (SPAN, LANES), 1)
    keys = slice(i * SPAN, (i + 1) * SPAN)
    first = i * SPAN
    dk_sums = [None] * (2 * KEY_VALUE_HEADS)
    dv_sums = [None] * (2 * KEY_VALUE_HEADS)
    for b in range((QUERY_HEADS + 1) // 2):
        columns = slice(b * LANES, (b + 1) * LANES)
        q = qk[first:, columns]
        a = ab[first:, columns]
        dq = None
        for h in range(2 * b, min(2 * b + 2, QUERY_HEADS)):
            slot = 2 * (h // groups) + h % 2
            s = dot_nt(kpad[slot, keys, :], q)
            s = s - lse_rows[h : h + 1, first:]
            s_first = jnp.where(diagonal, s[:, :SPAN], -1e30)
            s = (
                s_first
                if first + SPAN == rows
                else jnp.concatenate([s_first, s[:, SPAN:]], axis=1)
            )
            p = jnp.exp(s)
            dp = dot_nt(vpad[slot, keys, :], a)
            ds = low(p * (dp - correction[h : h + 1, first:]))
            dk = dot_nn(ds, q)
            dvh = dot_nn(low(p), a)
            dk_sums[slot] = dk if dk_sums[slot] is None else dk_sums[slot] + dk
            dv_sums[slot] = dvh if dv_sums[slot] is None else dv_sums[slot] + dvh
            part = dot_tn(ds, kpad[slot, keys, :])
            dq = part if dq is None else dq + part
        if i == 0:
            dqk[first:, columns] = dq
        else:
            dqk[first:, columns] += dq

    def both(sums, j):
        return sums[2 * j] + pltpu.roll(sums[2 * j + 1], HEAD_WIDTH, 1)

    dk_heads = [both(dk_sums, j) for j in range(KEY_VALUE_HEADS)]
    dv_heads = [both(dv_sums, j) for j in range(KEY_VALUE_HEADS)]
    key_scale = 1.0 / FACTOR
    q_tail = dqk[keys, 4 * LANES : 5 * LANES]
    dqk[keys, 4 * LANES : 5 * LANES] = jnp.where(
        lane < HEAD_WIDTH, q_tail, pltpu.roll(dk_heads[0], HEAD_WIDTH, 1) * key_scale
    )
    dqk[keys, 5 * LANES :] = (
        jnp.where(lane < HEAD_WIDTH, dk_heads[1], pltpu.roll(dk_heads[2], HEAD_WIDTH, 1))
        * key_scale
    )
    dv[keys, :LANES] = low(
        jnp.where(lane < HEAD_WIDTH, dv_heads[0], pltpu.roll(dv_heads[1], HEAD_WIDTH, 1))
    )
    dv[keys, LANES:] = low(dv_heads[2])


def attend_back_first_kernel(
    qk, kpad, vpad, lse, attn, merged, back_middle, place, wab, wab2,
    keep_out, send_out, ab, lse_rows, correction, dqk, dv,
):
    rows = qk.shape[0]
    half = wab.shape[0]
    wb, wb2 = wab.at[:, QK_WIDTH:], wab2.at[:, QK_WIDTH:]
    middle_low = low(back_middle[...])
    d_out = low(dot_tn(merged[...], middle_low))
    out_columns = slice(QK_WIDTH, QK_WIDTH + MODEL_WIDTH)
    keep_out[:half, out_columns] = d_out[:half]
    send_out[:half, out_columns] = d_out[half:]
    ab_first = low(dot_nt(middle_low, wb[:, :MODEL_WIDTH]))
    ab_second = low(dot_nt(middle_low, wb2[:, :MODEL_WIDTH]))
    ab[:, :Q_WIDTH] = low(
        dot_nt(ab_first, place[:, :half]) + dot_nt(ab_second, place[:, half:])
    )
    ab[:, Q_WIDTH:] = jnp.zeros((rows, ab.shape[1] - Q_WIDTH), jnp.bfloat16)
    terms = ab[...].astype(jnp.float32) * attn[...]
    mask = low(
        (
            lax.broadcasted_iota(jnp.int32, (16, terms.shape[1]), 1) // HEAD_WIDTH
            == lax.broadcasted_iota(jnp.int32, (16, terms.shape[1]), 0)
        ).astype(jnp.float32)
    )
    high = low(terms)
    correction[...] = dot_nt(mask, high) + dot_nt(mask, low(terms - high.astype(jnp.float32)))
    lse_rows[...] = jnp.transpose(lse[...])
    score_back(0, qk, kpad, vpad, ab, lse_rows, correction, dqk, dv)


def attend_back_second_kernel(
    dqk_in, dv_in, qk, kpad, vpad, lse_rows, correction, ab, dqk, dv,
):
    for i in range(1, qk.shape[0] // SPAN):
        score_back(i, qk, kpad, vpad, ab, lse_rows, correction, dqk, dv)


def project_back_kernel(
    keep_in, send_in, gain_two_in, spans, x, normed, dqk, dv, back_middle, gain_one,
    place, cosine, sine, wab, wab2,
    mine, near, far, d1, d2,
    grad, grad_full,
):
    rows = x.shape[0]
    half = wab.shape[0]
    lane = lax.broadcasted_iota(jnp.int32, (rows, LANES), 1)
    cos, sin = cosine[...], sine[...]
    for b in range(QK_WIDTH // LANES):
        u = dqk[:, b * LANES : (b + 1) * LANES] * FACTOR
        grad[:, b * LANES : (b + 1) * LANES] = low(u * cos - half_turn(u, lane) * sin)
    d_qk = low(dot_tn(normed[...], grad[...]))
    d1[:half, :QK_WIDTH] = d_qk[:half]
    d2[:half, :QK_WIDTH] = d_qk[half:]
    dv_low = dv[:, :KV_WIDTH]
    d_v = low(dot_tn(normed[...], dv_low))
    d1[:half, QK_WIDTH + MODEL_WIDTH :] = d_v[:half]
    d2[:half, QK_WIDTH + MODEL_WIDTH :] = d_v[half:]
    parts = [
        dot_nt(grad[...], w[:, :QK_WIDTH]) + dot_nt(dv_low, w[:, QK_WIDTH + MODEL_WIDTH :])
        for w in (wab, wab2)
    ]
    back_norm = place_back(jnp.concatenate(parts, axis=1), place[...])
    xf = x[...].astype(jnp.float32)
    scale = lax.rsqrt(jnp.mean(xf * xf, axis=-1, keepdims=True) + EPSILON)
    unit = xf * scale
    gain_row = lax.broadcasted_iota(jnp.int32, (16, MODEL_WIDTH), 0)
    gains = jnp.where(
        gain_row == 0, jnp.sum(back_norm * unit, axis=0, keepdims=True), gain_two_in[...]
    )
    for d in (d1, d2):
        d[half:, :MODEL_WIDTH] = low(gains)
        d[half:, MODEL_WIDTH:] = jnp.zeros((16, d.shape[1] - MODEL_WIDTH), jnp.bfloat16)
    back_unit = back_norm * gain_one[...]
    grad_full[...] = back_middle[...] + scale * (
        back_unit - unit * jnp.mean(back_unit * unit, axis=-1, keepdims=True)
    )
    for k, (block, at) in enumerate(((mine, 0), (near, 0), (far, 0), (near, SPAN))):
        source = pl.ds(pl.multiple_of(spans[k] * SPAN, SPAN), SPAN)
        block[at : at + SPAN] = low(grad_full[source, :])


VMEM_SPEC = pl.BlockSpec(memory_space=pltpu.VMEM)
SMEM_SPEC = pl.BlockSpec(memory_space=pltpu.SMEM)
ANY_SPEC = pl.BlockSpec(memory_space=pl.ANY)


def shaped(rows, columns, kind):
    return jax.ShapeDtypeStruct((rows, columns), kind)


def call(body, outs, args, scratch, micros, scalars=(), after=(), alias=None, megabytes=16, out_specs=None):
    def run(*refs):
        body(*refs[: len(args)], *refs[len(args) + len(after) :])

    return pl.pallas_call(
        run,
        out_shape=outs,
        in_specs=[SMEM_SPEC if at in scalars else VMEM_SPEC for at in range(len(args))]
        + [ANY_SPEC] * len(after),
        out_specs=out_specs or [VMEM_SPEC] * len(outs),
        scratch_shapes=scratch,
        input_output_aliases=alias or {},
        compiler_params=vmem_params(megabytes),
        cost_estimate=pl.CostEstimate(
            flops=int(micros * 1.1e9), bytes_accessed=1_000_000, transcendentals=0
        ),
    )(*args, *after)


def whole_sequence_plan(mesh):
    axes = ("dp", "seq")
    n_dp, n_seq = mesh.shape["dp"], mesh.shape["seq"]
    count = n_dp * n_seq
    bits = count.bit_length() - 1
    seq_bits = n_seq.bit_length() - 1
    core, y_bit = 0, 1
    x_bit = seq_bits
    z_bits = tuple(range(seq_bits + 1, bits))[::-1]
    order_bits = z_bits + (x_bit, y_bit, core)

    def hold(v, *others):
        return lax.optimization_barrier((v, *others))[0] if others else v

    def together(*arrays):
        return lax.optimization_barrier(arrays)

    def swap(v, flip, until=()):
        return hold(lax.ppermute(v, axes, [(d, d ^ flip) for d in range(count)]), *until)

    def relative(slot):
        return sum(1 << bit for at, bit in enumerate(order_bits) if slot >> at & 1)

    order = tuple(relative(slot) for slot in range(count))
    z_count = 1 << len(z_bits)
    z_flips = [relative(slot) for slot in range(1, z_count)]
    flip_x, flip_y, flip_core = 1 << x_bit, 1 << y_bit, 1 << core

    def gather_z(v, until=()):
        return jnp.concatenate([v] + [swap(v, flip, until) for flip in z_flips], axis=0)

    def gather_z_stepwise(v, untils):
        for bit, until in zip(z_bits, untils):
            v = jnp.concatenate([v, swap(v, 1 << bit, until)], axis=0)
        return v

    def gather_one(v, x_first, until=()):
        return jnp.concatenate([v, swap(v, flip_x if x_first else flip_y, until)], axis=0)

    def gather_two(v, x_first, until=()):
        w = swap(v, flip_y if x_first else flip_x, until)
        size = v.shape[0] // 2
        if x_first:
            return jnp.concatenate([v, w], axis=0)
        return jnp.concatenate([v[:size], w[:size], v[size:], w[size:]], axis=0)

    def scatter_core(keep, send, until=()):
        return wide(keep) + wide(swap(send, flip_core, until))

    def scatter_one(total, x_first, until=()):
        size = total.shape[0] // 4
        if x_first:
            mine = jnp.concatenate([total[:size], total[2 * size : 3 * size]], axis=0)
            theirs = jnp.concatenate([total[size : 2 * size], total[3 * size :]], axis=0)
            return mine + wide(swap(low(theirs), flip_x, until))
        return total[: 2 * size] + wide(swap(low(total[2 * size :]), flip_y, until))

    def scatter_two(total, x_first, until=()):
        size = total.shape[0] // 2
        sent = swap(low(total[size:]), flip_y if x_first else flip_x, until)
        return total[:size] + wide(sent)

    def scatter_bit(total, bit):
        size = total.shape[0] // 2
        return total[:size] + wide(swap(low(total[size:]), 1 << bit))

    def scatter_z_with_sums(total, sums):
        size = total.shape[0] // z_count
        sums = lax.reduce_precision(sums.reshape(size, -1), 8, 7)
        width, wanted = total.shape[1], sums.shape[1]
        beside = jnp.pad(low(sums), ((0, 0), (0, -wanted % LANES)))
        out, terms = total[:size], [sums]
        for at, flip in enumerate(z_flips):
            theirs = low(total[(at + 1) * size : (at + 2) * size])
            sent = swap(jnp.concatenate([theirs, beside], axis=1), flip)
            out = out + wide(sent[:, :width])
            terms.append(wide(sent[:, width : width + wanted]))
        while len(terms) > 1:
            terms = [a + b for a, b in zip(terms[::2], terms[1::2])]
        return out, terms[0].reshape(-1)

    def exchange(parts, near_until=(), far_until=(), far_after=()):
        mine, near, far = parts
        size = mine.shape[0]
        near = swap(near, flip_core, near_until)
        far = hold(jnp.concatenate([far, near[size:]], axis=0), *far_after)
        return mine, near[:size], swap(far, flip_y, far_until)

    def scatter_with_sums(mine, theirs, sums, flip, until=()):
        sums = lax.reduce_precision(sums, 8, 7)
        sent = swap(jnp.concatenate([low(theirs), low(sums)], axis=0), flip, until)
        return mine + wide(sent[: mine.shape[0]]), sums + wide(sent[mine.shape[0] :])

    def on_sequence_device(
        hidden_in, span_order, attention_norm_gain, query_weight, key_weight, value_weight,
        output_weight, feedforward_gain, gate_weight, up_weight, down_weight, out_grad,
    ):
        rows = hidden_in.shape[0]
        model_rows = MODEL_WIDTH // count
        hidden_rows = HIDDEN_UNITS // count
        bf, f4 = jnp.bfloat16, jnp.float32
        half = MODEL_WIDTH // 2
        gain_one = attention_norm_gain.astype(jnp.float32).reshape(1, MODEL_WIDTH)
        gain_two = feedforward_gain.astype(jnp.float32).reshape(1, MODEL_WIDTH)
        model_low, model_full = shaped(rows, MODEL_WIDTH, bf), shaped(rows, MODEL_WIDTH, f4)

        def rows_of(w, columns):
            return w.reshape(model_rows, columns)

        def unpack(parts):
            return call(unpack_kernel, [model_low], parts, [], 1, megabytes=4)[0]

        slots = np.repeat(np.asarray(order, np.int32), model_rows)[None, :]
        offsets = np.tile(np.arange(model_rows, dtype=np.int32), count)[None, :]
        packed = call(
            functools.partial(pack_kernel, n_seq=n_seq),
            [
                *[shaped(n * (SPAN + 16), MODEL_WIDTH, bf) for n in (1, 2, 1)],
                *[shaped(n * SPAN, MODEL_WIDTH, bf) for n in (1, 2, 1)],
                shaped(MODEL_WIDTH, MODEL_WIDTH, bf),
            ],
            [span_order, hidden_in, out_grad, slots, offsets],
            [],
            2,
            scalars=(0,),
        )
        place = packed[6]
        first = jnp.concatenate(
            [
                rows_of(query_weight, Q_WIDTH),
                rows_of(key_weight, KV_WIDTH),
                rows_of(output_weight, MODEL_WIDTH),
                rows_of(value_weight, KV_WIDTH),
            ],
            axis=1,
        )

        down = down_weight.reshape(3, 16, MODEL_WIDTH).swapaxes(0, 1)
        down = jnp.pad(down, ((0, model_rows - 16), (0, 0), (0, DOWN_PITCH - MODEL_WIDTH)))
        gate, up = rows_of(gate_weight, HIDDEN_UNITS), rows_of(up_weight, HIDDEN_UNITS)
        ffn = jnp.concatenate(
            [gate[:, :HALF_FFN], down.reshape(model_rows, 3 * DOWN_PITCH), up[:, :HALF_FFN]], axis=1
        )
        later = jnp.concatenate([gate[:, HALF_FFN:], up[:, HALF_FFN:]], axis=1)
        first = gather_z(first, until=(ffn, place))
        first_a, first_b = first[:, :QK_WIDTH], first[:, QK_WIDTH:]
        first_a, first_b = gather_one(first_a, False), gather_one(first_b, True)
        x_parts = exchange(packed[:3], (first,), (first_a, first_b))
        one = (first_a, first_b)
        first_a, first_b = gather_two(first_a, False), gather_two(first_b, True)
        first = jnp.concatenate([first_a, first_b], axis=1)
        ffn = gather_z_stepwise(ffn, ((), (first,)))
        o_mine, o_near, o_far = hold(tuple(packed[3:6]), *one)
        o_near = swap(o_near, flip_core, (first,))
        o_far = jnp.concatenate([o_far, o_near[SPAN:]], axis=0)
        first_other = swap(first, flip_core)
        ffn_a, ffn_b = ffn[:, :FFN_CUT], ffn[:, FFN_CUT:]

        frequency = np.exp(np.arange(HEAD_WIDTH // 2) * (-2.0 * math.log(10000.0) / HEAD_WIDTH))
        angles = np.arange(rows)[:, None] * frequency[None, :]
        cosine = np.tile(np.cos(angles), (1, 4)).astype(np.float32)
        sine = np.sin(angles)
        sine = np.concatenate([-sine, sine, -sine, sine], axis=1).astype(np.float32)

        padded = jax.ShapeDtypeStruct((2 * KEY_VALUE_HEADS, rows, LANES), bf)
        spans, x, normed, qk, kpad, vpad = call(
            project_kernel,
            [
                jax.ShapeDtypeStruct((n_seq,), jnp.int32),
                model_low,
                model_low,
                shaped(rows, QK_WIDTH, bf),
                padded,
                padded,
            ],
            [*x_parts, gain_one, place, cosine, sine, first, first_other],
            [pltpu.VMEM((MODEL_WIDTH, QK_WIDTH), bf)] * 2,
            5,
            out_specs=[SMEM_SPEC] + [VMEM_SPEC] * 5,
        )
        stats = [shaped(rows, LANES, f4), shaped(rows, 5 * LANES, f4)]
        ffn_a, ffn_b = gather_one(ffn_a, False, (x,)), gather_one(ffn_b, True, (x,))
        later = gather_z_stepwise(hold(later, ffn), ((first,), (x,)))
        lse, attn, merged, middle, normed_two = call(
            attend_kernel,
            [*stats, model_low, model_full, model_low],
            [x, qk, kpad, vpad, gain_two, place, first, first_other],
            [],
            10,
        )
        o_far, second_a, second_b, later_y, later_x, middle = together(
            swap(o_far, flip_y),
            swap(ffn_a, flip_x),
            swap(ffn_b, flip_y),
            swap(later[:, :HALF_FFN], flip_y),
            swap(later[:, HALF_FFN:], flip_x),
            middle,
        )
        o_parts = (o_mine, o_near[:SPAN], o_far)
        ffn = []
        for part, second in ((ffn_a, second_a), (ffn_b, second_b)):
            ffn += [part, second, swap(part, flip_core), swap(second, flip_core)]
        later_a = jnp.concatenate([later[:, :HALF_FFN], later_y], axis=0)
        later_b = jnp.concatenate([later[:, HALF_FFN:], later_x], axis=0)
        weight_scratch = [pltpu.VMEM((MODEL_WIDTH, HALF_FFN), bf)] * 2
        og, result, back, r1, r1_send, dd, w_down = call(
            functools.partial(ffn_first_kernel, order=order, n_seq=n_seq),
            [
                model_low,
                model_full,
                model_full,
                *[shaped(half, 2 * HALF_FFN, bf)] * 2,
                shaped(HALF_FFN, MODEL_WIDTH, bf),
                shaped(HIDDEN_UNITS, MODEL_WIDTH, bf),
            ],
            [spans, *o_parts, normed_two, *ffn],
            weight_scratch,
            10,
            scalars=(0,),
        )
        r1_own = r1
        later = []
        for part, flip in ((later_a, flip_x), (later_b, flip_y)):
            second = swap(part, flip, (og,))
            later += [part, second, swap(part, flip_core, (og,)), swap(second, flip_core)]
        *h_parts, back_middle, gain_two_grad, r2, r2_send = call(
            functools.partial(ffn_second_kernel, order=order, n_seq=n_seq),
            [
                *[shaped(n * SPAN, MODEL_WIDTH, bf) for n in (1, 2, 1)],
                model_full,
                shaped(1, MODEL_WIDTH, f4),
                *[shaped(half, SECOND_WIDTH, bf)] * 2,
            ],
            [spans, og, normed_two, *later, w_down, result, back, dd, middle, gain_two, place],
            weight_scratch
            + [
                pltpu.VMEM((HALF_FFN, MODEL_WIDTH), bf),
                pltpu.VMEM((HIDDEN_UNITS, MODEL_WIDTH), bf),
                pltpu.VMEM((MODEL_WIDTH, DOWN_PITCH), f4),
                pltpu.VMEM((rows, MODEL_WIDTH), f4),
                pltpu.VMEM((rows, MODEL_WIDTH), f4),
            ],
            13,
            scalars=(0,),
            megabytes=18,
        )
        r1 = scatter_core(r1_own, r1_send, (back_middle,))
        r3, r3_send, ab, lse_rows, correction, dqk, dv = call(
            attend_back_first_kernel,
            [
                *[shaped(half + 16, 2 * HALF_FFN, bf)] * 2,
                shaped(rows, 5 * LANES, bf),
                shaped(LANES, rows, f4),
                shaped(16, rows, f4),
                shaped(rows, QK_WIDTH, f4),
                shaped(rows, 2 * LANES, bf),
            ],
            [qk, kpad, vpad, lse, attn, merged, back_middle, place, first, first_other],
            [],
            7,
            after=[r1],
        )
        r2 = scatter_core(r2, r2_send, (ab,))
        h_near = swap(h_parts[1], flip_core, (ab,))
        dqk, dv = call(
            attend_back_second_kernel,
            [shaped(rows, QK_WIDTH, f4), shaped(rows, 2 * LANES, bf)],
            [dqk, dv, qk, kpad, vpad, lse_rows, correction, ab],
            [],
            6,
            after=[r2],
            alias={0: 0, 1: 1},
        )
        p1 = scatter_one(r2[:, :SECOND_CUT], True, (dqk,))
        p2 = scatter_one(r2[:, SECOND_CUT : 2 * SECOND_CUT], False, (dqk,))
        *g_parts, r3, r3_send = call(
            project_back_kernel,
            [
                *[shaped(n * SPAN, MODEL_WIDTH, bf) for n in (1, 2, 1)],
                *[shaped(half + 16, 2 * HALF_FFN, bf)] * 2,
            ],
            [
                r3, r3_send, gain_two_grad, spans, x, normed, dqk, dv, back_middle,
                gain_one, place, cosine, sine, first, first_other,
            ],
            [pltpu.VMEM((rows, QK_WIDTH), bf), pltpu.VMEM((rows, MODEL_WIDTH), f4)],
            5,
            scalars=(3,),
            after=[p1, p2],
            alias={0: 3, 1: 4},
        )
        p1, p2 = scatter_two(p1, True, (r3,)), scatter_two(p2, False, (r3,))
        p3 = scatter_one(r2[:, 2 * SECOND_CUT :], True, (r3,))
        r1 = scatter_one(r1, False, (r3,))
        sent = wide(swap(r3_send, flip_core))
        r3 = wide(r3)
        r1, p3 = scatter_two(r1, False), scatter_two(p3, True)
        total, sums, r1, p1, p2, p3 = together(
            r3[:half] + sent[:half], r3[half:] + sent[half:], r1, p1, p2, p3
        )
        size = half // 4
        r3_a, r3_b = total[:, :QK_WIDTH], total[:, QK_WIDTH:]
        r3_a, sums = scatter_with_sums(
            jnp.concatenate([r3_a[:size], r3_a[2 * size : 3 * size]], axis=0),
            jnp.concatenate([r3_a[size : 2 * size], r3_a[3 * size :]], axis=0),
            sums[:, :QK_WIDTH],
            flip_x,
        )
        r3_b = scatter_one(r3_b, False)
        early = jnp.concatenate([p1, p2, r1], axis=1)
        early = scatter_bit(early, z_bits[-1])
        g_near = swap(g_parts[1], flip_core)
        r3_a, r3_b, sums, early, g_near, h_near = together(
            r3_a, r3_b, sums, early, g_near, h_near
        )
        r3_a, sums = scatter_with_sums(r3_a[:size], r3_a[size:], sums, flip_y)
        r3_b = scatter_two(r3_b, False)
        for bit in z_bits[-2::-1]:
            early = scatter_bit(early, bit)
        h_far = swap(jnp.concatenate([h_parts[2], h_near[SPAN:]], axis=0), flip_y)
        r3_a, r3_b, sums, early, h_far, g_near = together(
            r3_a, r3_b, sums, early, h_far, g_near
        )
        g_far = swap(jnp.concatenate([g_parts[2], g_near[SPAN:]], axis=0), flip_y)
        late = jnp.concatenate([r3_a, r3_b, p3], axis=1)
        late, sums = scatter_z_with_sums(late, sums[:2, :MODEL_WIDTH])
        hidden_out = unpack([h_parts[0], h_near[:SPAN], h_far])
        r1 = early[:, 2 * SECOND_CUT :]
        r2 = jnp.concatenate([early[:, : 2 * SECOND_CUT], late[:, 2 * HALF_FFN :]], axis=1)
        r3 = late
        hidden_grad = unpack([g_parts[0], g_near[:SPAN], g_far])
        gu1 = r2[:, SECOND_GATE_AT:]
        gate_grad = jnp.concatenate([r1[:, :HALF_FFN], gu1[:, :HALF_FFN]], axis=1)
        up_grad = jnp.concatenate([r1[:, HALF_FFN:], gu1[:, HALF_FFN : 2 * HALF_FFN]], axis=1)
        down_grad = r2[:16, :SECOND_GATE_AT].reshape(16, 3, DOWN_PITCH)[:, :, :MODEL_WIDTH]
        return (
            hidden_out,
            hidden_grad,
            sums[:MODEL_WIDTH],
            r3[:, :Q_WIDTH].reshape(-1),
            r3[:, Q_WIDTH:QK_WIDTH].reshape(-1),
            r3[:, QK_WIDTH + MODEL_WIDTH : 2 * HALF_FFN].reshape(-1),
            r3[:, QK_WIDTH : QK_WIDTH + MODEL_WIDTH].reshape(-1),
            sums[MODEL_WIDTH:],
            gate_grad.reshape(-1),
            up_grad.reshape(-1),
            down_grad.swapaxes(0, 1).reshape(-1),
        )

    return on_sequence_device


def pick_plan(mesh):
    count = mesh.shape["dp"] * mesh.shape["seq"]
    fits = (
        mesh.shape["seq"] == MB * SLOTS
        and SLOTS == 1
        and count & (count - 1) == 0
        and MODEL_WIDTH % count == 0
        and (HIDDEN_UNITS // count) % 16 == 0
    )
    return whole_sequence_plan(mesh) if fits else on_device


def solution(mesh):
    return jax.shard_map(
        pick_plan(mesh),
        mesh=mesh,
        in_specs=(
            P(("dp", "seq"), None),
            P(("dp", "seq")),
            P(),
            P(("dp", "seq")),
            P(("dp", "seq")),
            P(("dp", "seq")),
            P(("dp", "seq")),
            P(),
            P(("dp", "seq")),
            P(("dp", "seq")),
            P(("dp", "seq")),
            P(("dp", "seq"), None),
        ),
        out_specs=(
            P(("dp", "seq"), None),
            P(("dp", "seq"), None),
            P(),
            P(("dp", "seq")),
            P(("dp", "seq")),
            P(("dp", "seq")),
            P(("dp", "seq")),
            P(),
            P(("dp", "seq")),
            P(("dp", "seq")),
            P(("dp", "seq")),
        ),
        check_vma=False,
    )
```
